128 devices in a mesh: dp: 16 (over x, z_hi, core), tensor: 8 (over z_lo, y).
Axes of the slice: x: 4, y: 4, z: 4 (z_hi: 2, z_lo: 2; z = z_hi * 2 + z_lo), core: 2. Of those that a mesh axis runs over, the one named last changes fastest.
Arguments:
- queries: bfloat16 [4096, 8192], P('dp', 'tensor'), may hold values from -5 to 5
- keys: bfloat16 [4096, 1024], P('dp', 'tensor'), may hold values from -5 to 5
- values: bfloat16 [4096, 1024], P('dp', 'tensor'), may hold values from -6 to 6
- grad_out: bfloat16 [4096, 8192], P('dp', 'tensor'), may hold values from -6 to 6
- out_weight: bfloat16 [8192, 8192], P('tensor', 'dp'), may hold values from -0.0625 to 0.0625
- lengths: int32 [8], replicated, may hold values from 1 to 2560, 4096 in all
Outputs:
- grad_queries: bfloat16 [4096, 8192], P('dp', 'tensor')
- key_gradient: bfloat16 [4096, 1024], P('dp', 'tensor')
- value_gradient: bfloat16 [4096, 1024], P('dp', 'tensor')
The draws below stay inside these ranges and needn't reach their ends.
All inputs are finite; a program needn't handle non-finite values.
Results may differ from the reference program's by a relative error of at most 0.0083.
Values may be sent and summed in bfloat16 or wider, within the bound.
No kernel may reach another device: no remote copies, remote signals or barrier semaphores. Data moves between devices by JAX's collectives and lax.ppermute only.
A program may use at most 128 MiB of HBM per device.

```python
import math
import jax
import jax.numpy as jnp
import numpy as np
from jax import lax

D = 8192
QUERY_HEAD_COUNT = 64
KEY_VALUE_HEADS = 8
HEAD_WIDTH = 128
NDOCS = 8
PACKED_TOKENS = 4096
MOST = 2560


def draw_keys(key, part):
    key = jax.random.fold_in(key, 1)
    return jnp.clip(jax.random.normal(key, (PACKED_TOKENS, KEY_VALUE_HEADS * HEAD_WIDTH), jnp.float32), -5.0, 5.0).astype(jnp.bfloat16)


def draw_queries(key, part):
    key = jax.random.fold_in(key, 2)
    return jnp.clip(jax.random.normal(key, (PACKED_TOKENS, QUERY_HEAD_COUNT * HEAD_WIDTH), jnp.float32), -5.0, 5.0).astype(jnp.bfloat16)


def steps_of(stream_key, shape, cuts, low, high):
    level, own = 1.0, jax.random.fold_in(stream_key, 6)
    for dim, parts in cuts:
        draws = jnp.exp(jax.random.uniform(jax.random.fold_in(own, dim), (parts,), jnp.float32, low / len(cuts), high / len(cuts)))
        level = level * jnp.repeat(draws, shape[dim] // parts).reshape([-1 if axis == dim else 1 for axis in range(len(shape))])
    return level


def split_up(count, total, bound, lean):
    weights = [(1 << 20) // math.isqrt(rank ** lean) + 1 for rank in range(2, count + 1)]
    surplus, given = total - bound - (count - 1), [1] * (count - 1)
    while surplus > 0:
        free = [i for i in range(count - 1) if given[i] < bound]
        pool, left = sum([weights[i] for i in free]), surplus
        for i in free:
            extra = min(bound - given[i], max(1, left * weights[i] // pool), surplus)
            given[i] = given[i] + extra
            surplus = surplus - extra
    return np.array([bound] + given)


def ragged(key, amount, total, reach, slope):
    if amount == 2:
        one = jax.random.randint(key, (), max(1, total - reach), min(reach, total - 1) + 1)
        return jnp.stack([one, total - one])
    tallies = jnp.asarray(split_up(amount, total, reach, slope), jnp.int32)
    couples = (amount - 1) // 2
    donor, taker = tallies[1:1 + 2 * couples:2], tallies[2:2 + 2 * couples:2]
    margin = jnp.minimum(donor - 1, reach - taker)
    moved = jax.random.randint(jax.random.fold_in(key, 1), (couples,), 0, 1 << 20) % (margin + 1)
    tallies = tallies.at[1:1 + 2 * couples:2].set(donor - moved).at[2:2 + 2 * couples:2].set(taker + moved)
    return tallies[jax.random.permutation(jax.random.fold_in(key, 2), amount)]


def normal_values(key, dims, scale, most, split=(), kind=jnp.bfloat16):
    drawn = scale * jax.random.normal(key, dims, jnp.float32)
    if split:
        drawn = drawn * steps_of(key, dims, split, -0.22, 0.18)
    return jnp.clip(drawn, -most, most).astype(kind)


def setup_inputs(seed: int = 0) -> dict:
    key_list = jax.random.split(jax.random.key(seed), 7)
    queries = draw_queries(jax.random.fold_in(key_list[6], 71), 0)
    keys = draw_keys(jax.random.fold_in(key_list[6], 71), 0)
    values = normal_values(key_list[2], (PACKED_TOKENS, KEY_VALUE_HEADS * HEAD_WIDTH), 1.0, 6.0, ((0, 16), (1, 8)))
    grad_out = normal_values(key_list[3], (PACKED_TOKENS, D), 1.0, 6.0, ((0, 16), (1, 8)))
    out_weight = normal_values(key_list[4], (QUERY_HEAD_COUNT * HEAD_WIDTH, D), D ** -0.5, 0.0625, ((0, 8), (1, 16)))
    lengths = ragged(key_list[5], NDOCS, PACKED_TOKENS, MOST, 2).astype(jnp.int32)
    return {"queries": queries, "keys": keys, "values": values, "grad_out": grad_out, "out_weight": out_weight, "lengths": lengths}


def doc_index(lengths, positions):
    bounds = jnp.cumsum(lengths)[:-1]
    return lax.optimization_barrier(jnp.sum((bounds[None, :] <= positions[:, None]).astype(jnp.int32), axis=1))

def reference(queries, keys, values, grad_out, out_weight, lengths):
    scale_factor = 1.0 / math.sqrt(HEAD_WIDTH)
    group_index = QUERY_HEAD_COUNT // KEY_VALUE_HEADS
    gradient_heads = jnp.dot(grad_out, out_weight.T, preferred_element_type=jnp.float32).astype(jnp.bfloat16)
    query_block = min(512, PACKED_TOKENS)
    positions = jnp.arange(PACKED_TOKENS, dtype=jnp.int32)
    docs = doc_index(lengths, positions)
    grouped_queries = queries.reshape(PACKED_TOKENS, KEY_VALUE_HEADS, group_index, HEAD_WIDTH).transpose(1, 0, 2, 3)
    gradient_groups = gradient_heads.reshape(PACKED_TOKENS, KEY_VALUE_HEADS, group_index, HEAD_WIDTH).transpose(1, 0, 2, 3)
    grouped_keys = keys.reshape(PACKED_TOKENS, KEY_VALUE_HEADS, HEAD_WIDTH).transpose(1, 0, 2)
    grouped_values = values.reshape(PACKED_TOKENS, KEY_VALUE_HEADS, HEAD_WIDTH).transpose(1, 0, 2)

    def one_group(items):
        query_rows, key_rows, value_rows, grad_rows = items
        key_float = key_rows.astype(jnp.float32)
        value_float = value_rows.astype(jnp.float32)

        def one_block(carry, index):
            key_sum, value_sum = carry
            start = (index * query_block).astype(jnp.int32)
            query_here = lax.dynamic_slice_in_dim(query_rows, start, query_block, 0).astype(jnp.float32)
            grad_here = lax.dynamic_slice_in_dim(grad_rows, start, query_block, 0).astype(jnp.float32)
            query_pos = start + jnp.arange(query_block, dtype=jnp.int32)
            query_docs = lax.dynamic_slice_in_dim(docs, start, query_block, 0)
            live = (query_docs[:, None] == docs[None, :]) & (positions[None, :] <= query_pos[:, None])
            score = scale_factor * jnp.einsum('tcd,ud->ctu', query_here, key_float)
            lse = jax.nn.logsumexp(jnp.where(live, score, -jnp.inf), axis=-1)
            probs = jnp.where(live, jnp.exp(score - lse[..., None]), 0.0)
            dprob = jnp.einsum('tcd,ud->ctu', grad_here, value_float)
            delta = lax.optimization_barrier(jnp.sum(probs * dprob, axis=-1))
            dscore = (probs * (dprob - delta[..., None])).astype(jnp.bfloat16)
            dscore = lax.optimization_barrier(dscore).astype(jnp.float32)
            probs_b = lax.optimization_barrier(probs.astype(jnp.bfloat16)).astype(jnp.float32)
            grad_q = (scale_factor * jnp.einsum('ctu,ud->tcd', dscore, key_float)).astype(jnp.bfloat16)
            key_sum = key_sum + scale_factor * jnp.einsum('ctu,tcd->ud', dscore, query_here)
            value_sum = value_sum + jnp.einsum('ctu,tcd->ud', probs_b, grad_here)
            return ((key_sum, value_sum), grad_q)
        init = (jnp.zeros((PACKED_TOKENS, HEAD_WIDTH), jnp.float32), jnp.zeros((PACKED_TOKENS, HEAD_WIDTH), jnp.float32))
        sums, grad_blocks = lax.scan(one_block, init, jnp.arange(PACKED_TOKENS // query_block, dtype=jnp.int32))
        return (grad_blocks.reshape(PACKED_TOKENS, group_index, HEAD_WIDTH), sums[0].astype(jnp.bfloat16), sums[1].astype(jnp.bfloat16))
    grad_q_groups, key_gradient_groups, value_gradient_groups = lax.map(one_group, (grouped_queries, grouped_keys, grouped_values, gradient_groups))
    grad_queries = grad_q_groups.transpose(1, 0, 2, 3).reshape(PACKED_TOKENS, QUERY_HEAD_COUNT * HEAD_WIDTH)
    key_gradient = key_gradient_groups.transpose(1, 0, 2).reshape(PACKED_TOKENS, KEY_VALUE_HEADS * HEAD_WIDTH)
    value_gradient = value_gradient_groups.transpose(1, 0, 2).reshape(PACKED_TOKENS, KEY_VALUE_HEADS * HEAD_WIDTH)
    return (grad_queries, key_gradient, value_gradient)
```

```python
import functools
import math

import jax
import jax.numpy as jnp
from jax import lax
from jax.experimental import pallas as pl
from jax.experimental.pallas import tpu as pltpu
from jax.sharding import PartitionSpec as P

HEAD_WIDTH = 128
KEY_BLOCK = 256
MOST = 2560
CHUNKS = 2
MASKED = -1e30
SCALE = 1.0 / math.sqrt(HEAD_WIDTH)
BF16 = jnp.bfloat16
F32 = jnp.float32


def dp_move(value, dx, dz, dc):
    pairs = []
    for x in range(4):
        for z in range(2):
            for c in range(2):
                target = ((x + dx) % 4) * 4 + ((z + dz) % 2) * 2 + (c + dc) % 2
                pairs.append((x * 4 + z * 2 + c, target))
    return lax.ppermute(value, "dp", pairs)


def dot(left, right):
    return lax.dot_general(left, right, (((1,), (0,)), ((), ())), preferred_element_type=F32)


def forward_kernel(
    range_ref, pos_ref, start_ref, q_ref, k_ref, v_ref, probs_ref, out_ref, score, vt
):
    head = pl.program_id(0)
    first = range_ref[0]
    count = range_ref[1]
    rows = q_ref.shape[0]
    query_t = q_ref[...].T
    query_pos = pos_ref[...]
    query_start = start_ref[...]

    @pl.when(head == 0)
    def _():
        def turn(index, _):
            at = pl.multiple_of((first + index) * KEY_BLOCK, KEY_BLOCK)
            vt[:, pl.ds(at, KEY_BLOCK)] = v_ref[pl.ds(at, KEY_BLOCK), :].T
            return 0

        lax.fori_loop(0, count, turn, 0)

    def score_step(index, top):
        at = pl.multiple_of((first + index) * KEY_BLOCK, KEY_BLOCK)
        raw = dot(k_ref[pl.ds(at, KEY_BLOCK), :], query_t)
        key_pos = at + lax.broadcasted_iota(jnp.int32, (KEY_BLOCK, rows), 0)
        live = (key_pos >= query_start) & (key_pos <= query_pos)
        raw = jnp.where(live, raw, MASKED)
        score[pl.ds(at, KEY_BLOCK), :] = raw
        return jnp.maximum(top, jnp.max(raw, axis=0, keepdims=True))

    top = lax.fori_loop(0, count, score_step, jnp.full((1, rows), MASKED, F32))

    def mass_step(index, mass):
        at = pl.multiple_of((first + index) * KEY_BLOCK, KEY_BLOCK)
        weights = jnp.exp((score[pl.ds(at, KEY_BLOCK), :] - top) * SCALE)
        score[pl.ds(at, KEY_BLOCK), :] = weights
        return mass + jnp.sum(weights, axis=0, keepdims=True)

    mass = lax.fori_loop(0, count, mass_step, jnp.zeros((1, rows), F32))
    share = 1.0 / mass

    def probs_step(index, total):
        at = pl.multiple_of((first + index) * KEY_BLOCK, KEY_BLOCK)
        probs = (score[pl.ds(at, KEY_BLOCK), :] * share).astype(BF16)
        probs_ref[pl.ds(at, KEY_BLOCK), :] = probs
        return total + dot(vt[:, pl.ds(at, KEY_BLOCK)], probs)

    out_ref[...] = lax.fori_loop(0, count, probs_step, jnp.zeros((HEAD_WIDTH, rows), F32))


def forward(live_range, query_pos, query_start, queries, keys_all, values_all):
    rows, width = queries.shape
    heads = width // HEAD_WIDTH
    total = keys_all.shape[0]
    whole = pl.BlockSpec((total, HEAD_WIDTH), lambda h, r: (0, 0))
    line = pl.BlockSpec((1, rows), lambda h, r: (0, 0))
    return pl.pallas_call(
        forward_kernel,
        grid_spec=pltpu.PrefetchScalarGridSpec(
            num_scalar_prefetch=1,
            grid=(heads,),
            in_specs=[line, line, pl.BlockSpec((rows, HEAD_WIDTH), lambda h, r: (0, h)), whole, whole],
            out_specs=[
                pl.BlockSpec((total, rows), lambda h, r: (0, h)),
                pl.BlockSpec((HEAD_WIDTH, rows), lambda h, r: (0, h)),
            ],
            scratch_shapes=[
                pltpu.VMEM((total, rows), F32),
                pltpu.VMEM((HEAD_WIDTH, total), BF16),
            ],
        ),
        out_shape=[
            jax.ShapeDtypeStruct((total, heads * rows), BF16),
            jax.ShapeDtypeStruct((HEAD_WIDTH, heads * rows), F32),
        ],
        compiler_params=pltpu.CompilerParams(vmem_limit_bytes=40 * 2**20),
        cost_estimate=pl.CostEstimate(
            flops=6 * rows * heads * 1024 * HEAD_WIDTH * 8, bytes_accessed=20 * 2**20, transcendentals=0
        ),
        name="forward",
    )(live_range, query_pos, query_start, queries, keys_all, values_all)


def backward_kernel(
    heads, range_ref, probs_ref, out_ref, grad_ref, q_ref, k_ref, v_ref, *rest
):
    if len(rest) == 8:
        old_k_ref, old_v_ref, gq_ref, gk_ref, gv_ref, grad_t, delta, total_q = rest
    else:
        gq_ref, gk_ref, gv_ref, grad_t, delta, total_q = rest
        old_k_ref = old_v_ref = None
    step = pl.program_id(0)
    rows = q_ref.shape[0]

    @pl.when(step == 0)
    def _():
        if old_k_ref is None:
            gk_ref[...] = jnp.zeros_like(gk_ref)
            gv_ref[...] = jnp.zeros_like(gv_ref)
        else:
            gk_ref[...] = old_k_ref[...]
            gv_ref[...] = old_v_ref[...]
        total_q[...] = jnp.zeros_like(total_q)
        for h in range(heads):
            at = h * rows
            turned = grad_ref[:, h * HEAD_WIDTH : (h + 1) * HEAD_WIDTH].T
            grad_t[:, at : at + rows] = turned
            delta[:, at : at + rows] = jnp.sum(
                turned.astype(F32) * out_ref[:, at : at + rows], axis=0, keepdims=True
            )

    @pl.when(step < range_ref[1])
    def _():
        at = pl.multiple_of((range_ref[0] + step) * KEY_BLOCK, KEY_BLOCK)
        values = v_ref[...]
        keys_t = k_ref[...].T
        key_sum = jnp.zeros((KEY_BLOCK, HEAD_WIDTH), F32)
        value_sum = jnp.zeros((KEY_BLOCK, HEAD_WIDTH), F32)
        for h in range(heads):
            cols = slice(h * rows, (h + 1) * rows)
            wide = slice(h * HEAD_WIDTH, (h + 1) * HEAD_WIDTH)
            probs = probs_ref[:, cols]
            dprob = dot(values, grad_t[:, cols])
            dscore = (probs.astype(F32) * (dprob - delta[:, cols])).astype(BF16)
            value_sum = value_sum + dot(probs, grad_ref[:, wide])
            key_sum = key_sum + dot(dscore, q_ref[:, wide])
            total_q[:, cols] += dot(keys_t, dscore)
        gk_ref[pl.ds(at, KEY_BLOCK), :] += key_sum * SCALE
        gv_ref[pl.ds(at, KEY_BLOCK), :] += value_sum

    @pl.when(step == range_ref[1] - 1)
    def _():
        for h in range(heads):
            cols = slice(h * rows, (h + 1) * rows)
            wide = slice(h * HEAD_WIDTH, (h + 1) * HEAD_WIDTH)
            gq_ref[:, wide] = (total_q[:, cols].T * SCALE).astype(BF16)


def backward(live_range, part, parts, probs, outs, grads, queries, keys_all, values_all, sums):
    rows, width = queries.shape
    heads = width // HEAD_WIDTH // parts
    total = keys_all.shape[0]
    steps = (MOST + rows - 2) // KEY_BLOCK + 1

    def block(i, r):
        return r[0] + jnp.minimum(i, r[1] - 1)

    key_spec = pl.BlockSpec((KEY_BLOCK, HEAD_WIDTH), lambda i, r: (block(i, r), 0))
    sum_spec = pl.BlockSpec((total, HEAD_WIDTH), lambda i, r: (0, 0))
    return pl.pallas_call(
        functools.partial(backward_kernel, heads),
        grid_spec=pltpu.PrefetchScalarGridSpec(
            num_scalar_prefetch=1,
            grid=(steps,),
            in_specs=[
                pl.BlockSpec((KEY_BLOCK, heads * rows), lambda i, r: (block(i, r), part)),
                pl.BlockSpec((HEAD_WIDTH, heads * rows), lambda i, r: (0, part)),
                pl.BlockSpec((rows, heads * HEAD_WIDTH), lambda i, r: (0, 0)),
                pl.BlockSpec((rows, heads * HEAD_WIDTH), lambda i, r: (0, part)),
                key_spec,
                key_spec,
            ]
            + [sum_spec] * len(sums),
            out_specs=[
                pl.BlockSpec((rows, heads * HEAD_WIDTH), lambda i, r: (0, 0)),
                sum_spec,
                sum_spec,
            ],
            scratch_shapes=[
                pltpu.VMEM((HEAD_WIDTH, heads * rows), BF16),
                pltpu.VMEM((1, heads * rows), F32),
                pltpu.VMEM((HEAD_WIDTH, heads * rows), F32),
            ],
        ),
        out_shape=[
            jax.ShapeDtypeStruct((rows, heads * HEAD_WIDTH), BF16),
            jax.ShapeDtypeStruct((total, HEAD_WIDTH), F32),
            jax.ShapeDtypeStruct((total, HEAD_WIDTH), F32),
        ],
        compiler_params=pltpu.CompilerParams(vmem_limit_bytes=40 * 2**20),
        cost_estimate=pl.CostEstimate(
            flops=8 * rows * heads * 1024 * HEAD_WIDTH * 4, bytes_accessed=10 * 2**20, transcendentals=0
        ),
        name="backward%d" % part,
    )(live_range, probs, outs, grads, queries, keys_all, values_all, *sums)


def by_core(core, mine_at_zero, mine_at_one):
    return jnp.where(core == 0, mine_at_zero, mine_at_one)


def gather_keys_values(keys, values, core, rank):
    rows = keys.shape[0]
    kept = by_core(core, keys, values)
    got = dp_move(by_core(core, values, keys), 0, 0, 1)
    chip = jnp.concatenate([by_core(core, kept, got), by_core(core, got, kept)], axis=0)
    pair = dp_move(chip, 0, 1, 0)
    x, z = rank // 4, (rank // 2) % 2
    near = jnp.concatenate([jnp.where(z == 0, chip, pair), jnp.where(z == 0, pair, chip)], axis=0)
    left = dp_move(near, 1, 0, 0)
    right = dp_move(near, -1, 0, 0)
    half = near.shape[0] // 2
    far = jnp.concatenate(
        [dp_move(left[:half], 1, 0, 0), dp_move(right[half:], -1, 0, 0)], axis=0
    )
    ring = jnp.stack([near, right, far, left])
    order = (jnp.arange(4, dtype=jnp.int32) - x) % 4
    mine = jnp.concatenate(
        [lax.dynamic_index_in_dim(ring, order[i], 0, keepdims=False) for i in range(4)], axis=0
    )
    other = dp_move(mine, 0, 0, 1)
    return by_core(core, mine, other), by_core(core, other, mine)


def gather_weight(block):
    found = []
    for start, dz in ((block, 0), (dp_move(block, 0, 1, 0), 1)):
        left = dp_move(start, 1, 0, 0)
        right = dp_move(start, -1, 0, 0)
        half = start.shape[0] // 2
        far = jnp.concatenate(
            [dp_move(left[:half], 1, 0, 0), dp_move(right[half:], -1, 0, 0)], axis=0
        )
        found += [(start, 0, dz), (left, 3, dz), (right, 1, dz), (far, 2, dz)]
    return found


def local(queries, keys, values, grad_out, out_weight, lengths):
    rows = queries.shape[0]
    rank = lax.axis_index("dp")
    core = rank % 2
    x, z = rank // 4, (rank // 2) % 2

    query_pos = rank * rows + jnp.arange(rows, dtype=jnp.int32)
    ends = jnp.cumsum(lengths)[:-1]
    query_start = jnp.max(
        jnp.where(ends[None, :] <= query_pos[:, None], ends[None, :], 0), axis=1
    )
    first = query_start[0] // KEY_BLOCK
    last = query_pos[-1] // KEY_BLOCK
    live_range = jnp.stack([first, last - first + 1]).astype(jnp.int32)

    depth = out_weight.shape[1]
    halves = grad_out.reshape(rows, 2, depth)
    mine = lax.dynamic_index_in_dim(halves, core, 1, keepdims=False)
    other = lax.dynamic_index_in_dim(halves, 1 - core, 1, keepdims=False)
    chip_grad = jnp.concatenate([mine, dp_move(other, 0, 0, 1)], axis=0)
    all_grad = lax.all_gather(chip_grad, "tensor", axis=0, tiled=False)

    keys_all, values_all = gather_keys_values(keys, values, core, rank)
    probs, outs = forward(
        live_range, query_pos[None, :], query_start[None, :], queries, keys_all, values_all
    )

    features = out_weight.shape[0] // CHUNKS
    sums = ()
    grad_queries = []
    for part in range(CHUNKS):
        total = jnp.zeros((2 * rows, features), F32)
        for block, dx, dz in gather_weight(out_weight[part * features : (part + 1) * features]):
            source = 2 * ((x + dx) % 4) + (z + dz) % 2
            piece = lax.dynamic_index_in_dim(all_grad, source, 0, keepdims=False)
            total = total + lax.dot_general(
                piece, block, (((1,), (1,)), ((), ())), preferred_element_type=F32
            )
        grads = (total[:rows] + dp_move(total[rows:], 0, 0, 1)).astype(BF16)
        grad_q, *sums = backward(
            live_range, part, CHUNKS, probs, outs, grads, queries, keys_all, values_all, sums
        )
        grad_queries.append(grad_q)
    grad_queries = jnp.concatenate(grad_queries, axis=1)

    key_terms, value_terms = sums
    kept = by_core(core, key_terms, value_terms)
    got = dp_move(by_core(core, value_terms, key_terms), 0, 0, 1)
    chip_terms = (kept + got).astype(BF16).reshape(8, 2 * rows, HEAD_WIDTH)
    groups = [[2 * i + c for i in range(8)] for c in range(2)]
    terms = lax.all_to_all(
        chip_terms, "dp", 0, 0, axis_index_groups=groups, tiled=True
    )
    done = jnp.sum(terms.astype(F32), axis=0).astype(BF16)
    upper, lower = done[:rows], done[rows:]
    kept = by_core(core, upper, lower)
    got = dp_move(by_core(core, lower, upper), 0, 0, 1)
    return grad_queries, by_core(core, kept, got), by_core(core, got, kept)


def solution(mesh):
    return jax.shard_map(
        local,
        mesh=mesh,
        in_specs=(
            P("dp", "tensor"),
            P("dp", "tensor"),
            P("dp", "tensor"),
            P("dp", "tensor"),
            P("tensor", "dp"),
            P(),
        ),
        out_specs=(P("dp", "tensor"), P("dp", "tensor"), P("dp", "tensor")),
        check_vma=False,
    )
```

```python
import functools
import math

import jax
import jax.numpy as jnp
from jax import lax
from jax.experimental import pallas as pl
from jax.experimental.pallas import tpu as pltpu
from jax.sharding import PartitionSpec as P

HEAD_WIDTH = 128
KEY_BLOCK = 256
MOST = 2560
CHUNKS = 2
PIECES = 4
MASKED = -1e30
SCALE = 1.0 / math.sqrt(HEAD_WIDTH)
LOG2E = 1.0 / math.log(2.0)
BF16 = jnp.bfloat16
F32 = jnp.float32
VMEM_LIMIT = 48 * 2**20

FIRST, COUNT, CLEAR, CORE, TABLE = 0, 1, 2, 3, 4


def dp_move(value, dx, dz, dc):
    pairs = []
    for x in range(4):
        for z in range(2):
            for c in range(2):
                target = ((x + dx) % 4) * 4 + ((z + dz) % 2) * 2 + (c + dc) % 2
                pairs.append((x * 4 + z * 2 + c, target))
    return lax.ppermute(value, "dp", pairs)


def after(value, *others):
    return lax.optimization_barrier((value, *others))[0]


def dot(left, right):
    return lax.dot_general(left, right, (((1,), (0,)), ((), ())), preferred_element_type=F32)


def dot_t(left, right):
    return lax.dot_general(left, right, (((1,), (1,)), ((), ())), preferred_element_type=F32)


def block_rows(index):
    return pl.ds(pl.multiple_of(index * KEY_BLOCK, KEY_BLOCK), KEY_BLOCK)


def forward_kernel(info, pos_ref, start_ref, q_ref, kv_ref, probs_ref, out_ref, score, vt):
    first, count = info[FIRST], info[COUNT]
    rows = q_ref.shape[0]
    query_t = q_ref[...].T

    @pl.when(pl.program_id(0) == 0)
    def _():
        def turn(index, _):
            source = info[TABLE + 16 + first + index]
            vt[:, block_rows(index)] = kv_ref[block_rows(source), :].T
            return 0

        lax.fori_loop(0, count, turn, 0)

    def product(index):
        return dot(kv_ref[block_rows(info[TABLE + first + index]), :], query_t)

    def masked_step(index, top):
        key_pos = (first + index) * KEY_BLOCK + lax.broadcasted_iota(jnp.int32, (KEY_BLOCK, rows), 0)
        live = (key_pos >= start_ref[...]) & (key_pos <= pos_ref[...])
        raw = jnp.where(live, product(index), MASKED)
        score[block_rows(index), :] = raw
        return jnp.maximum(top, jnp.max(raw, axis=0, keepdims=True))

    def clear_step(index, top):
        raw = product(index)
        score[block_rows(index), :] = raw
        return jnp.maximum(top, jnp.max(raw, axis=0, keepdims=True))

    clear = jnp.minimum(info[CLEAR] - first, count - 1)
    top = jnp.full((1, rows), MASKED, F32)
    top = lax.fori_loop(0, clear, masked_step, top)
    top = lax.fori_loop(clear, count - 1, clear_step, top)
    top = masked_step(count - 1, top)

    def mass_step(index, mass):
        weights = jnp.exp2((score[block_rows(index), :] - top) * (SCALE * LOG2E))
        score[block_rows(index), :] = weights
        return mass + jnp.sum(weights, axis=0, keepdims=True)

    mass = lax.fori_loop(0, count, mass_step, jnp.zeros((1, rows), F32))
    share = 1.0 / mass

    def probs_step(index, total):
        probs = (score[block_rows(index), :] * share).astype(BF16)
        probs_ref[block_rows(index), :] = probs
        return total + dot(vt[:, block_rows(index)], probs)

    out_ref[...] = lax.fori_loop(0, count, probs_step, jnp.zeros((HEAD_WIDTH, rows), F32))


def most_blocks(rows):
    return (MOST + rows - 2) // KEY_BLOCK + 1


def forward(part, info, query_pos, query_start, queries, kv):
    rows, width = queries.shape
    heads = width // HEAD_WIDTH // CHUNKS
    live = most_blocks(rows) * KEY_BLOCK
    line = pl.BlockSpec((1, rows), lambda h, r: (0, 0))
    return pl.pallas_call(
        forward_kernel,
        grid_spec=pltpu.PrefetchScalarGridSpec(
            num_scalar_prefetch=1,
            grid=(heads,),
            in_specs=[
                line,
                line,
                pl.BlockSpec((rows, HEAD_WIDTH), lambda h, r: (0, part * heads + h)),
                pl.BlockSpec(kv.shape, lambda h, r: (0, 0)),
            ],
            out_specs=[
                pl.BlockSpec((live, rows), lambda h, r: (0, h)),
                pl.BlockSpec((HEAD_WIDTH, rows), lambda h, r: (0, h)),
            ],
            scratch_shapes=[
                pltpu.VMEM((live, rows), F32),
                pltpu.VMEM((HEAD_WIDTH, live), BF16),
            ],
        ),
        out_shape=[
            jax.ShapeDtypeStruct((live, heads * rows), BF16),
            jax.ShapeDtypeStruct((HEAD_WIDTH, heads * rows), F32),
        ],
        compiler_params=pltpu.CompilerParams(vmem_limit_bytes=VMEM_LIMIT),
        cost_estimate=pl.CostEstimate(
            flops=16 * 10**9, bytes_accessed=10 * 2**20, transcendentals=0
        ),
        name="forward%d" % part,
    )(info, query_pos, query_start, queries, kv)


def backward_kernel(heads, part, info, probs_ref, out_ref, grad_ref, q_ref, k_ref, v_ref, *rest):
    if part:
        old_own, old_other, _, gq_ref, own_ref, other_ref, grad_t, delta, total_q, other = rest
    else:
        gq_ref, own_ref, other_ref, grad_t, delta, total_q = rest
        other = other_ref
    step = pl.program_id(0)
    count = info[COUNT]
    rows = q_ref.shape[0]

    @pl.when(step == 0)
    def _():
        if part:
            own_ref[...] = old_own[...]
            other[...] = old_other[...]
        else:
            own_ref[...] = jnp.zeros_like(own_ref)
            other[...] = jnp.zeros_like(other)
        total_q[...] = jnp.zeros_like(total_q)
        for h in range(heads):
            cols = slice(h * rows, (h + 1) * rows)
            turned = grad_ref[:, h * HEAD_WIDTH : (h + 1) * HEAD_WIDTH].T
            grad_t[:, cols] = turned
            delta[:, cols] = jnp.sum(turned.astype(F32) * out_ref[:, cols], axis=0, keepdims=True)

    @pl.when(step < count)
    def _():
        block = info[FIRST] + step
        values = v_ref[...]
        keys_t = k_ref[...].T
        key_sum = jnp.zeros((KEY_BLOCK, HEAD_WIDTH), F32)
        value_sum = jnp.zeros((KEY_BLOCK, HEAD_WIDTH), F32)
        for h in range(heads):
            cols = slice(h * rows, (h + 1) * rows)
            wide = slice(h * HEAD_WIDTH, (h + 1) * HEAD_WIDTH)
            probs = probs_ref[:, cols]
            dprob = dot(values, grad_t[:, cols])
            dscore = (probs.astype(F32) * (dprob - delta[:, cols])).astype(BF16)
            value_sum = value_sum + dot(probs, grad_ref[:, wide])
            key_sum = key_sum + dot(dscore, q_ref[:, wide])
            total_q[:, cols] += dot(keys_t, dscore)

        def add(ref):
            ref[block // 2, :, :HEAD_WIDTH] += key_sum * SCALE
            ref[block // 2, :, HEAD_WIDTH:] += value_sum

        pl.when(block % 2 == info[CORE])(lambda: add(own_ref))
        pl.when(block % 2 != info[CORE])(lambda: add(other))

    @pl.when(step == count - 1)
    def _():
        for h in range(heads):
            cols = slice(h * rows, (h + 1) * rows)
            wide = slice(h * HEAD_WIDTH, (h + 1) * HEAD_WIDTH)
            gq_ref[:, wide] = (total_q[:, cols].T * SCALE).astype(BF16)
        if part:
            other_ref[...] = other[...].astype(BF16)


def backward(part, info, probs, outs, grads, queries, kv, carried):
    rows, width = queries.shape
    heads = width // HEAD_WIDTH // CHUNKS
    last = part == CHUNKS - 1
    sums = (8, KEY_BLOCK, 2 * HEAD_WIDTH)

    def near(i, r):
        return jnp.minimum(i, r[COUNT] - 1)

    sum_spec = pl.BlockSpec(sums, lambda i, r: (0, 0, 0))
    gq_spec = pl.BlockSpec((rows, heads * HEAD_WIDTH), lambda i, r: (0, part))
    scratch = [
        pltpu.VMEM((HEAD_WIDTH, heads * rows), BF16),
        pltpu.VMEM((1, heads * rows), F32),
        pltpu.VMEM((HEAD_WIDTH, heads * rows), F32),
    ]
    in_specs = [
        pl.BlockSpec((KEY_BLOCK, heads * rows), lambda i, r: (near(i, r), 0)),
        pl.BlockSpec((HEAD_WIDTH, heads * rows), lambda i, r: (0, 0)),
        pl.BlockSpec((rows, heads * HEAD_WIDTH), lambda i, r: (0, 0)),
        pl.BlockSpec((rows, heads * HEAD_WIDTH), lambda i, r: (0, part)),
        pl.BlockSpec((KEY_BLOCK, HEAD_WIDTH), lambda i, r: (r[TABLE + r[FIRST] + near(i, r)], 0)),
        pl.BlockSpec(
            (KEY_BLOCK, HEAD_WIDTH), lambda i, r: (r[TABLE + 16 + r[FIRST] + near(i, r)], 0)
        ),
    ]
    aliases = {}
    if part:
        in_specs += [sum_spec, sum_spec, pl.BlockSpec(memory_space=pl.ANY)]
        scratch.append(pltpu.VMEM(sums, F32))
        aliases = {9: 0}
    return pl.pallas_call(
        functools.partial(backward_kernel, heads, part),
        grid_spec=pltpu.PrefetchScalarGridSpec(
            num_scalar_prefetch=1,
            grid=(most_blocks(rows),),
            in_specs=in_specs,
            out_specs=[gq_spec, sum_spec, sum_spec],
            scratch_shapes=scratch,
        ),
        out_shape=[
            jax.ShapeDtypeStruct((rows, width), BF16),
            jax.ShapeDtypeStruct(sums, F32),
            jax.ShapeDtypeStruct(sums, BF16 if last else F32),
        ],
        input_output_aliases=aliases,
        compiler_params=pltpu.CompilerParams(vmem_limit_bytes=VMEM_LIMIT),
        cost_estimate=pl.CostEstimate(
            flops=8 * 10**9, bytes_accessed=10 * 2**20, transcendentals=0
        ),
        name="backward%d" % part,
    )(info, probs, outs, grads, queries, kv, kv, *carried)


def project_kernel(pieces, source, grad_ref, *rest):
    weights, (own_ref, other_ref, grad, weight, grad_sem, weight_sem) = rest[:-6], rest[-6:]
    chips = len(weights) // pieces
    part_rows = weights[0].shape[0]
    copies = []
    for i in range(chips):
        one = [pltpu.make_async_copy(grad_ref.at[source[i]], grad.at[i], grad_sem.at[i])]
        for j in range(pieces):
            k = i * pieces + j
            rows = pl.ds(j * part_rows, part_rows)
            one.append(pltpu.make_async_copy(weights[k], weight.at[i, rows], weight_sem.at[k]))
        for copy in one:
            copy.start()
        copies.append(one)
    half = own_ref.shape[0]
    for i in range(chips):
        for copy in copies[i]:
            copy.wait()
        for ref, at in ((own_ref, 0), (other_ref, half)):
            term = dot_t(grad[i, at : at + half, :], weight[i])
            if i == 0:
                ref[...] = term
            else:
                ref[...] += term


def project(part, source, all_grad, weights):
    chips, tokens, depth = all_grad.shape
    pieces = len(weights[0])
    features = pieces * weights[0][0].shape[0]
    flat = [piece for chip in weights for piece in chip]
    half = jax.ShapeDtypeStruct((tokens // 2, features), F32)
    return pl.pallas_call(
        functools.partial(project_kernel, pieces),
        in_specs=[pl.BlockSpec(memory_space=pltpu.SMEM)]
        + [pl.BlockSpec(memory_space=pl.ANY)] * (1 + len(flat)),
        out_specs=[pl.BlockSpec(memory_space=pltpu.VMEM)] * 2,
        out_shape=[half, half],
        scratch_shapes=[
            pltpu.VMEM((chips, tokens, depth), BF16),
            pltpu.VMEM((chips, features, depth), BF16),
            pltpu.SemaphoreType.DMA((chips,)),
            pltpu.SemaphoreType.DMA((chips * pieces,)),
        ],
        compiler_params=pltpu.CompilerParams(vmem_limit_bytes=VMEM_LIMIT),
        cost_estimate=pl.CostEstimate(
            flops=2 * tokens * features * depth * chips,
            bytes_accessed=12 * 2**20,
            transcendentals=0,
        ),
        name="project%d" % part,
    )(source, all_grad, *flat)


def local(queries, keys, values, grad_out, out_weight, lengths):
    rows = queries.shape[0]
    rank = lax.axis_index("dp")
    core = rank % 2
    x, z = rank // 4, (rank // 2) % 2

    query_pos = rank * rows + jnp.arange(rows, dtype=jnp.int32)
    ends = jnp.cumsum(lengths)[:-1]
    query_start = jnp.max(
        jnp.where(ends[None, :] <= query_pos[:, None], ends[None, :], 0), axis=1
    )
    first = query_start[0] // KEY_BLOCK
    last = query_pos[-1] // KEY_BLOCK
    clear = (query_start[-1] + KEY_BLOCK - 1) // KEY_BLOCK
    block = jnp.arange(16, dtype=jnp.int32)
    distance = (block // 4 - x) % 4
    turn = jnp.where(distance == 0, 0, jnp.where(distance == 3, 1, distance + 1))
    place = jnp.where((block // 2) % 2 == z, 0, 8) + turn * 2
    here = place + jnp.where(block % 2 == core, 0, 1)
    there = 16 + place + jnp.where(block % 2 == core, 1, 0)
    table = [jnp.where(core == 0, here, there), jnp.where(core == 0, there, here)]
    scalars = jnp.stack([first, last - first + 1, clear, core])
    info = jnp.concatenate([scalars, *table]).astype(jnp.int32)
    query_pos, query_start = query_pos[None, :], query_start[None, :]

    depth = out_weight.shape[1]
    mine = lax.dynamic_slice_in_dim(grad_out, core * depth, depth, 1)
    other = lax.dynamic_slice_in_dim(grad_out, (1 - core) * depth, depth, 1)
    chip_grad = jnp.concatenate([mine, dp_move(other, 0, 0, 1)], axis=0)
    all_grad = lax.all_gather(chip_grad, "tensor", axis=0, tiled=False)

    kept = jnp.where(core == 0, keys, values)
    got = dp_move(jnp.where(core == 0, values, keys), 0, 0, 1)
    chip = jnp.concatenate([kept, got], axis=0)
    quad = jnp.concatenate(
        [chip, dp_move(chip, 1, 0, 0), dp_move(chip, -1, 0, 0), dp_move(chip, 2, 0, 0)], axis=0
    )
    ring = jnp.concatenate([quad, dp_move(quad, 0, 1, 0)], axis=0)
    kv = jnp.concatenate([ring, dp_move(ring, 0, 0, 1)], axis=0)

    size = out_weight.shape[0] // PIECES
    own = [out_weight[j * size : (j + 1) * size] for j in range(PIECES)]
    pair = [dp_move(piece, 0, 1, 0) for piece in own]
    held = own + pair
    left = [dp_move(piece, 1, 0, 0) for piece in held]
    right = [dp_move(piece, -1, 0, 0) for piece in held]

    kv = after(kv, *pair)
    parts = [forward(0, info, query_pos, query_start, queries, kv)]

    tied = lax.optimization_barrier((parts[0], left, right))
    parts[0], left, right = tied
    far = [
        dp_move(left[j], 1, 0, 0) if j % 2 == 0 else dp_move(right[j], -1, 0, 0)
        for j in range(2 * PIECES)
    ]
    parts.append(forward(1, info, query_pos, query_start, after(queries, parts[0][1]), kv))

    distances = [(0, 0), (3, 0), (1, 0), (2, 0), (0, 1), (3, 1), (1, 1), (2, 1)]
    source = jnp.stack(
        [2 * ((x + dx) % 4) + (z + dz) % 2 for dx, dz in distances]
    ).astype(jnp.int32)
    carried = ()
    share = PIECES // CHUNKS
    for part in range(CHUNKS):
        weights = [
            [group[dz * PIECES + j] for j in range(part * share, (part + 1) * share)]
            for dz in range(2)
            for group in (held, left, right, far)
        ]
        mine, other = project(part, source, all_grad, weights)
        grads = (mine + dp_move(other, 0, 0, 1)).astype(BF16)
        probs, outs = parts[part]
        grad_queries, own_sums, other_sums = backward(
            part, info, probs, outs, grads, queries, kv, carried
        )
        carried = (own_sums, other_sums, grad_queries)

    chip_sums = (own_sums + dp_move(other_sums, 0, 0, 1).astype(F32)).astype(BF16)
    groups = [[2 * i + c for i in range(8)] for c in range(2)]
    terms = lax.all_to_all(chip_sums, "dp", 0, 0, axis_index_groups=groups, tiled=True)
    done = jnp.sum(terms.astype(F32), axis=0).astype(BF16)
    return grad_queries, done[:, :HEAD_WIDTH], done[:, HEAD_WIDTH:]


def solution(mesh):
    return jax.shard_map(
        local,
        mesh=mesh,
        in_specs=(
            P("dp", "tensor"),
            P("dp", "tensor"),
            P("dp", "tensor"),
            P("dp", "tensor"),
            P("tensor", "dp"),
            P(),
        ),
        out_specs=(P("dp", "tensor"), P("dp", "tensor"), P("dp", "tensor")),
        check_vma=False,
    )
```

```python
import functools
import math

import jax
import jax.numpy as jnp
from jax import lax
from jax.experimental import pallas as pl
from jax.experimental.pallas import tpu as pltpu
from jax.sharding import PartitionSpec as P

HEAD_WIDTH = 128
KEY_BLOCK = 256
MOST = 2560
CHUNKS = 2
MASKED = -1e30
SCALE = 1.0 / math.sqrt(HEAD_WIDTH)
LOG2E = 1.0 / math.log(2.0)
BF16 = jnp.bfloat16
F32 = jnp.float32
VMEM_LIMIT = 32 * 2**20

FIRST, COUNT, CLEAR, CORE, TABLE = 0, 1, 2, 3, 4


def dp_move(value, dx, dz, dc):
    pairs = []
    for x in range(4):
        for z in range(2):
            for c in range(2):
                target = ((x + dx) % 4) * 4 + ((z + dz) % 2) * 2 + (c + dc) % 2
                pairs.append((x * 4 + z * 2 + c, target))
    return lax.ppermute(value, "dp", pairs)


def tensor_move(value, dz, dy):
    pairs = []
    for z in range(2):
        for y in range(4):
            pairs.append((z * 4 + y, ((z + dz) % 2) * 4 + (y + dy) % 4))
    return lax.ppermute(value, "tensor", pairs)


def after(value, *others):
    return lax.optimization_barrier((value, *others))[0]


def dot(left, right):
    return lax.dot_general(left, right, (((1,), (0,)), ((), ())), preferred_element_type=F32)


def dot_t(left, right):
    return lax.dot_general(left, right, (((1,), (1,)), ((), ())), preferred_element_type=F32)


def block_rows(index):
    return pl.ds(pl.multiple_of(index * KEY_BLOCK, KEY_BLOCK), KEY_BLOCK)


def forward_kernel(info, pos_ref, start_ref, q_ref, kv_ref, probs_ref, out_ref, score, vt):
    first, count = info[FIRST], info[COUNT]
    rows = q_ref.shape[0]
    query_t = q_ref[...].T

    @pl.when(pl.program_id(0) == 0)
    def _():
        def turn(index, _):
            source = info[TABLE + 16 + first + index]
            vt[:, block_rows(index)] = kv_ref[block_rows(source), :].T
            return 0

        lax.fori_loop(0, count, turn, 0)

    def product(index):
        return dot(kv_ref[block_rows(info[TABLE + first + index]), :], query_t)

    def masked_step(index, top):
        key_pos = (first + index) * KEY_BLOCK + lax.broadcasted_iota(jnp.int32, (KEY_BLOCK, rows), 0)
        live = (key_pos >= start_ref[...]) & (key_pos <= pos_ref[...])
        raw = jnp.where(live, product(index), MASKED)
        score[block_rows(index), :] = raw
        return jnp.maximum(top, jnp.max(raw, axis=0, keepdims=True))

    def clear_step(index, top):
        raw = product(index)
        score[block_rows(index), :] = raw
        return jnp.maximum(top, jnp.max(raw, axis=0, keepdims=True))

    clear = jnp.minimum(info[CLEAR] - first, count - 1)
    top = jnp.full((1, rows), MASKED, F32)
    top = lax.fori_loop(0, clear, masked_step, top)
    top = lax.fori_loop(clear, count - 1, clear_step, top)
    top = masked_step(count - 1, top)

    def mass_step(index, mass):
        weights = jnp.exp2((score[block_rows(index), :] - top) * (SCALE * LOG2E))
        score[block_rows(index), :] = weights
        return mass + jnp.sum(weights, axis=0, keepdims=True)

    mass = lax.fori_loop(0, count, mass_step, jnp.zeros((1, rows), F32))
    share = 1.0 / mass

    def probs_step(index, total):
        probs = (score[block_rows(index), :] * share).astype(BF16)
        probs_ref[block_rows(index), :] = probs
        return total + dot(vt[:, block_rows(index)], probs)

    out_ref[...] = lax.fori_loop(0, count, probs_step, jnp.zeros((HEAD_WIDTH, rows), F32))


def most_blocks(rows):
    return (MOST + rows - 2) // KEY_BLOCK + 1


def forward(part, info, query_pos, query_start, queries, kv):
    rows, width = queries.shape
    heads = width // HEAD_WIDTH // CHUNKS
    live = most_blocks(rows) * KEY_BLOCK
    line = pl.BlockSpec((1, rows), lambda h, r: (0, 0))
    return pl.pallas_call(
        forward_kernel,
        grid_spec=pltpu.PrefetchScalarGridSpec(
            num_scalar_prefetch=1,
            grid=(heads,),
            in_specs=[
                line,
                line,
                pl.BlockSpec((rows, HEAD_WIDTH), lambda h, r: (0, part * heads + h)),
                pl.BlockSpec(kv.shape, lambda h, r: (0, 0)),
            ],
            out_specs=[
                pl.BlockSpec((live, rows), lambda h, r: (0, h)),
                pl.BlockSpec((HEAD_WIDTH, rows), lambda h, r: (0, h)),
            ],
            scratch_shapes=[
                pltpu.VMEM((live, rows), F32),
                pltpu.VMEM((HEAD_WIDTH, live), BF16),
            ],
        ),
        out_shape=[
            jax.ShapeDtypeStruct((live, heads * rows), BF16),
            jax.ShapeDtypeStruct((HEAD_WIDTH, heads * rows), F32),
        ],
        compiler_params=pltpu.CompilerParams(vmem_limit_bytes=VMEM_LIMIT // 2),
        cost_estimate=pl.CostEstimate(
            flops=16 * 10**9, bytes_accessed=10 * 2**20, transcendentals=0
        ),
        name="forward%d" % part,
    )(info, query_pos, query_start, queries, kv)


def backward_kernel(heads, part, info, probs_ref, out_ref, grad_ref, q_ref, k_ref, v_ref, *rest):
    if part:
        old_own, old_other, _, gq_ref, own_ref, other_ref, grad_t, delta, total_q, other = rest
    else:
        gq_ref, own_ref, other_ref, grad_t, delta, total_q = rest
        other = other_ref
    step = pl.program_id(0)
    count = info[COUNT]
    rows = q_ref.shape[0]

    @pl.when(step == 0)
    def _():
        if part:
            own_ref[...] = old_own[...]
            other[...] = old_other[...]
        else:
            own_ref[...] = jnp.zeros_like(own_ref)
            other[...] = jnp.zeros_like(other)
        total_q[...] = jnp.zeros_like(total_q)
        for h in range(heads):
            cols = slice(h * rows, (h + 1) * rows)
            turned = grad_ref[:, h * HEAD_WIDTH : (h + 1) * HEAD_WIDTH].T
            grad_t[:, cols] = turned
            delta[:, cols] = jnp.sum(turned.astype(F32) * out_ref[:, cols], axis=0, keepdims=True)

    @pl.when(step < count)
    def _():
        block = info[FIRST] + step
        values = v_ref[...]
        keys_t = k_ref[...].T
        key_sum = jnp.zeros((KEY_BLOCK, HEAD_WIDTH), F32)
        value_sum = jnp.zeros((KEY_BLOCK, HEAD_WIDTH), F32)
        for h in range(heads):
            cols = slice(h * rows, (h + 1) * rows)
            wide = slice(h * HEAD_WIDTH, (h + 1) * HEAD_WIDTH)
            probs = probs_ref[:, cols]
            dprob = dot(values, grad_t[:, cols])
            dscore = (probs.astype(F32) * (dprob - delta[:, cols])).astype(BF16)
            value_sum = value_sum + dot(probs, grad_ref[:, wide])
            key_sum = key_sum + dot(dscore, q_ref[:, wide])
            total_q[:, cols] += dot(keys_t, dscore)

        def add(ref):
            ref[block // 2, :, :HEAD_WIDTH] += key_sum * SCALE
            ref[block // 2, :, HEAD_WIDTH:] += value_sum

        pl.when(block % 2 == info[CORE])(lambda: add(own_ref))
        pl.when(block % 2 != info[CORE])(lambda: add(other))

    @pl.when(step == count - 1)
    def _():
        for h in range(heads):
            cols = slice(h * rows, (h + 1) * rows)
            wide = slice(h * HEAD_WIDTH, (h + 1) * HEAD_WIDTH)
            gq_ref[:, wide] = (total_q[:, cols].T * SCALE).astype(BF16)
        if part:
            other_ref[...] = other[...].astype(BF16)


def backward(part, info, probs, outs, grads, queries, kv, carried):
    rows, width = queries.shape
    heads = width // HEAD_WIDTH // CHUNKS
    last = part == CHUNKS - 1
    sums = (8, KEY_BLOCK, 2 * HEAD_WIDTH)

    def near(i, r):
        return jnp.minimum(i, r[COUNT] - 1)

    sum_spec = pl.BlockSpec(sums, lambda i, r: (0, 0, 0))
    gq_spec = pl.BlockSpec((rows, heads * HEAD_WIDTH), lambda i, r: (0, part))
    scratch = [
        pltpu.VMEM((HEAD_WIDTH, heads * rows), BF16),
        pltpu.VMEM((1, heads * rows), F32),
        pltpu.VMEM((HEAD_WIDTH, heads * rows), F32),
    ]
    in_specs = [
        pl.BlockSpec((KEY_BLOCK, heads * rows), lambda i, r: (near(i, r), 0)),
        pl.BlockSpec((HEAD_WIDTH, heads * rows), lambda i, r: (0, 0)),
        pl.BlockSpec((rows, heads * HEAD_WIDTH), lambda i, r: (0, 0)),
        pl.BlockSpec((rows, heads * HEAD_WIDTH), lambda i, r: (0, part)),
        pl.BlockSpec((KEY_BLOCK, HEAD_WIDTH), lambda i, r: (r[TABLE + r[FIRST] + near(i, r)], 0)),
        pl.BlockSpec(
            (KEY_BLOCK, HEAD_WIDTH), lambda i, r: (r[TABLE + 16 + r[FIRST] + near(i, r)], 0)
        ),
    ]
    aliases = {}
    if part:
        in_specs += [sum_spec, sum_spec, pl.BlockSpec(memory_space=pl.ANY)]
        scratch.append(pltpu.VMEM(sums, F32))
        aliases = {9: 0}
    return pl.pallas_call(
        functools.partial(backward_kernel, heads, part),
        grid_spec=pltpu.PrefetchScalarGridSpec(
            num_scalar_prefetch=1,
            grid=(most_blocks(rows),),
            in_specs=in_specs,
            out_specs=[gq_spec, sum_spec, sum_spec],
            scratch_shapes=scratch,
        ),
        out_shape=[
            jax.ShapeDtypeStruct((rows, width), BF16),
            jax.ShapeDtypeStruct(sums, F32),
            jax.ShapeDtypeStruct(sums, BF16 if last else F32),
        ],
        input_output_aliases=aliases,
        compiler_params=pltpu.CompilerParams(vmem_limit_bytes=VMEM_LIMIT),
        cost_estimate=pl.CostEstimate(
            flops=8 * 10**9, bytes_accessed=10 * 2**20, transcendentals=0
        ),
        name="backward%d" % part,
    )(info, probs, outs, grads, queries, kv, kv, *carried)


def project_kernel(layout, tokens, slots, *rest):
    count = sum(len(sizes) for both in layout for sizes in both)
    pieces, (own_ref, other_ref, grad, weight, grad_sem, weight_sem) = rest[:count], rest[count:]
    pieces = list(pieces)
    copies = []
    for target, sems, chips in ((grad, grad_sem, layout[0]), (weight, weight_sem, layout[1])):
        lists, k = [], 0
        for i, sizes in enumerate(chips):
            at, one = 0, []
            for size in sizes:
                copy = pltpu.make_async_copy(pieces.pop(0), target.at[i, pl.ds(at, size)], sems.at[k])
                copy.start()
                one.append(copy)
                at, k = at + size, k + 1
            lists.append(one)
        copies.append(lists)
    for one in copies[0]:
        for copy in one:
            copy.wait()
    half = tokens // 2
    for i, one in enumerate(copies[1]):
        for copy in one:
            copy.wait()
        for ref, at in ((own_ref, 0), (other_ref, half)):
            term = dot_t(grad[slots[i], at : at + half, :], weight[i])
            if i == 0:
                ref[...] = term
            else:
                ref[...] += term


def project(part, slots, grads, weights):
    layout = [[[piece.shape[0] for piece in chip] for chip in both] for both in (grads, weights)]
    flat = [piece for both in (grads, weights) for chip in both for piece in chip]
    tokens, features = sum(layout[0][0]), sum(layout[1][0])
    depth, chips = flat[0].shape[1], len(weights)
    half = jax.ShapeDtypeStruct((tokens // 2, features), F32)
    return pl.pallas_call(
        functools.partial(project_kernel, layout, tokens),
        in_specs=[pl.BlockSpec(memory_space=pltpu.SMEM)]
        + [pl.BlockSpec(memory_space=pl.ANY)] * len(flat),
        out_specs=[pl.BlockSpec(memory_space=pltpu.VMEM)] * 2,
        out_shape=[half, half],
        scratch_shapes=[
            pltpu.VMEM((chips, tokens, depth), BF16),
            pltpu.VMEM((chips, features, depth), BF16),
            pltpu.SemaphoreType.DMA((sum(len(sizes) for sizes in layout[0]),)),
            pltpu.SemaphoreType.DMA((sum(len(sizes) for sizes in layout[1]),)),
        ],
        compiler_params=pltpu.CompilerParams(vmem_limit_bytes=16 * 2**20),
        cost_estimate=pl.CostEstimate(
            flops=2 * tokens * features * depth * chips,
            bytes_accessed=10 * 2**20,
            transcendentals=0,
        ),
        name="project%d" % part,
    )(slots, *flat)


def local(queries, keys, values, grad_out, out_weight, lengths):
    rows = queries.shape[0]
    rank = lax.axis_index("dp")
    core = rank % 2
    x, z = rank // 4, (rank // 2) % 2

    query_pos = rank * rows + jnp.arange(rows, dtype=jnp.int32)
    ends = jnp.cumsum(lengths)[:-1]
    query_start = jnp.max(
        jnp.where(ends[None, :] <= query_pos[:, None], ends[None, :], 0), axis=1
    )
    first = query_start[0] // KEY_BLOCK
    last = query_pos[-1] // KEY_BLOCK
    clear = (query_start[-1] + KEY_BLOCK - 1) // KEY_BLOCK
    block = jnp.arange(16, dtype=jnp.int32)
    distance = (block // 4 - x) % 4
    turn = jnp.where(distance == 0, 0, jnp.where(distance == 3, 1, distance + 1))
    place = turn * 4 + jnp.where((block // 2) % 2 == z, 0, 2)
    here = place + jnp.where(block % 2 == core, 0, 1)
    there = 16 + place + jnp.where(block % 2 == core, 1, 0)
    table = [jnp.where(core == 0, here, there), jnp.where(core == 0, there, here)]
    scalars = jnp.stack([first, last - first + 1, clear, core])
    info = jnp.concatenate([scalars, *table]).astype(jnp.int32)
    query_pos, query_start = query_pos[None, :], query_start[None, :]

    depth = out_weight.shape[1]
    mine = lax.dynamic_slice_in_dim(grad_out, core * depth, depth, 1)
    other = lax.dynamic_slice_in_dim(grad_out, (1 - core) * depth, depth, 1)
    chip_grad = jnp.concatenate([mine, dp_move(other, 0, 0, 1)], axis=0)

    kept = jnp.where(core == 0, keys, values)
    got = dp_move(jnp.where(core == 0, values, keys), 0, 0, 1)
    chip = jnp.concatenate([kept, got], axis=0)
    pair = jnp.concatenate([chip, dp_move(chip, 0, 1, 0)], axis=0)
    ring = jnp.concatenate(
        [pair, dp_move(pair, 1, 0, 0), dp_move(pair, -1, 0, 0), dp_move(pair, 2, 0, 0)], axis=0
    )
    kv = jnp.concatenate([ring, dp_move(ring, 0, 0, 1)], axis=0)

    size = out_weight.shape[0] // CHUNKS
    own = [out_weight[j * size : (j + 1) * size] for j in range(CHUNKS)]

    def both(move, block):
        return block, move(block, 1), move(block, -1)

    def far(move, ring):
        half = ring[0].shape[0] // 2
        return move(ring[1][:half], 1), move(ring[2][half:], -1)

    def along_x(block, step):
        return dp_move(block, step, 0, 0)

    def along_y(block, step):
        return tensor_move(block, 0, step)

    paired = [dp_move(block, 0, 1, 0) for block in own]
    ring00 = both(along_x, own[0])
    grad0 = both(along_y, chip_grad)
    grad_pair = tensor_move(chip_grad, 1, 0)
    kv, ring00, paired, grad0, grad_pair = lax.optimization_barrier(
        (kv, ring00, paired, grad0, grad_pair)
    )

    ring01 = both(along_x, paired[0])
    far00 = far(along_x, ring00)
    ring10 = both(along_x, own[1])
    grad1 = both(along_y, grad_pair)
    grad_far0 = far(along_y, grad0)
    first_part = forward(0, info, query_pos, query_start, queries, kv)
    second_part = forward(1, info, query_pos, query_start, after(queries, first_part[1]), kv)
    parts = [first_part, second_part]
    parts, ring01, far00, ring10, grad1, grad_far0 = lax.optimization_barrier(
        (parts, ring01, far00, ring10, grad1, grad_far0)
    )

    far01 = far(along_x, ring01)
    grad_far1 = far(along_y, grad1)
    ring11 = both(along_x, paired[1])
    far10 = far(along_x, ring10)

    t = lax.axis_index("tensor")
    slots = []
    for dz in range(2):
        for dx in (0, -1, 1, 2):
            source = 2 * ((x + dx) % 4) + (z + dz) % 2
            y_distance = (source - t) % 4
            turn = jnp.where(
                y_distance == 0, 0, jnp.where(y_distance == 3, 1, jnp.where(y_distance == 1, 2, 3))
            )
            slots.append(jnp.where(source // 4 == t // 4, 0, 4) + turn)
    slots = jnp.stack(slots).astype(jnp.int32)
    all_grad = [[block] for block in grad0] + [grad_far0] + [[block] for block in grad1] + [grad_far1]

    def one_part(part, weights, carried):
        mine, other = project(part, slots, all_grad, weights)
        grads = (mine + dp_move(other, 0, 0, 1)).astype(BF16)
        probs, outs = parts[part]
        return backward(part, info, probs, outs, grads, queries, kv, carried)

    weights = [[block] for block in ring00] + [far00] + [[block] for block in ring01] + [far01]
    grad_queries, own_sums, other_sums = one_part(0, weights, ())
    carried = (own_sums, other_sums, grad_queries)
    far11 = far(along_x, ring11)
    weights = [[block] for block in ring10] + [far10] + [[block] for block in ring11] + [far11]
    grad_queries, own_sums, other_sums = one_part(1, weights, carried)

    chip_sums = (own_sums + dp_move(other_sums, 0, 0, 1).astype(F32)).astype(BF16)
    groups = [[2 * i + c for i in range(8)] for c in range(2)]
    terms = lax.all_to_all(chip_sums, "dp", 0, 0, axis_index_groups=groups, tiled=True)
    done = jnp.sum(terms.astype(F32), axis=0).astype(BF16)
    return grad_queries, done[:, :HEAD_WIDTH], done[:, HEAD_WIDTH:]


def solution(mesh):
    return jax.shard_map(
        local,
        mesh=mesh,
        in_specs=(
            P("dp", "tensor"),
            P("dp", "tensor"),
            P("dp", "tensor"),
            P("dp", "tensor"),
            P("tensor", "dp"),
            P(),
        ),
        out_specs=(P("dp", "tensor"), P("dp", "tensor"), P("dp", "tensor")),
        check_vma=False,
    )
```

```python
import functools
import math

import jax
import jax.numpy as jnp
from jax import lax
from jax.experimental import pallas as pl
from jax.experimental.pallas import tpu as pltpu
from jax.sharding import PartitionSpec as P

HEAD_WIDTH = 128
KEY_BLOCK = 256
MOST = 2560
CHUNKS = 2
MASKED = -1e30
SCALE = 1.0 / math.sqrt(HEAD_WIDTH)
LOG2E = 1.0 / math.log(2.0)
BF16 = jnp.bfloat16
F32 = jnp.float32
VMEM_LIMIT = 32 * 2**20

FIRST, COUNT, CLEAR, CORE, TABLE = 0, 1, 2, 3, 4


def dp_move(value, dx, dz, dc):
    pairs = []
    for x in range(4):
        for z in range(2):
            for c in range(2):
                target = ((x + dx) % 4) * 4 + ((z + dz) % 2) * 2 + (c + dc) % 2
                pairs.append((x * 4 + z * 2 + c, target))
    return lax.ppermute(value, "dp", pairs)


def tensor_move(value, dz, dy):
    pairs = []
    for z in range(2):
        for y in range(4):
            pairs.append((z * 4 + y, ((z + dz) % 2) * 4 + (y + dy) % 4))
    return lax.ppermute(value, "tensor", pairs)


def after(value, *others):
    return lax.optimization_barrier((value, *others))[0]


def dot(left, right):
    return lax.dot_general(left, right, (((1,), (0,)), ((), ())), preferred_element_type=F32)


def dot_t(left, right):
    return lax.dot_general(left, right, (((1,), (1,)), ((), ())), preferred_element_type=F32)


def block_rows(index):
    return pl.ds(pl.multiple_of(index * KEY_BLOCK, KEY_BLOCK), KEY_BLOCK)


def forward_kernel(info, pos_ref, start_ref, q_ref, kv_ref, probs_ref, out_ref, score, vt):
    first, count = info[FIRST], info[COUNT]
    rows = q_ref.shape[0]
    query_t = q_ref[...].T

    @pl.when(pl.program_id(0) == 0)
    def _():
        def turn(index, _):
            source = info[TABLE + 16 + first + index]
            vt[:, block_rows(index)] = kv_ref[block_rows(source), :].T
            return 0

        lax.fori_loop(0, count, turn, 0)

    def product(index):
        return dot(kv_ref[block_rows(info[TABLE + first + index]), :], query_t)

    def masked_step(index, top):
        key_pos = (first + index) * KEY_BLOCK + lax.broadcasted_iota(jnp.int32, (KEY_BLOCK, rows), 0)
        live = (key_pos >= start_ref[...]) & (key_pos <= pos_ref[...])
        raw = jnp.where(live, product(index), MASKED)
        score[block_rows(index), :] = raw
        return jnp.maximum(top, jnp.max(raw, axis=0, keepdims=True))

    def clear_step(index, top):
        raw = product(index)
        score[block_rows(index), :] = raw
        return jnp.maximum(top, jnp.max(raw, axis=0, keepdims=True))

    clear = jnp.minimum(info[CLEAR] - first, count - 1)
    top = jnp.full((1, rows), MASKED, F32)
    top = lax.fori_loop(0, clear, masked_step, top)
    top = lax.fori_loop(clear, count - 1, clear_step, top)
    top = masked_step(count - 1, top)

    def mass_step(index, mass):
        weights = jnp.exp2((score[block_rows(index), :] - top) * (SCALE * LOG2E))
        score[block_rows(index), :] = weights
        return mass + jnp.sum(weights, axis=0, keepdims=True)

    mass = lax.fori_loop(0, count, mass_step, jnp.zeros((1, rows), F32))
    share = 1.0 / mass

    def probs_step(index, total):
        probs = (score[block_rows(index), :] * share).astype(BF16)
        probs_ref[block_rows(index), :] = probs
        return total + dot(vt[:, block_rows(index)], probs)

    out_ref[...] = lax.fori_loop(0, count, probs_step, jnp.zeros((HEAD_WIDTH, rows), F32))


def most_blocks(rows):
    return (MOST + rows - 2) // KEY_BLOCK + 1


def forward(part, info, query_pos, query_start, queries, kv):
    rows, width = queries.shape
    heads = width // HEAD_WIDTH // CHUNKS
    live = most_blocks(rows) * KEY_BLOCK
    line = pl.BlockSpec((1, rows), lambda h, r: (0, 0))
    return pl.pallas_call(
        forward_kernel,
        grid_spec=pltpu.PrefetchScalarGridSpec(
            num_scalar_prefetch=1,
            grid=(heads,),
            in_specs=[
                line,
                line,
                pl.BlockSpec((rows, HEAD_WIDTH), lambda h, r: (0, part * heads + h)),
                pl.BlockSpec(kv.shape, lambda h, r: (0, 0)),
            ],
            out_specs=[
                pl.BlockSpec((live, rows), lambda h, r: (0, h)),
                pl.BlockSpec((HEAD_WIDTH, rows), lambda h, r: (0, h)),
            ],
            scratch_shapes=[
                pltpu.VMEM((live, rows), F32),
                pltpu.VMEM((HEAD_WIDTH, live), BF16),
            ],
        ),
        out_shape=[
            jax.ShapeDtypeStruct((live, heads * rows), BF16),
            jax.ShapeDtypeStruct((HEAD_WIDTH, heads * rows), F32),
        ],
        compiler_params=pltpu.CompilerParams(vmem_limit_bytes=VMEM_LIMIT // 2),
        cost_estimate=pl.CostEstimate(
            flops=16 * 10**9, bytes_accessed=10 * 2**20, transcendentals=0
        ),
        name="forward%d" % part,
    )(info, query_pos, query_start, queries, kv)


def backward_kernel(heads, part, info, probs_ref, out_ref, grad_ref, q_ref, k_ref, v_ref, *rest):
    if part:
        old_own, old_other, _, gq_ref, own_ref, other_ref, grad_t, delta, total_q, other = rest
    else:
        gq_ref, own_ref, other_ref, grad_t, delta, total_q = rest
        other = other_ref
    step = pl.program_id(0)
    count = info[COUNT]
    rows = q_ref.shape[0]

    @pl.when(step == 0)
    def _():
        if part:
            own_ref[...] = old_own[...]
            other[...] = old_other[...]
        else:
            own_ref[...] = jnp.zeros_like(own_ref)
            other[...] = jnp.zeros_like(other)
        total_q[...] = jnp.zeros_like(total_q)
        for h in range(heads):
            cols = slice(h * rows, (h + 1) * rows)
            turned = grad_ref[:, h * HEAD_WIDTH : (h + 1) * HEAD_WIDTH].T
            grad_t[:, cols] = turned
            delta[:, cols] = jnp.sum(turned.astype(F32) * out_ref[:, cols], axis=0, keepdims=True)

    @pl.when(step < count)
    def _():
        block = info[FIRST] + step
        values = v_ref[...]
        keys_t = k_ref[...].T
        key_sum = jnp.zeros((KEY_BLOCK, HEAD_WIDTH), F32)
        value_sum = jnp.zeros((KEY_BLOCK, HEAD_WIDTH), F32)
        for h in range(heads):
            cols = slice(h * rows, (h + 1) * rows)
            wide = slice(h * HEAD_WIDTH, (h + 1) * HEAD_WIDTH)
            probs = probs_ref[:, cols]
            dprob = dot(values, grad_t[:, cols])
            dscore = (probs.astype(F32) * (dprob - delta[:, cols])).astype(BF16)
            value_sum = value_sum + dot(probs, grad_ref[:, wide])
            key_sum = key_sum + dot(dscore, q_ref[:, wide])
            total_q[:, cols] += dot(keys_t, dscore)

        def add(ref):
            ref[block // 2, :, :HEAD_WIDTH] += key_sum * SCALE
            ref[block // 2, :, HEAD_WIDTH:] += value_sum

        pl.when(block % 2 == info[CORE])(lambda: add(own_ref))
        pl.when(block % 2 != info[CORE])(lambda: add(other))

    @pl.when(step == count - 1)
    def _():
        for h in range(heads):
            cols = slice(h * rows, (h + 1) * rows)
            wide = slice(h * HEAD_WIDTH, (h + 1) * HEAD_WIDTH)
            gq_ref[:, wide] = (total_q[:, cols].T * SCALE).astype(BF16)
        if part:
            other_ref[...] = other[...].astype(BF16)


def backward(part, info, probs, outs, grads, queries, kv, carried):
    rows, width = queries.shape
    heads = width // HEAD_WIDTH // CHUNKS
    last = part == CHUNKS - 1
    sums = (8, KEY_BLOCK, 2 * HEAD_WIDTH)

    def near(i, r):
        return jnp.minimum(i, r[COUNT] - 1)

    sum_spec = pl.BlockSpec(sums, lambda i, r: (0, 0, 0))
    gq_spec = pl.BlockSpec((rows, heads * HEAD_WIDTH), lambda i, r: (0, part))
    scratch = [
        pltpu.VMEM((HEAD_WIDTH, heads * rows), BF16),
        pltpu.VMEM((1, heads * rows), F32),
        pltpu.VMEM((HEAD_WIDTH, heads * rows), F32),
    ]
    in_specs = [
        pl.BlockSpec((KEY_BLOCK, heads * rows), lambda i, r: (near(i, r), 0)),
        pl.BlockSpec((HEAD_WIDTH, heads * rows), lambda i, r: (0, 0)),
        pl.BlockSpec((rows, heads * HEAD_WIDTH), lambda i, r: (0, 0)),
        pl.BlockSpec((rows, heads * HEAD_WIDTH), lambda i, r: (0, part)),
        pl.BlockSpec((KEY_BLOCK, HEAD_WIDTH), lambda i, r: (r[TABLE + r[FIRST] + near(i, r)], 0)),
        pl.BlockSpec(
            (KEY_BLOCK, HEAD_WIDTH), lambda i, r: (r[TABLE + 16 + r[FIRST] + near(i, r)], 0)
        ),
    ]
    aliases = {}
    if part:
        in_specs += [sum_spec, sum_spec, pl.BlockSpec(memory_space=pl.ANY)]
        scratch.append(pltpu.VMEM(sums, F32))
        aliases = {9: 0}
    return pl.pallas_call(
        functools.partial(backward_kernel, heads, part),
        grid_spec=pltpu.PrefetchScalarGridSpec(
            num_scalar_prefetch=1,
            grid=(most_blocks(rows),),
            in_specs=in_specs,
            out_specs=[gq_spec, sum_spec, sum_spec],
            scratch_shapes=scratch,
        ),
        out_shape=[
            jax.ShapeDtypeStruct((rows, width), BF16),
            jax.ShapeDtypeStruct(sums, F32),
            jax.ShapeDtypeStruct(sums, BF16 if last else F32),
        ],
        input_output_aliases=aliases,
        compiler_params=pltpu.CompilerParams(vmem_limit_bytes=VMEM_LIMIT),
        cost_estimate=pl.CostEstimate(
            flops=8 * 10**9, bytes_accessed=10 * 2**20, transcendentals=0
        ),
        name="backward%d" % part,
    )(info, probs, outs, grads, queries, kv, kv, *carried)


def project_kernel(layout, slots, *rest):
    *pieces, own_ref, other_ref, grad = rest
    at_piece = 0
    half = own_ref.shape[0]
    for i, sizes in enumerate(layout[0]):
        at = 0
        for size in sizes:
            grad[i, at : at + size, :] = pieces[at_piece][...]
            at, at_piece = at + size, at_piece + 1
    for i, sizes in enumerate(layout[1]):
        at = 0
        for size in sizes:
            for ref, row in ((own_ref, 0), (other_ref, half)):
                term = dot_t(grad[slots[i], row : row + half, :], pieces[at_piece][...])
                if i == 0:
                    ref[:, at : at + size] = term
                else:
                    ref[:, at : at + size] += term
            at, at_piece = at + size, at_piece + 1


def project(part, slots, grads, weights):
    layout = [[[piece.shape[0] for piece in chip] for chip in both] for both in (grads, weights)]
    flat = [piece for both in (grads, weights) for chip in both for piece in chip]
    tokens, features = sum(layout[0][0]), sum(layout[1][0])
    depth, chips = flat[0].shape[1], len(weights)
    half = jax.ShapeDtypeStruct((tokens // 2, features), F32)
    return pl.pallas_call(
        functools.partial(project_kernel, layout),
        in_specs=[pl.BlockSpec(memory_space=pltpu.SMEM)]
        + [pl.BlockSpec(memory_space=pltpu.VMEM)] * len(flat),
        out_specs=[pl.BlockSpec(memory_space=pltpu.VMEM)] * 2,
        out_shape=[half, half],
        scratch_shapes=[pltpu.VMEM((chips, tokens, depth), BF16)],
        compiler_params=pltpu.CompilerParams(vmem_limit_bytes=20 * 2**20),
        cost_estimate=pl.CostEstimate(
            flops=2 * tokens * features * depth * chips,
            bytes_accessed=10 * 2**20,
            transcendentals=0,
        ),
        name="project%d" % part,
    )(slots, *flat)


def local(queries, keys, values, grad_out, out_weight, lengths):
    rows = queries.shape[0]
    rank = lax.axis_index("dp")
    core = rank % 2
    x, z = rank // 4, (rank // 2) % 2

    query_pos = rank * rows + jnp.arange(rows, dtype=jnp.int32)
    ends = jnp.cumsum(lengths)[:-1]
    query_start = jnp.max(
        jnp.where(ends[None, :] <= query_pos[:, None], ends[None, :], 0), axis=1
    )
    first = query_start[0] // KEY_BLOCK
    last = query_pos[-1] // KEY_BLOCK
    clear = (query_start[-1] + KEY_BLOCK - 1) // KEY_BLOCK
    block = jnp.arange(16, dtype=jnp.int32)
    distance = (block // 4 - x) % 4
    turn = jnp.where(distance == 0, 0, jnp.where(distance == 3, 1, distance + 1))
    place = turn * 4 + jnp.where((block // 2) % 2 == z, 0, 2)
    here = place + jnp.where(block % 2 == core, 0, 1)
    there = 16 + place + jnp.where(block % 2 == core, 1, 0)
    table = [jnp.where(core == 0, here, there), jnp.where(core == 0, there, here)]
    scalars = jnp.stack([first, last - first + 1, clear, core])
    info = jnp.concatenate([scalars, *table]).astype(jnp.int32)
    query_pos, query_start = query_pos[None, :], query_start[None, :]

    depth = out_weight.shape[1]
    mine = lax.dynamic_slice_in_dim(grad_out, core * depth, depth, 1)
    other = lax.dynamic_slice_in_dim(grad_out, (1 - core) * depth, depth, 1)
    chip_grad = jnp.concatenate([mine, dp_move(other, 0, 0, 1)], axis=0)

    size = out_weight.shape[0] // CHUNKS
    own = [out_weight[j * size : (j + 1) * size] for j in range(CHUNKS)]

    def both(move, block):
        return block, move(block, 1), move(block, -1)

    def far(move, ring):
        half = ring[0].shape[0] // 2
        return move(ring[1][:half], 1), move(ring[2][half:], -1)

    def along_x(block, step):
        return dp_move(block, step, 0, 0)

    def along_y(block, step):
        return tensor_move(block, 0, step)

    kept = jnp.where(core == 0, keys, values)
    got = dp_move(jnp.where(core == 0, values, keys), 0, 0, 1)
    chip = jnp.concatenate([kept, got], axis=0)
    ring00 = both(along_x, own[0])
    grad0 = both(along_y, chip_grad)
    grad_pair = tensor_move(chip_grad, 1, 0)
    pair = jnp.concatenate([chip, dp_move(chip, 0, 1, 0)], axis=0)
    pair, ring00, grad0, grad_pair = lax.optimization_barrier((pair, ring00, grad0, grad_pair))

    ring = jnp.concatenate(
        [pair, dp_move(pair, 1, 0, 0), dp_move(pair, -1, 0, 0), dp_move(pair, 2, 0, 0)], axis=0
    )
    paired = [dp_move(block, 0, 1, 0) for block in own]
    grad1 = both(along_y, grad_pair)
    grad_far0 = far(along_y, grad0)
    ring, paired, grad1, grad_far0 = lax.optimization_barrier((ring, paired, grad1, grad_far0))
    kv = jnp.concatenate([ring, dp_move(ring, 0, 0, 1)], axis=0)

    ring01 = both(along_x, paired[0])
    far00 = far(along_x, ring00)
    ring10 = both(along_x, own[1])
    grad_far1 = far(along_y, grad1)
    first_part = forward(0, info, query_pos, query_start, queries, kv)
    second_part = forward(1, info, query_pos, query_start, after(queries, first_part[1]), kv)
    parts = [first_part, second_part]
    parts, ring01, far00, ring10, grad_far1 = lax.optimization_barrier(
        (parts, ring01, far00, ring10, grad_far1)
    )

    far01 = far(along_x, ring01)
    ring11 = both(along_x, paired[1])
    far10 = far(along_x, ring10)

    t = lax.axis_index("tensor")
    slots = []
    for dz in range(2):
        for dx in (0, -1, 1, 2):
            source = 2 * ((x + dx) % 4) + (z + dz) % 2
            y_distance = (source - t) % 4
            turn = jnp.where(
                y_distance == 0, 0, jnp.where(y_distance == 3, 1, jnp.where(y_distance == 1, 2, 3))
            )
            slots.append(jnp.where(source // 4 == t // 4, 0, 4) + turn)
    slots = jnp.stack(slots).astype(jnp.int32)
    all_grad = [[block] for block in grad0] + [grad_far0] + [[block] for block in grad1] + [grad_far1]

    def one_part(part, weights, carried):
        mine, other = project(part, slots, all_grad, weights)
        grads = (mine + dp_move(other, 0, 0, 1)).astype(BF16)
        probs, outs = parts[part]
        return backward(part, info, probs, outs, grads, queries, kv, carried)

    weights = [[block] for block in ring00] + [far00] + [[block] for block in ring01] + [far01]
    grad_queries, own_sums, other_sums = one_part(0, weights, ())
    carried = (own_sums, other_sums, grad_queries)
    far11 = far(along_x, ring11)
    far11 = after(far11, grad_queries)
    weights = [[block] for block in ring10] + [far10] + [[block] for block in ring11] + [far11]
    grad_queries, own_sums, other_sums = one_part(1, weights, carried)

    chip_sums = (own_sums + dp_move(other_sums, 0, 0, 1).astype(F32)).astype(BF16)
    groups = [[2 * i + c for i in range(8)] for c in range(2)]
    terms = lax.all_to_all(chip_sums, "dp", 0, 0, axis_index_groups=groups, tiled=True)
    done = jnp.sum(terms.astype(F32), axis=0).astype(BF16)
    return grad_queries, done[:, :HEAD_WIDTH], done[:, HEAD_WIDTH:]


def solution(mesh):
    return jax.shard_map(
        local,
        mesh=mesh,
        in_specs=(
            P("dp", "tensor"),
            P("dp", "tensor"),
            P("dp", "tensor"),
            P("dp", "tensor"),
            P("tensor", "dp"),
            P(),
        ),
        out_specs=(P("dp", "tensor"), P("dp", "tensor"), P("dp", "tensor")),
        check_vma=False,
    )
```

```python
import functools
import math

import jax
import jax.numpy as jnp
from jax import lax
from jax.experimental import pallas as pl
from jax.experimental.pallas import tpu as pltpu
from jax.sharding import PartitionSpec as P

HEAD_WIDTH = 128
KEY_BLOCK = 256
MOST = 2560
CHUNKS = 2
MASKED = -1e30
SCALE = 1.0 / math.sqrt(HEAD_WIDTH)
LOG2E = 1.0 / math.log(2.0)
BF16 = jnp.bfloat16
F32 = jnp.float32
VMEM_LIMIT = 18 * 2**20

FIRST, COUNT, CLEAR, CORE, TABLE = 0, 1, 2, 3, 4


def dp_move(value, dx, dz, dc):
    pairs = []
    for x in range(4):
        for z in range(2):
            for c in range(2):
                target = ((x + dx) % 4) * 4 + ((z + dz) % 2) * 2 + (c + dc) % 2
                pairs.append((x * 4 + z * 2 + c, target))
    return lax.ppermute(value, "dp", pairs)


def tensor_move(value, dz, dy):
    pairs = []
    for z in range(2):
        for y in range(4):
            pairs.append((z * 4 + y, ((z + dz) % 2) * 4 + (y + dy) % 4))
    return lax.ppermute(value, "tensor", pairs)


def after(value, *others):
    return lax.optimization_barrier((value, *others))[0]


def dot(left, right):
    return lax.dot_general(left, right, (((1,), (0,)), ((), ())), preferred_element_type=F32)


def dot_t(left, right):
    return lax.dot_general(left, right, (((1,), (1,)), ((), ())), preferred_element_type=F32)


def block_rows(index):
    return pl.ds(pl.multiple_of(index * KEY_BLOCK, KEY_BLOCK), KEY_BLOCK)


def forward_kernel(info, pos_ref, start_ref, q_ref, kv_ref, probs_ref, out_ref, score, vt):
    first, count = info[FIRST], info[COUNT]
    rows = q_ref.shape[0]
    query_t = q_ref[...].T

    @pl.when(pl.program_id(0) == 0)
    def _():
        def turn(index, _):
            source = info[TABLE + 16 + first + index]
            vt[:, block_rows(index)] = kv_ref[block_rows(source), :].T
            return 0

        lax.fori_loop(0, count, turn, 0)

    def product(index):
        return dot(kv_ref[block_rows(info[TABLE + first + index]), :], query_t)

    def masked_step(index, top):
        key_pos = (first + index) * KEY_BLOCK + lax.broadcasted_iota(jnp.int32, (KEY_BLOCK, rows), 0)
        live = (key_pos >= start_ref[...]) & (key_pos <= pos_ref[...])
        raw = jnp.where(live, product(index), MASKED)
        score[block_rows(index), :] = raw
        return jnp.maximum(top, jnp.max(raw, axis=0, keepdims=True))

    def clear_step(index, top):
        raw = product(index)
        score[block_rows(index), :] = raw
        return jnp.maximum(top, jnp.max(raw, axis=0, keepdims=True))

    clear = jnp.minimum(info[CLEAR] - first, count - 1)
    top = jnp.full((1, rows), MASKED, F32)
    top = lax.fori_loop(0, clear, masked_step, top)
    top = lax.fori_loop(clear, count - 1, clear_step, top)
    top = masked_step(count - 1, top)

    def mass_step(index, mass):
        weights = jnp.exp2((score[block_rows(index), :] - top) * (SCALE * LOG2E))
        score[block_rows(index), :] = weights
        return mass + jnp.sum(weights, axis=0, keepdims=True)

    mass = lax.fori_loop(0, count, mass_step, jnp.zeros((1, rows), F32))
    share = 1.0 / mass

    def probs_step(index, total):
        probs = (score[block_rows(index), :] * share).astype(BF16)
        probs_ref[block_rows(index), :] = probs
        return total + dot(vt[:, block_rows(index)], probs)

    out_ref[...] = lax.fori_loop(0, count, probs_step, jnp.zeros((HEAD_WIDTH, rows), F32))


def most_blocks(rows):
    return (MOST + rows - 2) // KEY_BLOCK + 1


def forward(part, info, query_pos, query_start, queries, kv):
    rows, width = queries.shape
    heads = width // HEAD_WIDTH // CHUNKS
    live = most_blocks(rows) * KEY_BLOCK
    line = pl.BlockSpec((1, rows), lambda h, r: (0, 0))
    return pl.pallas_call(
        forward_kernel,
        grid_spec=pltpu.PrefetchScalarGridSpec(
            num_scalar_prefetch=1,
            grid=(heads,),
            in_specs=[
                line,
                line,
                pl.BlockSpec((rows, HEAD_WIDTH), lambda h, r: (0, part * heads + h)),
                pl.BlockSpec(kv.shape, lambda h, r: (0, 0)),
            ],
            out_specs=[
                pl.BlockSpec((live, rows), lambda h, r: (0, h)),
                pl.BlockSpec((HEAD_WIDTH, rows), lambda h, r: (0, h)),
            ],
            scratch_shapes=[
                pltpu.VMEM((live, rows), F32),
                pltpu.VMEM((HEAD_WIDTH, live), BF16),
            ],
        ),
        out_shape=[
            pltpu.HBM((live, heads * rows), BF16),
            jax.ShapeDtypeStruct((HEAD_WIDTH, heads * rows), F32),
        ],
        compiler_params=pltpu.CompilerParams(vmem_limit_bytes=VMEM_LIMIT),
        cost_estimate=pl.CostEstimate(
            flops=16 * 10**9, bytes_accessed=10 * 2**20, transcendentals=0
        ),
        name="forward%d" % part,
    )(info, query_pos, query_start, queries, kv)


def backward_kernel(heads, part, info, probs_ref, out_ref, grad_ref, q_ref, k_ref, v_ref, *rest):
    if part:
        old_own, old_other, _, gq_ref, own_ref, other_ref, grad_t, delta, total_q, other = rest
    else:
        gq_ref, own_ref, other_ref, grad_t, delta, total_q = rest
        other = other_ref
    step = pl.program_id(0)
    count = info[COUNT]
    rows = q_ref.shape[0]

    @pl.when(step == 0)
    def _():
        if part:
            own_ref[...] = old_own[...]
            other[...] = old_other[...]
        else:
            own_ref[...] = jnp.zeros_like(own_ref)
            other[...] = jnp.zeros_like(other)
        total_q[...] = jnp.zeros_like(total_q)
        for h in range(heads):
            cols = slice(h * rows, (h + 1) * rows)
            turned = grad_ref[:, h * HEAD_WIDTH : (h + 1) * HEAD_WIDTH].T
            grad_t[:, cols] = turned
            delta[:, cols] = jnp.sum(turned.astype(F32) * out_ref[:, cols], axis=0, keepdims=True)

    @pl.when(step < count)
    def _():
        block = info[FIRST] + step
        values = v_ref[...]
        keys_t = k_ref[...].T
        key_sum = jnp.zeros((KEY_BLOCK, HEAD_WIDTH), F32)
        value_sum = jnp.zeros((KEY_BLOCK, HEAD_WIDTH), F32)
        for h in range(heads):
            cols = slice(h * rows, (h + 1) * rows)
            wide = slice(h * HEAD_WIDTH, (h + 1) * HEAD_WIDTH)
            probs = probs_ref[:, cols]
            dprob = dot(values, grad_t[:, cols])
            dscore = (probs.astype(F32) * (dprob - delta[:, cols])).astype(BF16)
            value_sum = value_sum + dot(probs, grad_ref[:, wide])
            key_sum = key_sum + dot(dscore, q_ref[:, wide])
            total_q[:, cols] += dot(keys_t, dscore)

        def add(ref):
            ref[block // 2, :, :HEAD_WIDTH] += key_sum * SCALE
            ref[block // 2, :, HEAD_WIDTH:] += value_sum

        pl.when(block % 2 == info[CORE])(lambda: add(own_ref))
        pl.when(block % 2 != info[CORE])(lambda: add(other))

    @pl.when(step == count - 1)
    def _():
        for h in range(heads):
            cols = slice(h * rows, (h + 1) * rows)
            wide = slice(h * HEAD_WIDTH, (h + 1) * HEAD_WIDTH)
            gq_ref[:, wide] = (total_q[:, cols].T * SCALE).astype(BF16)
        if part:
            other_ref[...] = other[...].astype(BF16)


def backward(part, info, probs, outs, grads, queries, kv, carried):
    rows, width = queries.shape
    heads = width // HEAD_WIDTH // CHUNKS
    last = part == CHUNKS - 1
    sums = (8, KEY_BLOCK, 2 * HEAD_WIDTH)

    def near(i, r):
        return jnp.minimum(i, r[COUNT] - 1)

    sum_spec = pl.BlockSpec(sums, lambda i, r: (0, 0, 0), pipeline_mode=pl.Buffered(1))
    gq_spec = pl.BlockSpec((rows, heads * HEAD_WIDTH), lambda i, r: (0, part))
    scratch = [
        pltpu.VMEM((HEAD_WIDTH, heads * rows), BF16),
        pltpu.VMEM((1, heads * rows), F32),
        pltpu.VMEM((HEAD_WIDTH, heads * rows), F32),
    ]
    in_specs = [
        pl.BlockSpec((KEY_BLOCK, heads * rows), lambda i, r: (near(i, r), 0)),
        pl.BlockSpec((HEAD_WIDTH, heads * rows), lambda i, r: (0, 0)),
        pl.BlockSpec((rows, heads * HEAD_WIDTH), lambda i, r: (0, 0)),
        pl.BlockSpec((rows, heads * HEAD_WIDTH), lambda i, r: (0, part)),
        pl.BlockSpec((KEY_BLOCK, HEAD_WIDTH), lambda i, r: (r[TABLE + r[FIRST] + near(i, r)], 0)),
        pl.BlockSpec(
            (KEY_BLOCK, HEAD_WIDTH), lambda i, r: (r[TABLE + 16 + r[FIRST] + near(i, r)], 0)
        ),
    ]
    aliases = {}
    if part:
        in_specs += [sum_spec, sum_spec, pl.BlockSpec(memory_space=pl.ANY)]
        scratch.append(pltpu.VMEM(sums, F32))
        aliases = {9: 0}
    return pl.pallas_call(
        functools.partial(backward_kernel, heads, part),
        grid_spec=pltpu.PrefetchScalarGridSpec(
            num_scalar_prefetch=1,
            grid=(most_blocks(rows),),
            in_specs=in_specs,
            out_specs=[gq_spec, sum_spec, sum_spec],
            scratch_shapes=scratch,
        ),
        out_shape=[
            jax.ShapeDtypeStruct((rows, width), BF16),
            jax.ShapeDtypeStruct(sums, F32),
            jax.ShapeDtypeStruct(sums, BF16 if last else F32),
        ],
        input_output_aliases=aliases,
        compiler_params=pltpu.CompilerParams(vmem_limit_bytes=VMEM_LIMIT),
        cost_estimate=pl.CostEstimate(
            flops=8 * 10**9, bytes_accessed=10 * 2**20, transcendentals=0
        ),
        name="backward%d" % part,
    )(info, probs, outs, grads, queries, kv, kv, *carried)


def project_kernel(grad_count, slots, *rest):
    grads, (*stacks, own_ref, other_ref, grad) = rest[:grad_count], rest[grad_count:]
    half = own_ref.shape[0]
    at = 0
    for ref in grads:
        chip, row, size = at // (2 * half), at % (2 * half), ref.shape[0]
        grad[chip, row : row + size, :] = ref[...]
        at += size
    k = 0
    for ref in stacks:
        for j in range(ref.shape[0]):
            for out, row in ((own_ref, 0), (other_ref, half)):
                term = dot_t(grad[slots[k], row : row + half, :], ref[j])
                if k == 0:
                    out[...] = term
                else:
                    out[...] += term
            k += 1


def project(part, slots, grads, stacks):
    depth = grads[0].shape[1]
    chips = slots.shape[0]
    tokens = sum(ref.shape[0] for ref in grads) // chips
    features = stacks[0][0].shape[1] // CHUNKS
    half = jax.ShapeDtypeStruct((tokens // 2, features), F32)
    out_spec = pl.BlockSpec((tokens // 2, features), lambda i: (0, 0))
    stack_specs = [
        pl.BlockSpec((stack.shape[0], features, depth), lambda i, at=at: (0, at, 0))
        for stack, at in stacks
    ]
    return pl.pallas_call(
        functools.partial(project_kernel, len(grads)),
        grid=(1,),
        in_specs=[pl.BlockSpec(memory_space=pltpu.SMEM)]
        + [pl.BlockSpec(ref.shape, lambda i: (0, 0)) for ref in grads]
        + stack_specs,
        out_specs=[out_spec, out_spec],
        out_shape=[half, half],
        scratch_shapes=[pltpu.VMEM((chips, tokens, depth), BF16)],
        compiler_params=pltpu.CompilerParams(vmem_limit_bytes=24 * 2**20),
        cost_estimate=pl.CostEstimate(
            flops=2 * tokens * features * depth * chips,
            bytes_accessed=10 * 2**20,
            transcendentals=0,
        ),
        name="project%d" % part,
    )(slots, *grads, *[stack for stack, _ in stacks])


def local(queries, keys, values, grad_out, out_weight, lengths):
    rows = queries.shape[0]
    rank = lax.axis_index("dp")
    core = rank % 2
    x, z = rank // 4, (rank // 2) % 2

    query_pos = rank * rows + jnp.arange(rows, dtype=jnp.int32)
    ends = jnp.cumsum(lengths)[:-1]
    query_start = jnp.max(
        jnp.where(ends[None, :] <= query_pos[:, None], ends[None, :], 0), axis=1
    )
    first = query_start[0] // KEY_BLOCK
    last = query_pos[-1] // KEY_BLOCK
    clear = (query_start[-1] + KEY_BLOCK - 1) // KEY_BLOCK
    block = jnp.arange(16, dtype=jnp.int32)
    place = block // 2 * 2
    here = place + jnp.where(block % 2 == core, 0, 1)
    there = 16 + place + jnp.where(block % 2 == core, 1, 0)
    table = [jnp.where(core == 0, here, there), jnp.where(core == 0, there, here)]
    scalars = jnp.stack([first, last - first + 1, clear, core])
    info = jnp.concatenate([scalars, *table]).astype(jnp.int32)
    query_pos, query_start = query_pos[None, :], query_start[None, :]

    depth = out_weight.shape[1]
    mine = lax.dynamic_slice_in_dim(grad_out, core * depth, depth, 1)
    other = lax.dynamic_slice_in_dim(grad_out, (1 - core) * depth, depth, 1)
    chip_grad = jnp.concatenate([mine, dp_move(other, 0, 0, 1)], axis=0)

    groups_x = [[x_ * 4 + zc for x_ in range(4)] for zc in range(4)]
    plane = lax.all_gather(out_weight, "dp", axis=0, axis_index_groups=groups_x)
    size = out_weight.shape[0] // CHUNKS
    paired = [dp_move(out_weight[j * size : (j + 1) * size], 0, 1, 0) for j in range(CHUNKS)]
    other_plane = lax.all_gather(paired[0], "dp", axis=0, axis_index_groups=groups_x)

    groups = [[2 * i + c for i in range(8)] for c in range(2)]
    kept = jnp.where(core == 0, keys, values)
    got = dp_move(jnp.where(core == 0, values, keys), 0, 0, 1)
    chip = jnp.concatenate([kept, got], axis=0)
    ring = lax.all_to_all(
        jnp.broadcast_to(chip, (8, *chip.shape)), "dp", 0, 0, axis_index_groups=groups, tiled=True
    ).reshape(-1, HEAD_WIDTH)
    kv = jnp.concatenate([ring, dp_move(ring, 0, 0, 1)], axis=0)

    def far(ring):
        half = ring[0].shape[0] // 2
        return [tensor_move(ring[1][:half], 0, 1), tensor_move(ring[2][half:], 0, -1)]

    def both(block):
        return [block, tensor_move(block, 0, 1), tensor_move(block, 0, -1)]

    grad0 = both(chip_grad)
    grad_pair = tensor_move(chip_grad, 1, 0)
    kv, grad0, grad_pair, paired = lax.optimization_barrier((kv, grad0, grad_pair, paired))
    first_part = forward(0, info, query_pos, query_start, queries, kv)
    grad_far0 = far(grad0)
    grad1 = both(grad_pair)
    first_part, grad_far0, grad1 = lax.optimization_barrier((first_part, grad_far0, grad1))
    second_part = forward(1, info, query_pos, query_start, after(queries, first_part[1]), kv)
    grad_far1 = far(grad1)
    parts = [first_part, second_part]
    all_grad = grad0 + grad_far0 + grad1 + grad_far1

    rest = jnp.concatenate(
        [
            lax.dynamic_slice(plane, ((x + i) % 4, size, 0), (1, size, depth))
            for i in range(1, 4)
        ],
        axis=0,
    )
    rest = dp_move(rest, 0, 1, 0)

    t = lax.axis_index("tensor")

    def slot(x_, z_):
        source = 2 * (x_ % 4) + z_
        y_distance = (source - t) % 4
        turn = jnp.where(
            y_distance == 0, 0, jnp.where(y_distance == 3, 1, jnp.where(y_distance == 1, 2, 3))
        )
        return jnp.where(source // 4 == t // 4, 0, 4) + turn

    same = [slot(i, z) for i in range(4)]
    slots = [
        jnp.stack(same + [slot(i, 1 - z) for i in range(4)]).astype(jnp.int32),
        jnp.stack(same + [slot(x + i, 1 - z) for i in range(4)]).astype(jnp.int32),
    ]
    stacks = [
        [(plane, 0), (other_plane, 0)],
        [(plane, 1), (paired[1][None], 0), (rest, 0)],
    ]

    slots[0] = after(slots[0], second_part[1])
    carried = ()
    for part in range(CHUNKS):
        mine, other = project(part, slots[part], all_grad, stacks[part])
        grads = (mine + dp_move(other, 0, 0, 1)).astype(BF16)
        probs, outs = parts[part]
        grad_queries, own_sums, other_sums = backward(
            part, info, probs, outs, grads, queries, kv, carried
        )
        carried = (own_sums, other_sums, grad_queries)
        slots[-1] = after(slots[-1], grad_queries)

    chip_sums = (own_sums + dp_move(other_sums, 0, 0, 1).astype(F32)).astype(BF16)
    terms = lax.all_to_all(chip_sums, "dp", 0, 0, axis_index_groups=groups, tiled=True)
    done = jnp.sum(terms.astype(F32), axis=0).astype(BF16)
    return grad_queries, done[:, :HEAD_WIDTH], done[:, HEAD_WIDTH:]


def solution(mesh):
    return jax.shard_map(
        local,
        mesh=mesh,
        in_specs=(
            P("dp", "tensor"),
            P("dp", "tensor"),
            P("dp", "tensor"),
            P("dp", "tensor"),
            P("tensor", "dp"),
            P(),
        ),
        out_specs=(P("dp", "tensor"), P("dp", "tensor"), P("dp", "tensor")),
        check_vma=False,
    )
```

```python
import functools
import math

import jax
import jax.numpy as jnp
from jax import lax
from jax.experimental import pallas as pl
from jax.experimental.pallas import tpu as pltpu
from jax.sharding import PartitionSpec as P

HEAD_WIDTH = 128
KEY_BLOCK = 256
MOST = 2560
CHUNKS = 2
PAIR = 2
MASKED = -1e30
SCALE = 1.0 / math.sqrt(HEAD_WIDTH)
LOG2E = 1.0 / math.log(2.0)
BF16 = jnp.bfloat16
F32 = jnp.float32
VMEM_LIMIT = 22 * 2**20

FIRST, COUNT, CLEAR, CORE, TABLE = 0, 1, 2, 3, 4


def dp_move(value, dx, dz, dc):
    pairs = []
    for x in range(4):
        for z in range(2):
            for c in range(2):
                target = ((x + dx) % 4) * 4 + ((z + dz) % 2) * 2 + (c + dc) % 2
                pairs.append((x * 4 + z * 2 + c, target))
    return lax.ppermute(value, "dp", pairs)


def tensor_move(value, dz, dy):
    pairs = []
    for z in range(2):
        for y in range(4):
            pairs.append((z * 4 + y, ((z + dz) % 2) * 4 + (y + dy) % 4))
    return lax.ppermute(value, "tensor", pairs)


def after(value, *others):
    return lax.optimization_barrier((value, *others))[0]


def in_hbm(value):
    return pltpu.with_memory_space_constraint(value, pltpu.HBM)


def dot(left, right):
    return lax.dot_general(left, right, (((1,), (0,)), ((), ())), preferred_element_type=F32)


def dot_t(left, right):
    return lax.dot_general(left, right, (((1,), (1,)), ((), ())), preferred_element_type=F32)


def block_rows(index):
    return pl.ds(pl.multiple_of(index * KEY_BLOCK, KEY_BLOCK), KEY_BLOCK)


def forward_kernel(info, pos_ref, start_ref, q_ref, kv_ref, probs_ref, out_ref, score, vt):
    first, count = info[FIRST], info[COUNT]
    rows = q_ref.shape[0]
    heads = q_ref.shape[1] // HEAD_WIDTH
    query_t = jnp.concatenate(
        [q_ref[:, h * HEAD_WIDTH : (h + 1) * HEAD_WIDTH].T for h in range(heads)], axis=1
    )
    wide = heads * rows

    def groups(values):
        return values.reshape(KEY_BLOCK // 8, 8, wide)

    @pl.when(pl.program_id(0) == 0)
    def _():
        def turn(index, _):
            source = info[TABLE + 16 + first + index]
            vt[:, block_rows(index)] = kv_ref[block_rows(source), :].T
            return 0
        lax.fori_loop(0, count, turn, 0)

    def product(index):
        return dot(kv_ref[block_rows(info[TABLE + first + index]), :], query_t)

    def masked_step(index, top):
        key_pos = (first + index) * KEY_BLOCK + lax.broadcasted_iota(jnp.int32, (KEY_BLOCK, rows), 0)
        live = (key_pos >= start_ref[...]) & (key_pos <= pos_ref[...])
        raw = product(index)
        raw = jnp.concatenate(
            [jnp.where(live, raw[:, h * rows : (h + 1) * rows], MASKED) for h in range(heads)], axis=1
        )
        score[block_rows(index), :] = raw
        return jnp.maximum(top, jnp.max(groups(raw), axis=0))

    def clear_step(index, top):
        raw = product(index)
        score[block_rows(index), :] = raw
        return jnp.maximum(top, jnp.max(groups(raw), axis=0))

    clear = jnp.minimum(info[CLEAR] - first, count - 1)
    top = jnp.full((8, wide), MASKED, F32)
    top = lax.fori_loop(0, clear, masked_step, top)
    top = lax.fori_loop(clear, count - 1, clear_step, top)
    top = masked_step(count - 1, top)
    top = jnp.max(top, axis=0, keepdims=True) * (SCALE * LOG2E)

    def mass_step(index, mass):
        weights = jnp.exp2(score[block_rows(index), :] * (SCALE * LOG2E) - top)
        score[block_rows(index), :] = weights
        return mass + jnp.sum(groups(weights), axis=0)

    mass = lax.fori_loop(0, count, mass_step, jnp.zeros((8, wide), F32))
    share = 1.0 / jnp.sum(mass, axis=0, keepdims=True)
    out_ref[...] = jnp.zeros_like(out_ref)

    def probs_step(index, _):
        probs = (score[block_rows(index), :] * share).astype(BF16)
        probs_ref[block_rows(index), :] = probs
        out_ref[...] += dot(vt[:, block_rows(index)], probs)
        return 0

    lax.fori_loop(0, count, probs_step, 0)


def most_blocks(rows):
    return (MOST + rows - 2) // KEY_BLOCK + 1


def forward(part, info, query_pos, query_start, queries, kv):
    rows, width = queries.shape
    heads = width // HEAD_WIDTH // CHUNKS
    live = most_blocks(rows) * KEY_BLOCK
    line = pl.BlockSpec((1, rows), lambda h, r: (0, 0))
    steps = heads // PAIR
    return pl.pallas_call(
        forward_kernel,
        grid_spec=pltpu.PrefetchScalarGridSpec(
            num_scalar_prefetch=1,
            grid=(steps,),
            in_specs=[
                line,
                line,
                pl.BlockSpec((rows, PAIR * HEAD_WIDTH), lambda h, r: (0, part * steps + h)),
                pl.BlockSpec(kv.shape, lambda h, r: (0, 0)),
            ],
            out_specs=[
                pl.BlockSpec((live, PAIR * rows), lambda h, r: (0, h)),
                pl.BlockSpec((HEAD_WIDTH, PAIR * rows), lambda h, r: (0, h)),
            ],
            scratch_shapes=[
                pltpu.VMEM((live, PAIR * rows), F32),
                pltpu.VMEM((HEAD_WIDTH, live), BF16),
            ],
        ),
        out_shape=[
            pltpu.HBM((live, heads * rows), BF16),
            jax.ShapeDtypeStruct((HEAD_WIDTH, heads * rows), F32),
        ],
        compiler_params=pltpu.CompilerParams(vmem_limit_bytes=VMEM_LIMIT),
        cost_estimate=pl.CostEstimate(flops=10**10, bytes_accessed=10 * 2**20, transcendentals=0),
        name="forward%d" % part,
    )(info, query_pos, query_start, in_hbm(queries), in_hbm(kv))


def backward_kernel(heads, part, info, probs_ref, out_ref, grad_ref, q_ref, k_ref, v_ref, *rest):
    if part:
        old_own, old_other, _, gq_ref, own_ref, other_ref, grad_t, stack, delta, total_q, dscores, other = rest
    else:
        gq_ref, own_ref, other_ref, grad_t, stack, delta, total_q, dscores = rest
        other = other_ref
    step = pl.program_id(0)
    count = info[COUNT]
    rows = q_ref.shape[0]

    @pl.when(step == 0)
    def _():
        if part:
            own_ref[...] = old_own[...]
            other[...] = old_other[...]
        else:
            own_ref[...] = jnp.zeros_like(own_ref)
            other[...] = jnp.zeros_like(other)
        total_q[...] = jnp.zeros_like(total_q)
        for h in range(heads):
            cols = slice(h * rows, (h + 1) * rows)
            wide = slice(h * HEAD_WIDTH, (h + 1) * HEAD_WIDTH)
            turned = grad_ref[:, wide].T
            grad_t[:, cols] = turned
            stack[cols, :HEAD_WIDTH] = q_ref[:, wide]
            stack[cols, HEAD_WIDTH:] = grad_ref[:, wide]
            delta[:, cols] = jnp.sum(turned.astype(F32) * out_ref[:, cols], axis=0, keepdims=True)

    @pl.when(step < count)
    def _():
        block = info[FIRST] + step
        keys_t = k_ref[...].T
        for h in range(heads):
            cols = slice(h * rows, (h + 1) * rows)
            dprob = dot(v_ref[...], grad_t[:, cols])
            dscores[:, cols] = (probs_ref[:, cols].astype(F32) * (dprob - delta[:, cols])).astype(BF16)
        total_q[...] += dot(keys_t, dscores[...])
        key_sum = dot(dscores[...], stack[:, :HEAD_WIDTH])
        value_sum = dot(probs_ref[...], stack[:, HEAD_WIDTH:])

        def add(ref):
            ref[block // 2, :, :HEAD_WIDTH] += key_sum * SCALE
            ref[block // 2, :, HEAD_WIDTH:] += value_sum

        pl.when(block % 2 == info[CORE])(lambda: add(own_ref))
        pl.when(block % 2 != info[CORE])(lambda: add(other))

    @pl.when(step == count - 1)
    def _():
        for h in range(heads):
            cols = slice(h * rows, (h + 1) * rows)
            wide = slice(h * HEAD_WIDTH, (h + 1) * HEAD_WIDTH)
            gq_ref[:, wide] = (total_q[:, cols].T * SCALE).astype(BF16)
        if part:
            other_ref[...] = other[...].astype(BF16)


def backward(part, info, probs, outs, grads, queries, kv, carried):
    rows, width = queries.shape
    heads = width // HEAD_WIDTH // CHUNKS
    last = part == CHUNKS - 1
    sums = (8, KEY_BLOCK, 2 * HEAD_WIDTH)

    def near(i, r):
        return jnp.minimum(i, r[COUNT] - 1)

    sum_spec = pl.BlockSpec(sums, lambda i, r: (0, 0, 0), pipeline_mode=pl.Buffered(1))
    gq_spec = pl.BlockSpec((rows, heads * HEAD_WIDTH), lambda i, r: (0, part))
    scratch = [
        pltpu.VMEM((HEAD_WIDTH, heads * rows), BF16),
        pltpu.VMEM((heads * rows, 2 * HEAD_WIDTH), BF16),
        pltpu.VMEM((1, heads * rows), F32),
        pltpu.VMEM((HEAD_WIDTH, heads * rows), F32),
        pltpu.VMEM((KEY_BLOCK, heads * rows), BF16),
    ]
    in_specs = [
        pl.BlockSpec((KEY_BLOCK, heads * rows), lambda i, r: (near(i, r), 0)),
        pl.BlockSpec((HEAD_WIDTH, heads * rows), lambda i, r: (0, 0)),
        pl.BlockSpec((rows, heads * HEAD_WIDTH), lambda i, r: (0, 0)),
        pl.BlockSpec((rows, heads * HEAD_WIDTH), lambda i, r: (0, part)),
        pl.BlockSpec((KEY_BLOCK, HEAD_WIDTH), lambda i, r: (r[TABLE + r[FIRST] + near(i, r)], 0)),
        pl.BlockSpec(
            (KEY_BLOCK, HEAD_WIDTH), lambda i, r: (r[TABLE + 16 + r[FIRST] + near(i, r)], 0)
        ),
    ]
    aliases = {}
    if part:
        in_specs += [sum_spec, sum_spec, pl.BlockSpec(memory_space=pl.ANY)]
        scratch.append(pltpu.VMEM(sums, F32))
        aliases = {9: 0}
    return pl.pallas_call(
        functools.partial(backward_kernel, heads, part),
        grid_spec=pltpu.PrefetchScalarGridSpec(
            num_scalar_prefetch=1,
            grid=(most_blocks(rows),),
            in_specs=in_specs,
            out_specs=[gq_spec, sum_spec, sum_spec],
            scratch_shapes=scratch,
        ),
        out_shape=[
            jax.ShapeDtypeStruct((rows, width), BF16),
            jax.ShapeDtypeStruct(sums, F32),
            jax.ShapeDtypeStruct(sums, BF16 if last else F32),
        ],
        input_output_aliases=aliases,
        compiler_params=pltpu.CompilerParams(vmem_limit_bytes=VMEM_LIMIT),
        cost_estimate=pl.CostEstimate(flops=8 * 10**9, bytes_accessed=10 * 2**20, transcendentals=0),
        name="backward%d" % part,
    )(info, in_hbm(probs), outs, grads, in_hbm(queries), in_hbm(kv), in_hbm(kv), *carried)


def project_kernel(grad_count, slots, *rest):
    grads, (*stacks, own_ref, other_ref, grad) = rest[:grad_count], rest[grad_count:]
    half = own_ref.shape[0]
    at = 0
    for ref in grads:
        chip, row, size = at // (2 * half), at % (2 * half), ref.shape[0]
        grad[chip, row : row + size, :] = ref[...]
        at += size
    k = 0
    for ref in stacks:
        for j in range(ref.shape[0]):
            for out, row in ((own_ref, 0), (other_ref, half)):
                term = dot_t(grad[slots[k], row : row + half, :], ref[j])
                if k == 0:
                    out[...] = term
                else:
                    out[...] += term
            k += 1


def project(part, slots, grads, stacks):
    depth = grads[0].shape[1]
    chips = slots.shape[0]
    tokens = sum(ref.shape[0] for ref in grads) // chips
    features = stacks[0][0].shape[1] // CHUNKS
    half = jax.ShapeDtypeStruct((tokens // 2, features), F32)
    out_spec = pl.BlockSpec((tokens // 2, features), lambda i: (0, 0))
    stack_specs = [
        pl.BlockSpec((stack.shape[0], features, depth), lambda i, at=at: (0, at, 0))
        for stack, at in stacks
    ]
    return pl.pallas_call(
        functools.partial(project_kernel, len(grads)),
        grid=(1,),
        in_specs=[pl.BlockSpec(memory_space=pltpu.SMEM)]
        + [pl.BlockSpec(ref.shape, lambda i: (0, 0)) for ref in grads]
        + stack_specs,
        out_specs=[out_spec, out_spec],
        out_shape=[half, half],
        scratch_shapes=[pltpu.VMEM((chips, tokens, depth), BF16)],
        compiler_params=pltpu.CompilerParams(vmem_limit_bytes=24 * 2**20),
        cost_estimate=pl.CostEstimate(
            flops=2 * tokens * features * depth * chips,
            bytes_accessed=10 * 2**20,
            transcendentals=0,
        ),
        name="project%d" % part,
    )(slots, *grads, *[in_hbm(stack) for stack, _ in stacks])


def local(queries, keys, values, grad_out, out_weight, lengths):
    rows = queries.shape[0]
    rank = lax.axis_index("dp")
    core = rank % 2
    x, z = rank // 4, (rank // 2) % 2

    query_pos = rank * rows + jnp.arange(rows, dtype=jnp.int32)
    ends = jnp.cumsum(lengths)[:-1]
    query_start = jnp.max(
        jnp.where(ends[None, :] <= query_pos[:, None], ends[None, :], 0), axis=1
    )
    first = query_start[0] // KEY_BLOCK
    last = query_pos[-1] // KEY_BLOCK
    clear = (query_start[-1] + KEY_BLOCK - 1) // KEY_BLOCK
    block = jnp.arange(16, dtype=jnp.int32)
    place = block // 2 * 2
    here = place + jnp.where(block % 2 == core, 0, 1)
    there = 16 + place + jnp.where(block % 2 == core, 1, 0)
    table = [jnp.where(core == 0, here, there), jnp.where(core == 0, there, here)]
    scalars = jnp.stack([first, last - first + 1, clear, core])
    info = jnp.concatenate([scalars, *table]).astype(jnp.int32)
    query_pos, query_start = query_pos[None, :], query_start[None, :]

    depth = out_weight.shape[1]
    mine = lax.dynamic_slice_in_dim(grad_out, core * depth, depth, 1)
    other = lax.dynamic_slice_in_dim(grad_out, (1 - core) * depth, depth, 1)
    chip_grad = jnp.concatenate([mine, dp_move(other, 0, 0, 1)], axis=0)

    groups_x = [[x_ * 4 + zc for x_ in range(4)] for zc in range(4)]
    plane = lax.all_gather(out_weight, "dp", axis=0, axis_index_groups=groups_x)
    size = out_weight.shape[0] // CHUNKS
    paired = [dp_move(out_weight[j * size : (j + 1) * size], 0, 1, 0) for j in range(CHUNKS)]
    other_plane = lax.all_gather(paired[0], "dp", axis=0, axis_index_groups=groups_x)

    groups = [[2 * i + c for i in range(8)] for c in range(2)]
    kept = jnp.where(core == 0, keys, values)
    got = dp_move(jnp.where(core == 0, values, keys), 0, 0, 1)
    chip = jnp.concatenate([kept, got], axis=0)
    ring = lax.all_to_all(
        jnp.broadcast_to(chip, (8, *chip.shape)), "dp", 0, 0, axis_index_groups=groups, tiled=True
    ).reshape(-1, HEAD_WIDTH)

    def far(ring):
        half = ring[0].shape[0] // 2
        return [tensor_move(ring[1][:half], 0, 1), tensor_move(ring[2][half:], 0, -1)]

    def both(block):
        return [block, tensor_move(block, 0, 1), tensor_move(block, 0, -1)]

    grad0 = both(chip_grad)
    grad_pair = tensor_move(chip_grad, 1, 0)
    ring, grad0, grad_pair = lax.optimization_barrier((ring, grad0, grad_pair))
    kv = jnp.concatenate([ring, dp_move(ring, 0, 0, 1)], axis=0)
    grad_far0 = far(grad0)
    grad1 = both(grad_pair)
    kv, paired = lax.optimization_barrier((kv, paired))
    first_part = forward(0, info, query_pos, query_start, queries, kv)
    first_part, grad_far0, grad1 = lax.optimization_barrier((first_part, grad_far0, grad1))
    grad_far1 = far(grad1)

    rest = jnp.concatenate(
        [
            lax.dynamic_slice(plane, ((x + i) % 4, size, 0), (1, size, depth))
            for i in range(1, 4)
        ],
        axis=0,
    )
    later = lax.optimization_barrier((queries, rest, first_part[1]))
    rest = dp_move(later[1], 0, 1, 0)
    second_part = forward(1, info, query_pos, query_start, later[0], kv)
    parts = [first_part, second_part]
    all_grad = grad0 + grad_far0 + grad1 + grad_far1

    t = lax.axis_index("tensor")

    def slot(x_, z_):
        source = 2 * (x_ % 4) + z_
        y_distance = (source - t) % 4
        turn = jnp.where(
            y_distance == 0, 0, jnp.where(y_distance == 3, 1, jnp.where(y_distance == 1, 2, 3))
        )
        return jnp.where(source // 4 == t // 4, 0, 4) + turn

    same = [slot(i, z) for i in range(4)]
    slots = [
        jnp.stack(same + [slot(i, 1 - z) for i in range(4)]).astype(jnp.int32),
        jnp.stack(same + [slot(x + i, 1 - z) for i in range(4)]).astype(jnp.int32),
    ]
    stacks = [
        [(plane, 0), (other_plane, 0)],
        [(plane, 1), (paired[1][None], 0), (rest, 0)],
    ]

    slots[0] = after(slots[0], second_part[1])
    carried = ()
    for part in range(CHUNKS):
        mine, other = project(part, slots[part], all_grad, stacks[part])
        grads = (mine + dp_move(other, 0, 0, 1)).astype(BF16)
        probs, outs = parts[part]
        grad_queries, own_sums, other_sums = backward(
            part, info, probs, outs, grads, queries, kv, carried
        )
        carried = (own_sums, other_sums, grad_queries)
        slots[-1] = after(slots[-1], grad_queries)

    chip_sums = (own_sums + dp_move(other_sums, 0, 0, 1).astype(F32)).astype(BF16)
    terms = lax.all_to_all(chip_sums, "dp", 0, 0, axis_index_groups=groups, tiled=True)
    done = jnp.sum(terms.astype(F32), axis=0).astype(BF16)
    return grad_queries, done[:, :HEAD_WIDTH], done[:, HEAD_WIDTH:]


def solution(mesh):
    return jax.shard_map(
        local,
        mesh=mesh,
        in_specs=(
            P("dp", "tensor"),
            P("dp", "tensor"),
            P("dp", "tensor"),
            P("dp", "tensor"),
            P("tensor", "dp"),
            P(),
        ),
        out_specs=(P("dp", "tensor"), P("dp", "tensor"), P("dp", "tensor")),
        check_vma=False,
    )
```

```python
import functools
import math

import jax
import jax.numpy as jnp
from jax import lax
from jax.experimental import pallas as pl
from jax.experimental.pallas import tpu as pltpu
from jax.sharding import PartitionSpec as P

HEAD_WIDTH = 128
KEY_BLOCK = 256
MOST = 2560
CHUNKS = 2
PAIR = 2
MASKED = -1e30
SCALE = 1.0 / math.sqrt(HEAD_WIDTH)
LOG2E = 1.0 / math.log(2.0)
BF16 = jnp.bfloat16
F32 = jnp.float32
VMEM_LIMIT = 22 * 2**20

FIRST, COUNT, CLEAR, CORE, TABLE = 0, 1, 2, 3, 4


def dp_move(value, dx, dz, dc):
    pairs = []
    for x in range(4):
        for z in range(2):
            for c in range(2):
                target = ((x + dx) % 4) * 4 + ((z + dz) % 2) * 2 + (c + dc) % 2
                pairs.append((x * 4 + z * 2 + c, target))
    return lax.ppermute(value, "dp", pairs)


def tensor_move(value, dz, dy):
    pairs = []
    for z in range(2):
        for y in range(4):
            pairs.append((z * 4 + y, ((z + dz) % 2) * 4 + (y + dy) % 4))
    return lax.ppermute(value, "tensor", pairs)


def after(value, *others):
    return lax.optimization_barrier((value, *others))[0]


def in_hbm(value):
    return pltpu.with_memory_space_constraint(value, pltpu.HBM)


def dot(left, right):
    return lax.dot_general(left, right, (((1,), (0,)), ((), ())), preferred_element_type=F32)


def dot_t(left, right):
    return lax.dot_general(left, right, (((1,), (1,)), ((), ())), preferred_element_type=F32)


def block_rows(index):
    return pl.ds(pl.multiple_of(index * KEY_BLOCK, KEY_BLOCK), KEY_BLOCK)


def forward_kernel(info, pos_ref, start_ref, q_ref, kv_ref, probs_ref, out_ref, score, vt):
    first, count = info[FIRST], info[COUNT]
    rows = q_ref.shape[0]
    heads = q_ref.shape[1] // HEAD_WIDTH
    query_t = jnp.concatenate(
        [q_ref[:, h * HEAD_WIDTH : (h + 1) * HEAD_WIDTH].T for h in range(heads)], axis=1
    )
    wide = heads * rows

    def groups(values):
        return values.reshape(KEY_BLOCK // 8, 8, wide)

    @pl.when(pl.program_id(0) == 0)
    def _():
        def turn(index, _):
            source = info[TABLE + 16 + first + index]
            vt[:, block_rows(index)] = kv_ref[block_rows(source), :].T
            return 0
        lax.fori_loop(0, count, turn, 0)

    def product(index):
        return dot(kv_ref[block_rows(info[TABLE + first + index]), :], query_t)

    def masked_step(index, top):
        key_pos = (first + index) * KEY_BLOCK + lax.broadcasted_iota(jnp.int32, (KEY_BLOCK, rows), 0)
        live = (key_pos >= start_ref[...]) & (key_pos <= pos_ref[...])
        raw = product(index)
        raw = jnp.concatenate(
            [jnp.where(live, raw[:, h * rows : (h + 1) * rows], MASKED) for h in range(heads)], axis=1
        )
        score[block_rows(index), :] = raw
        return jnp.maximum(top, jnp.max(groups(raw), axis=0))

    def clear_step(index, top):
        raw = product(index)
        score[block_rows(index), :] = raw
        return jnp.maximum(top, jnp.max(groups(raw), axis=0))

    clear = jnp.minimum(info[CLEAR] - first, count - 1)
    top = jnp.full((8, wide), MASKED, F32)
    top = lax.fori_loop(0, clear, masked_step, top)
    top = lax.fori_loop(clear, count - 1, clear_step, top)
    top = masked_step(count - 1, top)
    top = jnp.max(top, axis=0, keepdims=True) * (SCALE * LOG2E)

    def mass_step(index, mass):
        weights = jnp.exp2(score[block_rows(index), :] * (SCALE * LOG2E) - top)
        score[block_rows(index), :] = weights
        return mass + jnp.sum(groups(weights), axis=0)

    mass = lax.fori_loop(0, count, mass_step, jnp.zeros((8, wide), F32))
    share = 1.0 / jnp.sum(mass, axis=0, keepdims=True)
    out_ref[...] = jnp.zeros_like(out_ref)

    def probs_step(index, _):
        probs = (score[block_rows(index), :] * share).astype(BF16)
        probs_ref[block_rows(index), :] = probs
        out_ref[...] += dot(vt[:, block_rows(index)], probs)
        return 0

    lax.fori_loop(0, count, probs_step, 0)


def most_blocks(rows):
    return (MOST + rows - 2) // KEY_BLOCK + 1


def forward(part, info, query_pos, query_start, queries, kv):
    rows, width = queries.shape
    heads = width // HEAD_WIDTH // CHUNKS
    live = most_blocks(rows) * KEY_BLOCK
    line = pl.BlockSpec((1, rows), lambda h, r: (0, 0))
    steps = heads // PAIR
    return pl.pallas_call(
        forward_kernel,
        grid_spec=pltpu.PrefetchScalarGridSpec(
            num_scalar_prefetch=1,
            grid=(steps,),
            in_specs=[
                line,
                line,
                pl.BlockSpec((rows, PAIR * HEAD_WIDTH), lambda h, r: (0, part * steps + h)),
                pl.BlockSpec(kv.shape, lambda h, r: (0, 0)),
            ],
            out_specs=[
                pl.BlockSpec((live, PAIR * rows), lambda h, r: (0, h)),
                pl.BlockSpec((HEAD_WIDTH, PAIR * rows), lambda h, r: (0, h)),
            ],
            scratch_shapes=[
                pltpu.VMEM((live, PAIR * rows), F32),
                pltpu.VMEM((HEAD_WIDTH, live), BF16),
            ],
        ),
        out_shape=[
            pltpu.HBM((live, heads * rows), BF16),
            jax.ShapeDtypeStruct((HEAD_WIDTH, heads * rows), F32),
        ],
        compiler_params=pltpu.CompilerParams(vmem_limit_bytes=VMEM_LIMIT),
        cost_estimate=pl.CostEstimate(flops=10**10, bytes_accessed=10 * 2**20, transcendentals=0),
        name="forward%d" % part,
    )(info, query_pos, query_start, in_hbm(queries), in_hbm(kv))


def backward_kernel(heads, part, info, probs_ref, out_ref, mine_ref, got_ref, q_ref, k_ref, v_ref, *rest):
    if part:
        old_own, old_other, _, gq_ref, own_ref, other_ref, grad_t, stack, delta, total_q, dscores, other = rest
    else:
        gq_ref, own_ref, other_ref, grad_t, stack, delta, total_q, dscores = rest
        other = other_ref
    step = pl.program_id(0)
    count = info[COUNT]
    rows = q_ref.shape[0]

    @pl.when(step == 0)
    def _():
        if part:
            own_ref[...] = old_own[...]
            other[...] = old_other[...]
        else:
            own_ref[...] = jnp.zeros_like(own_ref)
            other[...] = jnp.zeros_like(other)
        total_q[...] = jnp.zeros_like(total_q)
        for h in range(heads):
            cols = slice(h * rows, (h + 1) * rows)
            wide = slice(h * HEAD_WIDTH, (h + 1) * HEAD_WIDTH)
            grad = (mine_ref[:, wide] + got_ref[:, wide]).astype(BF16)
            turned = grad.T
            grad_t[:, cols] = turned
            stack[cols, :HEAD_WIDTH] = q_ref[:, wide]
            stack[cols, HEAD_WIDTH:] = grad
            delta[:, cols] = jnp.sum(turned.astype(F32) * out_ref[:, cols], axis=0, keepdims=True)

    @pl.when(step < count)
    def _():
        block = info[FIRST] + step
        keys_t = k_ref[...].T
        for h in range(heads):
            cols = slice(h * rows, (h + 1) * rows)
            dprob = dot(v_ref[...], grad_t[:, cols])
            dscores[:, cols] = (probs_ref[:, cols].astype(F32) * (dprob - delta[:, cols])).astype(BF16)
        total_q[...] += dot(keys_t, dscores[...])
        key_sum = dot(dscores[...], stack[:, :HEAD_WIDTH])
        value_sum = dot(probs_ref[...], stack[:, HEAD_WIDTH:])

        def add(ref):
            ref[block // 2, :, :HEAD_WIDTH] += key_sum * SCALE
            ref[block // 2, :, HEAD_WIDTH:] += value_sum

        pl.when(block % 2 == info[CORE])(lambda: add(own_ref))
        pl.when(block % 2 != info[CORE])(lambda: add(other))

    @pl.when(step == count - 1)
    def _():
        for h in range(heads):
            cols = slice(h * rows, (h + 1) * rows)
            wide = slice(h * HEAD_WIDTH, (h + 1) * HEAD_WIDTH)
            gq_ref[:, wide] = (total_q[:, cols].T * SCALE).astype(BF16)
        if part:
            other_ref[...] = other[...].astype(BF16)


def backward(part, info, probs, outs, mine, got, queries, kv, carried):
    rows, width = queries.shape
    heads = width // HEAD_WIDTH // CHUNKS
    last = part == CHUNKS - 1
    sums = (8, KEY_BLOCK, 2 * HEAD_WIDTH)

    def near(i, r):
        return jnp.minimum(i, r[COUNT] - 1)

    sum_spec = pl.BlockSpec(sums, lambda i, r: (0, 0, 0), pipeline_mode=pl.Buffered(1))
    gq_spec = pl.BlockSpec((rows, heads * HEAD_WIDTH), lambda i, r: (0, part))
    scratch = [
        pltpu.VMEM((HEAD_WIDTH, heads * rows), BF16),
        pltpu.VMEM((heads * rows, 2 * HEAD_WIDTH), BF16),
        pltpu.VMEM((1, heads * rows), F32),
        pltpu.VMEM((HEAD_WIDTH, heads * rows), F32),
        pltpu.VMEM((KEY_BLOCK, heads * rows), BF16),
    ]
    in_specs = [
        pl.BlockSpec((KEY_BLOCK, heads * rows), lambda i, r: (near(i, r), 0)),
        pl.BlockSpec((HEAD_WIDTH, heads * rows), lambda i, r: (0, 0)),
        pl.BlockSpec((rows, heads * HEAD_WIDTH), lambda i, r: (0, 0)),
        pl.BlockSpec((rows, heads * HEAD_WIDTH), lambda i, r: (0, 0)),
        pl.BlockSpec((rows, heads * HEAD_WIDTH), lambda i, r: (0, part)),
        pl.BlockSpec((KEY_BLOCK, HEAD_WIDTH), lambda i, r: (r[TABLE + r[FIRST] + near(i, r)], 0)),
        pl.BlockSpec(
            (KEY_BLOCK, HEAD_WIDTH), lambda i, r: (r[TABLE + 16 + r[FIRST] + near(i, r)], 0)
        ),
    ]
    aliases = {}
    if part:
        in_specs += [sum_spec, sum_spec, pl.BlockSpec(memory_space=pl.ANY)]
        scratch.append(pltpu.VMEM(sums, F32))
        aliases = {10: 0}
    return pl.pallas_call(
        functools.partial(backward_kernel, heads, part),
        grid_spec=pltpu.PrefetchScalarGridSpec(
            num_scalar_prefetch=1,
            grid=(most_blocks(rows),),
            in_specs=in_specs,
            out_specs=[gq_spec, sum_spec, sum_spec],
            scratch_shapes=scratch,
        ),
        out_shape=[
            jax.ShapeDtypeStruct((rows, width), BF16),
            jax.ShapeDtypeStruct(sums, F32),
            jax.ShapeDtypeStruct(sums, BF16 if last else F32),
        ],
        input_output_aliases=aliases,
        compiler_params=pltpu.CompilerParams(vmem_limit_bytes=VMEM_LIMIT),
        cost_estimate=pl.CostEstimate(flops=8 * 10**9, bytes_accessed=10 * 2**20, transcendentals=0),
        name="backward%d" % part,
    )(info, in_hbm(probs), outs, mine, got, in_hbm(queries), in_hbm(kv), in_hbm(kv), *carried)


def project_kernel(grad_count, slots, *rest):
    grads, (*stacks, own_ref, other_ref, grad) = rest[:grad_count], rest[grad_count:]
    half = own_ref.shape[0]
    at = 0
    for ref in grads:
        chip, row, size = at // (2 * half), at % (2 * half), ref.shape[0]
        grad[chip, row : row + size, :] = ref[...]
        at += size
    k = 0
    for ref in stacks:
        for j in range(ref.shape[0]):
            for out, row in ((own_ref, 0), (other_ref, half)):
                term = dot_t(grad[slots[k], row : row + half, :], ref[j])
                if k == 0:
                    out[...] = term
                else:
                    out[...] += term
            k += 1


def project(part, slots, grads, stacks):
    depth = grads[0].shape[1]
    chips = slots.shape[0]
    tokens = sum(ref.shape[0] for ref in grads) // chips
    features = stacks[0].shape[1]
    half = jax.ShapeDtypeStruct((tokens // 2, features), F32)
    out_spec = pl.BlockSpec((tokens // 2, features), lambda i: (0, 0))
    stack_specs = [pl.BlockSpec(stack.shape, lambda i: (0, 0, 0)) for stack in stacks]
    return pl.pallas_call(
        functools.partial(project_kernel, len(grads)),
        grid=(1,),
        in_specs=[pl.BlockSpec(memory_space=pltpu.SMEM)]
        + [pl.BlockSpec(ref.shape, lambda i: (0, 0)) for ref in grads]
        + stack_specs,
        out_specs=[out_spec, out_spec],
        out_shape=[half, half],
        scratch_shapes=[pltpu.VMEM((chips, tokens, depth), BF16)],
        compiler_params=pltpu.CompilerParams(vmem_limit_bytes=24 * 2**20),
        cost_estimate=pl.CostEstimate(
            flops=2 * tokens * features * depth * chips,
            bytes_accessed=10 * 2**20,
            transcendentals=0,
        ),
        name="project%d" % part,
    )(slots, *grads, *[in_hbm(stack) for stack in stacks])


def local(queries, keys, values, grad_out, out_weight, lengths):
    rows = queries.shape[0]
    rank = lax.axis_index("dp")
    core = rank % 2
    x, z = rank // 4, (rank // 2) % 2

    query_pos = rank * rows + jnp.arange(rows, dtype=jnp.int32)
    ends = jnp.cumsum(lengths)[:-1]
    query_start = jnp.max(
        jnp.where(ends[None, :] <= query_pos[:, None], ends[None, :], 0), axis=1
    )
    first = query_start[0] // KEY_BLOCK
    last = query_pos[-1] // KEY_BLOCK
    clear = (query_start[-1] + KEY_BLOCK - 1) // KEY_BLOCK
    block = jnp.arange(16, dtype=jnp.int32)
    place = block // 2 * 2
    here = place + jnp.where(block % 2 == core, 0, 1)
    there = 16 + place + jnp.where(block % 2 == core, 1, 0)
    table = [jnp.where(core == 0, here, there), jnp.where(core == 0, there, here)]
    scalars = jnp.stack([first, last - first + 1, clear, core])
    info = jnp.concatenate([scalars, *table]).astype(jnp.int32)
    query_pos, query_start = query_pos[None, :], query_start[None, :]

    depth = out_weight.shape[1]
    mine = lax.dynamic_slice_in_dim(grad_out, core * depth, depth, 1)
    other = lax.dynamic_slice_in_dim(grad_out, (1 - core) * depth, depth, 1)
    chip_grad = jnp.concatenate([mine, dp_move(other, 0, 0, 1)], axis=0)

    groups_x = [[x_ * 4 + zc for x_ in range(4)] for zc in range(4)]

    def gather_x(block):
        return lax.all_gather(block, "dp", axis=0, axis_index_groups=groups_x)

    size = out_weight.shape[0] // CHUNKS
    own = [out_weight[:size], out_weight[size:]]
    planes = [gather_x(own[0])]
    planes.append(gather_x(after(own[1], planes[0])))

    groups = [[2 * i + c for i in range(8)] for c in range(2)]
    kept = jnp.where(core == 0, keys, values)
    got = dp_move(jnp.where(core == 0, values, keys), 0, 0, 1)
    chip = jnp.concatenate([kept, got], axis=0)
    ring = lax.all_to_all(
        jnp.broadcast_to(chip, (8, *chip.shape)), "dp", 0, 0, axis_index_groups=groups, tiled=True
    ).reshape(-1, HEAD_WIDTH)

    def far(ring):
        half = ring[0].shape[0] // 2
        return [tensor_move(ring[1][:half], 0, 1), tensor_move(ring[2][half:], 0, -1)]

    def both(block):
        return [block, tensor_move(block, 0, 1), tensor_move(block, 0, -1)]

    grad0 = both(chip_grad)
    grad_pair = tensor_move(chip_grad, 1, 0)
    ring, grad0, grad_pair = lax.optimization_barrier((ring, grad0, grad_pair))
    kv = jnp.concatenate([ring, dp_move(ring, 0, 0, 1)], axis=0)
    own, _ = lax.optimization_barrier((own, ring))
    paired = [dp_move(block, 0, 1, 0) for block in own]
    other_plane = gather_x(after(paired[1], planes[1]))
    grad_far0 = far(grad0)
    grad1 = both(grad_pair)
    first_part = forward(0, info, query_pos, query_start, queries, kv)
    first_part, grad_far0, grad1 = lax.optimization_barrier((first_part, grad_far0, grad1))
    grad_far1 = far(grad1)

    rest = jnp.concatenate(
        [lax.dynamic_slice_in_dim(planes[0], (x + i) % 4, 1, 0) for i in range(1, 4)], axis=0
    )
    later = lax.optimization_barrier((queries, rest, first_part[1]))
    rest = dp_move(later[1], 0, 1, 0)
    second_part = forward(1, info, query_pos, query_start, later[0], kv)
    parts = [first_part, second_part]
    all_grad = grad0 + grad_far0 + grad1 + grad_far1

    t = lax.axis_index("tensor")

    def slot(x_, z_):
        source = 2 * (x_ % 4) + z_
        y_distance = (source - t) % 4
        turn = jnp.where(
            y_distance == 0, 0, jnp.where(y_distance == 3, 1, jnp.where(y_distance == 1, 2, 3))
        )
        return jnp.where(source // 4 == t // 4, 0, 4) + turn

    same = [slot(i, z) for i in range(4)]
    slots = [
        jnp.stack(same + [slot(x + i, 1 - z) for i in range(4)]).astype(jnp.int32),
        jnp.stack(same + [slot(i, 1 - z) for i in range(4)]).astype(jnp.int32),
    ]
    stacks = [[planes[0], paired[0][None], rest], [planes[1], other_plane]]

    slots[0] = after(slots[0], second_part[1])
    carried = ()
    for part in range(CHUNKS):
        mine, other = project(part, slots[part], all_grad, stacks[part])
        got = dp_move(other, 0, 0, 1)
        probs, outs = parts[part]
        grad_queries, own_sums, other_sums = backward(
            part, info, probs, outs, mine, got, queries, kv, carried
        )
        carried = (own_sums, other_sums, grad_queries)
        slots[-1] = after(slots[-1], grad_queries)

    chip_sums = (own_sums + dp_move(other_sums, 0, 0, 1).astype(F32)).astype(BF16)
    terms = lax.all_to_all(chip_sums, "dp", 0, 0, axis_index_groups=groups, tiled=True)
    done = jnp.sum(terms.astype(F32), axis=0).astype(BF16)
    return grad_queries, done[:, :HEAD_WIDTH], done[:, HEAD_WIDTH:]


def solution(mesh):
    return jax.shard_map(
        local,
        mesh=mesh,
        in_specs=(
            P("dp", "tensor"),
            P("dp", "tensor"),
            P("dp", "tensor"),
            P("dp", "tensor"),
            P("tensor", "dp"),
            P(),
        ),
        out_specs=(P("dp", "tensor"), P("dp", "tensor"), P("dp", "tensor")),
        check_vma=False,
    )
```

```python
import functools
import math

import jax
import jax.numpy as jnp
from jax import lax
from jax.experimental import pallas as pl
from jax.experimental.pallas import tpu as pltpu
from jax.sharding import PartitionSpec as P

HEAD_WIDTH = 128
KEY_BLOCK = 256
MOST = 2560
CHUNKS = 2
PAIR = 2
MASKED = -1e30
SCALE = 1.0 / math.sqrt(HEAD_WIDTH)
LOG2E = 1.0 / math.log(2.0)
BF16 = jnp.bfloat16
F32 = jnp.float32
VMEM_LIMIT = 22 * 2**20

FIRST, COUNT, CLEAR, CORE, TABLE = 0, 1, 2, 3, 4


def dp_move(value, dx, dz, dc):
    pairs = []
    for x in range(4):
        for z in range(2):
            for c in range(2):
                target = ((x + dx) % 4) * 4 + ((z + dz) % 2) * 2 + (c + dc) % 2
                pairs.append((x * 4 + z * 2 + c, target))
    return lax.ppermute(value, "dp", pairs)


def tensor_move(value, dz, dy):
    pairs = []
    for z in range(2):
        for y in range(4):
            pairs.append((z * 4 + y, ((z + dz) % 2) * 4 + (y + dy) % 4))
    return lax.ppermute(value, "tensor", pairs)


def after(value, *others):
    return lax.optimization_barrier((value, *others))[0]


def in_hbm(value):
    return pltpu.with_memory_space_constraint(value, pltpu.HBM)


def dot(left, right):
    return lax.dot_general(left, right, (((1,), (0,)), ((), ())), preferred_element_type=F32)


def dot_t(left, right):
    return lax.dot_general(left, right, (((1,), (1,)), ((), ())), preferred_element_type=F32)


def block_rows(index):
    return pl.ds(pl.multiple_of(index * KEY_BLOCK, KEY_BLOCK), KEY_BLOCK)


def forward_kernel(info, pos_ref, start_ref, q_ref, kv_ref, probs_ref, out_ref, score, vt):
    first, count = info[FIRST], info[COUNT]
    rows = q_ref.shape[0]
    heads = q_ref.shape[1] // HEAD_WIDTH
    query_t = jnp.concatenate(
        [q_ref[:, h * HEAD_WIDTH : (h + 1) * HEAD_WIDTH].T for h in range(heads)], axis=1
    )
    wide = heads * rows

    def groups(values):
        return values.reshape(KEY_BLOCK // 8, 8, wide)

    @pl.when(pl.program_id(0) == 0)
    def _():
        def turn(index, _):
            source = info[TABLE + 16 + first + index]
            vt[:, block_rows(index)] = kv_ref[block_rows(source), :].T
            return 0
        lax.fori_loop(0, count, turn, 0)

    def product(index):
        return dot(kv_ref[block_rows(info[TABLE + first + index]), :], query_t)

    def masked_step(index, top):
        key_pos = (first + index) * KEY_BLOCK + lax.broadcasted_iota(jnp.int32, (KEY_BLOCK, rows), 0)
        live = (key_pos >= start_ref[...]) & (key_pos <= pos_ref[...])
        raw = product(index)
        raw = jnp.concatenate(
            [jnp.where(live, raw[:, h * rows : (h + 1) * rows], MASKED) for h in range(heads)], axis=1
        )
        score[block_rows(index), :] = raw
        return jnp.maximum(top, jnp.max(groups(raw), axis=0))

    def clear_step(index, top):
        raw = product(index)
        score[block_rows(index), :] = raw
        return jnp.maximum(top, jnp.max(groups(raw), axis=0))

    clear = jnp.minimum(info[CLEAR] - first, count - 1)
    top = jnp.full((8, wide), MASKED, F32)
    top = lax.fori_loop(0, clear, masked_step, top)
    top = lax.fori_loop(clear, count - 1, clear_step, top)
    top = masked_step(count - 1, top)
    top = jnp.max(top, axis=0, keepdims=True) * (SCALE * LOG2E)

    def mass_step(index, mass):
        weights = jnp.exp2(score[block_rows(index), :] * (SCALE * LOG2E) - top)
        score[block_rows(index), :] = weights
        return mass + jnp.sum(groups(weights), axis=0)

    mass = lax.fori_loop(0, count, mass_step, jnp.zeros((8, wide), F32))
    share = 1.0 / jnp.sum(mass, axis=0, keepdims=True)
    out_ref[...] = jnp.zeros_like(out_ref)

    def probs_step(index, _):
        probs = (score[block_rows(index), :] * share).astype(BF16)
        probs_ref[block_rows(index), :] = probs
        out_ref[...] += dot(vt[:, block_rows(index)], probs)
        return 0

    lax.fori_loop(0, count, probs_step, 0)


def most_blocks(rows):
    return (MOST + rows - 2) // KEY_BLOCK + 1


def forward(part, info, query_pos, query_start, queries, kv):
    rows, width = queries.shape
    heads = width // HEAD_WIDTH // CHUNKS
    live = most_blocks(rows) * KEY_BLOCK
    line = pl.BlockSpec((1, rows), lambda h, r: (0, 0))
    steps = heads // PAIR
    return pl.pallas_call(
        forward_kernel,
        grid_spec=pltpu.PrefetchScalarGridSpec(
            num_scalar_prefetch=1,
            grid=(steps,),
            in_specs=[
                line,
                line,
                pl.BlockSpec((rows, PAIR * HEAD_WIDTH), lambda h, r: (0, part * steps + h)),
                pl.BlockSpec(kv.shape, lambda h, r: (0, 0)),
            ],
            out_specs=[
                pl.BlockSpec((live, PAIR * rows), lambda h, r: (0, h)),
                pl.BlockSpec((HEAD_WIDTH, PAIR * rows), lambda h, r: (0, h)),
            ],
            scratch_shapes=[
                pltpu.VMEM((live, PAIR * rows), F32),
                pltpu.VMEM((HEAD_WIDTH, live), BF16),
            ],
        ),
        out_shape=[
            pltpu.HBM((live, heads * rows), BF16),
            jax.ShapeDtypeStruct((HEAD_WIDTH, heads * rows), F32),
        ],
        compiler_params=pltpu.CompilerParams(vmem_limit_bytes=VMEM_LIMIT),
        cost_estimate=pl.CostEstimate(flops=10**10, bytes_accessed=10 * 2**20, transcendentals=0),
        name="forward%d" % part,
    )(info, query_pos, query_start, in_hbm(queries), in_hbm(kv))


def backward_kernel(heads, part, info, probs_ref, out_ref, mine_ref, got_ref, q_ref, k_ref, v_ref, *rest):
    if part:
        old_own, old_other, _, gq_ref, own_ref, other_ref, grad_t, stack, delta, total_q, dscores, other = rest
    else:
        gq_ref, own_ref, other_ref, grad_t, stack, delta, total_q, dscores = rest
        other = other_ref
    step = pl.program_id(0)
    count = info[COUNT]
    rows = q_ref.shape[0]

    @pl.when(step == 0)
    def _():
        if part:
            own_ref[...] = old_own[...]
            other[...] = old_other[...]
        else:
            own_ref[...] = jnp.zeros_like(own_ref)
            other[...] = jnp.zeros_like(other)
        total_q[...] = jnp.zeros_like(total_q)
        for h in range(heads):
            cols = slice(h * rows, (h + 1) * rows)
            wide = slice(h * HEAD_WIDTH, (h + 1) * HEAD_WIDTH)
            grad = (mine_ref[:, wide] + got_ref[:, wide]).astype(BF16)
            turned = grad.T
            grad_t[:, cols] = turned
            stack[cols, :HEAD_WIDTH] = q_ref[:, wide]
            stack[cols, HEAD_WIDTH:] = grad
            delta[:, cols] = jnp.sum(turned.astype(F32) * out_ref[:, cols], axis=0, keepdims=True)

    @pl.when(step < count)
    def _():
        block = info[FIRST] + step
        keys_t = k_ref[...].T
        for h in range(heads):
            cols = slice(h * rows, (h + 1) * rows)
            dprob = dot(v_ref[...], grad_t[:, cols])
            dscores[:, cols] = (probs_ref[:, cols].astype(F32) * (dprob - delta[:, cols])).astype(BF16)
        total_q[...] += dot(keys_t, dscores[...])
        key_sum = dot(dscores[...], stack[:, :HEAD_WIDTH])
        value_sum = dot(probs_ref[...], stack[:, HEAD_WIDTH:])

        def add(ref):
            ref[block // 2, :, :HEAD_WIDTH] += key_sum * SCALE
            ref[block // 2, :, HEAD_WIDTH:] += value_sum

        pl.when(block % 2 == info[CORE])(lambda: add(own_ref))
        pl.when(block % 2 != info[CORE])(lambda: add(other))

    @pl.when(step == count - 1)
    def _():
        for h in range(heads):
            cols = slice(h * rows, (h + 1) * rows)
            wide = slice(h * HEAD_WIDTH, (h + 1) * HEAD_WIDTH)
            gq_ref[:, wide] = (total_q[:, cols].T * SCALE).astype(BF16)
        if part:
            other_ref[...] = other[...].astype(BF16)


def backward(part, info, probs, outs, mine, got, queries, kv, carried):
    rows, width = queries.shape
    heads = width // HEAD_WIDTH // CHUNKS
    last = part == CHUNKS - 1
    sums = (8, KEY_BLOCK, 2 * HEAD_WIDTH)

    def near(i, r):
        return jnp.minimum(i, r[COUNT] - 1)

    sum_spec = pl.BlockSpec(sums, lambda i, r: (0, 0, 0), pipeline_mode=pl.Buffered(1))
    gq_spec = pl.BlockSpec((rows, heads * HEAD_WIDTH), lambda i, r: (0, part))
    scratch = [
        pltpu.VMEM((HEAD_WIDTH, heads * rows), BF16),
        pltpu.VMEM((heads * rows, 2 * HEAD_WIDTH), BF16),
        pltpu.VMEM((1, heads * rows), F32),
        pltpu.VMEM((HEAD_WIDTH, heads * rows), F32),
        pltpu.VMEM((KEY_BLOCK, heads * rows), BF16),
    ]
    in_specs = [
        pl.BlockSpec((KEY_BLOCK, heads * rows), lambda i, r: (near(i, r), 0)),
        pl.BlockSpec((HEAD_WIDTH, heads * rows), lambda i, r: (0, 0)),
        pl.BlockSpec((rows, heads * HEAD_WIDTH), lambda i, r: (0, 0)),
        pl.BlockSpec((rows, heads * HEAD_WIDTH), lambda i, r: (0, 0)),
        pl.BlockSpec((rows, heads * HEAD_WIDTH), lambda i, r: (0, part)),
        pl.BlockSpec((KEY_BLOCK, HEAD_WIDTH), lambda i, r: (r[TABLE + r[FIRST] + near(i, r)], 0)),
        pl.BlockSpec(
            (KEY_BLOCK, HEAD_WIDTH), lambda i, r: (r[TABLE + 16 + r[FIRST] + near(i, r)], 0)
        ),
    ]
    aliases = {}
    if part:
        in_specs += [sum_spec, sum_spec, pl.BlockSpec(memory_space=pl.ANY)]
        scratch.append(pltpu.VMEM(sums, F32))
        aliases = {10: 0}
    return pl.pallas_call(
        functools.partial(backward_kernel, heads, part),
        grid_spec=pltpu.PrefetchScalarGridSpec(
            num_scalar_prefetch=1,
            grid=(most_blocks(rows),),
            in_specs=in_specs,
            out_specs=[gq_spec, sum_spec, sum_spec],
            scratch_shapes=scratch,
        ),
        out_shape=[
            jax.ShapeDtypeStruct((rows, width), BF16),
            jax.ShapeDtypeStruct(sums, F32),
            jax.ShapeDtypeStruct(sums, BF16 if last else F32),
        ],
        input_output_aliases=aliases,
        compiler_params=pltpu.CompilerParams(vmem_limit_bytes=VMEM_LIMIT),
        cost_estimate=pl.CostEstimate(flops=8 * 10**9, bytes_accessed=10 * 2**20, transcendentals=0),
        name="backward%d" % part,
    )(info, in_hbm(probs), outs, mine, got, in_hbm(queries), in_hbm(kv), in_hbm(kv), *carried)


def project_kernel(grad_count, places, slots, *rest):
    grads, (*blocks, own_ref, other_ref, grad) = rest[:grad_count], rest[grad_count:]
    half = own_ref.shape[0]
    at = 0
    for ref in grads:
        chip, row, size = at // (2 * half), at % (2 * half), ref.shape[0]
        grad[chip, row : row + size, :] = ref[...]
        at += size
    for i, (ref, (slot, feature)) in enumerate(zip(blocks, places)):
        cols = slice(feature, feature + ref.shape[1])
        for j in range(ref.shape[0]):
            for out, row in ((own_ref, 0), (other_ref, half)):
                term = dot_t(grad[slots[slot + j], row : row + half, :], ref[j])
                if i == 0 and j == 0:
                    out[:, cols] = term
                else:
                    out[:, cols] += term


def project(part, slots, grads, blocks):
    depth = grads[0].shape[1]
    chips = slots.shape[0]
    tokens = sum(ref.shape[0] for ref in grads) // chips
    features = blocks[0][0].shape[1]
    half = jax.ShapeDtypeStruct((tokens // 2, features), F32)
    out_spec = pl.BlockSpec((tokens // 2, features), lambda i: (0, 0))
    return pl.pallas_call(
        functools.partial(project_kernel, len(grads), [(slot, at) for _, slot, at in blocks]),
        grid=(1,),
        in_specs=[pl.BlockSpec(memory_space=pltpu.SMEM)]
        + [pl.BlockSpec(ref.shape, lambda i: (0, 0)) for ref in grads]
        + [pl.BlockSpec(block.shape, lambda i: (0, 0, 0)) for block, _, _ in blocks],
        out_specs=[out_spec, out_spec],
        out_shape=[half, half],
        scratch_shapes=[pltpu.VMEM((chips, tokens, depth), BF16)],
        compiler_params=pltpu.CompilerParams(vmem_limit_bytes=24 * 2**20),
        cost_estimate=pl.CostEstimate(
            flops=2 * tokens * features * depth * chips,
            bytes_accessed=10 * 2**20,
            transcendentals=0,
        ),
        name="project%d" % part,
    )(slots, *grads, *[in_hbm(block) if block.shape[0] > 1 else block for block, _, _ in blocks])


def local(queries, keys, values, grad_out, out_weight, lengths):
    rows = queries.shape[0]
    rank = lax.axis_index("dp")
    core = rank % 2
    x, z = rank // 4, (rank // 2) % 2

    query_pos = rank * rows + jnp.arange(rows, dtype=jnp.int32)
    ends = jnp.cumsum(lengths)[:-1]
    query_start = jnp.max(
        jnp.where(ends[None, :] <= query_pos[:, None], ends[None, :], 0), axis=1
    )
    first = query_start[0] // KEY_BLOCK
    last = query_pos[-1] // KEY_BLOCK
    clear = (query_start[-1] + KEY_BLOCK - 1) // KEY_BLOCK
    block = jnp.arange(16, dtype=jnp.int32)
    place = block // 2 * 2
    here = place + jnp.where(block % 2 == core, 0, 1)
    there = 16 + place + jnp.where(block % 2 == core, 1, 0)
    table = [jnp.where(core == 0, here, there), jnp.where(core == 0, there, here)]
    scalars = jnp.stack([first, last - first + 1, clear, core])
    info = jnp.concatenate([scalars, *table]).astype(jnp.int32)
    query_pos, query_start = query_pos[None, :], query_start[None, :]

    depth = out_weight.shape[1]
    mine = lax.dynamic_slice_in_dim(grad_out, core * depth, depth, 1)
    other = lax.dynamic_slice_in_dim(grad_out, (1 - core) * depth, depth, 1)
    chip_grad = jnp.concatenate([mine, dp_move(other, 0, 0, 1)], axis=0)

    groups = [[2 * i + c for i in range(8)] for c in range(2)]
    kept = jnp.where(core == 0, keys, values)
    got = dp_move(jnp.where(core == 0, values, keys), 0, 0, 1)
    chip = jnp.concatenate([kept, got], axis=0)
    ring = lax.all_to_all(
        jnp.broadcast_to(chip, (8, *chip.shape)), "dp", 0, 0, axis_index_groups=groups, tiled=True
    ).reshape(-1, HEAD_WIDTH)

    def far(move, ring):
        half = ring[0].shape[0] // 2
        return [move(ring[1][:half], 1), move(ring[2][half:], -1)]

    def both(move, block):
        return [block, move(block, 1), move(block, -1)]

    def along_x(block, step):
        return dp_move(block, step, 0, 0)

    def along_y(block, step):
        return tensor_move(block, 0, step)

    grad0 = both(along_y, chip_grad)
    grad_pair = tensor_move(chip_grad, 1, 0)
    ring, grad0, grad_pair = lax.optimization_barrier((ring, grad0, grad_pair))
    kv = jnp.concatenate([ring, dp_move(ring, 0, 0, 1)], axis=0)

    groups_x = [[x_ * 4 + zc for x_ in range(4)] for zc in range(4)]

    def gather_x(block):
        return lax.all_gather(block, "dp", axis=0, axis_index_groups=groups_x)

    size = out_weight.shape[0] // CHUNKS
    own, _ = lax.optimization_barrier(([out_weight[:size], out_weight[size:]], ring))
    plane1 = gather_x(own[1])
    paired = [dp_move(block, 0, 1, 0) for block in own]
    kv, grad_pair, own0 = lax.optimization_barrier((kv, grad_pair, own[0]))
    plane0 = gather_x(own0)

    grad_far0 = far(along_y, grad0)
    grad1 = both(along_y, grad_pair)
    parts = [forward(0, info, query_pos, query_start, queries, kv)]
    parts[0], paired, grad_far0, grad1 = lax.optimization_barrier(
        (parts[0], paired, grad_far0, grad1)
    )
    ring0 = both(along_x, paired[0])
    grad_far1 = far(along_y, grad1)
    rest = jnp.concatenate(
        [lax.dynamic_slice_in_dim(plane1, (x + i) % 4, 1, 0) for i in range(1, 4)], axis=0
    )
    rest, later = lax.optimization_barrier((rest, queries))
    rest = dp_move(rest, 0, 1, 0)
    parts.append(forward(1, info, query_pos, query_start, later, kv))
    parts[1], ring0 = lax.optimization_barrier((parts[1], ring0))
    ring0 += far(along_x, ring0)
    all_grad = grad0 + grad_far0 + grad1 + grad_far1

    t = lax.axis_index("tensor")

    def slot(x_, z_):
        source = 2 * (x_ % 4) + z_
        y_distance = (source - t) % 4
        turn = jnp.where(
            y_distance == 0, 0, jnp.where(y_distance == 3, 1, jnp.where(y_distance == 1, 2, 3))
        )
        return jnp.where(source // 4 == t // 4, 0, 4) + turn

    same = [slot(i, z) for i in range(4)]
    slots = [
        jnp.stack(same + [slot(x + i, 1 - z) for i in (0, -1, 1, 2)]).astype(jnp.int32),
        jnp.stack(same + [slot(x + i, 1 - z) for i in range(4)]).astype(jnp.int32),
    ]
    blocks = [
        [(plane0, 0, 0)] + [(ring0[i][None], 4 + i, 0) for i in range(3)],
        [(plane1, 0, 0), (paired[1][None], 4, 0), (rest, 5, 0)],
    ]
    blocks[0] += [(ring0[3][None], 7, 0), (ring0[4][None], 7, size // 2)]

    carried = ()
    for part in range(CHUNKS):
        mine, other = project(part, slots[part], all_grad, blocks[part])
        got = dp_move(other, 0, 0, 1)
        probs, outs = parts[part]
        grad_queries, own_sums, other_sums = backward(
            part, info, probs, outs, mine, got, queries, kv, carried
        )
        carried = (own_sums, other_sums, grad_queries)

    chip_sums = (own_sums + dp_move(other_sums, 0, 0, 1).astype(F32)).astype(BF16)
    terms = lax.all_to_all(chip_sums, "dp", 0, 0, axis_index_groups=groups, tiled=True)
    done = jnp.sum(terms.astype(F32), axis=0).astype(BF16)
    return grad_queries, done[:, :HEAD_WIDTH], done[:, HEAD_WIDTH:]


def solution(mesh):
    return jax.shard_map(
        local,
        mesh=mesh,
        in_specs=(
            P("dp", "tensor"),
            P("dp", "tensor"),
            P("dp", "tensor"),
            P("dp", "tensor"),
            P("tensor", "dp"),
            P(),
        ),
        out_specs=(P("dp", "tensor"), P("dp", "tensor"), P("dp", "tensor")),
        check_vma=False,
    )
```

```python
import functools
import math

import jax
import jax.numpy as jnp
from jax import lax
from jax.experimental import pallas as pl
from jax.experimental.pallas import tpu as pltpu
from jax.sharding import PartitionSpec as P

HEAD_WIDTH = 128
KEY_BLOCK = 256
MOST = 2560
CHUNKS = 2
PAIR = 2
MASKED = -1e30
SCALE = 1.0 / math.sqrt(HEAD_WIDTH)
LOG2E = 1.0 / math.log(2.0)
BF16 = jnp.bfloat16
F32 = jnp.float32
VMEM_LIMIT = 24 * 2**20

FIRST, COUNT, CLEAR, CORE, TABLE = 0, 1, 2, 3, 4


def dp_move(value, dx, dz, dc):
    pairs = []
    for x in range(4):
        for z in range(2):
            for c in range(2):
                target = ((x + dx) % 4) * 4 + ((z + dz) % 2) * 2 + (c + dc) % 2
                pairs.append((x * 4 + z * 2 + c, target))
    return lax.ppermute(value, "dp", pairs)


def tensor_move(value, dz, dy):
    pairs = []
    for z in range(2):
        for y in range(4):
            pairs.append((z * 4 + y, ((z + dz) % 2) * 4 + (y + dy) % 4))
    return lax.ppermute(value, "tensor", pairs)


def after(value, *others):
    return lax.optimization_barrier((value, *others))[0]


def in_hbm(value):
    return pltpu.with_memory_space_constraint(value, pltpu.HBM)


def dot(left, right):
    return lax.dot_general(left, right, (((1,), (0,)), ((), ())), preferred_element_type=F32)


def dot_t(left, right):
    return lax.dot_general(left, right, (((1,), (1,)), ((), ())), preferred_element_type=F32)


def block_rows(index):
    return pl.ds(pl.multiple_of(index * KEY_BLOCK, KEY_BLOCK), KEY_BLOCK)


def forward_kernel(info, pos_ref, start_ref, q_ref, kv_ref, probs_ref, out_ref, score, vt):
    first, count = info[FIRST], info[COUNT]
    rows = q_ref.shape[0]
    heads = q_ref.shape[1] // HEAD_WIDTH
    query_t = jnp.concatenate(
        [q_ref[:, h * HEAD_WIDTH : (h + 1) * HEAD_WIDTH].T for h in range(heads)], axis=1
    )
    wide = heads * rows

    def groups(values):
        return values.reshape(KEY_BLOCK // 8, 8, wide)

    @pl.when(pl.program_id(0) == 0)
    def _():
        def turn(index, _):
            source = info[TABLE + 16 + first + index]
            vt[:, block_rows(index)] = kv_ref[block_rows(source), :].T
            return 0
        lax.fori_loop(0, count, turn, 0)

    def product(index):
        return dot(kv_ref[block_rows(info[TABLE + first + index]), :], query_t)

    def masked_step(index, top):
        key_pos = (first + index) * KEY_BLOCK + lax.broadcasted_iota(jnp.int32, (KEY_BLOCK, rows), 0)
        live = (key_pos >= start_ref[...]) & (key_pos <= pos_ref[...])
        raw = product(index)
        raw = jnp.concatenate(
            [jnp.where(live, raw[:, h * rows : (h + 1) * rows], MASKED) for h in range(heads)], axis=1
        )
        score[block_rows(index), :] = raw
        return jnp.maximum(top, jnp.max(groups(raw), axis=0))

    def clear_step(index, top):
        raw = product(index)
        score[block_rows(index), :] = raw
        return jnp.maximum(top, jnp.max(groups(raw), axis=0))

    clear = jnp.minimum(info[CLEAR] - first, count - 1)
    top = jnp.full((8, wide), MASKED, F32)
    top = lax.fori_loop(0, clear, masked_step, top)
    top = lax.fori_loop(clear, count - 1, clear_step, top)
    top = masked_step(count - 1, top)
    top = jnp.max(top, axis=0, keepdims=True) * (SCALE * LOG2E)

    def mass_step(index, mass):
        weights = jnp.exp2(score[block_rows(index), :] * (SCALE * LOG2E) - top)
        score[block_rows(index), :] = weights
        return mass + jnp.sum(groups(weights), axis=0)

    mass = lax.fori_loop(0, count, mass_step, jnp.zeros((8, wide), F32))
    share = 1.0 / jnp.sum(mass, axis=0, keepdims=True)
    out_ref[...] = jnp.zeros_like(out_ref)

    def probs_step(index, _):
        probs = (score[block_rows(index), :] * share).astype(BF16)
        probs_ref[block_rows(index), :] = probs
        out_ref[...] += dot(vt[:, block_rows(index)], probs)
        return 0

    lax.fori_loop(0, count, probs_step, 0)


def most_blocks(rows):
    return (MOST + rows - 2) // KEY_BLOCK + 1


def forward(info, query_pos, query_start, queries, kv):
    rows, width = queries.shape
    heads = width // HEAD_WIDTH
    live = most_blocks(rows) * KEY_BLOCK
    line = pl.BlockSpec((1, rows), lambda h, r: (0, 0))
    return pl.pallas_call(
        forward_kernel,
        grid_spec=pltpu.PrefetchScalarGridSpec(
            num_scalar_prefetch=1,
            grid=(heads // PAIR,),
            in_specs=[
                line,
                line,
                pl.BlockSpec((rows, PAIR * HEAD_WIDTH), lambda h, r: (0, h)),
                pl.BlockSpec(kv.shape, lambda h, r: (0, 0), pipeline_mode=pl.Buffered(1)),
            ],
            out_specs=[
                pl.BlockSpec((live, PAIR * rows), lambda h, r: (0, h)),
                pl.BlockSpec((HEAD_WIDTH, PAIR * rows), lambda h, r: (0, h)),
            ],
            scratch_shapes=[
                pltpu.VMEM((live, PAIR * rows), F32),
                pltpu.VMEM((HEAD_WIDTH, live), BF16),
            ],
        ),
        out_shape=[
            pltpu.HBM((live, heads * rows), BF16),
            jax.ShapeDtypeStruct((HEAD_WIDTH, heads * rows), F32),
        ],
        compiler_params=pltpu.CompilerParams(vmem_limit_bytes=VMEM_LIMIT),
        cost_estimate=pl.CostEstimate(flops=10**10, bytes_accessed=10 * 2**20, transcendentals=0),
        name="forward",
    )(info, query_pos, query_start, in_hbm(queries), in_hbm(kv))


def backward_kernel(heads, info, *rest):
    terms, rest = rest[: 2 * CHUNKS], rest[2 * CHUNKS :]
    probs_ref, out_ref, q_ref, k_ref, v_ref, gq_ref, own_ref, other_ref, *scratch = rest
    grad_t, stack, delta, total_q, dscores, other = scratch
    step = pl.program_id(0)
    count = info[COUNT]
    rows = q_ref.shape[0]

    @pl.when(step == 0)
    def _():
        own_ref[...] = jnp.zeros_like(own_ref)
        other[...] = jnp.zeros_like(other)
        total_q[...] = jnp.zeros_like(total_q)
        for h in range(heads):
            cols = slice(h * rows, (h + 1) * rows)
            wide = slice(h * HEAD_WIDTH, (h + 1) * HEAD_WIDTH)
            part, at = divmod(h * CHUNKS, heads)
            here = slice(at // CHUNKS * HEAD_WIDTH, (at // CHUNKS + 1) * HEAD_WIDTH)
            mine, got = terms[2 * part], terms[2 * part + 1]
            grad = (mine[:, here] + got[:, here]).astype(BF16)
            turned = grad.T
            grad_t[:, cols] = turned
            stack[cols, :HEAD_WIDTH] = q_ref[:, wide]
            stack[cols, HEAD_WIDTH:] = grad
            delta[:, cols] = jnp.sum(turned.astype(F32) * out_ref[:, cols], axis=0, keepdims=True)

    @pl.when(step < count)
    def _():
        block = info[FIRST] + step
        keys_t = k_ref[...].T
        for h in range(heads):
            cols = slice(h * rows, (h + 1) * rows)
            dprob = dot(v_ref[...], grad_t[:, cols])
            dscores[:, cols] = (probs_ref[:, cols].astype(F32) * (dprob - delta[:, cols])).astype(BF16)
        total_q[...] += dot(keys_t, dscores[...])
        key_sum = dot(dscores[...], stack[:, :HEAD_WIDTH])
        value_sum = dot(probs_ref[...], stack[:, HEAD_WIDTH:])

        def add(ref):
            ref[block // 2, :, :HEAD_WIDTH] += key_sum * SCALE
            ref[block // 2, :, HEAD_WIDTH:] += value_sum

        pl.when(block % 2 == info[CORE])(lambda: add(own_ref))
        pl.when(block % 2 != info[CORE])(lambda: add(other))

    @pl.when(step == count - 1)
    def _():
        for h in range(heads):
            cols = slice(h * rows, (h + 1) * rows)
            wide = slice(h * HEAD_WIDTH, (h + 1) * HEAD_WIDTH)
            gq_ref[:, wide] = (total_q[:, cols].T * SCALE).astype(BF16)
        other_ref[...] = other[...].astype(BF16)


def backward(info, terms, probs, outs, queries, kv):
    rows, width = queries.shape
    heads = width // HEAD_WIDTH
    sums = (8, KEY_BLOCK, 2 * HEAD_WIDTH)

    def near(i, r):
        return jnp.minimum(i, r[COUNT] - 1)

    def once(shape):
        return pl.BlockSpec(shape, lambda i, r: (0,) * len(shape), pipeline_mode=pl.Buffered(1))

    return pl.pallas_call(
        functools.partial(backward_kernel, heads),
        grid_spec=pltpu.PrefetchScalarGridSpec(
            num_scalar_prefetch=1,
            grid=(most_blocks(rows),),
            in_specs=[once(term.shape) for term in terms]
            + [
                pl.BlockSpec((KEY_BLOCK, heads * rows), lambda i, r: (near(i, r), 0)),
                once(outs.shape),
                once(queries.shape),
                pl.BlockSpec(
                    (KEY_BLOCK, HEAD_WIDTH), lambda i, r: (r[TABLE + r[FIRST] + near(i, r)], 0)
                ),
                pl.BlockSpec(
                    (KEY_BLOCK, HEAD_WIDTH), lambda i, r: (r[TABLE + 16 + r[FIRST] + near(i, r)], 0)
                ),
            ],
            out_specs=[once((rows, width)), once(sums), once(sums)],
            scratch_shapes=[
                pltpu.VMEM((HEAD_WIDTH, heads * rows), BF16),
                pltpu.VMEM((heads * rows, 2 * HEAD_WIDTH), BF16),
                pltpu.VMEM((1, heads * rows), F32),
                pltpu.VMEM((HEAD_WIDTH, heads * rows), F32),
                pltpu.VMEM((KEY_BLOCK, heads * rows), BF16),
                pltpu.VMEM(sums, F32),
            ],
        ),
        out_shape=[
            jax.ShapeDtypeStruct((rows, width), BF16),
            jax.ShapeDtypeStruct(sums, F32),
            jax.ShapeDtypeStruct(sums, BF16),
        ],
        compiler_params=pltpu.CompilerParams(vmem_limit_bytes=VMEM_LIMIT),
        cost_estimate=pl.CostEstimate(
            flops=8 * 10**9, bytes_accessed=10 * 2**20, transcendentals=0
        ),
        name="backward",
    )(info, *terms, in_hbm(probs), outs, in_hbm(queries), in_hbm(kv), in_hbm(kv))


def project_kernel(slots, grad_ref, *rest):
    *stacks, own_ref, other_ref = rest
    half = own_ref.shape[0]
    k = 0
    for ref in stacks:
        for j in range(ref.shape[0]):
            for out, row in ((own_ref, 0), (other_ref, half)):
                term = dot_t(grad_ref[slots[k], row : row + half, :], ref[j])
                if k == 0:
                    out[...] = term
                else:
                    out[...] += term
            k += 1


def project(part, slots, grads, stacks):
    chips, tokens, depth = grads.shape
    features = stacks[0].shape[1]
    half = jax.ShapeDtypeStruct((tokens // 2, features), F32)
    out_spec = pl.BlockSpec((tokens // 2, features), lambda i: (0, 0))
    return pl.pallas_call(
        project_kernel,
        grid=(1,),
        in_specs=[pl.BlockSpec(memory_space=pltpu.SMEM)]
        + [pl.BlockSpec(ref.shape, lambda i: (0, 0, 0)) for ref in (grads, *stacks)],
        out_specs=[out_spec, out_spec],
        out_shape=[half, half],
        compiler_params=pltpu.CompilerParams(vmem_limit_bytes=VMEM_LIMIT),
        cost_estimate=pl.CostEstimate(
            flops=2 * tokens * features * depth * chips,
            bytes_accessed=10 * 2**20,
            transcendentals=0,
        ),
        name="project%d" % part,
    )(slots, in_hbm(grads), *[in_hbm(stack) if stack.shape[0] > 1 else stack for stack in stacks])


def local(queries, keys, values, grad_out, out_weight, lengths):
    rows = queries.shape[0]
    rank = lax.axis_index("dp")
    core = rank % 2
    x, z = rank // 4, (rank // 2) % 2

    query_pos = rank * rows + jnp.arange(rows, dtype=jnp.int32)
    ends = jnp.cumsum(lengths)[:-1]
    query_start = jnp.max(
        jnp.where(ends[None, :] <= query_pos[:, None], ends[None, :], 0), axis=1
    )
    first = query_start[0] // KEY_BLOCK
    last = query_pos[-1] // KEY_BLOCK
    clear = (query_start[-1] + KEY_BLOCK - 1) // KEY_BLOCK
    block = jnp.arange(16, dtype=jnp.int32)
    place = block // 2 * 2
    here = place + jnp.where(block % 2 == core, 0, 1)
    there = 16 + place + jnp.where(block % 2 == core, 1, 0)
    table = [jnp.where(core == 0, here, there), jnp.where(core == 0, there, here)]
    scalars = jnp.stack([first, last - first + 1, clear, core])
    info = jnp.concatenate([scalars, *table]).astype(jnp.int32)
    query_pos, query_start = query_pos[None, :], query_start[None, :]

    groups_x = [[x_ * 4 + zc for x_ in range(4)] for zc in range(4)]

    def gather_x(block):
        return lax.all_gather(block, "dp", axis=0, axis_index_groups=groups_x)

    def spread(block, axis, groups):
        copies = jnp.broadcast_to(block, (len(groups[0]), *block.shape))
        return lax.all_to_all(copies, axis, 0, 0, axis_index_groups=groups, tiled=True)

    size = out_weight.shape[0] // CHUNKS
    own = [out_weight[:size], out_weight[size:]]
    plane1 = gather_x(own[1])

    groups = [[2 * i + c for i in range(8)] for c in range(2)]
    kept = jnp.where(core == 0, keys, values)
    got = dp_move(jnp.where(core == 0, values, keys), 0, 0, 1)
    plane0 = gather_x(after(own[0], got))
    ring = spread(jnp.concatenate([kept, got], axis=0), "dp", groups).reshape(-1, HEAD_WIDTH)

    depth = out_weight.shape[1]
    mine = lax.dynamic_slice_in_dim(grad_out, core * depth, depth, 1)
    other = lax.dynamic_slice_in_dim(grad_out, (1 - core) * depth, depth, 1)
    chip_grad = jnp.concatenate([mine, dp_move(other, 0, 0, 1)], axis=0)
    grad_pair = jnp.stack([chip_grad, tensor_move(chip_grad, 1, 0)])
    groups_y = [[z_ * 4 + y_ for y_ in range(4)] for z_ in range(2)]
    all_grad = spread(grad_pair, "tensor", groups_y).reshape(8, 2 * rows, depth)

    paired = [dp_move(block, 0, 1, 0) for block in own]
    ring, paired, grad_pair = lax.optimization_barrier((ring, paired, grad_pair))
    kv = jnp.concatenate([ring, dp_move(ring, 0, 0, 1)], axis=0)
    other_plane = spread(paired[0], "dp", groups_x).reshape(4, size, depth)
    rest = jnp.concatenate(
        [lax.dynamic_slice_in_dim(plane1, (x + i) % 4, 1, 0) for i in range(1, 4)], axis=0
    )
    rest, kv = lax.optimization_barrier((rest, kv))
    rest = dp_move(rest, 0, 1, 0)
    probs, outs = forward(info, query_pos, query_start, queries, kv)

    t = lax.axis_index("tensor")

    def slot(x_, z_):
        source = 2 * (x_ % 4) + z_
        return source % 4 * 2 + jnp.where(source // 4 == t // 4, 0, 1)

    same = [slot(i, z) for i in range(4)]
    slots = [
        jnp.stack(same + [slot(i, 1 - z) for i in range(4)]).astype(jnp.int32),
        jnp.stack(same + [slot(x + i, 1 - z) for i in range(4)]).astype(jnp.int32),
    ]
    slots[0] = after(slots[0], outs)
    stacks = [[plane0, other_plane], [plane1, paired[1][None], rest]]
    terms = []
    for part in range(CHUNKS):
        mine, other = project(part, slots[part], all_grad, stacks[part])
        terms += [mine, dp_move(other, 0, 0, 1)]
    grad_queries, own_sums, other_sums = backward(info, terms, probs, outs, queries, kv)

    chip_sums = (own_sums + dp_move(other_sums, 0, 0, 1).astype(F32)).astype(BF16)
    terms = lax.all_to_all(chip_sums, "dp", 0, 0, axis_index_groups=groups, tiled=True)
    done = jnp.sum(terms.astype(F32), axis=0).astype(BF16)
    return grad_queries, done[:, :HEAD_WIDTH], done[:, HEAD_WIDTH:]


def solution(mesh):
    return jax.shard_map(
        local,
        mesh=mesh,
        in_specs=(
            P("dp", "tensor"),
            P("dp", "tensor"),
            P("dp", "tensor"),
            P("dp", "tensor"),
            P("tensor", "dp"),
            P(),
        ),
        out_specs=(P("dp", "tensor"), P("dp", "tensor"), P("dp", "tensor")),
        check_vma=False,
    )
```

```python
import functools
import math

import jax
import jax.numpy as jnp
from jax import lax
from jax.experimental import pallas as pl
from jax.experimental.pallas import tpu as pltpu
from jax.sharding import PartitionSpec as P

HEAD_WIDTH = 128
KEY_BLOCK = 256
MOST = 2560
CHUNKS = 2
SPLIT = 5 * HEAD_WIDTH
PAIR = 2
MASKED = -1e30
SCALE = 1.0 / math.sqrt(HEAD_WIDTH)
LOG2E = 1.0 / math.log(2.0)
BF16 = jnp.bfloat16
F32 = jnp.float32
VMEM_LIMIT = 26 * 2**20

FIRST, COUNT, CLEAR, CORE, TABLE = 0, 1, 2, 3, 4


def dp_move(value, dx, dz, dc):
    pairs = []
    for x in range(4):
        for z in range(2):
            for c in range(2):
                target = ((x + dx) % 4) * 4 + ((z + dz) % 2) * 2 + (c + dc) % 2
                pairs.append((x * 4 + z * 2 + c, target))
    return lax.ppermute(value, "dp", pairs)


def tensor_move(value, dz, dy):
    pairs = []
    for z in range(2):
        for y in range(4):
            pairs.append((z * 4 + y, ((z + dz) % 2) * 4 + (y + dy) % 4))
    return lax.ppermute(value, "tensor", pairs)


def after(value, *others):
    return lax.optimization_barrier((value, *others))[0]


def in_hbm(value):
    return pltpu.with_memory_space_constraint(value, pltpu.HBM)


def dot(left, right):
    return lax.dot_general(left, right, (((1,), (0,)), ((), ())), preferred_element_type=F32)


def dot_t(left, right):
    return lax.dot_general(left, right, (((1,), (1,)), ((), ())), preferred_element_type=F32)


def block_rows(index):
    return pl.ds(pl.multiple_of(index * KEY_BLOCK, KEY_BLOCK), KEY_BLOCK)


def forward_kernel(info, pos_ref, start_ref, q_ref, kv_ref, probs_ref, out_ref, score, vt):
    first, count = info[FIRST], info[COUNT]
    rows = q_ref.shape[0]
    heads = q_ref.shape[1] // HEAD_WIDTH
    query_t = jnp.concatenate(
        [q_ref[:, h * HEAD_WIDTH : (h + 1) * HEAD_WIDTH].T for h in range(heads)], axis=1
    )
    wide = heads * rows

    def groups(values):
        return values.reshape(KEY_BLOCK // 8, 8, wide)

    @pl.when(pl.program_id(0) == 0)
    def _():
        def turn(index, _):
            source = info[TABLE + 16 + first + index]
            vt[:, block_rows(index)] = kv_ref[block_rows(source), :].T
            return 0
        lax.fori_loop(0, count, turn, 0)

    def product(index):
        return dot(kv_ref[block_rows(info[TABLE + first + index]), :], query_t)

    def masked_step(index, top):
        key_pos = (first + index) * KEY_BLOCK + lax.broadcasted_iota(jnp.int32, (KEY_BLOCK, rows), 0)
        live = (key_pos >= start_ref[...]) & (key_pos <= pos_ref[...])
        raw = product(index)
        raw = jnp.concatenate(
            [jnp.where(live, raw[:, h * rows : (h + 1) * rows], MASKED) for h in range(heads)], axis=1
        )
        score[block_rows(index), :] = raw
        return jnp.maximum(top, jnp.max(groups(raw), axis=0))

    def clear_step(index, top):
        raw = product(index)
        score[block_rows(index), :] = raw
        return jnp.maximum(top, jnp.max(groups(raw), axis=0))

    clear = jnp.minimum(info[CLEAR] - first, count - 1)
    top = jnp.full((8, wide), MASKED, F32)
    top = lax.fori_loop(0, clear, masked_step, top)
    top = lax.fori_loop(clear, count - 1, clear_step, top)
    top = masked_step(count - 1, top)
    top = jnp.max(top, axis=0, keepdims=True) * (SCALE * LOG2E)

    def mass_step(index, mass):
        weights = jnp.exp2(score[block_rows(index), :] * (SCALE * LOG2E) - top)
        score[block_rows(index), :] = weights
        return mass + jnp.sum(groups(weights), axis=0)

    mass = lax.fori_loop(0, count, mass_step, jnp.zeros((8, wide), F32))
    share = 1.0 / jnp.sum(mass, axis=0, keepdims=True)
    out_ref[...] = jnp.zeros_like(out_ref)

    def probs_step(index, _):
        probs = (score[block_rows(index), :] * share).astype(BF16)
        probs_ref[block_rows(index), :] = probs
        out_ref[...] += dot(vt[:, block_rows(index)], probs)
        return 0

    lax.fori_loop(0, count, probs_step, 0)


def most_blocks(rows):
    return (MOST + rows - 2) // KEY_BLOCK + 1


def forward(part, info, query_pos, query_start, queries, kv):
    rows, width = queries.shape
    heads = width // HEAD_WIDTH // CHUNKS
    steps = heads // PAIR
    live = most_blocks(rows) * KEY_BLOCK
    line = pl.BlockSpec((1, rows), lambda h, r: (0, 0))
    return pl.pallas_call(
        forward_kernel,
        grid_spec=pltpu.PrefetchScalarGridSpec(
            num_scalar_prefetch=1,
            grid=(steps,),
            in_specs=[
                line,
                line,
                pl.BlockSpec((rows, PAIR * HEAD_WIDTH), lambda h, r: (0, part * steps + h)),
                pl.BlockSpec(kv.shape, lambda h, r: (0, 0), pipeline_mode=pl.Buffered(1)),
            ],
            out_specs=[
                pl.BlockSpec((live, PAIR * rows), lambda h, r: (0, h)),
                pl.BlockSpec((HEAD_WIDTH, PAIR * rows), lambda h, r: (0, h)),
            ],
            scratch_shapes=[
                pltpu.VMEM((live, PAIR * rows), F32),
                pltpu.VMEM((HEAD_WIDTH, live), BF16),
            ],
        ),
        out_shape=[
            pltpu.HBM((live, heads * rows), BF16),
            jax.ShapeDtypeStruct((HEAD_WIDTH, heads * rows), F32),
        ],
        compiler_params=pltpu.CompilerParams(vmem_limit_bytes=VMEM_LIMIT),
        cost_estimate=pl.CostEstimate(flops=10**10, bytes_accessed=10 * 2**20, transcendentals=0),
        name="forward%d" % part,
    )(info, query_pos, query_start, in_hbm(queries), in_hbm(kv))


def backward_kernel(heads, info, *rest):
    terms, all_probs, all_outs = rest[:4], rest[4:6], rest[6:8]
    q_ref, k_ref, v_ref, gq_ref, own_ref, other_ref, *scratch = rest[8:]
    grad_t, stack, delta, total_q, dscores, other = scratch
    step = pl.program_id(0)
    count = info[COUNT]
    rows = q_ref.shape[0]
    width = heads // 2 * rows

    def columns(refs, h):
        at = h * rows % width
        return refs[h * rows // width][:, at : at + rows]

    @pl.when(step == 0)
    def _():
        own_ref[...] = jnp.zeros_like(own_ref)
        other[...] = jnp.zeros_like(other)
        total_q[...] = jnp.zeros_like(total_q)
        for h in range(heads):
            cols = slice(h * rows, (h + 1) * rows)
            wide = slice(h * HEAD_WIDTH, (h + 1) * HEAD_WIDTH)
            at = h * HEAD_WIDTH
            mine, got = terms[:2]
            if at >= mine.shape[1]:
                at -= mine.shape[1]
                mine, got = terms[2:]
            here = slice(at, at + HEAD_WIDTH)
            grad = (mine[:, here] + got[:, here]).astype(BF16)
            turned = grad.T
            grad_t[:, cols] = turned
            stack[cols, :HEAD_WIDTH] = q_ref[:, wide]
            stack[cols, HEAD_WIDTH:] = grad
            delta[:, cols] = jnp.sum(turned.astype(F32) * columns(all_outs, h), axis=0, keepdims=True)

    @pl.when(step < count)
    def _():
        block = info[FIRST] + step
        keys_t = k_ref[...].T
        for h in range(heads):
            cols = slice(h * rows, (h + 1) * rows)
            dprob = dot(v_ref[...], grad_t[:, cols])
            dscores[:, cols] = (columns(all_probs, h).astype(F32) * (dprob - delta[:, cols])).astype(BF16)
        total_q[...] += dot(keys_t, dscores[...])
        key_sum = dot(dscores[...], stack[:, :HEAD_WIDTH])
        value_sum = dot(all_probs[0][...], stack[:width, HEAD_WIDTH:])
        value_sum = value_sum + dot(all_probs[1][...], stack[width:, HEAD_WIDTH:])

        def add(ref):
            ref[block // 2, :, :HEAD_WIDTH] += key_sum * SCALE
            ref[block // 2, :, HEAD_WIDTH:] += value_sum

        pl.when(block % 2 == info[CORE])(lambda: add(own_ref))
        pl.when(block % 2 != info[CORE])(lambda: add(other))

    @pl.when(step == count - 1)
    def _():
        for h in range(heads):
            cols = slice(h * rows, (h + 1) * rows)
            wide = slice(h * HEAD_WIDTH, (h + 1) * HEAD_WIDTH)
            gq_ref[:, wide] = (total_q[:, cols].T * SCALE).astype(BF16)
        other_ref[...] = other[...].astype(BF16)


def backward(info, terms, probs, outs, queries, kv):
    rows, width = queries.shape
    heads = width // HEAD_WIDTH
    sums = (8, KEY_BLOCK, 2 * HEAD_WIDTH)

    def near(i, r):
        return jnp.minimum(i, r[COUNT] - 1)

    def once(shape):
        return pl.BlockSpec(shape, lambda i, r: (0,) * len(shape), pipeline_mode=pl.Buffered(1))

    return pl.pallas_call(
        functools.partial(backward_kernel, heads),
        grid_spec=pltpu.PrefetchScalarGridSpec(
            num_scalar_prefetch=1,
            grid=(most_blocks(rows),),
            in_specs=[once(term.shape) for term in terms]
            + [pl.BlockSpec((KEY_BLOCK, p.shape[1]), lambda i, r: (near(i, r), 0)) for p in probs]
            + [once(out.shape) for out in outs]
            + [
                once(queries.shape),
                pl.BlockSpec(
                    (KEY_BLOCK, HEAD_WIDTH), lambda i, r: (r[TABLE + r[FIRST] + near(i, r)], 0)
                ),
                pl.BlockSpec(
                    (KEY_BLOCK, HEAD_WIDTH), lambda i, r: (r[TABLE + 16 + r[FIRST] + near(i, r)], 0)
                ),
            ],
            out_specs=[once((rows, width)), once(sums), once(sums)],
            scratch_shapes=[
                pltpu.VMEM((HEAD_WIDTH, heads * rows), BF16),
                pltpu.VMEM((heads * rows, 2 * HEAD_WIDTH), BF16),
                pltpu.VMEM((1, heads * rows), F32),
                pltpu.VMEM((HEAD_WIDTH, heads * rows), F32),
                pltpu.VMEM((KEY_BLOCK, heads * rows), BF16),
                pltpu.VMEM(sums, F32),
            ],
        ),
        out_shape=[
            jax.ShapeDtypeStruct((rows, width), BF16),
            jax.ShapeDtypeStruct(sums, F32),
            jax.ShapeDtypeStruct(sums, BF16),
        ],
        compiler_params=pltpu.CompilerParams(vmem_limit_bytes=VMEM_LIMIT),
        cost_estimate=pl.CostEstimate(
            flops=8 * 10**9, bytes_accessed=10 * 2**20, transcendentals=0
        ),
        name="backward",
    )(info, *terms, *[in_hbm(p) for p in probs], *outs, in_hbm(queries), in_hbm(kv), in_hbm(kv))


def project_kernel(chips, slots, *rest):
    grads, (*stacks, own_ref, other_ref, grad) = rest[:chips], rest[chips:]
    for i, ref in enumerate(grads):
        grad[i] = ref[...]
    half = own_ref.shape[0]
    k = 0
    for ref in stacks:
        for j in range(ref.shape[0]):
            for out, row in ((own_ref, 0), (other_ref, half)):
                term = dot_t(grad[slots[k], row : row + half, :], ref[j])
                if k == 0:
                    out[...] = term
                else:
                    out[...] += term
            k += 1


def project(part, slots, grads, stacks):
    chips = len(grads)
    tokens, depth = grads[0].shape
    features = stacks[0].shape[1]
    half = jax.ShapeDtypeStruct((tokens // 2, features), F32)
    out_spec = pl.BlockSpec((tokens // 2, features), lambda i: (0, 0))
    return pl.pallas_call(
        functools.partial(project_kernel, chips),
        grid=(1,),
        in_specs=[pl.BlockSpec(memory_space=pltpu.SMEM)]
        + [pl.BlockSpec(ref.shape, lambda i: (0, 0)) for ref in grads]
        + [pl.BlockSpec(ref.shape, lambda i: (0, 0, 0)) for ref in stacks],
        out_specs=[out_spec, out_spec],
        out_shape=[half, half],
        scratch_shapes=[pltpu.VMEM((chips, tokens, depth), BF16)],
        compiler_params=pltpu.CompilerParams(vmem_limit_bytes=VMEM_LIMIT),
        cost_estimate=pl.CostEstimate(
            flops=2 * tokens * features * depth * chips,
            bytes_accessed=10 * 2**20,
            transcendentals=0,
        ),
        name="project%d" % part,
    )(slots, *grads, *[in_hbm(stack) if stack.shape[0] > 1 else stack for stack in stacks])


def local(queries, keys, values, grad_out, out_weight, lengths):
    rows = queries.shape[0]
    rank = lax.axis_index("dp")
    core = rank % 2
    x, z = rank // 4, (rank // 2) % 2

    query_pos = rank * rows + jnp.arange(rows, dtype=jnp.int32)
    ends = jnp.cumsum(lengths)[:-1]
    query_start = jnp.max(
        jnp.where(ends[None, :] <= query_pos[:, None], ends[None, :], 0), axis=1
    )
    first = query_start[0] // KEY_BLOCK
    last = query_pos[-1] // KEY_BLOCK
    clear = (query_start[-1] + KEY_BLOCK - 1) // KEY_BLOCK
    block = jnp.arange(16, dtype=jnp.int32)
    place = block // 2 * 2
    here = place + jnp.where(block % 2 == core, 0, 1)
    there = 16 + place + jnp.where(block % 2 == core, 1, 0)
    table = [jnp.where(core == 0, here, there), jnp.where(core == 0, there, here)]
    scalars = jnp.stack([first, last - first + 1, clear, core])
    info = jnp.concatenate([scalars, *table]).astype(jnp.int32)
    query_pos, query_start = query_pos[None, :], query_start[None, :]

    def spread(block, axis, groups):
        copies = jnp.broadcast_to(block, (len(groups[0]), *block.shape))
        return lax.all_to_all(copies, axis, 0, 0, axis_index_groups=groups, tiled=True)

    groups = [[2 * i + c for i in range(8)] for c in range(2)]
    kept = jnp.where(core == 0, keys, values)
    got = dp_move(jnp.where(core == 0, values, keys), 0, 0, 1)
    ring = spread(jnp.concatenate([kept, got], axis=0), "dp", groups).reshape(-1, HEAD_WIDTH)

    depth = out_weight.shape[1]
    mine = lax.dynamic_slice_in_dim(grad_out, core * depth, depth, 1)
    other = lax.dynamic_slice_in_dim(grad_out, (1 - core) * depth, depth, 1)
    chip_grad = jnp.concatenate([mine, dp_move(other, 0, 0, 1)], axis=0)
    all_grad = [chip_grad] + [tensor_move(chip_grad, 0, step) for step in (-1, -2, 1)]

    groups_x = [[x_ * 4 + zc for x_ in range(4)] for zc in range(4)]

    def gather_x(block):
        return lax.all_gather(block, "dp", axis=0, axis_index_groups=groups_x)

    own = [out_weight[:SPLIT], out_weight[SPLIT:]]
    ring, own, chip_grad = lax.optimization_barrier((ring, own, chip_grad))
    plane1 = gather_x(own[1])
    swapped = dp_move(ring, 0, 0, 1)
    grad_pair = tensor_move(chip_grad, 1, 0)
    paired = [dp_move(block, 0, 1, 0) for block in own]
    swapped, own0 = lax.optimization_barrier((swapped, own[0]))
    plane0 = gather_x(own0)
    kv = jnp.concatenate([ring, swapped], axis=0)

    first = forward(0, info, query_pos, query_start, queries, kv)
    first, grad_pair, pair0 = lax.optimization_barrier((first, grad_pair, paired[0]))
    all_grad += [grad_pair] + [tensor_move(grad_pair, 0, step) for step in (-1, -2, 1)]
    other_plane = spread(pair0, "dp", groups_x).reshape(4, SPLIT, depth)
    rest = jnp.concatenate(
        [lax.dynamic_slice_in_dim(plane1, (x + i) % 4, 1, 0) for i in range(1, 4)], axis=0
    )
    rest, later, _ = lax.optimization_barrier((rest, queries, first[1]))
    rest = dp_move(rest, 0, 1, 0)
    second = forward(1, info, query_pos, query_start, later, kv)

    t = lax.axis_index("tensor")

    def slot(x_, z_):
        source = 2 * (x_ % 4) + z_
        return (source - t) % 4 + jnp.where(source // 4 == t // 4, 0, 4)

    same = [slot(i, z) for i in range(4)]
    slots = [
        jnp.stack(same + [slot(i, 1 - z) for i in range(4)]).astype(jnp.int32),
        jnp.stack(same + [slot(x + i, 1 - z) for i in range(4)]).astype(jnp.int32),
    ]
    slots[0] = after(slots[0], second[1])
    stacks = [[plane0, other_plane], [plane1, paired[1][None], rest]]
    terms = []
    for part in range(CHUNKS):
        mine, other = project(part, slots[part], all_grad, stacks[part])
        terms += [mine, dp_move(other, 0, 0, 1)]
    probs, outs = zip(first, second)
    grad_queries, own_sums, other_sums = backward(info, terms, probs, outs, queries, kv)

    chip_sums = (own_sums + dp_move(other_sums, 0, 0, 1).astype(F32)).astype(BF16)
    terms = lax.all_to_all(chip_sums, "dp", 0, 0, axis_index_groups=groups, tiled=True)
    done = jnp.sum(terms.astype(F32), axis=0).astype(BF16)
    return grad_queries, done[:, :HEAD_WIDTH], done[:, HEAD_WIDTH:]


def solution(mesh):
    return jax.shard_map(
        local,
        mesh=mesh,
        in_specs=(
            P("dp", "tensor"),
            P("dp", "tensor"),
            P("dp", "tensor"),
            P("dp", "tensor"),
            P("tensor", "dp"),
            P(),
        ),
        out_specs=(P("dp", "tensor"), P("dp", "tensor"), P("dp", "tensor")),
        check_vma=False,
    )
```

```python
import functools
import math

import jax
import jax.numpy as jnp
from jax import lax
from jax.experimental import pallas as pl
from jax.experimental.pallas import tpu as pltpu
from jax.sharding import PartitionSpec as P

HEAD_WIDTH = 128
KEY_BLOCK = 256
MOST = 2560
CHUNKS = 2
SPLIT = 5 * HEAD_WIDTH
PAIR = 2
MASKED = -1e30
SCALE = 1.0 / math.sqrt(HEAD_WIDTH)
LOG2E = 1.0 / math.log(2.0)
BF16 = jnp.bfloat16
F32 = jnp.float32
VMEM_LIMIT = 26 * 2**20

FIRST, COUNT, CLEAR, CORE, TABLE = 0, 1, 2, 3, 4


def dp_move(value, dx, dz, dc):
    pairs = []
    for x in range(4):
        for z in range(2):
            for c in range(2):
                target = ((x + dx) % 4) * 4 + ((z + dz) % 2) * 2 + (c + dc) % 2
                pairs.append((x * 4 + z * 2 + c, target))
    return lax.ppermute(value, "dp", pairs)


def tensor_move(value, dz, dy):
    pairs = []
    for z in range(2):
        for y in range(4):
            pairs.append((z * 4 + y, ((z + dz) % 2) * 4 + (y + dy) % 4))
    return lax.ppermute(value, "tensor", pairs)


def after(value, *others):
    return lax.optimization_barrier((value, *others))[0]


def in_hbm(value):
    return pltpu.with_memory_space_constraint(value, pltpu.HBM)


def dot(left, right):
    return lax.dot_general(left, right, (((1,), (0,)), ((), ())), preferred_element_type=F32)


def dot_t(left, right):
    return lax.dot_general(left, right, (((1,), (1,)), ((), ())), preferred_element_type=F32)


def block_rows(index):
    return pl.ds(pl.multiple_of(index * KEY_BLOCK, KEY_BLOCK), KEY_BLOCK)


def forward_kernel(info, pos_ref, start_ref, q_ref, kv_ref, probs_ref, out_ref, score, vt):
    first, count = info[FIRST], info[COUNT]
    rows = q_ref.shape[0]
    heads = q_ref.shape[1] // HEAD_WIDTH
    query_t = jnp.concatenate(
        [q_ref[:, h * HEAD_WIDTH : (h + 1) * HEAD_WIDTH].T for h in range(heads)], axis=1
    )
    wide = heads * rows

    def groups(values):
        return values.reshape(KEY_BLOCK // 8, 8, wide)

    @pl.when(pl.program_id(0) == 0)
    def _():
        def turn(index, _):
            source = info[TABLE + 16 + first + index]
            vt[:, block_rows(index)] = kv_ref[block_rows(source), :].T
            return 0
        lax.fori_loop(0, count, turn, 0)

    def product(index):
        return dot(kv_ref[block_rows(info[TABLE + first + index]), :], query_t)

    def masked_step(index, top):
        key_pos = (first + index) * KEY_BLOCK + lax.broadcasted_iota(jnp.int32, (KEY_BLOCK, rows), 0)
        live = (key_pos >= start_ref[...]) & (key_pos <= pos_ref[...])
        raw = product(index)
        raw = jnp.concatenate(
            [jnp.where(live, raw[:, h * rows : (h + 1) * rows], MASKED) for h in range(heads)], axis=1
        )
        score[block_rows(index), :] = raw
        return jnp.maximum(top, jnp.max(groups(raw), axis=0))

    def clear_step(index, top):
        raw = product(index)
        score[block_rows(index), :] = raw
        return jnp.maximum(top, jnp.max(groups(raw), axis=0))

    clear = jnp.minimum(info[CLEAR] - first, count - 1)
    top = jnp.full((8, wide), MASKED, F32)
    top = lax.fori_loop(0, clear, masked_step, top)
    top = lax.fori_loop(clear, count - 1, clear_step, top)
    top = masked_step(count - 1, top)
    top = jnp.max(top, axis=0, keepdims=True) * (SCALE * LOG2E)

    def mass_step(index, mass):
        weights = jnp.exp2(score[block_rows(index), :] * (SCALE * LOG2E) - top)
        score[block_rows(index), :] = weights
        return mass + jnp.sum(groups(weights), axis=0)

    mass = lax.fori_loop(0, count, mass_step, jnp.zeros((8, wide), F32))
    share = 1.0 / jnp.sum(mass, axis=0, keepdims=True)
    out_ref[...] = jnp.zeros_like(out_ref)

    def probs_step(index, _):
        probs = (score[block_rows(index), :] * share).astype(BF16)
        probs_ref[block_rows(index), :] = probs
        out_ref[...] += dot(vt[:, block_rows(index)], probs)
        return 0

    lax.fori_loop(0, count, probs_step, 0)


def most_blocks(rows):
    return (MOST + rows - 2) // KEY_BLOCK + 1


def forward(part, info, query_pos, query_start, queries, kv):
    rows, width = queries.shape
    heads = width // HEAD_WIDTH // CHUNKS
    steps = heads // PAIR
    live = most_blocks(rows) * KEY_BLOCK
    line = pl.BlockSpec((1, rows), lambda h, r: (0, 0))
    return pl.pallas_call(
        forward_kernel,
        grid_spec=pltpu.PrefetchScalarGridSpec(
            num_scalar_prefetch=1,
            grid=(steps,),
            in_specs=[
                line,
                line,
                pl.BlockSpec((rows, PAIR * HEAD_WIDTH), lambda h, r: (0, part * steps + h)),
                pl.BlockSpec(kv.shape, lambda h, r: (0, 0), pipeline_mode=pl.Buffered(1)),
            ],
            out_specs=[
                pl.BlockSpec((live, PAIR * rows), lambda h, r: (0, h)),
                pl.BlockSpec((HEAD_WIDTH, PAIR * rows), lambda h, r: (0, h)),
            ],
            scratch_shapes=[
                pltpu.VMEM((live, PAIR * rows), F32),
                pltpu.VMEM((HEAD_WIDTH, live), BF16),
            ],
        ),
        out_shape=[
            pltpu.HBM((live, heads * rows), BF16),
            jax.ShapeDtypeStruct((HEAD_WIDTH, heads * rows), F32),
        ],
        compiler_params=pltpu.CompilerParams(vmem_limit_bytes=VMEM_LIMIT),
        cost_estimate=pl.CostEstimate(flops=10**10, bytes_accessed=10 * 2**20, transcendentals=0),
        name="forward%d" % part,
    )(info, query_pos, query_start, in_hbm(queries), in_hbm(kv))


def backward_kernel(heads, info, *rest):
    terms, all_probs, all_outs = rest[:4], rest[4:6], rest[6:8]
    q_ref, k_ref, v_ref, gq_ref, own_ref, other_ref, *scratch = rest[8:]
    grad_t, stack, delta, total_q, dscores, other = scratch
    step = pl.program_id(0)
    count = info[COUNT]
    rows = q_ref.shape[0]
    width = heads // 2 * rows

    def columns(refs, h):
        at = h * rows % width
        return refs[h * rows // width][:, at : at + rows]

    @pl.when(step == 0)
    def _():
        own_ref[...] = jnp.zeros_like(own_ref)
        other[...] = jnp.zeros_like(other)
        total_q[...] = jnp.zeros_like(total_q)
        for h in range(heads):
            cols = slice(h * rows, (h + 1) * rows)
            wide = slice(h * HEAD_WIDTH, (h + 1) * HEAD_WIDTH)
            at = h * HEAD_WIDTH
            mine, got = terms[:2]
            if at >= mine.shape[1]:
                at -= mine.shape[1]
                mine, got = terms[2:]
            here = slice(at, at + HEAD_WIDTH)
            grad = (mine[:, here] + got[:, here]).astype(BF16)
            turned = grad.T
            grad_t[:, cols] = turned
            stack[cols, :HEAD_WIDTH] = q_ref[:, wide]
            stack[cols, HEAD_WIDTH:] = grad
            delta[:, cols] = jnp.sum(turned.astype(F32) * columns(all_outs, h), axis=0, keepdims=True)

    @pl.when(step < count)
    def _():
        block = info[FIRST] + step
        keys_t = k_ref[...].T
        for h in range(heads):
            cols = slice(h * rows, (h + 1) * rows)
            dprob = dot(v_ref[...], grad_t[:, cols])
            dscores[:, cols] = (columns(all_probs, h).astype(F32) * (dprob - delta[:, cols])).astype(BF16)
        total_q[...] += dot(keys_t, dscores[...])
        key_sum = dot(dscores[...], stack[:, :HEAD_WIDTH])
        value_sum = dot(all_probs[0][...], stack[:width, HEAD_WIDTH:])
        value_sum = value_sum + dot(all_probs[1][...], stack[width:, HEAD_WIDTH:])

        def add(ref):
            ref[block // 2, :, :HEAD_WIDTH] += key_sum * SCALE
            ref[block // 2, :, HEAD_WIDTH:] += value_sum

        pl.when(block % 2 == info[CORE])(lambda: add(own_ref))
        pl.when(block % 2 != info[CORE])(lambda: add(other))

    @pl.when(step == count - 1)
    def _():
        for h in range(heads):
            cols = slice(h * rows, (h + 1) * rows)
            wide = slice(h * HEAD_WIDTH, (h + 1) * HEAD_WIDTH)
            gq_ref[:, wide] = (total_q[:, cols].T * SCALE).astype(BF16)
        other_ref[...] = other[...].astype(BF16)


def backward(info, terms, probs, outs, queries, kv):
    rows, width = queries.shape
    heads = width // HEAD_WIDTH
    sums = (8, KEY_BLOCK, 2 * HEAD_WIDTH)

    def near(i, r):
        return jnp.minimum(i, r[COUNT] - 1)

    def once(shape):
        return pl.BlockSpec(shape, lambda i, r: (0,) * len(shape), pipeline_mode=pl.Buffered(1))

    return pl.pallas_call(
        functools.partial(backward_kernel, heads),
        grid_spec=pltpu.PrefetchScalarGridSpec(
            num_scalar_prefetch=1,
            grid=(most_blocks(rows),),
            in_specs=[once(term.shape) for term in terms]
            + [pl.BlockSpec((KEY_BLOCK, p.shape[1]), lambda i, r: (near(i, r), 0)) for p in probs]
            + [once(out.shape) for out in outs]
            + [
                once(queries.shape),
                pl.BlockSpec(
                    (KEY_BLOCK, HEAD_WIDTH), lambda i, r: (r[TABLE + r[FIRST] + near(i, r)], 0)
                ),
                pl.BlockSpec(
                    (KEY_BLOCK, HEAD_WIDTH), lambda i, r: (r[TABLE + 16 + r[FIRST] + near(i, r)], 0)
                ),
            ],
            out_specs=[once((rows, width)), once(sums), once(sums)],
            scratch_shapes=[
                pltpu.VMEM((HEAD_WIDTH, heads * rows), BF16),
                pltpu.VMEM((heads * rows, 2 * HEAD_WIDTH), BF16),
                pltpu.VMEM((1, heads * rows), F32),
                pltpu.VMEM((HEAD_WIDTH, heads * rows), F32),
                pltpu.VMEM((KEY_BLOCK, heads * rows), BF16),
                pltpu.VMEM(sums, F32),
            ],
        ),
        out_shape=[
            jax.ShapeDtypeStruct((rows, width), BF16),
            jax.ShapeDtypeStruct(sums, F32),
            jax.ShapeDtypeStruct(sums, BF16),
        ],
        compiler_params=pltpu.CompilerParams(vmem_limit_bytes=VMEM_LIMIT),
        cost_estimate=pl.CostEstimate(
            flops=8 * 10**9, bytes_accessed=10 * 2**20, transcendentals=0
        ),
        name="backward",
    )(info, *terms, *[in_hbm(p) for p in probs], *outs, in_hbm(queries), in_hbm(kv), in_hbm(kv))


def project_kernel(chips, slots, *rest):
    grads, (*stacks, own_ref, other_ref, grad) = rest[:chips], rest[chips:]
    for i, ref in enumerate(grads):
        grad[i] = ref[...]
    half = own_ref.shape[0]
    k = 0
    for ref in stacks:
        for j in range(ref.shape[0]):
            for out, row in ((own_ref, 0), (other_ref, half)):
                term = dot_t(grad[slots[k], row : row + half, :], ref[j])
                if k == 0:
                    out[...] = term
                else:
                    out[...] += term
            k += 1


def project(part, slots, grads, stacks):
    chips = len(grads)
    tokens, depth = grads[0].shape
    features = stacks[0].shape[1]
    half = jax.ShapeDtypeStruct((tokens // 2, features), F32)
    out_spec = pl.BlockSpec((tokens // 2, features), lambda i: (0, 0))
    return pl.pallas_call(
        functools.partial(project_kernel, chips),
        grid=(1,),
        in_specs=[pl.BlockSpec(memory_space=pltpu.SMEM)]
        + [pl.BlockSpec(ref.shape, lambda i: (0, 0)) for ref in grads]
        + [pl.BlockSpec(ref.shape, lambda i: (0, 0, 0)) for ref in stacks],
        out_specs=[out_spec, out_spec],
        out_shape=[half, half],
        scratch_shapes=[pltpu.VMEM((chips, tokens, depth), BF16)],
        compiler_params=pltpu.CompilerParams(vmem_limit_bytes=VMEM_LIMIT),
        cost_estimate=pl.CostEstimate(
            flops=2 * tokens * features * depth * chips,
            bytes_accessed=10 * 2**20,
            transcendentals=0,
        ),
        name="project%d" % part,
    )(slots, *grads, *[in_hbm(stack) if stack.shape[0] > 1 else stack for stack in stacks])


def local(queries, keys, values, grad_out, out_weight, lengths):
    rows = queries.shape[0]
    rank = lax.axis_index("dp")
    core = rank % 2
    x, z = rank // 4, (rank // 2) % 2

    query_pos = rank * rows + jnp.arange(rows, dtype=jnp.int32)
    ends = jnp.cumsum(lengths)[:-1]
    query_start = jnp.max(
        jnp.where(ends[None, :] <= query_pos[:, None], ends[None, :], 0), axis=1
    )
    first = query_start[0] // KEY_BLOCK
    last = query_pos[-1] // KEY_BLOCK
    clear = (query_start[-1] + KEY_BLOCK - 1) // KEY_BLOCK
    block = jnp.arange(16, dtype=jnp.int32)
    place = block // 2 * 2
    here = place + jnp.where(block % 2 == core, 0, 1)
    there = 16 + place + jnp.where(block % 2 == core, 1, 0)
    table = [jnp.where(core == 0, here, there), jnp.where(core == 0, there, here)]
    scalars = jnp.stack([first, last - first + 1, clear, core])
    info = jnp.concatenate([scalars, *table]).astype(jnp.int32)
    query_pos, query_start = query_pos[None, :], query_start[None, :]

    def spread(block, axis, groups):
        copies = jnp.broadcast_to(block, (len(groups[0]), *block.shape))
        return lax.all_to_all(copies, axis, 0, 0, axis_index_groups=groups, tiled=True)

    groups = [[2 * i + c for i in range(8)] for c in range(2)]
    kept = jnp.where(core == 0, keys, values)
    got = dp_move(jnp.where(core == 0, values, keys), 0, 0, 1)
    ring = spread(jnp.concatenate([kept, got], axis=0), "dp", groups).reshape(-1, HEAD_WIDTH)

    depth = out_weight.shape[1]
    mine = lax.dynamic_slice_in_dim(grad_out, core * depth, depth, 1)
    other = lax.dynamic_slice_in_dim(grad_out, (1 - core) * depth, depth, 1)
    chip_grad = jnp.concatenate([mine, dp_move(other, 0, 0, 1)], axis=0)
    all_grad = [chip_grad] + [tensor_move(chip_grad, 0, step) for step in (-1, -2, 1)]

    groups_x = [[x_ * 4 + zc for x_ in range(4)] for zc in range(4)]

    def gather_x(block):
        return lax.all_gather(block, "dp", axis=0, axis_index_groups=groups_x)

    own = [out_weight[:SPLIT], out_weight[SPLIT:]]
    plane1 = gather_x(own[1])
    grad_pair = tensor_move(chip_grad, 1, 0)
    ring, own, all_grad, grad_pair = lax.optimization_barrier((ring, own, all_grad, grad_pair))
    swapped = dp_move(ring, 0, 0, 1)
    all_grad += [grad_pair] + [tensor_move(grad_pair, 0, step) for step in (-1, -2, 1)]
    paired = [dp_move(block, 0, 1, 0) for block in own]
    plane0 = gather_x(own[0])
    kv = jnp.concatenate([ring, swapped], axis=0)

    first = forward(0, info, query_pos, query_start, queries, kv)
    first, all_grad, paired = lax.optimization_barrier((first, all_grad, paired))
    other_plane = spread(paired[0], "dp", groups_x).reshape(4, SPLIT, depth)
    rest = jnp.concatenate(
        [lax.dynamic_slice_in_dim(plane1, (x + i) % 4, 1, 0) for i in range(1, 4)], axis=0
    )
    rest, later, _ = lax.optimization_barrier((rest, queries, first[1]))
    rest = dp_move(rest, 0, 1, 0)
    second = forward(1, info, query_pos, query_start, later, kv)

    t = lax.axis_index("tensor")

    def slot(x_, z_):
        source = 2 * (x_ % 4) + z_
        return (source - t) % 4 + jnp.where(source // 4 == t // 4, 0, 4)

    same = [slot(i, z) for i in range(4)]
    slots = [
        jnp.stack(same + [slot(i, 1 - z) for i in range(4)]).astype(jnp.int32),
        jnp.stack(same + [slot(x + i, 1 - z) for i in range(4)]).astype(jnp.int32),
    ]
    slots[0] = after(slots[0], second[1])
    stacks = [[plane0, other_plane], [plane1, paired[1][None], rest]]
    terms = []
    for part in range(CHUNKS):
        mine, other = project(part, slots[part], all_grad, stacks[part])
        terms += [mine, dp_move(other, 0, 0, 1)]
    probs, outs = zip(first, second)
    grad_queries, own_sums, other_sums = backward(info, terms, probs, outs, queries, kv)

    chip_sums = (own_sums + dp_move(other_sums, 0, 0, 1).astype(F32)).astype(BF16)
    terms = lax.all_to_all(chip_sums, "dp", 0, 0, axis_index_groups=groups, tiled=True)
    done = jnp.sum(terms.astype(F32), axis=0).astype(BF16)
    return grad_queries, done[:, :HEAD_WIDTH], done[:, HEAD_WIDTH:]


def solution(mesh):
    return jax.shard_map(
        local,
        mesh=mesh,
        in_specs=(
            P("dp", "tensor"),
            P("dp", "tensor"),
            P("dp", "tensor"),
            P("dp", "tensor"),
            P("tensor", "dp"),
            P(),
        ),
        out_specs=(P("dp", "tensor"), P("dp", "tensor"), P("dp", "tensor")),
        check_vma=False,
    )
```

```python
import functools
import math

import jax
import jax.numpy as jnp
from jax import lax
from jax.experimental import pallas as pl
from jax.experimental.pallas import tpu as pltpu
from jax.sharding import PartitionSpec as P

HEAD_WIDTH = 128
KEY_BLOCK = 256
MOST = 2560
CHUNKS = 2
SPLIT = 5 * HEAD_WIDTH
PAIR = 2
MASKED = -1e30
SCALE = 1.0 / math.sqrt(HEAD_WIDTH)
LOG2E = 1.0 / math.log(2.0)
BF16 = jnp.bfloat16
F32 = jnp.float32
VMEM_LIMIT = 20 * 2**20

FIRST, COUNT, CLEAR, CORE, TABLE = 0, 1, 2, 3, 4


def dp_move(value, dx, dz, dc):
    pairs = []
    for x in range(4):
        for z in range(2):
            for c in range(2):
                target = ((x + dx) % 4) * 4 + ((z + dz) % 2) * 2 + (c + dc) % 2
                pairs.append((x * 4 + z * 2 + c, target))
    return lax.ppermute(value, "dp", pairs)


def tensor_move(value, dz, dy):
    pairs = []
    for z in range(2):
        for y in range(4):
            pairs.append((z * 4 + y, ((z + dz) % 2) * 4 + (y + dy) % 4))
    return lax.ppermute(value, "tensor", pairs)


def after(value, *others):
    return lax.optimization_barrier((value, *others))[0]


def in_hbm(value):
    return pltpu.with_memory_space_constraint(value, pltpu.HBM)


def dot(left, right):
    return lax.dot_general(left, right, (((1,), (0,)), ((), ())), preferred_element_type=F32)


def dot_t(left, right):
    return lax.dot_general(left, right, (((1,), (1,)), ((), ())), preferred_element_type=F32)


def block_rows(index):
    return pl.ds(pl.multiple_of(index * KEY_BLOCK, KEY_BLOCK), KEY_BLOCK)


def forward_kernel(info, pos_ref, start_ref, q_ref, kv_ref, probs_ref, out_ref, score, vt):
    first, count = info[FIRST], info[COUNT]
    rows = q_ref.shape[0]
    heads = q_ref.shape[1] // HEAD_WIDTH
    query_t = jnp.concatenate(
        [q_ref[:, h * HEAD_WIDTH : (h + 1) * HEAD_WIDTH].T for h in range(heads)], axis=1
    )
    wide = heads * rows

    def groups(values):
        return values.reshape(KEY_BLOCK // 8, 8, wide)

    @pl.when(pl.program_id(0) == 0)
    def _():
        def turn(index, _):
            source = info[TABLE + 16 + first + index]
            vt[:, block_rows(index)] = kv_ref[block_rows(source), :].T
            return 0
        lax.fori_loop(0, count, turn, 0)

    def product(index):
        return dot(kv_ref[block_rows(info[TABLE + first + index]), :], query_t)

    def masked_step(index, top):
        key_pos = (first + index) * KEY_BLOCK + lax.broadcasted_iota(jnp.int32, (KEY_BLOCK, rows), 0)
        live = (key_pos >= start_ref[...]) & (key_pos <= pos_ref[...])
        raw = product(index)
        raw = jnp.concatenate(
            [jnp.where(live, raw[:, h * rows : (h + 1) * rows], MASKED) for h in range(heads)], axis=1
        )
        score[block_rows(index), :] = raw
        return jnp.maximum(top, jnp.max(groups(raw), axis=0))

    def clear_step(index, top):
        raw = product(index)
        score[block_rows(index), :] = raw
        return jnp.maximum(top, jnp.max(groups(raw), axis=0))

    clear = jnp.minimum(info[CLEAR] - first, count - 1)
    top = jnp.full((8, wide), MASKED, F32)
    top = lax.fori_loop(0, clear, masked_step, top)
    top = lax.fori_loop(clear, count - 1, clear_step, top)
    top = masked_step(count - 1, top)
    top = jnp.max(top, axis=0, keepdims=True) * (SCALE * LOG2E)

    def mass_step(index, mass):
        weights = jnp.exp2(score[block_rows(index), :] * (SCALE * LOG2E) - top)
        score[block_rows(index), :] = weights
        return mass + jnp.sum(groups(weights), axis=0)

    mass = lax.fori_loop(0, count, mass_step, jnp.zeros((8, wide), F32))
    share = 1.0 / jnp.sum(mass, axis=0, keepdims=True)
    out_ref[...] = jnp.zeros_like(out_ref)

    def probs_step(index, _):
        probs = (score[block_rows(index), :] * share).astype(BF16)
        probs_ref[block_rows(index), :] = probs
        out_ref[...] += dot(vt[:, block_rows(index)], probs)
        return 0

    lax.fori_loop(0, count, probs_step, 0)


def most_blocks(rows):
    return (MOST + rows - 2) // KEY_BLOCK + 1


def forward(part, info, query_pos, query_start, queries, kv):
    rows, width = queries.shape
    heads = width // HEAD_WIDTH // CHUNKS
    steps = heads // PAIR
    live = most_blocks(rows) * KEY_BLOCK
    line = pl.BlockSpec((1, rows), lambda h, r: (0, 0))
    return pl.pallas_call(
        forward_kernel,
        grid_spec=pltpu.PrefetchScalarGridSpec(
            num_scalar_prefetch=1,
            grid=(steps,),
            in_specs=[
                line,
                line,
                pl.BlockSpec((rows, PAIR * HEAD_WIDTH), lambda h, r: (0, part * steps + h)),
                pl.BlockSpec(kv.shape, lambda h, r: (0, 0), pipeline_mode=pl.Buffered(1)),
            ],
            out_specs=[
                pl.BlockSpec((live, PAIR * rows), lambda h, r: (0, h)),
                pl.BlockSpec((HEAD_WIDTH, PAIR * rows), lambda h, r: (0, h)),
            ],
            scratch_shapes=[
                pltpu.VMEM((live, PAIR * rows), F32),
                pltpu.VMEM((HEAD_WIDTH, live), BF16),
            ],
        ),
        out_shape=[
            pltpu.HBM((live, heads * rows), BF16),
            pltpu.HBM((HEAD_WIDTH, heads * rows), F32),
        ],
        compiler_params=pltpu.CompilerParams(vmem_limit_bytes=VMEM_LIMIT),
        cost_estimate=pl.CostEstimate(flops=10**8, bytes_accessed=2**20, transcendentals=0),
        name="forward%d" % part,
    )(info, query_pos, query_start, in_hbm(queries), in_hbm(kv))


def backward_kernel(heads, info, *rest):
    terms, all_probs, all_outs = rest[:4], rest[4:6], rest[6:8]
    q_ref, k_ref, v_ref, gq_ref, own_ref, other_ref, *scratch = rest[8:]
    grad_t, stack, delta, total_q, dscores, other = scratch
    step = pl.program_id(0)
    count = info[COUNT]
    rows = q_ref.shape[0]
    width = heads // 2 * rows

    def columns(refs, h):
        at = h * rows % width
        return refs[h * rows // width][:, at : at + rows]

    @pl.when(step == 0)
    def _():
        own_ref[...] = jnp.zeros_like(own_ref)
        other[...] = jnp.zeros_like(other)
        total_q[...] = jnp.zeros_like(total_q)
        for h in range(heads):
            cols = slice(h * rows, (h + 1) * rows)
            wide = slice(h * HEAD_WIDTH, (h + 1) * HEAD_WIDTH)
            at = h * HEAD_WIDTH
            mine, got = terms[:2]
            if at >= mine.shape[1]:
                at -= mine.shape[1]
                mine, got = terms[2:]
            here = slice(at, at + HEAD_WIDTH)
            grad = (mine[:, here] + got[:, here]).astype(BF16)
            turned = grad.T
            grad_t[:, cols] = turned
            stack[cols, :HEAD_WIDTH] = q_ref[:, wide]
            stack[cols, HEAD_WIDTH:] = grad
            delta[:, cols] = jnp.sum(turned.astype(F32) * columns(all_outs, h), axis=0, keepdims=True)

    @pl.when(step < count)
    def _():
        block = info[FIRST] + step
        keys_t = k_ref[...].T
        for h in range(heads):
            cols = slice(h * rows, (h + 1) * rows)
            dprob = dot(v_ref[...], grad_t[:, cols])
            dscores[:, cols] = (columns(all_probs, h).astype(F32) * (dprob - delta[:, cols])).astype(BF16)
        total_q[...] += dot(keys_t, dscores[...])
        key_sum = dot(dscores[...], stack[:, :HEAD_WIDTH])
        value_sum = dot(all_probs[0][...], stack[:width, HEAD_WIDTH:])
        value_sum = value_sum + dot(all_probs[1][...], stack[width:, HEAD_WIDTH:])

        def add(ref):
            ref[block // 2, :, :HEAD_WIDTH] += key_sum * SCALE
            ref[block // 2, :, HEAD_WIDTH:] += value_sum

        pl.when(block % 2 == info[CORE])(lambda: add(own_ref))
        pl.when(block % 2 != info[CORE])(lambda: add(other))

    @pl.when(step == count - 1)
    def _():
        for h in range(heads):
            cols = slice(h * rows, (h + 1) * rows)
            wide = slice(h * HEAD_WIDTH, (h + 1) * HEAD_WIDTH)
            gq_ref[:, wide] = (total_q[:, cols].T * SCALE).astype(BF16)
        other_ref[...] = other[...].astype(BF16)


def backward(info, terms, probs, outs, queries, kv):
    rows, width = queries.shape
    heads = width // HEAD_WIDTH
    sums = (8, KEY_BLOCK, 2 * HEAD_WIDTH)

    def near(i, r):
        return jnp.minimum(i, r[COUNT] - 1)

    def once(shape):
        return pl.BlockSpec(shape, lambda i, r: (0,) * len(shape), pipeline_mode=pl.Buffered(1))

    return pl.pallas_call(
        functools.partial(backward_kernel, heads),
        grid_spec=pltpu.PrefetchScalarGridSpec(
            num_scalar_prefetch=1,
            grid=(most_blocks(rows),),
            in_specs=[once(term.shape) for term in terms]
            + [pl.BlockSpec((KEY_BLOCK, p.shape[1]), lambda i, r: (near(i, r), 0)) for p in probs]
            + [once(out.shape) for out in outs]
            + [
                once(queries.shape),
                pl.BlockSpec(
                    (KEY_BLOCK, HEAD_WIDTH), lambda i, r: (r[TABLE + r[FIRST] + near(i, r)], 0)
                ),
                pl.BlockSpec(
                    (KEY_BLOCK, HEAD_WIDTH), lambda i, r: (r[TABLE + 16 + r[FIRST] + near(i, r)], 0)
                ),
            ],
            out_specs=[once((rows, width)), once(sums), once(sums)],
            scratch_shapes=[
                pltpu.VMEM((HEAD_WIDTH, heads * rows), BF16),
                pltpu.VMEM((heads * rows, 2 * HEAD_WIDTH), BF16),
                pltpu.VMEM((1, heads * rows), F32),
                pltpu.VMEM((HEAD_WIDTH, heads * rows), F32),
                pltpu.VMEM((KEY_BLOCK, heads * rows), BF16),
                pltpu.VMEM(sums, F32),
            ],
        ),
        out_shape=[
            jax.ShapeDtypeStruct((rows, width), BF16),
            jax.ShapeDtypeStruct(sums, F32),
            jax.ShapeDtypeStruct(sums, BF16),
        ],
        compiler_params=pltpu.CompilerParams(vmem_limit_bytes=VMEM_LIMIT),
        cost_estimate=pl.CostEstimate(
            flops=8 * 10**9, bytes_accessed=10 * 2**20, transcendentals=0
        ),
        name="backward",
    )(info, *terms, *[in_hbm(p) for p in probs], *outs, in_hbm(queries), in_hbm(kv), in_hbm(kv))


def project_kernel(chips, slots, *rest):
    grads, (*stacks, own_ref, other_ref, grad) = rest[:chips], rest[chips:]
    for i, ref in enumerate(grads):
        grad[i] = ref[...]
    half = own_ref.shape[0]
    k = 0
    for ref in stacks:
        for j in range(ref.shape[0]):
            for out, row in ((own_ref, 0), (other_ref, half)):
                term = dot_t(grad[slots[k], row : row + half, :], ref[j])
                if k == 0:
                    out[...] = term
                else:
                    out[...] += term
            k += 1


def project(part, slots, grads, stacks):
    chips = len(grads)
    tokens, depth = grads[0].shape
    features = stacks[0].shape[1]
    half = jax.ShapeDtypeStruct((tokens // 2, features), F32)

    def once(shape):
        return pl.BlockSpec(shape, lambda i: (0,) * len(shape), pipeline_mode=pl.Buffered(1))

    return pl.pallas_call(
        functools.partial(project_kernel, chips),
        grid=(1,),
        in_specs=[pl.BlockSpec(memory_space=pltpu.SMEM)]
        + [once(ref.shape) for ref in (*grads, *stacks)],
        out_specs=[once(half.shape)] * 2,
        out_shape=[half, half],
        scratch_shapes=[pltpu.VMEM((chips, tokens, depth), BF16)],
        compiler_params=pltpu.CompilerParams(vmem_limit_bytes=VMEM_LIMIT),
        cost_estimate=pl.CostEstimate(
            flops=2 * tokens * features * depth * chips,
            bytes_accessed=10 * 2**20,
            transcendentals=0,
        ),
        name="project%d" % part,
    )(slots, *grads, *[in_hbm(stack) if stack.shape[0] > 1 else stack for stack in stacks])


def local(queries, keys, values, grad_out, out_weight, lengths):
    rows = queries.shape[0]
    rank = lax.axis_index("dp")
    core = rank % 2
    x, z = rank // 4, (rank // 2) % 2

    query_pos = rank * rows + jnp.arange(rows, dtype=jnp.int32)
    ends = jnp.cumsum(lengths)[:-1]
    query_start = jnp.max(
        jnp.where(ends[None, :] <= query_pos[:, None], ends[None, :], 0), axis=1
    )
    first = query_start[0] // KEY_BLOCK
    last = query_pos[-1] // KEY_BLOCK
    clear = (query_start[-1] + KEY_BLOCK - 1) // KEY_BLOCK
    block = jnp.arange(16, dtype=jnp.int32)
    place = block // 2 * 2
    here = place + jnp.where(block % 2 == core, 0, 1)
    there = 16 + place + jnp.where(block % 2 == core, 1, 0)
    table = [jnp.where(core == 0, here, there), jnp.where(core == 0, there, here)]
    scalars = jnp.stack([first, last - first + 1, clear, core])
    info = jnp.concatenate([scalars, *table]).astype(jnp.int32)
    query_pos, query_start = query_pos[None, :], query_start[None, :]

    def copy(block, groups):
        return jnp.broadcast_to(block, (len(groups[0]), *block.shape))

    def exchange(copies, axis, groups):
        return lax.all_to_all(copies, axis, 0, 0, axis_index_groups=groups, tiled=True)

    def spread(block, axis, groups):
        return exchange(copy(block, groups), axis, groups)

    groups = [[2 * i + c for i in range(8)] for c in range(2)]
    kept = jnp.where(core == 0, keys, values)
    got = dp_move(jnp.where(core == 0, values, keys), 0, 0, 1)
    ring = spread(jnp.concatenate([kept, got], axis=0), "dp", groups).reshape(-1, HEAD_WIDTH)

    depth = out_weight.shape[1]
    mine = lax.dynamic_slice_in_dim(grad_out, core * depth, depth, 1)
    other = lax.dynamic_slice_in_dim(grad_out, (1 - core) * depth, depth, 1)
    chip_grad = jnp.concatenate([mine, dp_move(other, 0, 0, 1)], axis=0)
    all_grad = [chip_grad] + [tensor_move(chip_grad, 0, step) for step in (-1, -2, 1)]

    groups_x = [[x_ * 4 + zc for x_ in range(4)] for zc in range(4)]

    def gather_x(block):
        return lax.all_gather(block, "dp", axis=0, axis_index_groups=groups_x)

    own = [out_weight[:SPLIT], out_weight[SPLIT:]]
    plane1 = gather_x(own[1])
    pair0 = dp_move(own[0], 0, 1, 0)
    ring, own, all_grad, pair0, chip_grad = lax.optimization_barrier(
        (ring, own, all_grad, pair0, chip_grad)
    )
    plane0 = gather_x(own[0])
    swapped = dp_move(ring, 0, 0, 1)
    swapped, copies = lax.optimization_barrier((swapped, copy(pair0, groups_x)))
    other_plane = exchange(copies, "dp", groups_x).reshape(4, SPLIT, depth)
    grad_pair = tensor_move(chip_grad, 1, 0)
    pair1 = dp_move(own[1], 0, 1, 0)
    kv = jnp.concatenate([ring, swapped], axis=0)

    first = forward(0, info, query_pos, query_start, queries, kv)
    first, grad_pair, pair1 = lax.optimization_barrier((first, grad_pair, pair1))
    all_grad += [grad_pair] + [tensor_move(grad_pair, 0, step) for step in (-1, -2, 1)]
    rest = jnp.concatenate(
        [lax.dynamic_slice_in_dim(plane1, (x + i) % 4, 1, 0) for i in range(1, 4)], axis=0
    )
    rest, later, _ = lax.optimization_barrier((rest, queries, first[1]))
    rest = dp_move(rest, 0, 1, 0)
    second = forward(1, info, query_pos, query_start, later, kv)

    t = lax.axis_index("tensor")

    def slot(x_, z_):
        source = 2 * (x_ % 4) + z_
        return (source - t) % 4 + jnp.where(source // 4 == t // 4, 0, 4)

    same = [slot(i, z) for i in range(4)]
    slots = [
        jnp.stack(same + [slot(i, 1 - z) for i in range(4)]).astype(jnp.int32),
        jnp.stack(same + [slot(x + i, 1 - z) for i in range(4)]).astype(jnp.int32),
    ]
    slots[0] = after(slots[0], second[1])
    stacks = [[plane0, other_plane], [plane1, pair1[None], rest]]
    terms = []
    for part in range(CHUNKS):
        mine, other = project(part, slots[part], all_grad, stacks[part])
        terms += [mine, dp_move(other, 0, 0, 1)]
    probs, outs = zip(first, second)
    grad_queries, own_sums, other_sums = backward(info, terms, probs, outs, queries, kv)

    chip_sums = (own_sums + dp_move(other_sums, 0, 0, 1).astype(F32)).astype(BF16)
    terms = lax.all_to_all(chip_sums, "dp", 0, 0, axis_index_groups=groups, tiled=True)
    done = jnp.sum(terms.astype(F32), axis=0).astype(BF16)
    return grad_queries, done[:, :HEAD_WIDTH], done[:, HEAD_WIDTH:]


def solution(mesh):
    return jax.shard_map(
        local,
        mesh=mesh,
        in_specs=(
            P("dp", "tensor"),
            P("dp", "tensor"),
            P("dp", "tensor"),
            P("dp", "tensor"),
            P("tensor", "dp"),
            P(),
        ),
        out_specs=(P("dp", "tensor"), P("dp", "tensor"), P("dp", "tensor")),
        check_vma=False,
    )
```

```python
import functools
import math

import jax
import jax.numpy as jnp
from jax import lax
from jax.experimental import pallas as pl
from jax.experimental.pallas import tpu as pltpu
from jax.sharding import PartitionSpec as P

HEAD_WIDTH = 128
KEY_BLOCK = 256
MOST = 2560
CHUNKS = 2
SPLIT = 5 * HEAD_WIDTH
PAIR = 2
MASKED = -1e30
SCALE = 1.0 / math.sqrt(HEAD_WIDTH)
LOG2E = 1.0 / math.log(2.0)
BF16 = jnp.bfloat16
F32 = jnp.float32
VMEM_LIMIT = 22 * 2**20

FIRST, COUNT, CLEAR, CORE, TABLE = 0, 1, 2, 3, 4


def dp_move(value, dx, dz, dc):
    pairs = []
    for x in range(4):
        for z in range(2):
            for c in range(2):
                target = ((x + dx) % 4) * 4 + ((z + dz) % 2) * 2 + (c + dc) % 2
                pairs.append((x * 4 + z * 2 + c, target))
    return lax.ppermute(value, "dp", pairs)


def tensor_move(value, dz, dy):
    pairs = []
    for z in range(2):
        for y in range(4):
            pairs.append((z * 4 + y, ((z + dz) % 2) * 4 + (y + dy) % 4))
    return lax.ppermute(value, "tensor", pairs)


def after(value, *others):
    return lax.optimization_barrier((value, *others))[0]


def in_hbm(value):
    return pltpu.with_memory_space_constraint(value, pltpu.HBM)


def dot(left, right):
    return lax.dot_general(left, right, (((1,), (0,)), ((), ())), preferred_element_type=F32)


def dot_t(left, right):
    return lax.dot_general(left, right, (((1,), (1,)), ((), ())), preferred_element_type=F32)


def block_rows(index):
    return pl.ds(pl.multiple_of(index * KEY_BLOCK, KEY_BLOCK), KEY_BLOCK)


def forward_kernel(
    info, pos_ref, start_ref, q_ref, here_ref, there_ref, probs_ref, out_ref, score, keys, vt
):
    first, count = info[FIRST], info[COUNT]
    rows = q_ref.shape[0]
    heads = q_ref.shape[1] // HEAD_WIDTH
    query_t = jnp.concatenate(
        [q_ref[:, h * HEAD_WIDTH : (h + 1) * HEAD_WIDTH].T for h in range(heads)], axis=1
    )
    wide = heads * rows

    def groups(values):
        return values.reshape(KEY_BLOCK // 8, 8, wide)

    @pl.when(pl.program_id(0) == 0)
    def _():
        def turn(index, _):
            here = here_ref[block_rows(info[TABLE + first + index]), :]
            there = there_ref[block_rows(info[TABLE + 16 + first + index]), :]
            keys[block_rows(index), :] = jnp.where(info[CORE] == 0, here, there)
            vt[:, block_rows(index)] = jnp.where(info[CORE] == 0, there, here).T
            return 0
        lax.fori_loop(0, count, turn, 0)

    def product(index):
        return dot(keys[block_rows(index), :], query_t)

    def masked_step(index, top):
        key_pos = (first + index) * KEY_BLOCK + lax.broadcasted_iota(jnp.int32, (KEY_BLOCK, rows), 0)
        live = (key_pos >= start_ref[...]) & (key_pos <= pos_ref[...])
        raw = product(index)
        raw = jnp.concatenate(
            [jnp.where(live, raw[:, h * rows : (h + 1) * rows], MASKED) for h in range(heads)], axis=1
        )
        score[block_rows(index), :] = raw
        return jnp.maximum(top, jnp.max(groups(raw), axis=0))

    def clear_step(index, top):
        raw = product(index)
        score[block_rows(index), :] = raw
        return jnp.maximum(top, jnp.max(groups(raw), axis=0))

    clear = jnp.minimum(info[CLEAR] - first, count - 1)
    top = jnp.full((8, wide), MASKED, F32)
    top = lax.fori_loop(0, clear, masked_step, top)
    top = lax.fori_loop(clear, count - 1, clear_step, top)
    top = masked_step(count - 1, top)
    top = jnp.max(top, axis=0, keepdims=True) * (SCALE * LOG2E)

    def mass_step(index, mass):
        weights = jnp.exp2(score[block_rows(index), :] * (SCALE * LOG2E) - top)
        score[block_rows(index), :] = weights
        return mass + jnp.sum(groups(weights), axis=0)

    mass = lax.fori_loop(0, count, mass_step, jnp.zeros((8, wide), F32))
    share = 1.0 / jnp.sum(mass, axis=0, keepdims=True)
    out_ref[...] = jnp.zeros_like(out_ref)

    def probs_step(index, _):
        probs = (score[block_rows(index), :] * share).astype(BF16)
        probs_ref[block_rows(index), :] = probs
        out_ref[...] += dot(vt[:, block_rows(index)], probs)
        return 0

    lax.fori_loop(0, count, probs_step, 0)


def most_blocks(rows):
    return (MOST + rows - 2) // KEY_BLOCK + 1


def forward(info, query_pos, query_start, queries, here, there):
    rows, width = queries.shape
    heads = width // HEAD_WIDTH
    live = most_blocks(rows) * KEY_BLOCK
    line = pl.BlockSpec((1, rows), lambda h, r: (0, 0))
    return pl.pallas_call(
        forward_kernel,
        grid_spec=pltpu.PrefetchScalarGridSpec(
            num_scalar_prefetch=1,
            grid=(heads // PAIR,),
            in_specs=[
                line,
                line,
                pl.BlockSpec((rows, PAIR * HEAD_WIDTH), lambda h, r: (0, h)),
            ]
            + [pl.BlockSpec(here.shape, lambda h, r: (0, 0), pipeline_mode=pl.Buffered(1))] * 2,
            out_specs=[
                pl.BlockSpec((live, PAIR * rows), lambda h, r: (0, h)),
                pl.BlockSpec((HEAD_WIDTH, PAIR * rows), lambda h, r: (0, h)),
            ],
            scratch_shapes=[
                pltpu.VMEM((live, PAIR * rows), F32),
                pltpu.VMEM((live, HEAD_WIDTH), BF16),
                pltpu.VMEM((HEAD_WIDTH, live), BF16),
            ],
        ),
        out_shape=[
            pltpu.HBM((live, heads * rows), BF16),
            pltpu.HBM((HEAD_WIDTH, heads * rows), F32),
        ],
        compiler_params=pltpu.CompilerParams(vmem_limit_bytes=VMEM_LIMIT),
        cost_estimate=pl.CostEstimate(flops=10**8, bytes_accessed=2**20, transcendentals=0),
        name="forward",
    )(info, query_pos, query_start, in_hbm(queries), here, there)


def backward_kernel(heads, info, *rest):
    terms, rest = rest[:4], rest[4:]
    probs_ref, out_ref, q_ref, here_ref, there_ref, gq_ref, own_ref, other_ref, *scratch = rest
    grad_t, stack, delta, total_q, dscores, other = scratch
    step = pl.program_id(0)
    count = info[COUNT]
    rows = q_ref.shape[0]

    @pl.when(step == 0)
    def _():
        own_ref[...] = jnp.zeros_like(own_ref)
        other[...] = jnp.zeros_like(other)
        total_q[...] = jnp.zeros_like(total_q)
        for h in range(heads):
            cols = slice(h * rows, (h + 1) * rows)
            wide = slice(h * HEAD_WIDTH, (h + 1) * HEAD_WIDTH)
            at = h * HEAD_WIDTH
            mine, got = terms[:2]
            if at >= mine.shape[1]:
                at -= mine.shape[1]
                mine, got = terms[2:]
            here = slice(at, at + HEAD_WIDTH)
            grad = (mine[:, here] + got[:, here]).astype(BF16)
            turned = grad.T
            grad_t[:, cols] = turned
            stack[cols, :HEAD_WIDTH] = q_ref[:, wide]
            stack[cols, HEAD_WIDTH:] = grad
            delta[:, cols] = jnp.sum(turned.astype(F32) * out_ref[:, cols], axis=0, keepdims=True)

    @pl.when(step < count)
    def _():
        block = info[FIRST] + step
        keys_t = jnp.where(info[CORE] == 0, here_ref[...], there_ref[...]).T
        values = jnp.where(info[CORE] == 0, there_ref[...], here_ref[...])
        for h in range(heads):
            cols = slice(h * rows, (h + 1) * rows)
            dprob = dot(values, grad_t[:, cols])
            dscores[:, cols] = (probs_ref[:, cols].astype(F32) * (dprob - delta[:, cols])).astype(BF16)
        total_q[...] += dot(keys_t, dscores[...])
        key_sum = dot(dscores[...], stack[:, :HEAD_WIDTH])
        value_sum = dot(probs_ref[...], stack[:, HEAD_WIDTH:])

        def add(ref):
            ref[block // 2, :, :HEAD_WIDTH] += key_sum * SCALE
            ref[block // 2, :, HEAD_WIDTH:] += value_sum

        pl.when(block % 2 == info[CORE])(lambda: add(own_ref))
        pl.when(block % 2 != info[CORE])(lambda: add(other))

    @pl.when(step == count - 1)
    def _():
        for h in range(heads):
            cols = slice(h * rows, (h + 1) * rows)
            wide = slice(h * HEAD_WIDTH, (h + 1) * HEAD_WIDTH)
            gq_ref[:, wide] = (total_q[:, cols].T * SCALE).astype(BF16)
        other_ref[...] = other[...].astype(BF16)


def backward(info, terms, probs, outs, queries, here, there):
    rows, width = queries.shape
    heads = width // HEAD_WIDTH
    sums = (8, KEY_BLOCK, 2 * HEAD_WIDTH)

    def near(i, r):
        return jnp.minimum(i, r[COUNT] - 1)

    def once(shape):
        return pl.BlockSpec(shape, lambda i, r: (0,) * len(shape), pipeline_mode=pl.Buffered(1))

    return pl.pallas_call(
        functools.partial(backward_kernel, heads),
        grid_spec=pltpu.PrefetchScalarGridSpec(
            num_scalar_prefetch=1,
            grid=(most_blocks(rows),),
            in_specs=[once(term.shape) for term in terms]
            + [
                pl.BlockSpec((KEY_BLOCK, heads * rows), lambda i, r: (near(i, r), 0)),
                once(outs.shape),
                once(queries.shape),
                pl.BlockSpec(
                    (KEY_BLOCK, HEAD_WIDTH), lambda i, r: (r[TABLE + r[FIRST] + near(i, r)], 0)
                ),
                pl.BlockSpec(
                    (KEY_BLOCK, HEAD_WIDTH), lambda i, r: (r[TABLE + 16 + r[FIRST] + near(i, r)], 0)
                ),
            ],
            out_specs=[once((rows, width)), once(sums), once(sums)],
            scratch_shapes=[
                pltpu.VMEM((HEAD_WIDTH, heads * rows), BF16),
                pltpu.VMEM((heads * rows, 2 * HEAD_WIDTH), BF16),
                pltpu.VMEM((1, heads * rows), F32),
                pltpu.VMEM((HEAD_WIDTH, heads * rows), F32),
                pltpu.VMEM((KEY_BLOCK, heads * rows), BF16),
                pltpu.VMEM(sums, F32),
            ],
        ),
        out_shape=[
            jax.ShapeDtypeStruct((rows, width), BF16),
            jax.ShapeDtypeStruct(sums, F32),
            jax.ShapeDtypeStruct(sums, BF16),
        ],
        compiler_params=pltpu.CompilerParams(vmem_limit_bytes=VMEM_LIMIT),
        cost_estimate=pl.CostEstimate(
            flops=8 * 10**9, bytes_accessed=10 * 2**20, transcendentals=0
        ),
        name="backward",
    )(info, *terms, in_hbm(probs), outs, in_hbm(queries), here, there)


def project_kernel(chips, slots, *rest):
    grads, (*stacks, own_ref, other_ref, grad) = rest[:chips], rest[chips:]
    for i, ref in enumerate(grads):
        grad[i] = ref[...]
    half = own_ref.shape[0]
    k = 0
    for ref in stacks:
        for j in range(ref.shape[0]):
            for out, row in ((own_ref, 0), (other_ref, half)):
                term = dot_t(grad[slots[k], row : row + half, :], ref[j])
                if k == 0:
                    out[...] = term
                else:
                    out[...] += term
            k += 1


def project(part, slots, grads, stacks):
    chips = len(grads)
    tokens, depth = grads[0].shape
    features = stacks[0].shape[1]
    half = jax.ShapeDtypeStruct((tokens // 2, features), F32)

    def once(shape):
        return pl.BlockSpec(shape, lambda i: (0,) * len(shape), pipeline_mode=pl.Buffered(1))

    return pl.pallas_call(
        functools.partial(project_kernel, chips),
        grid=(1,),
        in_specs=[pl.BlockSpec(memory_space=pltpu.SMEM)]
        + [once(ref.shape) for ref in (*grads, *stacks)],
        out_specs=[once(half.shape)] * 2,
        out_shape=[half, half],
        scratch_shapes=[pltpu.VMEM((chips, tokens, depth), BF16)],
        compiler_params=pltpu.CompilerParams(vmem_limit_bytes=VMEM_LIMIT),
        cost_estimate=pl.CostEstimate(
            flops=2 * tokens * features * depth * chips,
            bytes_accessed=10 * 2**20,
            transcendentals=0,
        ),
        name="project%d" % part,
    )(slots, *grads, *[in_hbm(stack) if stack.shape[0] > 1 else stack for stack in stacks])


def local(queries, keys, values, grad_out, out_weight, lengths):
    rows = queries.shape[0]
    rank = lax.axis_index("dp")
    core = rank % 2
    x, z = rank // 4, (rank // 2) % 2

    query_pos = rank * rows + jnp.arange(rows, dtype=jnp.int32)
    ends = jnp.cumsum(lengths)[:-1]
    query_start = jnp.max(
        jnp.where(ends[None, :] <= query_pos[:, None], ends[None, :], 0), axis=1
    )
    first = query_start[0] // KEY_BLOCK
    last = query_pos[-1] // KEY_BLOCK
    clear = (query_start[-1] + KEY_BLOCK - 1) // KEY_BLOCK
    block = jnp.arange(16, dtype=jnp.int32)
    place = block // 2 * 2
    here = place + jnp.where(block % 2 == core, 0, 1)
    there = place + jnp.where(block % 2 == core, 1, 0)
    scalars = jnp.stack([first, last - first + 1, clear, core])
    info = jnp.concatenate([scalars, here, there]).astype(jnp.int32)
    query_pos, query_start = query_pos[None, :], query_start[None, :]

    def copy(block, groups):
        return jnp.broadcast_to(block, (len(groups[0]), *block.shape))

    def exchange(copies, axis, groups):
        return lax.all_to_all(copies, axis, 0, 0, axis_index_groups=groups, tiled=True)

    def spread(block, axis, groups):
        return exchange(copy(block, groups), axis, groups)

    groups = [[2 * i + c for i in range(8)] for c in range(2)]
    kept = jnp.where(core == 0, keys, values)
    got = dp_move(jnp.where(core == 0, values, keys), 0, 0, 1)
    ring = spread(jnp.concatenate([kept, got], axis=0), "dp", groups).reshape(-1, HEAD_WIDTH)

    depth = out_weight.shape[1]
    mine = lax.dynamic_slice_in_dim(grad_out, core * depth, depth, 1)
    other = lax.dynamic_slice_in_dim(grad_out, (1 - core) * depth, depth, 1)
    chip_grad = jnp.concatenate([mine, dp_move(other, 0, 0, 1)], axis=0)
    all_grad = [chip_grad] + [tensor_move(chip_grad, 0, step) for step in (-1, -2, 1)]

    groups_x = [[x_ * 4 + zc for x_ in range(4)] for zc in range(4)]

    def gather_x(block):
        return lax.all_gather(block, "dp", axis=0, axis_index_groups=groups_x)

    own = [out_weight[:SPLIT], out_weight[SPLIT:]]
    plane1 = gather_x(own[1])
    pair0 = dp_move(own[0], 0, 1, 0)
    ring, own, all_grad, pair0, chip_grad, info, query_pos, query_start = lax.optimization_barrier(
        (ring, own, all_grad, pair0, chip_grad, info, query_pos, query_start)
    )
    plane0 = gather_x(own[0])
    grad_pair = tensor_move(chip_grad, 1, 0)
    pair1 = dp_move(own[1], 0, 1, 0)
    swapped = dp_move(ring, 0, 0, 1)
    swapped, copies = lax.optimization_barrier((swapped, copy(pair0, groups_x)))
    other_plane = exchange(copies, "dp", groups_x).reshape(4, SPLIT, depth)
    rest = jnp.concatenate(
        [lax.dynamic_slice_in_dim(plane1, (x + i) % 4, 1, 0) for i in range(1, 4)], axis=0
    )
    rest, grad_pair, later = lax.optimization_barrier((rest, grad_pair, queries))
    rest = dp_move(rest, 0, 1, 0)
    all_grad += [grad_pair] + [tensor_move(grad_pair, 0, step) for step in (-1, -2, 1)]
    probs, outs = forward(info, query_pos, query_start, later, ring, swapped)

    t = lax.axis_index("tensor")

    def slot(x_, z_):
        source = 2 * (x_ % 4) + z_
        return (source - t) % 4 + jnp.where(source // 4 == t // 4, 0, 4)

    same = [slot(i, z) for i in range(4)]
    slots = [
        jnp.stack(same + [slot(i, 1 - z) for i in range(4)]).astype(jnp.int32),
        jnp.stack(same + [slot(x + i, 1 - z) for i in range(4)]).astype(jnp.int32),
    ]
    slots[0] = after(slots[0], outs)
    stacks = [[plane0, other_plane], [plane1, pair1[None], rest]]
    terms = []
    for part in range(CHUNKS):
        mine, other = project(part, slots[part], all_grad, stacks[part])
        terms += [mine, dp_move(other, 0, 0, 1)]
    grad_queries, own_sums, other_sums = backward(info, terms, probs, outs, queries, ring, swapped)

    chip_sums = (own_sums + dp_move(other_sums, 0, 0, 1).astype(F32)).astype(BF16)
    terms = lax.all_to_all(chip_sums, "dp", 0, 0, axis_index_groups=groups, tiled=True)
    done = jnp.sum(terms.astype(F32), axis=0).astype(BF16)
    return grad_queries, done[:, :HEAD_WIDTH], done[:, HEAD_WIDTH:]


def solution(mesh):
    return jax.shard_map(
        local,
        mesh=mesh,
        in_specs=(
            P("dp", "tensor"),
            P("dp", "tensor"),
            P("dp", "tensor"),
            P("dp", "tensor"),
            P("tensor", "dp"),
            P(),
        ),
        out_specs=(P("dp", "tensor"), P("dp", "tensor"), P("dp", "tensor")),
        check_vma=False,
    )
```

```python
import functools
import math

import jax
import jax.numpy as jnp
from jax import lax
from jax.experimental import pallas as pl
from jax.experimental.pallas import tpu as pltpu
from jax.sharding import PartitionSpec as P

HEAD_WIDTH = 128
KEY_BLOCK = 256
MOST = 2560
CHUNKS = 2
SPLIT = 4 * HEAD_WIDTH
PAIR = 2
MASKED = -1e30
SCALE = 1.0 / math.sqrt(HEAD_WIDTH)
LOG2E = 1.0 / math.log(2.0)
BF16 = jnp.bfloat16
F32 = jnp.float32
VMEM_LIMIT = 22 * 2**20

FIRST, COUNT, CLEAR, CORE, TABLE = 0, 1, 2, 3, 4


def dp_move(value, dx, dz, dc):
    pairs = []
    for x in range(4):
        for z in range(2):
            for c in range(2):
                target = ((x + dx) % 4) * 4 + ((z + dz) % 2) * 2 + (c + dc) % 2
                pairs.append((x * 4 + z * 2 + c, target))
    return lax.ppermute(value, "dp", pairs)


def tensor_move(value, dz, dy):
    pairs = []
    for z in range(2):
        for y in range(4):
            pairs.append((z * 4 + y, ((z + dz) % 2) * 4 + (y + dy) % 4))
    return lax.ppermute(value, "tensor", pairs)


def after(value, *others):
    return lax.optimization_barrier((value, *others))[0]


def in_hbm(value):
    return pltpu.with_memory_space_constraint(value, pltpu.HBM)


def dot(left, right):
    return lax.dot_general(left, right, (((1,), (0,)), ((), ())), preferred_element_type=F32)


def dot_t(left, right):
    return lax.dot_general(left, right, (((1,), (1,)), ((), ())), preferred_element_type=F32)


def block_rows(index):
    return pl.ds(pl.multiple_of(index * KEY_BLOCK, KEY_BLOCK), KEY_BLOCK)


def forward_kernel(
    info, pos_ref, start_ref, q_ref, here_ref, there_ref, probs_ref, out_ref, score, keys, vt
):
    first, count = info[FIRST], info[COUNT]
    rows = q_ref.shape[0]
    heads = q_ref.shape[1] // HEAD_WIDTH
    query_t = jnp.concatenate(
        [q_ref[:, h * HEAD_WIDTH : (h + 1) * HEAD_WIDTH].T for h in range(heads)], axis=1
    )
    wide = heads * rows

    def groups(values):
        return values.reshape(KEY_BLOCK // 8, 8, wide)

    @pl.when(pl.program_id(0) == 0)
    def _():
        def turn(index, _):
            here = here_ref[block_rows(info[TABLE + first + index]), :]
            there = there_ref[block_rows(info[TABLE + 16 + first + index]), :]
            keys[block_rows(index), :] = jnp.where(info[CORE] == 0, here, there)
            vt[:, block_rows(index)] = jnp.where(info[CORE] == 0, there, here).T
            return 0
        lax.fori_loop(0, count, turn, 0)

    def product(index):
        return dot(keys[block_rows(index), :], query_t)

    def masked_step(index, top):
        key_pos = (first + index) * KEY_BLOCK + lax.broadcasted_iota(jnp.int32, (KEY_BLOCK, rows), 0)
        live = (key_pos >= start_ref[...]) & (key_pos <= pos_ref[...])
        raw = product(index)
        raw = jnp.concatenate(
            [jnp.where(live, raw[:, h * rows : (h + 1) * rows], MASKED) for h in range(heads)], axis=1
        )
        score[block_rows(index), :] = raw
        return jnp.maximum(top, jnp.max(groups(raw), axis=0))

    def clear_step(index, top):
        raw = product(index)
        score[block_rows(index), :] = raw
        return jnp.maximum(top, jnp.max(groups(raw), axis=0))

    clear = jnp.minimum(info[CLEAR] - first, count - 1)
    top = jnp.full((8, wide), MASKED, F32)
    top = lax.fori_loop(0, clear, masked_step, top)
    top = lax.fori_loop(clear, count - 1, clear_step, top)
    top = masked_step(count - 1, top)
    top = jnp.max(top, axis=0, keepdims=True) * (SCALE * LOG2E)

    def mass_step(index, mass):
        weights = jnp.exp2(score[block_rows(index), :] * (SCALE * LOG2E) - top)
        score[block_rows(index), :] = weights
        return mass + jnp.sum(groups(weights), axis=0)

    mass = lax.fori_loop(0, count, mass_step, jnp.zeros((8, wide), F32))
    share = 1.0 / jnp.sum(mass, axis=0, keepdims=True)
    out_ref[...] = jnp.zeros_like(out_ref)

    def probs_step(index, _):
        probs = (score[block_rows(index), :] * share).astype(BF16)
        probs_ref[block_rows(index), :] = probs
        out_ref[...] += dot(vt[:, block_rows(index)], probs)
        return 0

    lax.fori_loop(0, count, probs_step, 0)


def most_blocks(rows):
    return (MOST + rows - 2) // KEY_BLOCK + 1


def forward(info, query_pos, query_start, queries, here, there):
    rows, width = queries.shape
    heads = width // HEAD_WIDTH
    live = most_blocks(rows) * KEY_BLOCK
    line = pl.BlockSpec((1, rows), lambda h, r: (0, 0))
    return pl.pallas_call(
        forward_kernel,
        grid_spec=pltpu.PrefetchScalarGridSpec(
            num_scalar_prefetch=1,
            grid=(heads // PAIR,),
            in_specs=[
                line,
                line,
                pl.BlockSpec((rows, PAIR * HEAD_WIDTH), lambda h, r: (0, h)),
            ]
            + [pl.BlockSpec(here.shape, lambda h, r: (0, 0), pipeline_mode=pl.Buffered(1))] * 2,
            out_specs=[
                pl.BlockSpec((live, PAIR * rows), lambda h, r: (0, h)),
                pl.BlockSpec((HEAD_WIDTH, PAIR * rows), lambda h, r: (0, h)),
            ],
            scratch_shapes=[
                pltpu.VMEM((live, PAIR * rows), F32),
                pltpu.VMEM((live, HEAD_WIDTH), BF16),
                pltpu.VMEM((HEAD_WIDTH, live), BF16),
            ],
        ),
        out_shape=[
            pltpu.HBM((live, heads * rows), BF16),
            pltpu.HBM((HEAD_WIDTH, heads * rows), F32),
        ],
        compiler_params=pltpu.CompilerParams(vmem_limit_bytes=VMEM_LIMIT),
        cost_estimate=pl.CostEstimate(flops=10**8, bytes_accessed=2**20, transcendentals=0),
        name="forward",
    )(info, query_pos, query_start, in_hbm(queries), here, there)


def backward_kernel(heads, info, *rest):
    terms, rest = rest[:4], rest[4:]
    probs_ref, out_ref, q_ref, here_ref, there_ref, gq_ref, own_ref, other_ref, *scratch = rest
    grad_t, stack, delta, total_q, dscores, other = scratch
    step = pl.program_id(0)
    count = info[COUNT]
    rows = q_ref.shape[0]

    @pl.when(step == 0)
    def _():
        own_ref[...] = jnp.zeros_like(own_ref)
        other[...] = jnp.zeros_like(other)
        total_q[...] = jnp.zeros_like(total_q)
        for h in range(heads):
            cols = slice(h * rows, (h + 1) * rows)
            wide = slice(h * HEAD_WIDTH, (h + 1) * HEAD_WIDTH)
            at = h * HEAD_WIDTH
            mine, got = terms[:2]
            if at >= mine.shape[1]:
                at -= mine.shape[1]
                mine, got = terms[2:]
            here = slice(at, at + HEAD_WIDTH)
            grad = (mine[:, here] + got[:, here]).astype(BF16)
            turned = grad.T
            grad_t[:, cols] = turned
            stack[cols, :HEAD_WIDTH] = q_ref[:, wide]
            stack[cols, HEAD_WIDTH:] = grad
            delta[:, cols] = jnp.sum(turned.astype(F32) * out_ref[:, cols], axis=0, keepdims=True)

    @pl.when(step < count)
    def _():
        block = info[FIRST] + step
        keys_t = jnp.where(info[CORE] == 0, here_ref[...], there_ref[...]).T
        values = jnp.where(info[CORE] == 0, there_ref[...], here_ref[...])
        for h in range(heads):
            cols = slice(h * rows, (h + 1) * rows)
            dprob = dot(values, grad_t[:, cols])
            dscores[:, cols] = (probs_ref[:, cols].astype(F32) * (dprob - delta[:, cols])).astype(BF16)
        total_q[...] += dot(keys_t, dscores[...])
        key_sum = dot(dscores[...], stack[:, :HEAD_WIDTH])
        value_sum = dot(probs_ref[...], stack[:, HEAD_WIDTH:])

        def add(ref):
            ref[block // 2, :, :HEAD_WIDTH] += key_sum * SCALE
            ref[block // 2, :, HEAD_WIDTH:] += value_sum

        pl.when(block % 2 == info[CORE])(lambda: add(own_ref))
        pl.when(block % 2 != info[CORE])(lambda: add(other))

    @pl.when(step == count - 1)
    def _():
        for h in range(heads):
            cols = slice(h * rows, (h + 1) * rows)
            wide = slice(h * HEAD_WIDTH, (h + 1) * HEAD_WIDTH)
            gq_ref[:, wide] = (total_q[:, cols].T * SCALE).astype(BF16)
        other_ref[...] = other[...].astype(BF16)


def backward(info, terms, probs, outs, queries, here, there):
    rows, width = queries.shape
    heads = width // HEAD_WIDTH
    sums = (8, KEY_BLOCK, 2 * HEAD_WIDTH)

    def near(i, r):
        return jnp.minimum(i, r[COUNT] - 1)

    def once(shape):
        return pl.BlockSpec(shape, lambda i, r: (0,) * len(shape), pipeline_mode=pl.Buffered(1))

    return pl.pallas_call(
        functools.partial(backward_kernel, heads),
        grid_spec=pltpu.PrefetchScalarGridSpec(
            num_scalar_prefetch=1,
            grid=(most_blocks(rows),),
            in_specs=[once(term.shape) for term in terms]
            + [
                pl.BlockSpec((KEY_BLOCK, heads * rows), lambda i, r: (near(i, r), 0)),
                once(outs.shape),
                once(queries.shape),
                pl.BlockSpec(
                    (KEY_BLOCK, HEAD_WIDTH), lambda i, r: (r[TABLE + r[FIRST] + near(i, r)], 0)
                ),
                pl.BlockSpec(
                    (KEY_BLOCK, HEAD_WIDTH), lambda i, r: (r[TABLE + 16 + r[FIRST] + near(i, r)], 0)
                ),
            ],
            out_specs=[once((rows, width)), once(sums), once(sums)],
            scratch_shapes=[
                pltpu.VMEM((HEAD_WIDTH, heads * rows), BF16),
                pltpu.VMEM((heads * rows, 2 * HEAD_WIDTH), BF16),
                pltpu.VMEM((1, heads * rows), F32),
                pltpu.VMEM((HEAD_WIDTH, heads * rows), F32),
                pltpu.VMEM((KEY_BLOCK, heads * rows), BF16),
                pltpu.VMEM(sums, F32),
            ],
        ),
        out_shape=[
            jax.ShapeDtypeStruct((rows, width), BF16),
            jax.ShapeDtypeStruct(sums, F32),
            jax.ShapeDtypeStruct(sums, BF16),
        ],
        compiler_params=pltpu.CompilerParams(vmem_limit_bytes=VMEM_LIMIT),
        cost_estimate=pl.CostEstimate(
            flops=8 * 10**9, bytes_accessed=10 * 2**20, transcendentals=0
        ),
        name="backward",
    )(info, *terms, in_hbm(probs), outs, in_hbm(queries), here, there)


def project_kernel(chips, slots, *rest):
    grads, (*stacks, own_ref, other_ref, grad) = rest[:chips], rest[chips:]
    for i, ref in enumerate(grads):
        grad[i] = ref[...]
    half = own_ref.shape[0]
    k = 0
    for ref in stacks:
        for j in range(ref.shape[0]):
            for out, row in ((own_ref, 0), (other_ref, half)):
                term = dot_t(grad[slots[k], row : row + half, :], ref[j])
                if k == 0:
                    out[...] = term
                else:
                    out[...] += term
            k += 1


def project(part, slots, grads, stacks):
    chips = len(grads)
    tokens, depth = grads[0].shape
    features = stacks[0].shape[1]
    half = jax.ShapeDtypeStruct((tokens // 2, features), F32)

    def once(shape):
        return pl.BlockSpec(shape, lambda i: (0,) * len(shape), pipeline_mode=pl.Buffered(1))

    return pl.pallas_call(
        functools.partial(project_kernel, chips),
        grid=(1,),
        in_specs=[pl.BlockSpec(memory_space=pltpu.SMEM)]
        + [once(ref.shape) for ref in (*grads, *stacks)],
        out_specs=[once(half.shape)] * 2,
        out_shape=[half, half],
        scratch_shapes=[pltpu.VMEM((chips, tokens, depth), BF16)],
        compiler_params=pltpu.CompilerParams(vmem_limit_bytes=VMEM_LIMIT),
        cost_estimate=pl.CostEstimate(
            flops=2 * tokens * features * depth * chips,
            bytes_accessed=10 * 2**20,
            transcendentals=0,
        ),
        name="project%d" % part,
    )(slots, *grads, *[in_hbm(stack) if stack.shape[0] > 1 else stack for stack in stacks])


def local(queries, keys, values, grad_out, out_weight, lengths):
    rows = queries.shape[0]
    rank = lax.axis_index("dp")
    core = rank % 2
    x, z = rank // 4, (rank // 2) % 2

    query_pos = rank * rows + jnp.arange(rows, dtype=jnp.int32)
    ends = jnp.cumsum(lengths)[:-1]
    query_start = jnp.max(
        jnp.where(ends[None, :] <= query_pos[:, None], ends[None, :], 0), axis=1
    )
    first = query_start[0] // KEY_BLOCK
    last = query_pos[-1] // KEY_BLOCK
    clear = (query_start[-1] + KEY_BLOCK - 1) // KEY_BLOCK
    block = jnp.arange(16, dtype=jnp.int32)
    place = block // 4 * 4 + jnp.where(block // 2 % 2 == z, 0, 2)
    here = place + jnp.where(block % 2 == core, 0, 1)
    there = place + jnp.where(block % 2 == core, 1, 0)
    scalars = jnp.stack([first, last - first + 1, clear, core])
    info = jnp.concatenate([scalars, here, there]).astype(jnp.int32)
    query_pos, query_start = query_pos[None, :], query_start[None, :]

    def copy(block, groups):
        return jnp.broadcast_to(block, (len(groups[0]), *block.shape))

    def exchange(copies, axis, groups):
        return lax.all_to_all(copies, axis, 0, 0, axis_index_groups=groups, tiled=True)

    def spread(block, axis, groups):
        return exchange(copy(block, groups), axis, groups)

    groups_x = [[x_ * 4 + zc for x_ in range(4)] for zc in range(4)]
    kept = jnp.where(core == 0, keys, values)
    got = dp_move(jnp.where(core == 0, values, keys), 0, 0, 1)
    chip = jnp.concatenate([kept, got], axis=0)
    chip_pair = jnp.concatenate([chip, dp_move(chip, 0, 1, 0)], axis=0)
    ring = spread(chip_pair, "dp", groups_x).reshape(-1, HEAD_WIDTH)

    depth = out_weight.shape[1]
    mine = lax.dynamic_slice_in_dim(grad_out, core * depth, depth, 1)
    other = lax.dynamic_slice_in_dim(grad_out, (1 - core) * depth, depth, 1)
    chip_grad = jnp.concatenate([mine, dp_move(other, 0, 0, 1)], axis=0)
    all_grad = [chip_grad] + [tensor_move(chip_grad, 0, step) for step in (-1, -2, 1)]

    def gather_x(block):
        return lax.all_gather(block, "dp", axis=0, axis_index_groups=groups_x)

    own = [out_weight[:SPLIT], out_weight[SPLIT:]]
    plane1 = gather_x(own[1])
    pair0 = dp_move(after(own[0], chip_pair), 0, 1, 0)
    grad_pair = tensor_move(chip_grad, 1, 0)
    ring, own, all_grad, pair0, grad_pair, info, query_pos, query_start = lax.optimization_barrier(
        (ring, own, all_grad, pair0, grad_pair, info, query_pos, query_start)
    )
    plane0 = gather_x(own[0])
    all_grad += [grad_pair] + [tensor_move(grad_pair, 0, step) for step in (-1, -2, 1)]
    pair1 = dp_move(own[1], 0, 1, 0)
    swapped = dp_move(ring, 0, 0, 1)
    swapped, copies = lax.optimization_barrier((swapped, copy(pair0, groups_x)))
    other_plane = exchange(copies, "dp", groups_x).reshape(4, SPLIT, depth)
    rest = jnp.concatenate(
        [lax.dynamic_slice_in_dim(plane1, (x + i) % 4, 1, 0) for i in range(1, 4)], axis=0
    )
    rest, later = lax.optimization_barrier((rest, queries))
    rest = dp_move(rest, 0, 1, 0)
    probs, outs = forward(info, query_pos, query_start, later, ring, swapped)

    t = lax.axis_index("tensor")

    def slot(x_, z_):
        source = 2 * (x_ % 4) + z_
        return (source - t) % 4 + jnp.where(source // 4 == t // 4, 0, 4)

    same = [slot(i, z) for i in range(4)]
    slots = [
        jnp.stack(same + [slot(i, 1 - z) for i in range(4)]).astype(jnp.int32),
        jnp.stack(same + [slot(x + i, 1 - z) for i in range(4)]).astype(jnp.int32),
    ]
    slots[0] = after(slots[0], outs)
    stacks = [[plane0, other_plane], [plane1, pair1[None], rest]]
    terms = []
    for part in range(CHUNKS):
        mine, other = project(part, slots[part], all_grad, stacks[part])
        terms += [mine, dp_move(other, 0, 0, 1)]
    grad_queries, own_sums, other_sums = backward(info, terms, probs, outs, queries, ring, swapped)

    groups = [[2 * i + c for i in range(8)] for c in range(2)]
    chip_sums = (own_sums + dp_move(other_sums, 0, 0, 1).astype(F32)).astype(BF16)
    terms = lax.all_to_all(chip_sums, "dp", 0, 0, axis_index_groups=groups, tiled=True)
    done = jnp.sum(terms.astype(F32), axis=0).astype(BF16)
    return grad_queries, done[:, :HEAD_WIDTH], done[:, HEAD_WIDTH:]


def solution(mesh):
    return jax.shard_map(
        local,
        mesh=mesh,
        in_specs=(
            P("dp", "tensor"),
            P("dp", "tensor"),
            P("dp", "tensor"),
            P("dp", "tensor"),
            P("tensor", "dp"),
            P(),
        ),
        out_specs=(P("dp", "tensor"), P("dp", "tensor"), P("dp", "tensor")),
        check_vma=False,
    )
```

```python
import functools
import math

import jax
import jax.numpy as jnp
from jax import lax
from jax.experimental import pallas as pl
from jax.experimental.pallas import tpu as pltpu
from jax.sharding import PartitionSpec as P

HEAD_WIDTH = 128
KEY_BLOCK = 256
MOST = 2560
CHUNKS = 2
SPLIT = 4 * HEAD_WIDTH
PAIR = 2
MASKED = -1e30
SCALE = 1.0 / math.sqrt(HEAD_WIDTH)
LOG2E = 1.0 / math.log(2.0)
BF16 = jnp.bfloat16
F32 = jnp.float32
VMEM_LIMIT = 22 * 2**20

FIRST, COUNT, CLEAR, CORE, TABLE = 0, 1, 2, 3, 4


def dp_move(value, dx, dz, dc):
    pairs = []
    for x in range(4):
        for z in range(2):
            for c in range(2):
                target = ((x + dx) % 4) * 4 + ((z + dz) % 2) * 2 + (c + dc) % 2
                pairs.append((x * 4 + z * 2 + c, target))
    return lax.ppermute(value, "dp", pairs)


def tensor_move(value, dz, dy):
    pairs = []
    for z in range(2):
        for y in range(4):
            pairs.append((z * 4 + y, ((z + dz) % 2) * 4 + (y + dy) % 4))
    return lax.ppermute(value, "tensor", pairs)


def after(value, *others):
    return lax.optimization_barrier((value, *others))[0]


def in_hbm(value):
    return pltpu.with_memory_space_constraint(value, pltpu.HBM)


def dot(left, right):
    return lax.dot_general(left, right, (((1,), (0,)), ((), ())), preferred_element_type=F32)


def dot_t(left, right):
    return lax.dot_general(left, right, (((1,), (1,)), ((), ())), preferred_element_type=F32)


def block_rows(index):
    return pl.ds(pl.multiple_of(index * KEY_BLOCK, KEY_BLOCK), KEY_BLOCK)


def forward_kernel(
    info, pos_ref, start_ref, q_ref, here_ref, there_ref, probs_ref, out_ref, score, keys, vt
):
    first, count = info[FIRST], info[COUNT]
    rows = q_ref.shape[0]
    heads = q_ref.shape[1] // HEAD_WIDTH
    query_t = jnp.concatenate(
        [q_ref[:, h * HEAD_WIDTH : (h + 1) * HEAD_WIDTH].T for h in range(heads)], axis=1
    )
    wide = heads * rows

    def groups(values):
        return values.reshape(KEY_BLOCK // 8, 8, wide)

    @pl.when(pl.program_id(0) == 0)
    def _():
        def turn(index, _):
            here = here_ref[block_rows(info[TABLE + first + index]), :]
            there = there_ref[block_rows(info[TABLE + 16 + first + index]), :]
            keys[block_rows(index), :] = jnp.where(info[CORE] == 0, here, there)
            vt[:, block_rows(index)] = jnp.where(info[CORE] == 0, there, here).T
            return 0
        lax.fori_loop(0, count, turn, 0)

    def product(index):
        return dot(keys[block_rows(index), :], query_t)

    def masked_step(index, top):
        key_pos = (first + index) * KEY_BLOCK + lax.broadcasted_iota(jnp.int32, (KEY_BLOCK, rows), 0)
        live = (key_pos >= start_ref[...]) & (key_pos <= pos_ref[...])
        raw = product(index)
        raw = jnp.concatenate(
            [jnp.where(live, raw[:, h * rows : (h + 1) * rows], MASKED) for h in range(heads)], axis=1
        )
        score[block_rows(index), :] = raw
        return jnp.maximum(top, jnp.max(groups(raw), axis=0))

    def clear_step(index, top):
        raw = product(index)
        score[block_rows(index), :] = raw
        return jnp.maximum(top, jnp.max(groups(raw), axis=0))

    clear = jnp.minimum(info[CLEAR] - first, count - 1)
    top = jnp.full((8, wide), MASKED, F32)
    top = lax.fori_loop(0, clear, masked_step, top)
    top = lax.fori_loop(clear, count - 1, clear_step, top)
    top = masked_step(count - 1, top)
    top = jnp.max(top, axis=0, keepdims=True) * (SCALE * LOG2E)

    def mass_step(index, mass):
        weights = jnp.exp2(score[block_rows(index), :] * (SCALE * LOG2E) - top)
        score[block_rows(index), :] = weights
        return mass + jnp.sum(groups(weights), axis=0)

    mass = lax.fori_loop(0, count, mass_step, jnp.zeros((8, wide), F32))
    share = 1.0 / jnp.sum(mass, axis=0, keepdims=True)
    out_ref[...] = jnp.zeros_like(out_ref)

    def probs_step(index, _):
        probs = (score[block_rows(index), :] * share).astype(BF16)
        probs_ref[block_rows(index), :] = probs
        out_ref[...] += dot(vt[:, block_rows(index)], probs)
        return 0

    lax.fori_loop(0, count, probs_step, 0)


def most_blocks(rows):
    return (MOST + rows - 2) // KEY_BLOCK + 1


def forward(info, query_pos, query_start, queries, here, there):
    rows, width = queries.shape
    heads = width // HEAD_WIDTH
    live = most_blocks(rows) * KEY_BLOCK
    line = pl.BlockSpec((1, rows), lambda h, r: (0, 0))
    return pl.pallas_call(
        forward_kernel,
        grid_spec=pltpu.PrefetchScalarGridSpec(
            num_scalar_prefetch=1,
            grid=(heads // PAIR,),
            in_specs=[
                line,
                line,
                pl.BlockSpec((rows, PAIR * HEAD_WIDTH), lambda h, r: (0, h)),
            ]
            + [pl.BlockSpec(here.shape, lambda h, r: (0, 0), pipeline_mode=pl.Buffered(1))] * 2,
            out_specs=[
                pl.BlockSpec((live, PAIR * rows), lambda h, r: (0, h)),
                pl.BlockSpec((HEAD_WIDTH, PAIR * rows), lambda h, r: (0, h)),
            ],
            scratch_shapes=[
                pltpu.VMEM((live, PAIR * rows), F32),
                pltpu.VMEM((live, HEAD_WIDTH), BF16),
                pltpu.VMEM((HEAD_WIDTH, live), BF16),
            ],
        ),
        out_shape=[
            pltpu.HBM((live, heads * rows), BF16),
            pltpu.HBM((HEAD_WIDTH, heads * rows), F32),
        ],
        compiler_params=pltpu.CompilerParams(vmem_limit_bytes=VMEM_LIMIT),
        cost_estimate=pl.CostEstimate(flops=10**8, bytes_accessed=2**20, transcendentals=0),
        name="forward",
    )(info, query_pos, query_start, in_hbm(queries), here, there)


def backward_kernel(heads, info, *rest):
    terms, rest = rest[:4], rest[4:]
    probs_ref, out_ref, q_ref, here_ref, there_ref, gq_ref, own_ref, other_ref, *scratch = rest
    grad_t, stack, delta, total_q, dscores, other = scratch
    step = pl.program_id(0)
    count = info[COUNT]
    rows = q_ref.shape[0]

    @pl.when(step == 0)
    def _():
        own_ref[...] = jnp.zeros_like(own_ref)
        other[...] = jnp.zeros_like(other)
        total_q[...] = jnp.zeros_like(total_q)
        for h in range(heads):
            cols = slice(h * rows, (h + 1) * rows)
            wide = slice(h * HEAD_WIDTH, (h + 1) * HEAD_WIDTH)
            at = h * HEAD_WIDTH
            mine, got = terms[:2]
            if at >= mine.shape[1]:
                at -= mine.shape[1]
                mine, got = terms[2:]
            here = slice(at, at + HEAD_WIDTH)
            grad = (mine[:, here] + got[:, here]).astype(BF16)
            turned = grad.T
            grad_t[:, cols] = turned
            stack[cols, :HEAD_WIDTH] = q_ref[:, wide]
            stack[cols, HEAD_WIDTH:] = grad
            delta[:, cols] = jnp.sum(turned.astype(F32) * out_ref[:, cols], axis=0, keepdims=True)

    @pl.when(step < count)
    def _():
        block = info[FIRST] + step
        keys_t = jnp.where(info[CORE] == 0, here_ref[...], there_ref[...]).T
        values = jnp.where(info[CORE] == 0, there_ref[...], here_ref[...])
        for h in range(heads):
            cols = slice(h * rows, (h + 1) * rows)
            dprob = dot(values, grad_t[:, cols])
            dscores[:, cols] = (probs_ref[:, cols].astype(F32) * (dprob - delta[:, cols])).astype(BF16)
        total_q[...] += dot(keys_t, dscores[...])
        key_sum = dot(dscores[...], stack[:, :HEAD_WIDTH])
        value_sum = dot(probs_ref[...], stack[:, HEAD_WIDTH:])

        def add(ref):
            ref[block // 2, :, :HEAD_WIDTH] += key_sum * SCALE
            ref[block // 2, :, HEAD_WIDTH:] += value_sum

        pl.when(block % 2 == info[CORE])(lambda: add(own_ref))
        pl.when(block % 2 != info[CORE])(lambda: add(other))

    @pl.when(step == count - 1)
    def _():
        for h in range(heads):
            cols = slice(h * rows, (h + 1) * rows)
            wide = slice(h * HEAD_WIDTH, (h + 1) * HEAD_WIDTH)
            gq_ref[:, wide] = (total_q[:, cols].T * SCALE).astype(BF16)
        other_ref[...] = other[...].astype(BF16)


def backward(info, terms, probs, outs, queries, here, there):
    rows, width = queries.shape
    heads = width // HEAD_WIDTH
    sums = (8, KEY_BLOCK, 2 * HEAD_WIDTH)

    def near(i, r):
        return jnp.minimum(i, r[COUNT] - 1)

    def once(shape):
        return pl.BlockSpec(shape, lambda i, r: (0,) * len(shape), pipeline_mode=pl.Buffered(1))

    return pl.pallas_call(
        functools.partial(backward_kernel, heads),
        grid_spec=pltpu.PrefetchScalarGridSpec(
            num_scalar_prefetch=1,
            grid=(most_blocks(rows),),
            in_specs=[once(term.shape) for term in terms]
            + [
                pl.BlockSpec((KEY_BLOCK, heads * rows), lambda i, r: (near(i, r), 0)),
                once(outs.shape),
                once(queries.shape),
                pl.BlockSpec(
                    (KEY_BLOCK, HEAD_WIDTH), lambda i, r: (r[TABLE + r[FIRST] + near(i, r)], 0)
                ),
                pl.BlockSpec(
                    (KEY_BLOCK, HEAD_WIDTH), lambda i, r: (r[TABLE + 16 + r[FIRST] + near(i, r)], 0)
                ),
            ],
            out_specs=[once((rows, width)), once(sums), once(sums)],
            scratch_shapes=[
                pltpu.VMEM((HEAD_WIDTH, heads * rows), BF16),
                pltpu.VMEM((heads * rows, 2 * HEAD_WIDTH), BF16),
                pltpu.VMEM((1, heads * rows), F32),
                pltpu.VMEM((HEAD_WIDTH, heads * rows), F32),
                pltpu.VMEM((KEY_BLOCK, heads * rows), BF16),
                pltpu.VMEM(sums, F32),
            ],
        ),
        out_shape=[
            jax.ShapeDtypeStruct((rows, width), BF16),
            jax.ShapeDtypeStruct(sums, F32),
            jax.ShapeDtypeStruct(sums, BF16),
        ],
        compiler_params=pltpu.CompilerParams(vmem_limit_bytes=VMEM_LIMIT),
        cost_estimate=pl.CostEstimate(
            flops=8 * 10**9, bytes_accessed=10 * 2**20, transcendentals=0
        ),
        name="backward",
    )(info, *terms, in_hbm(probs), outs, in_hbm(queries), here, there)


def project_kernel(chips, slots, *rest):
    grads, (*stacks, own_ref, other_ref, grad) = rest[:chips], rest[chips:]
    for i, ref in enumerate(grads):
        grad[i] = ref[...]
    half = own_ref.shape[0]
    k = 0
    for ref in stacks:
        blocks = [ref] if len(ref.shape) == 2 else [ref.at[j] for j in range(ref.shape[0])]
        for block in blocks:
            for out, row in ((own_ref, 0), (other_ref, half)):
                term = dot_t(grad[slots[k], row : row + half, :], block[...])
                if k == 0:
                    out[...] = term
                else:
                    out[...] += term
            k += 1


def project(part, slots, grads, stacks):
    chips = len(grads)
    tokens, depth = grads[0].shape
    features = stacks[0].shape[-2]
    half = jax.ShapeDtypeStruct((tokens // 2, features), F32)

    def once(shape):
        return pl.BlockSpec(shape, lambda i: (0,) * len(shape), pipeline_mode=pl.Buffered(1))

    return pl.pallas_call(
        functools.partial(project_kernel, chips),
        grid=(1,),
        in_specs=[pl.BlockSpec(memory_space=pltpu.SMEM)]
        + [once(ref.shape) for ref in (*grads, *stacks)],
        out_specs=[once(half.shape)] * 2,
        out_shape=[half, half],
        scratch_shapes=[pltpu.VMEM((chips, tokens, depth), BF16)],
        compiler_params=pltpu.CompilerParams(vmem_limit_bytes=VMEM_LIMIT),
        cost_estimate=pl.CostEstimate(
            flops=2 * tokens * features * depth * chips,
            bytes_accessed=10 * 2**20,
            transcendentals=0,
        ),
        name="project%d" % part,
    )(slots, *grads, *[in_hbm(stack) if len(stack.shape) == 3 else stack for stack in stacks])


def local(queries, keys, values, grad_out, out_weight, lengths):
    rows = queries.shape[0]
    rank = lax.axis_index("dp")
    core = rank % 2
    x, z = rank // 4, (rank // 2) % 2

    query_pos = rank * rows + jnp.arange(rows, dtype=jnp.int32)
    ends = jnp.cumsum(lengths)[:-1]
    query_start = jnp.max(
        jnp.where(ends[None, :] <= query_pos[:, None], ends[None, :], 0), axis=1
    )
    first = query_start[0] // KEY_BLOCK
    last = query_pos[-1] // KEY_BLOCK
    clear = (query_start[-1] + KEY_BLOCK - 1) // KEY_BLOCK
    block = jnp.arange(16, dtype=jnp.int32)
    place = block // 4 * 4 + jnp.where(block // 2 % 2 == z, 0, 2)
    here = place + jnp.where(block % 2 == core, 0, 1)
    there = place + jnp.where(block % 2 == core, 1, 0)
    scalars = jnp.stack([first, last - first + 1, clear, core])
    info = jnp.concatenate([scalars, here, there]).astype(jnp.int32)
    query_pos, query_start = query_pos[None, :], query_start[None, :]

    def copy(block, groups):
        return jnp.broadcast_to(block, (len(groups[0]), *block.shape))

    def exchange(copies, axis, groups):
        return lax.all_to_all(copies, axis, 0, 0, axis_index_groups=groups, tiled=True)

    def spread(block, axis, groups):
        return exchange(copy(block, groups), axis, groups)

    groups_x = [[x_ * 4 + zc for x_ in range(4)] for zc in range(4)]
    kept = jnp.where(core == 0, keys, values)
    got = dp_move(jnp.where(core == 0, values, keys), 0, 0, 1)
    chip = jnp.concatenate([kept, got], axis=0)
    chip_pair = jnp.concatenate([chip, dp_move(chip, 0, 1, 0)], axis=0)
    ring = spread(chip_pair, "dp", groups_x).reshape(-1, HEAD_WIDTH)

    depth = out_weight.shape[1]
    mine = lax.dynamic_slice_in_dim(grad_out, core * depth, depth, 1)
    other = lax.dynamic_slice_in_dim(grad_out, (1 - core) * depth, depth, 1)
    chip_grad = jnp.concatenate([mine, dp_move(other, 0, 0, 1)], axis=0)
    all_grad = [chip_grad] + [tensor_move(chip_grad, 0, step) for step in (-1, -2, 1)]

    def around_x(block):
        return [dp_move(block, step, 0, 0) for step in (1, -1, 2)]

    own = [out_weight[:SPLIT], out_weight[SPLIT:]]
    plane1 = around_x(own[1])
    own0 = after(own[0], chip_pair)
    pair0 = dp_move(own0, 0, 1, 0)
    grad_pair = tensor_move(chip_grad, 1, 0)
    ring, plane1, all_grad, pair0, grad_pair, info, query_pos, query_start = lax.optimization_barrier(
        (ring, plane1, all_grad, pair0, grad_pair, info, query_pos, query_start)
    )
    plane0 = around_x(own0)
    all_grad += [grad_pair] + [tensor_move(grad_pair, 0, step) for step in (-1, -2, 1)]
    rest = jnp.stack(plane1)
    swapped = dp_move(ring, 0, 0, 1)
    swapped, copies, rest = lax.optimization_barrier((swapped, copy(pair0, groups_x), rest))
    other_plane = exchange(copies, "dp", groups_x).reshape(4, SPLIT, depth)
    pair1 = dp_move(after(own[1], ring), 0, 1, 0)
    rest = dp_move(rest, 0, 1, 0)
    probs, outs = forward(info, query_pos, query_start, queries, ring, swapped)

    t = lax.axis_index("tensor")

    def slot(x_, z_):
        source = 2 * (x_ % 4) + z_
        return (source - t) % 4 + jnp.where(source // 4 == t // 4, 0, 4)

    near = [slot(x + i, z) for i in (0, -1, 1, 2)]
    slots = [
        jnp.stack(near + [slot(i, 1 - z) for i in range(4)]).astype(jnp.int32),
        jnp.stack(near + [slot(x + i, 1 - z) for i in (0, -1, 1, 2)]).astype(jnp.int32),
    ]
    slots[0] = after(slots[0], outs)
    stacks = [[own0, *plane0, other_plane], [own[1], *plane1, pair1, rest]]
    terms = []
    for part in range(CHUNKS):
        mine, other = project(part, slots[part], all_grad, stacks[part])
        terms += [mine, dp_move(other, 0, 0, 1)]
    grad_queries, own_sums, other_sums = backward(info, terms, probs, outs, queries, ring, swapped)

    groups = [[2 * i + c for i in range(8)] for c in range(2)]
    chip_sums = (own_sums + dp_move(other_sums, 0, 0, 1).astype(F32)).astype(BF16)
    terms = lax.all_to_all(chip_sums, "dp", 0, 0, axis_index_groups=groups, tiled=True)
    done = jnp.sum(terms.astype(F32), axis=0).astype(BF16)
    return grad_queries, done[:, :HEAD_WIDTH], done[:, HEAD_WIDTH:]


def solution(mesh):
    return jax.shard_map(
        local,
        mesh=mesh,
        in_specs=(
            P("dp", "tensor"),
            P("dp", "tensor"),
            P("dp", "tensor"),
            P("dp", "tensor"),
            P("tensor", "dp"),
            P(),
        ),
        out_specs=(P("dp", "tensor"), P("dp", "tensor"), P("dp", "tensor")),
        check_vma=False,
    )
```

```python
import functools
import math

import jax
import jax.numpy as jnp
from jax import lax
from jax.experimental import pallas as pl
from jax.experimental.pallas import tpu as pltpu
from jax.sharding import PartitionSpec as P

HEAD_WIDTH = 128
KEY_BLOCK = 256
MOST = 2560
CHUNKS = 2
SPLIT = 4 * HEAD_WIDTH
PAIR = 2
MASKED = -1e30
SCALE = 1.0 / math.sqrt(HEAD_WIDTH)
LOG2E = 1.0 / math.log(2.0)
BF16 = jnp.bfloat16
F32 = jnp.float32
VMEM_LIMIT = 22 * 2**20

FIRST, COUNT, CLEAR, CORE, TABLE = 0, 1, 2, 3, 4


def dp_move(value, dx, dz, dc):
    pairs = []
    for x in range(4):
        for z in range(2):
            for c in range(2):
                target = ((x + dx) % 4) * 4 + ((z + dz) % 2) * 2 + (c + dc) % 2
                pairs.append((x * 4 + z * 2 + c, target))
    return lax.ppermute(value, "dp", pairs)


def tensor_move(value, dz, dy):
    pairs = []
    for z in range(2):
        for y in range(4):
            pairs.append((z * 4 + y, ((z + dz) % 2) * 4 + (y + dy) % 4))
    return lax.ppermute(value, "tensor", pairs)


def after(value, *others):
    return lax.optimization_barrier((value, *others))[0]


def in_hbm(value):
    return pltpu.with_memory_space_constraint(value, pltpu.HBM)


def dot(left, right):
    return lax.dot_general(left, right, (((1,), (0,)), ((), ())), preferred_element_type=F32)


def dot_t(left, right):
    return lax.dot_general(left, right, (((1,), (1,)), ((), ())), preferred_element_type=F32)


def block_rows(index):
    return pl.ds(pl.multiple_of(index * KEY_BLOCK, KEY_BLOCK), KEY_BLOCK)


def forward_kernel(
    info, pos_ref, start_ref, q_ref, here_ref, there_ref, probs_ref, out_ref, score, keys, vt
):
    first, count = info[FIRST], info[COUNT]
    rows = q_ref.shape[0]
    heads = q_ref.shape[1] // HEAD_WIDTH
    query_t = jnp.concatenate(
        [q_ref[:, h * HEAD_WIDTH : (h + 1) * HEAD_WIDTH].T for h in range(heads)], axis=1
    )
    wide = heads * rows

    def groups(values):
        return values.reshape(KEY_BLOCK // 8, 8, wide)

    @pl.when(pl.program_id(0) == 0)
    def _():
        def turn(index, _):
            here = here_ref[block_rows(info[TABLE + first + index]), :]
            there = there_ref[block_rows(info[TABLE + 16 + first + index]), :]
            keys[block_rows(index), :] = jnp.where(info[CORE] == 0, here, there)
            vt[:, block_rows(index)] = jnp.where(info[CORE] == 0, there, here).T
            return 0
        lax.fori_loop(0, count, turn, 0)

    def product(index):
        return dot(keys[block_rows(index), :], query_t)

    def masked_step(index, top):
        key_pos = (first + index) * KEY_BLOCK + lax.broadcasted_iota(jnp.int32, (KEY_BLOCK, rows), 0)
        live = (key_pos >= start_ref[...]) & (key_pos <= pos_ref[...])
        raw = product(index)
        raw = jnp.concatenate(
            [jnp.where(live, raw[:, h * rows : (h + 1) * rows], MASKED) for h in range(heads)], axis=1
        )
        score[block_rows(index), :] = raw
        return jnp.maximum(top, jnp.max(groups(raw), axis=0))

    def clear_step(index, top):
        raw = product(index)
        score[block_rows(index), :] = raw
        return jnp.maximum(top, jnp.max(groups(raw), axis=0))

    clear = jnp.minimum(info[CLEAR] - first, count - 1)
    top = jnp.full((8, wide), MASKED, F32)
    top = lax.fori_loop(0, clear, masked_step, top)
    top = lax.fori_loop(clear, count - 1, clear_step, top)
    top = masked_step(count - 1, top)
    top = jnp.max(top, axis=0, keepdims=True) * (SCALE * LOG2E)

    def mass_step(index, mass):
        weights = jnp.exp2(score[block_rows(index), :] * (SCALE * LOG2E) - top)
        score[block_rows(index), :] = weights
        return mass + jnp.sum(groups(weights), axis=0)

    mass = lax.fori_loop(0, count, mass_step, jnp.zeros((8, wide), F32))
    share = 1.0 / jnp.sum(mass, axis=0, keepdims=True)
    out_ref[...] = jnp.zeros_like(out_ref)

    def probs_step(index, _):
        probs = (score[block_rows(index), :] * share).astype(BF16)
        probs_ref[block_rows(index), :] = probs
        out_ref[...] += dot(vt[:, block_rows(index)], probs)
        return 0

    lax.fori_loop(0, count, probs_step, 0)


def most_blocks(rows):
    return (MOST + rows - 2) // KEY_BLOCK + 1


def forward(info, query_pos, query_start, queries, here, there):
    rows, width = queries.shape
    heads = width // HEAD_WIDTH
    live = most_blocks(rows) * KEY_BLOCK
    line = pl.BlockSpec((1, rows), lambda h, r: (0, 0))
    return pl.pallas_call(
        forward_kernel,
        grid_spec=pltpu.PrefetchScalarGridSpec(
            num_scalar_prefetch=1,
            grid=(heads // PAIR,),
            in_specs=[
                line,
                line,
                pl.BlockSpec((rows, PAIR * HEAD_WIDTH), lambda h, r: (0, h)),
            ]
            + [pl.BlockSpec(here.shape, lambda h, r: (0, 0), pipeline_mode=pl.Buffered(1))] * 2,
            out_specs=[
                pl.BlockSpec((live, PAIR * rows), lambda h, r: (0, h)),
                pl.BlockSpec((HEAD_WIDTH, PAIR * rows), lambda h, r: (0, h)),
            ],
            scratch_shapes=[
                pltpu.VMEM((live, PAIR * rows), F32),
                pltpu.VMEM((live, HEAD_WIDTH), BF16),
                pltpu.VMEM((HEAD_WIDTH, live), BF16),
            ],
        ),
        out_shape=[
            pltpu.HBM((live, heads * rows), BF16),
            pltpu.HBM((HEAD_WIDTH, heads * rows), F32),
        ],
        compiler_params=pltpu.CompilerParams(vmem_limit_bytes=VMEM_LIMIT),
        cost_estimate=pl.CostEstimate(flops=10**8, bytes_accessed=2**20, transcendentals=0),
        name="forward",
    )(info, query_pos, query_start, in_hbm(queries), here, there)


def backward_kernel(heads, info, *rest):
    terms, rest = rest[:4], rest[4:]
    probs_ref, out_ref, q_ref, here_ref, there_ref, gq_ref, own_ref, other_ref, *scratch = rest
    grad_t, stack, delta, total_q, dscores, other = scratch
    step = pl.program_id(0)
    count = info[COUNT]
    rows = q_ref.shape[0]

    @pl.when(step == 0)
    def _():
        own_ref[...] = jnp.zeros_like(own_ref)
        other[...] = jnp.zeros_like(other)
        total_q[...] = jnp.zeros_like(total_q)
        for h in range(heads):
            cols = slice(h * rows, (h + 1) * rows)
            wide = slice(h * HEAD_WIDTH, (h + 1) * HEAD_WIDTH)
            at = h * HEAD_WIDTH
            mine, got = terms[:2]
            if at >= mine.shape[1]:
                at -= mine.shape[1]
                mine, got = terms[2:]
            here = slice(at, at + HEAD_WIDTH)
            grad = (mine[:, here] + got[:, here]).astype(BF16)
            turned = grad.T
            grad_t[:, cols] = turned
            stack[cols, :HEAD_WIDTH] = q_ref[:, wide]
            stack[cols, HEAD_WIDTH:] = grad
            delta[:, cols] = jnp.sum(turned.astype(F32) * out_ref[:, cols], axis=0, keepdims=True)

    @pl.when(step < count)
    def _():
        block = info[FIRST] + step
        keys_t = jnp.where(info[CORE] == 0, here_ref[...], there_ref[...]).T
        values = jnp.where(info[CORE] == 0, there_ref[...], here_ref[...])
        for h in range(heads):
            cols = slice(h * rows, (h + 1) * rows)
            dprob = dot(values, grad_t[:, cols])
            dscores[:, cols] = (probs_ref[:, cols].astype(F32) * (dprob - delta[:, cols])).astype(BF16)
        total_q[...] += dot(keys_t, dscores[...])
        key_sum = dot(dscores[...], stack[:, :HEAD_WIDTH])
        value_sum = dot(probs_ref[...], stack[:, HEAD_WIDTH:])

        def add(ref):
            ref[block // 2, :, :HEAD_WIDTH] += key_sum * SCALE
            ref[block // 2, :, HEAD_WIDTH:] += value_sum

        pl.when(block % 2 == info[CORE])(lambda: add(own_ref))
        pl.when(block % 2 != info[CORE])(lambda: add(other))

    @pl.when(step == count - 1)
    def _():
        for h in range(heads):
            cols = slice(h * rows, (h + 1) * rows)
            wide = slice(h * HEAD_WIDTH, (h + 1) * HEAD_WIDTH)
            gq_ref[:, wide] = (total_q[:, cols].T * SCALE).astype(BF16)
        other_ref[...] = other[...].astype(BF16)


def backward(info, terms, probs, outs, queries, here, there):
    rows, width = queries.shape
    heads = width // HEAD_WIDTH
    sums = (8, KEY_BLOCK, 2 * HEAD_WIDTH)

    def near(i, r):
        return jnp.minimum(i, r[COUNT] - 1)

    def once(shape):
        return pl.BlockSpec(shape, lambda i, r: (0,) * len(shape), pipeline_mode=pl.Buffered(1))

    return pl.pallas_call(
        functools.partial(backward_kernel, heads),
        grid_spec=pltpu.PrefetchScalarGridSpec(
            num_scalar_prefetch=1,
            grid=(most_blocks(rows),),
            in_specs=[once(term.shape) for term in terms]
            + [
                pl.BlockSpec((KEY_BLOCK, heads * rows), lambda i, r: (near(i, r), 0)),
                once(outs.shape),
                once(queries.shape),
                pl.BlockSpec(
                    (KEY_BLOCK, HEAD_WIDTH), lambda i, r: (r[TABLE + r[FIRST] + near(i, r)], 0)
                ),
                pl.BlockSpec(
                    (KEY_BLOCK, HEAD_WIDTH), lambda i, r: (r[TABLE + 16 + r[FIRST] + near(i, r)], 0)
                ),
            ],
            out_specs=[once((rows, width)), once(sums), once(sums)],
            scratch_shapes=[
                pltpu.VMEM((HEAD_WIDTH, heads * rows), BF16),
                pltpu.VMEM((heads * rows, 2 * HEAD_WIDTH), BF16),
                pltpu.VMEM((1, heads * rows), F32),
                pltpu.VMEM((HEAD_WIDTH, heads * rows), F32),
                pltpu.VMEM((KEY_BLOCK, heads * rows), BF16),
                pltpu.VMEM(sums, F32),
            ],
        ),
        out_shape=[
            jax.ShapeDtypeStruct((rows, width), BF16),
            jax.ShapeDtypeStruct(sums, F32),
            jax.ShapeDtypeStruct(sums, BF16),
        ],
        compiler_params=pltpu.CompilerParams(vmem_limit_bytes=VMEM_LIMIT),
        cost_estimate=pl.CostEstimate(
            flops=8 * 10**9, bytes_accessed=10 * 2**20, transcendentals=0
        ),
        name="backward",
    )(info, *terms, in_hbm(probs), outs, in_hbm(queries), here, there)


def project_kernel(chips, slots, *rest):
    grads, (*stacks, own_ref, other_ref, grad) = rest[: chips // 2], rest[chips // 2 :]
    for i, ref in enumerate(grads):
        grad[2 * i : 2 * i + 2] = ref[...]
    half = own_ref.shape[0]
    k = 0
    for ref in stacks:
        blocks = [ref] if len(ref.shape) == 2 else [ref.at[j] for j in range(ref.shape[0])]
        for block in blocks:
            for out, row in ((own_ref, 0), (other_ref, half)):
                term = dot_t(grad[slots[k], row : row + half, :], block[...])
                if k == 0:
                    out[...] = term
                else:
                    out[...] += term
            k += 1


def project(part, slots, grads, stacks):
    chips = 2 * len(grads)
    _, tokens, depth = grads[0].shape
    features = stacks[0].shape[-2]
    half = jax.ShapeDtypeStruct((tokens // 2, features), F32)

    def once(shape):
        return pl.BlockSpec(shape, lambda i: (0,) * len(shape), pipeline_mode=pl.Buffered(1))

    return pl.pallas_call(
        functools.partial(project_kernel, chips),
        grid=(1,),
        in_specs=[pl.BlockSpec(memory_space=pltpu.SMEM)]
        + [once(ref.shape) for ref in (*grads, *stacks)],
        out_specs=[once(half.shape)] * 2,
        out_shape=[half, half],
        scratch_shapes=[pltpu.VMEM((chips, tokens, depth), BF16)],
        compiler_params=pltpu.CompilerParams(vmem_limit_bytes=VMEM_LIMIT),
        cost_estimate=pl.CostEstimate(
            flops=2 * tokens * features * depth * chips,
            bytes_accessed=10 * 2**20,
            transcendentals=0,
        ),
        name="project%d" % part,
    )(slots, *grads, *[in_hbm(stack) if len(stack.shape) == 3 else stack for stack in stacks])


def local(queries, keys, values, grad_out, out_weight, lengths):
    rows = queries.shape[0]
    rank = lax.axis_index("dp")
    core = rank % 2
    x, z = rank // 4, (rank // 2) % 2

    query_pos = rank * rows + jnp.arange(rows, dtype=jnp.int32)
    ends = jnp.cumsum(lengths)[:-1]
    query_start = jnp.max(
        jnp.where(ends[None, :] <= query_pos[:, None], ends[None, :], 0), axis=1
    )
    first = query_start[0] // KEY_BLOCK
    last = query_pos[-1] // KEY_BLOCK
    clear = (query_start[-1] + KEY_BLOCK - 1) // KEY_BLOCK
    block = jnp.arange(16, dtype=jnp.int32)
    place = block // 4 * 4 + jnp.where(block // 2 % 2 == z, 0, 2)
    here = place + jnp.where(block % 2 == core, 0, 1)
    there = place + jnp.where(block % 2 == core, 1, 0)
    scalars = jnp.stack([first, last - first + 1, clear, core])
    info = jnp.concatenate([scalars, here, there]).astype(jnp.int32)
    query_pos, query_start = query_pos[None, :], query_start[None, :]

    def copy(block, groups):
        return jnp.broadcast_to(block, (len(groups[0]), *block.shape))

    def exchange(copies, axis, groups):
        return lax.all_to_all(copies, axis, 0, 0, axis_index_groups=groups, tiled=True)

    def spread(block, axis, groups):
        return exchange(copy(block, groups), axis, groups)

    groups_x = [[x_ * 4 + zc for x_ in range(4)] for zc in range(4)]
    kept = jnp.where(core == 0, keys, values)
    got = dp_move(jnp.where(core == 0, values, keys), 0, 0, 1)
    chip = jnp.concatenate([kept, got], axis=0)
    chip_pair = jnp.concatenate([chip, dp_move(chip, 0, 1, 0)], axis=0)
    ring = spread(chip_pair, "dp", groups_x).reshape(-1, HEAD_WIDTH)

    depth = out_weight.shape[1]
    mine = lax.dynamic_slice_in_dim(grad_out, core * depth, depth, 1)
    other = lax.dynamic_slice_in_dim(grad_out, (1 - core) * depth, depth, 1)
    chip_grad = jnp.concatenate([mine, dp_move(other, 0, 0, 1)], axis=0)

    def around_x(block):
        return [dp_move(block, step, 0, 0) for step in (1, -1, 2)]

    own = [out_weight[:SPLIT], out_weight[SPLIT:]]
    plane1 = around_x(own[1])
    own0 = after(own[0], chip_pair)
    pair0 = dp_move(own0, 0, 1, 0)
    grad_pair = tensor_move(chip_grad, 1, 0)
    ring, plane1, pair0, grad_pair, info, query_pos, query_start = lax.optimization_barrier(
        (ring, plane1, pair0, grad_pair, info, query_pos, query_start)
    )
    swapped = dp_move(ring, 0, 0, 1)
    all_grad = [jnp.stack([chip_grad, grad_pair])]
    all_grad += [tensor_move(all_grad[0], 0, step) for step in (-1, -2, 1)]
    copies = copy(jnp.stack([own0, pair0]), groups_x)
    plane0 = exchange(copies, "dp", groups_x).reshape(8, SPLIT, depth)
    pair1 = dp_move(after(own[1], ring), 0, 1, 0)
    rest = dp_move(jnp.stack(plane1), 0, 1, 0)
    probs, outs = forward(info, query_pos, query_start, queries, ring, swapped)

    t = lax.axis_index("tensor")

    def slot(x_, z_):
        source = 2 * (x_ % 4) + z_
        return (source - t) % 4 * 2 + jnp.where(source // 4 == t // 4, 0, 1)

    near = [slot(x + i, z) for i in (0, -1, 1, 2)]
    slots = [
        jnp.stack([slot(i, z_) for i in range(4) for z_ in (z, 1 - z)]).astype(jnp.int32),
        jnp.stack(near + [slot(x + i, 1 - z) for i in (0, -1, 1, 2)]).astype(jnp.int32),
    ]
    slots[0] = after(slots[0], outs)
    stacks = [[plane0], [own[1], *plane1, pair1, rest]]
    terms = []
    for part in range(CHUNKS):
        mine, other = project(part, slots[part], all_grad, stacks[part])
        terms += [mine, dp_move(other, 0, 0, 1)]
    grad_queries, own_sums, other_sums = backward(info, terms, probs, outs, queries, ring, swapped)

    groups = [[2 * i + c for i in range(8)] for c in range(2)]
    chip_sums = (own_sums + dp_move(other_sums, 0, 0, 1).astype(F32)).astype(BF16)
    terms = lax.all_to_all(chip_sums, "dp", 0, 0, axis_index_groups=groups, tiled=True)
    done = jnp.sum(terms.astype(F32), axis=0).astype(BF16)
    return grad_queries, done[:, :HEAD_WIDTH], done[:, HEAD_WIDTH:]


def solution(mesh):
    return jax.shard_map(
        local,
        mesh=mesh,
        in_specs=(
            P("dp", "tensor"),
            P("dp", "tensor"),
            P("dp", "tensor"),
            P("dp", "tensor"),
            P("tensor", "dp"),
            P(),
        ),
        out_specs=(P("dp", "tensor"), P("dp", "tensor"), P("dp", "tensor")),
        check_vma=False,
    )
```

```python
import functools
import math

import jax
import jax.numpy as jnp
from jax import lax
from jax.experimental import pallas as pl
from jax.experimental.pallas import tpu as pltpu
from jax.sharding import PartitionSpec as P

HEAD_WIDTH = 128
KEY_BLOCK = 256
MOST = 2560
CHUNKS = 2
SPLIT = 4 * HEAD_WIDTH
PAIR = 2
MASKED = -1e30
SCALE = 1.0 / math.sqrt(HEAD_WIDTH)
LOG2E = 1.0 / math.log(2.0)
BF16 = jnp.bfloat16
F32 = jnp.float32
VMEM_LIMIT = 22 * 2**20

FIRST, COUNT, CLEAR, CORE, TABLE = 0, 1, 2, 3, 4


def dp_move(value, dx, dz, dc):
    pairs = []
    for x in range(4):
        for z in range(2):
            for c in range(2):
                target = ((x + dx) % 4) * 4 + ((z + dz) % 2) * 2 + (c + dc) % 2
                pairs.append((x * 4 + z * 2 + c, target))
    return lax.ppermute(value, "dp", pairs)


def tensor_move(value, dz, dy):
    pairs = []
    for z in range(2):
        for y in range(4):
            pairs.append((z * 4 + y, ((z + dz) % 2) * 4 + (y + dy) % 4))
    return lax.ppermute(value, "tensor", pairs)


def after(value, *others):
    return lax.optimization_barrier((value, *others))[0]


def in_hbm(value):
    return pltpu.with_memory_space_constraint(value, pltpu.HBM)


def dot(left, right):
    return lax.dot_general(left, right, (((1,), (0,)), ((), ())), preferred_element_type=F32)


def dot_t(left, right):
    return lax.dot_general(left, right, (((1,), (1,)), ((), ())), preferred_element_type=F32)


def block_rows(index):
    return pl.ds(pl.multiple_of(index * KEY_BLOCK, KEY_BLOCK), KEY_BLOCK)


def forward_kernel(
    info, pos_ref, start_ref, q_ref, here_ref, there_ref, probs_ref, out_ref, score, keys, vt
):
    first, count = info[FIRST], info[COUNT]
    rows = q_ref.shape[0]
    heads = q_ref.shape[1] // HEAD_WIDTH
    query_t = jnp.concatenate(
        [q_ref[:, h * HEAD_WIDTH : (h + 1) * HEAD_WIDTH].T for h in range(heads)], axis=1
    )
    wide = heads * rows

    def groups(values):
        return values.reshape(KEY_BLOCK // 8, 8, wide)

    @pl.when(pl.program_id(0) == 0)
    def _():
        def turn(index, _):
            here = here_ref[block_rows(info[TABLE + first + index]), :]
            there = there_ref[block_rows(info[TABLE + 16 + first + index]), :]
            keys[block_rows(index), :] = jnp.where(info[CORE] == 0, here, there)
            vt[:, block_rows(index)] = jnp.where(info[CORE] == 0, there, here).T
            return 0
        lax.fori_loop(0, count, turn, 0)

    def product(index):
        return dot(keys[block_rows(index), :], query_t)

    def masked_step(index, top):
        key_pos = (first + index) * KEY_BLOCK + lax.broadcasted_iota(jnp.int32, (KEY_BLOCK, rows), 0)
        live = (key_pos >= start_ref[...]) & (key_pos <= pos_ref[...])
        raw = product(index)
        raw = jnp.concatenate(
            [jnp.where(live, raw[:, h * rows : (h + 1) * rows], MASKED) for h in range(heads)], axis=1
        )
        score[block_rows(index), :] = raw
        return jnp.maximum(top, jnp.max(groups(raw), axis=0))

    def clear_step(index, top):
        raw = product(index)
        score[block_rows(index), :] = raw
        return jnp.maximum(top, jnp.max(groups(raw), axis=0))

    clear = jnp.minimum(info[CLEAR] - first, count - 1)
    top = jnp.full((8, wide), MASKED, F32)
    top = lax.fori_loop(0, clear, masked_step, top)
    top = lax.fori_loop(clear, count - 1, clear_step, top)
    top = masked_step(count - 1, top)
    top = jnp.max(top, axis=0, keepdims=True) * (SCALE * LOG2E)

    def mass_step(index, mass):
        weights = jnp.exp2(score[block_rows(index), :] * (SCALE * LOG2E) - top)
        score[block_rows(index), :] = weights
        return mass + jnp.sum(groups(weights), axis=0)

    mass = lax.fori_loop(0, count, mass_step, jnp.zeros((8, wide), F32))
    share = 1.0 / jnp.sum(mass, axis=0, keepdims=True)
    out_ref[...] = jnp.zeros_like(out_ref)

    def probs_step(index, _):
        probs = (score[block_rows(index), :] * share).astype(BF16)
        probs_ref[block_rows(index), :] = probs
        out_ref[...] += dot(vt[:, block_rows(index)], probs)
        return 0

    lax.fori_loop(0, count, probs_step, 0)


def most_blocks(rows):
    return (MOST + rows - 2) // KEY_BLOCK + 1


def forward(info, query_pos, query_start, queries, here, there):
    rows, width = queries.shape
    heads = width // HEAD_WIDTH
    live = most_blocks(rows) * KEY_BLOCK
    line = pl.BlockSpec((1, rows), lambda h, r: (0, 0))
    return pl.pallas_call(
        forward_kernel,
        grid_spec=pltpu.PrefetchScalarGridSpec(
            num_scalar_prefetch=1,
            grid=(heads // PAIR,),
            in_specs=[
                line,
                line,
                pl.BlockSpec((rows, PAIR * HEAD_WIDTH), lambda h, r: (0, h)),
            ]
            + [pl.BlockSpec(here.shape, lambda h, r: (0, 0), pipeline_mode=pl.Buffered(1))] * 2,
            out_specs=[
                pl.BlockSpec((live, PAIR * rows), lambda h, r: (0, h)),
                pl.BlockSpec((HEAD_WIDTH, PAIR * rows), lambda h, r: (0, h)),
            ],
            scratch_shapes=[
                pltpu.VMEM((live, PAIR * rows), F32),
                pltpu.VMEM((live, HEAD_WIDTH), BF16),
                pltpu.VMEM((HEAD_WIDTH, live), BF16),
            ],
        ),
        out_shape=[
            pltpu.HBM((live, heads * rows), BF16),
            pltpu.HBM((HEAD_WIDTH, heads * rows), F32),
        ],
        compiler_params=pltpu.CompilerParams(vmem_limit_bytes=VMEM_LIMIT),
        cost_estimate=pl.CostEstimate(flops=10**8, bytes_accessed=2**20, transcendentals=0),
        name="forward",
    )(info, query_pos, query_start, in_hbm(queries), here, there)


def backward_kernel(heads, info, *rest):
    terms, rest = rest[:4], rest[4:]
    probs_ref, out_ref, q_ref, here_ref, there_ref, gq_ref, own_ref, other_ref, *scratch = rest
    grad_t, stack, delta, total_q, dscores, other = scratch
    step = pl.program_id(0)
    count = info[COUNT]
    rows = q_ref.shape[0]

    @pl.when(step == 0)
    def _():
        own_ref[...] = jnp.zeros_like(own_ref)
        other[...] = jnp.zeros_like(other)
        total_q[...] = jnp.zeros_like(total_q)
        for h in range(heads):
            cols = slice(h * rows, (h + 1) * rows)
            wide = slice(h * HEAD_WIDTH, (h + 1) * HEAD_WIDTH)
            at = h * HEAD_WIDTH
            mine, got = terms[:2]
            if at >= mine.shape[1]:
                at -= mine.shape[1]
                mine, got = terms[2:]
            here = slice(at, at + HEAD_WIDTH)
            grad = (mine[:, here] + got[:, here]).astype(BF16)
            turned = grad.T
            grad_t[:, cols] = turned
            stack[cols, :HEAD_WIDTH] = q_ref[:, wide]
            stack[cols, HEAD_WIDTH:] = grad
            delta[:, cols] = jnp.sum(turned.astype(F32) * out_ref[:, cols], axis=0, keepdims=True)

    @pl.when(step < count)
    def _():
        block = info[FIRST] + step
        keys_t = jnp.where(info[CORE] == 0, here_ref[...], there_ref[...]).T
        values = jnp.where(info[CORE] == 0, there_ref[...], here_ref[...])
        for h in range(heads):
            cols = slice(h * rows, (h + 1) * rows)
            dprob = dot(values, grad_t[:, cols])
            dscores[:, cols] = (probs_ref[:, cols].astype(F32) * (dprob - delta[:, cols])).astype(BF16)
        total_q[...] += dot(keys_t, dscores[...])
        key_sum = dot(dscores[...], stack[:, :HEAD_WIDTH])
        value_sum = dot(probs_ref[...], stack[:, HEAD_WIDTH:])

        def add(ref):
            ref[block // 2, :, :HEAD_WIDTH] += key_sum * SCALE
            ref[block // 2, :, HEAD_WIDTH:] += value_sum

        pl.when(block % 2 == info[CORE])(lambda: add(own_ref))
        pl.when(block % 2 != info[CORE])(lambda: add(other))

    @pl.when(step == count - 1)
    def _():
        for h in range(heads):
            cols = slice(h * rows, (h + 1) * rows)
            wide = slice(h * HEAD_WIDTH, (h + 1) * HEAD_WIDTH)
            gq_ref[:, wide] = (total_q[:, cols].T * SCALE).astype(BF16)
        other_ref[...] = other[...].astype(BF16)


def backward(info, terms, probs, outs, queries, here, there):
    rows, width = queries.shape
    heads = width // HEAD_WIDTH
    sums = (8, KEY_BLOCK, 2 * HEAD_WIDTH)

    def near(i, r):
        return jnp.minimum(i, r[COUNT] - 1)

    def once(shape):
        return pl.BlockSpec(shape, lambda i, r: (0,) * len(shape), pipeline_mode=pl.Buffered(1))

    return pl.pallas_call(
        functools.partial(backward_kernel, heads),
        grid_spec=pltpu.PrefetchScalarGridSpec(
            num_scalar_prefetch=1,
            grid=(most_blocks(rows),),
            in_specs=[once(term.shape) for term in terms]
            + [
                pl.BlockSpec((KEY_BLOCK, heads * rows), lambda i, r: (near(i, r), 0)),
                once(outs.shape),
                once(queries.shape),
                pl.BlockSpec(
                    (KEY_BLOCK, HEAD_WIDTH), lambda i, r: (r[TABLE + r[FIRST] + near(i, r)], 0)
                ),
                pl.BlockSpec(
                    (KEY_BLOCK, HEAD_WIDTH), lambda i, r: (r[TABLE + 16 + r[FIRST] + near(i, r)], 0)
                ),
            ],
            out_specs=[once((rows, width)), once(sums), once(sums)],
            scratch_shapes=[
                pltpu.VMEM((HEAD_WIDTH, heads * rows), BF16),
                pltpu.VMEM((heads * rows, 2 * HEAD_WIDTH), BF16),
                pltpu.VMEM((1, heads * rows), F32),
                pltpu.VMEM((HEAD_WIDTH, heads * rows), F32),
                pltpu.VMEM((KEY_BLOCK, heads * rows), BF16),
                pltpu.VMEM(sums, F32),
            ],
        ),
        out_shape=[
            jax.ShapeDtypeStruct((rows, width), BF16),
            jax.ShapeDtypeStruct(sums, F32),
            jax.ShapeDtypeStruct(sums, BF16),
        ],
        compiler_params=pltpu.CompilerParams(vmem_limit_bytes=VMEM_LIMIT),
        cost_estimate=pl.CostEstimate(
            flops=8 * 10**9, bytes_accessed=10 * 2**20, transcendentals=0
        ),
        name="backward",
    )(info, *terms, in_hbm(probs), outs, in_hbm(queries), here, there)


def project_kernel(chips, slots, *rest):
    grads, (*stacks, own_ref, other_ref, grad) = rest[:chips], rest[chips:]
    for i, ref in enumerate(grads):
        grad[i] = ref[...]
    half = own_ref.shape[0]
    k = 0
    for ref in stacks:
        blocks = [ref] if len(ref.shape) == 2 else [ref.at[j] for j in range(ref.shape[0])]
        for block in blocks:
            for out, row in ((own_ref, 0), (other_ref, half)):
                term = dot_t(grad[slots[k], row : row + half, :], block[...])
                if k == 0:
                    out[...] = term
                else:
                    out[...] += term
            k += 1


def project(part, slots, grads, stacks):
    chips = len(grads)
    tokens, depth = grads[0].shape
    features = stacks[0].shape[-2]
    half = jax.ShapeDtypeStruct((tokens // 2, features), F32)

    def once(shape):
        return pl.BlockSpec(shape, lambda i: (0,) * len(shape), pipeline_mode=pl.Buffered(1))

    return pl.pallas_call(
        functools.partial(project_kernel, chips),
        grid=(1,),
        in_specs=[pl.BlockSpec(memory_space=pltpu.SMEM)]
        + [once(ref.shape) for ref in (*grads, *stacks)],
        out_specs=[once(half.shape)] * 2,
        out_shape=[half, half],
        scratch_shapes=[pltpu.VMEM((chips, tokens, depth), BF16)],
        compiler_params=pltpu.CompilerParams(vmem_limit_bytes=VMEM_LIMIT),
        cost_estimate=pl.CostEstimate(
            flops=2 * tokens * features * depth * chips,
            bytes_accessed=10 * 2**20,
            transcendentals=0,
        ),
        name="project%d" % part,
    )(slots, *grads, *[in_hbm(stack) if len(stack.shape) == 3 else stack for stack in stacks])


def local(queries, keys, values, grad_out, out_weight, lengths):
    rows = queries.shape[0]
    rank = lax.axis_index("dp")
    core = rank % 2
    x, z = rank // 4, (rank // 2) % 2

    query_pos = rank * rows + jnp.arange(rows, dtype=jnp.int32)
    ends = jnp.cumsum(lengths)[:-1]
    query_start = jnp.max(
        jnp.where(ends[None, :] <= query_pos[:, None], ends[None, :], 0), axis=1
    )
    first = query_start[0] // KEY_BLOCK
    last = query_pos[-1] // KEY_BLOCK
    clear = (query_start[-1] + KEY_BLOCK - 1) // KEY_BLOCK
    block = jnp.arange(16, dtype=jnp.int32)
    place = block // 4 * 4 + jnp.where(block // 2 % 2 == z, 0, 2)
    here = place + jnp.where(block % 2 == core, 0, 1)
    there = place + jnp.where(block % 2 == core, 1, 0)
    scalars = jnp.stack([first, last - first + 1, clear, core])
    info = jnp.concatenate([scalars, here, there]).astype(jnp.int32)
    query_pos, query_start = query_pos[None, :], query_start[None, :]

    def copy(block, groups):
        return jnp.broadcast_to(block, (len(groups[0]), *block.shape))

    def exchange(copies, axis, groups):
        return lax.all_to_all(copies, axis, 0, 0, axis_index_groups=groups, tiled=True)

    def spread(block, axis, groups):
        return exchange(copy(block, groups), axis, groups)

    groups_x = [[x_ * 4 + zc for x_ in range(4)] for zc in range(4)]
    kept = jnp.where(core == 0, keys, values)
    got = dp_move(jnp.where(core == 0, values, keys), 0, 0, 1)
    chip = jnp.concatenate([kept, got], axis=0)
    chip_pair = jnp.concatenate([chip, dp_move(chip, 0, 1, 0)], axis=0)
    ring = spread(chip_pair, "dp", groups_x).reshape(-1, HEAD_WIDTH)

    depth = out_weight.shape[1]
    mine = lax.dynamic_slice_in_dim(grad_out, core * depth, depth, 1)
    other = lax.dynamic_slice_in_dim(grad_out, (1 - core) * depth, depth, 1)
    chip_grad = jnp.concatenate([mine, dp_move(other, 0, 0, 1)], axis=0)

    def around_x(block):
        return [dp_move(block, step, 0, 0) for step in (1, -1, 2)]

    def around_y(block):
        return [tensor_move(block, 0, step) for step in (-1, -2, 1)]

    own = [out_weight[:SPLIT], out_weight[SPLIT:]]
    plane1 = around_x(own[1])
    own0 = after(own[0], chip_pair)
    pair0 = dp_move(own0, 0, 1, 0)
    grad_pair = tensor_move(chip_grad, 1, 0)
    plane1, chip_grad = lax.optimization_barrier((plane1, chip_grad))
    rest = dp_move(jnp.stack([own[1], *plane1]), 0, 1, 0)
    grads_own = around_y(chip_grad)
    copies = copy(jnp.stack([own0, pair0]), groups_x)
    ring, copies, grad_pair, info, query_pos, query_start = lax.optimization_barrier(
        (ring, copies, grad_pair, info, query_pos, query_start)
    )
    plane0 = exchange(copies, "dp", groups_x).reshape(8, SPLIT, depth)
    swapped = dp_move(ring, 0, 0, 1)
    grads_own, grad_pair, later = lax.optimization_barrier((grads_own, grad_pair, queries))
    all_grad = [chip_grad, *grads_own, grad_pair, *around_y(grad_pair)]
    probs, outs = forward(info, query_pos, query_start, later, ring, swapped)

    t = lax.axis_index("tensor")

    def slot(x_, z_):
        source = 2 * (x_ % 4) + z_
        return (source - t) % 4 + jnp.where(source // 4 == t // 4, 0, 4)

    near = [slot(x + i, z) for i in (0, -1, 1, 2)]
    slots = [
        jnp.stack([slot(i, z_) for i in range(4) for z_ in (z, 1 - z)]).astype(jnp.int32),
        jnp.stack(near + [slot(x + i, 1 - z) for i in (0, -1, 1, 2)]).astype(jnp.int32),
    ]
    slots = list(lax.optimization_barrier((*slots, outs))[:2])
    stacks = [[plane0], [own[1], *plane1, rest]]
    mine1, other1 = project(1, slots[1], all_grad, stacks[1])
    mine0, other0 = project(0, slots[0], all_grad, stacks[0])
    terms = [mine0, dp_move(other0, 0, 0, 1), mine1, dp_move(other1, 0, 0, 1)]
    grad_queries, own_sums, other_sums = backward(info, terms, probs, outs, queries, ring, swapped)

    groups = [[2 * i + c for i in range(8)] for c in range(2)]
    chip_sums = (own_sums + dp_move(other_sums, 0, 0, 1).astype(F32)).astype(BF16)
    terms = lax.all_to_all(chip_sums, "dp", 0, 0, axis_index_groups=groups, tiled=True)
    done = jnp.sum(terms.astype(F32), axis=0).astype(BF16)
    return grad_queries, done[:, :HEAD_WIDTH], done[:, HEAD_WIDTH:]


def solution(mesh):
    return jax.shard_map(
        local,
        mesh=mesh,
        in_specs=(
            P("dp", "tensor"),
            P("dp", "tensor"),
            P("dp", "tensor"),
            P("dp", "tensor"),
            P("tensor", "dp"),
            P(),
        ),
        out_specs=(P("dp", "tensor"), P("dp", "tensor"), P("dp", "tensor")),
        check_vma=False,
    )
```

```python
import functools
import math

import jax
import jax.numpy as jnp
from jax import lax
from jax.experimental import pallas as pl
from jax.experimental.pallas import tpu as pltpu
from jax.sharding import PartitionSpec as P

HEAD_WIDTH = 128
KEY_BLOCK = 256
MOST = 2560
CHUNKS = 2
SPLIT = 4 * HEAD_WIDTH
PAIR = 2
MASKED = -1e30
SCALE = 1.0 / math.sqrt(HEAD_WIDTH)
LOG2E = 1.0 / math.log(2.0)
BF16 = jnp.bfloat16
F32 = jnp.float32
VMEM_LIMIT = 22 * 2**20

FIRST, COUNT, CLEAR, CORE, TABLE = 0, 1, 2, 3, 4


def dp_move(value, dx, dz, dc):
    pairs = []
    for x in range(4):
        for z in range(2):
            for c in range(2):
                target = ((x + dx) % 4) * 4 + ((z + dz) % 2) * 2 + (c + dc) % 2
                pairs.append((x * 4 + z * 2 + c, target))
    return lax.ppermute(value, "dp", pairs)


def tensor_move(value, dz, dy):
    pairs = []
    for z in range(2):
        for y in range(4):
            pairs.append((z * 4 + y, ((z + dz) % 2) * 4 + (y + dy) % 4))
    return lax.ppermute(value, "tensor", pairs)


def after(value, *others):
    return lax.optimization_barrier((value, *others))[0]


def in_hbm(value):
    return pltpu.with_memory_space_constraint(value, pltpu.HBM)


def dot(left, right):
    return lax.dot_general(left, right, (((1,), (0,)), ((), ())), preferred_element_type=F32)


def dot_t(left, right):
    return lax.dot_general(left, right, (((1,), (1,)), ((), ())), preferred_element_type=F32)


def block_rows(index):
    return pl.ds(pl.multiple_of(index * KEY_BLOCK, KEY_BLOCK), KEY_BLOCK)


def forward_kernel(
    info, pos_ref, start_ref, q_ref, here_ref, there_ref, probs_ref, out_ref, score, keys, vt
):
    first, count = info[FIRST], info[COUNT]
    rows = q_ref.shape[0]
    heads = q_ref.shape[1] // HEAD_WIDTH
    query_t = jnp.concatenate(
        [q_ref[:, h * HEAD_WIDTH : (h + 1) * HEAD_WIDTH].T for h in range(heads)], axis=1
    )
    wide = heads * rows

    def groups(values):
        return values.reshape(KEY_BLOCK // 8, 8, wide)

    @pl.when(pl.program_id(0) == 0)
    def _():
        def turn(index, _):
            here = here_ref[block_rows(info[TABLE + first + index]), :]
            there = there_ref[block_rows(info[TABLE + 16 + first + index]), :]
            keys[block_rows(index), :] = jnp.where(info[CORE] == 0, here, there)
            vt[:, block_rows(index)] = jnp.where(info[CORE] == 0, there, here).T
            return 0
        lax.fori_loop(0, count, turn, 0)

    def product(index):
        return dot(keys[block_rows(index), :], query_t)

    def masked_step(index, top):
        key_pos = (first + index) * KEY_BLOCK + lax.broadcasted_iota(jnp.int32, (KEY_BLOCK, rows), 0)
        live = (key_pos >= start_ref[...]) & (key_pos <= pos_ref[...])
        raw = product(index)
        raw = jnp.concatenate(
            [jnp.where(live, raw[:, h * rows : (h + 1) * rows], MASKED) for h in range(heads)], axis=1
        )
        score[block_rows(index), :] = raw
        return jnp.maximum(top, jnp.max(groups(raw), axis=0))

    def clear_step(index, top):
        raw = product(index)
        score[block_rows(index), :] = raw
        return jnp.maximum(top, jnp.max(groups(raw), axis=0))

    clear = jnp.minimum(info[CLEAR] - first, count - 1)
    top = jnp.full((8, wide), MASKED, F32)
    top = lax.fori_loop(0, clear, masked_step, top)
    top = lax.fori_loop(clear, count - 1, clear_step, top)
    top = masked_step(count - 1, top)
    top = jnp.max(top, axis=0, keepdims=True) * (SCALE * LOG2E)

    def mass_step(index, mass):
        weights = jnp.exp2(score[block_rows(index), :] * (SCALE * LOG2E) - top)
        score[block_rows(index), :] = weights
        return mass + jnp.sum(groups(weights), axis=0)

    mass = lax.fori_loop(0, count, mass_step, jnp.zeros((8, wide), F32))
    share = 1.0 / jnp.sum(mass, axis=0, keepdims=True)
    out_ref[...] = jnp.zeros_like(out_ref)

    def probs_step(index, _):
        probs = (score[block_rows(index), :] * share).astype(BF16)
        probs_ref[block_rows(index), :] = probs
        out_ref[...] += dot(vt[:, block_rows(index)], probs)
        return 0

    lax.fori_loop(0, count, probs_step, 0)


def most_blocks(rows):
    return (MOST + rows - 2) // KEY_BLOCK + 1


def forward(info, query_pos, query_start, queries, here, there):
    rows, width = queries.shape
    heads = width // HEAD_WIDTH
    live = most_blocks(rows) * KEY_BLOCK
    line = pl.BlockSpec((1, rows), lambda h, r: (0, 0))
    return pl.pallas_call(
        forward_kernel,
        grid_spec=pltpu.PrefetchScalarGridSpec(
            num_scalar_prefetch=1,
            grid=(heads // PAIR,),
            in_specs=[
                line,
                line,
                pl.BlockSpec((rows, PAIR * HEAD_WIDTH), lambda h, r: (0, h)),
            ]
            + [pl.BlockSpec(here.shape, lambda h, r: (0, 0), pipeline_mode=pl.Buffered(1))] * 2,
            out_specs=[
                pl.BlockSpec((live, PAIR * rows), lambda h, r: (0, h)),
                pl.BlockSpec((HEAD_WIDTH, PAIR * rows), lambda h, r: (0, h)),
            ],
            scratch_shapes=[
                pltpu.VMEM((live, PAIR * rows), F32),
                pltpu.VMEM((live, HEAD_WIDTH), BF16),
                pltpu.VMEM((HEAD_WIDTH, live), BF16),
            ],
        ),
        out_shape=[
            pltpu.HBM((live, heads * rows), BF16),
            pltpu.HBM((HEAD_WIDTH, heads * rows), F32),
        ],
        compiler_params=pltpu.CompilerParams(vmem_limit_bytes=VMEM_LIMIT),
        cost_estimate=pl.CostEstimate(flops=10**8, bytes_accessed=2**20, transcendentals=0),
        name="forward",
    )(info, query_pos, query_start, in_hbm(queries), here, there)


def backward_kernel(heads, info, *rest):
    terms, rest = rest[:4], rest[4:]
    probs_ref, out_ref, q_ref, here_ref, there_ref, gq_ref, own_ref, other_ref, *scratch = rest
    grad_t, stack, delta, total_q, dscores, other = scratch
    step = pl.program_id(0)
    count = info[COUNT]
    rows = q_ref.shape[0]

    @pl.when(step == 0)
    def _():
        own_ref[...] = jnp.zeros_like(own_ref)
        other[...] = jnp.zeros_like(other)
        total_q[...] = jnp.zeros_like(total_q)
        for h in range(heads):
            cols = slice(h * rows, (h + 1) * rows)
            wide = slice(h * HEAD_WIDTH, (h + 1) * HEAD_WIDTH)
            at = h * HEAD_WIDTH
            mine, got = terms[:2]
            if at >= mine.shape[1]:
                at -= mine.shape[1]
                mine, got = terms[2:]
            here = slice(at, at + HEAD_WIDTH)
            grad = (mine[:, here] + got[:, here]).astype(BF16)
            turned = grad.T
            grad_t[:, cols] = turned
            stack[cols, :HEAD_WIDTH] = q_ref[:, wide]
            stack[cols, HEAD_WIDTH:] = grad
            delta[:, cols] = jnp.sum(turned.astype(F32) * out_ref[:, cols], axis=0, keepdims=True)

    @pl.when(step < count)
    def _():
        block = info[FIRST] + step
        keys_t = jnp.where(info[CORE] == 0, here_ref[...], there_ref[...]).T
        values = jnp.where(info[CORE] == 0, there_ref[...], here_ref[...])
        for h in range(heads):
            cols = slice(h * rows, (h + 1) * rows)
            dprob = dot(values, grad_t[:, cols])
            dscores[:, cols] = (probs_ref[:, cols].astype(F32) * (dprob - delta[:, cols])).astype(BF16)
        total_q[...] += dot(keys_t, dscores[...])
        key_sum = dot(dscores[...], stack[:, :HEAD_WIDTH])
        value_sum = dot(probs_ref[...], stack[:, HEAD_WIDTH:])

        def add(ref):
            ref[block // 2, :, :HEAD_WIDTH] += key_sum * SCALE
            ref[block // 2, :, HEAD_WIDTH:] += value_sum

        pl.when(block % 2 == info[CORE])(lambda: add(own_ref))
        pl.when(block % 2 != info[CORE])(lambda: add(other))

    @pl.when(step == count - 1)
    def _():
        for h in range(heads):
            cols = slice(h * rows, (h + 1) * rows)
            wide = slice(h * HEAD_WIDTH, (h + 1) * HEAD_WIDTH)
            gq_ref[:, wide] = (total_q[:, cols].T * SCALE).astype(BF16)
        other_ref[...] = other[...].astype(BF16)


def backward(info, terms, probs, outs, queries, here, there):
    rows, width = queries.shape
    heads = width // HEAD_WIDTH
    sums = (8, KEY_BLOCK, 2 * HEAD_WIDTH)

    def near(i, r):
        return jnp.minimum(i, r[COUNT] - 1)

    def once(shape):
        return pl.BlockSpec(shape, lambda i, r: (0,) * len(shape), pipeline_mode=pl.Buffered(1))

    return pl.pallas_call(
        functools.partial(backward_kernel, heads),
        grid_spec=pltpu.PrefetchScalarGridSpec(
            num_scalar_prefetch=1,
            grid=(most_blocks(rows),),
            in_specs=[once(term.shape) for term in terms]
            + [
                pl.BlockSpec((KEY_BLOCK, heads * rows), lambda i, r: (near(i, r), 0)),
                once(outs.shape),
                once(queries.shape),
                pl.BlockSpec(
                    (KEY_BLOCK, HEAD_WIDTH), lambda i, r: (r[TABLE + r[FIRST] + near(i, r)], 0)
                ),
                pl.BlockSpec(
                    (KEY_BLOCK, HEAD_WIDTH), lambda i, r: (r[TABLE + 16 + r[FIRST] + near(i, r)], 0)
                ),
            ],
            out_specs=[once((rows, width)), once(sums), once(sums)],
            scratch_shapes=[
                pltpu.VMEM((HEAD_WIDTH, heads * rows), BF16),
                pltpu.VMEM((heads * rows, 2 * HEAD_WIDTH), BF16),
                pltpu.VMEM((1, heads * rows), F32),
                pltpu.VMEM((HEAD_WIDTH, heads * rows), F32),
                pltpu.VMEM((KEY_BLOCK, heads * rows), BF16),
                pltpu.VMEM(sums, F32),
            ],
        ),
        out_shape=[
            jax.ShapeDtypeStruct((rows, width), BF16),
            jax.ShapeDtypeStruct(sums, F32),
            jax.ShapeDtypeStruct(sums, BF16),
        ],
        compiler_params=pltpu.CompilerParams(vmem_limit_bytes=VMEM_LIMIT),
        cost_estimate=pl.CostEstimate(
            flops=8 * 10**9, bytes_accessed=10 * 2**20, transcendentals=0
        ),
        name="backward",
    )(info, *terms, in_hbm(probs), outs, in_hbm(queries), here, there)


def project_kernel(chips, slots, *rest):
    grads, (*stacks, own_ref, other_ref, grad) = rest[: chips // 2], rest[chips // 2 :]
    for i, ref in enumerate(grads):
        grad[2 * i : 2 * i + 2] = ref[...]
    half = own_ref.shape[0]
    k = 0
    for ref in stacks:
        blocks = [ref] if len(ref.shape) == 2 else [ref.at[j] for j in range(ref.shape[0])]
        for block in blocks:
            for out, row in ((own_ref, 0), (other_ref, half)):
                term = dot_t(grad[slots[k], row : row + half, :], block[...])
                if k == 0:
                    out[...] = term
                else:
                    out[...] += term
            k += 1


def project(part, slots, grads, stacks):
    chips = 2 * len(grads)
    _, tokens, depth = grads[0].shape
    features = stacks[0].shape[-2]
    half = jax.ShapeDtypeStruct((tokens // 2, features), F32)

    def once(shape):
        return pl.BlockSpec(shape, lambda i: (0,) * len(shape), pipeline_mode=pl.Buffered(1))

    return pl.pallas_call(
        functools.partial(project_kernel, chips),
        grid=(1,),
        in_specs=[pl.BlockSpec(memory_space=pltpu.SMEM)]
        + [once(ref.shape) for ref in (*grads, *stacks)],
        out_specs=[once(half.shape)] * 2,
        out_shape=[half, half],
        scratch_shapes=[pltpu.VMEM((chips, tokens, depth), BF16)],
        compiler_params=pltpu.CompilerParams(vmem_limit_bytes=VMEM_LIMIT),
        cost_estimate=pl.CostEstimate(
            flops=2 * tokens * features * depth * chips,
            bytes_accessed=10 * 2**20,
            transcendentals=0,
        ),
        name="project%d" % part,
    )(slots, *grads, *[in_hbm(stack) if len(stack.shape) == 3 else stack for stack in stacks])


def local(queries, keys, values, grad_out, out_weight, lengths):
    rows = queries.shape[0]
    rank = lax.axis_index("dp")
    core = rank % 2
    x, z = rank // 4, (rank // 2) % 2

    query_pos = rank * rows + jnp.arange(rows, dtype=jnp.int32)
    ends = jnp.cumsum(lengths)[:-1]
    query_start = jnp.max(
        jnp.where(ends[None, :] <= query_pos[:, None], ends[None, :], 0), axis=1
    )
    first = query_start[0] // KEY_BLOCK
    last = query_pos[-1] // KEY_BLOCK
    clear = (query_start[-1] + KEY_BLOCK - 1) // KEY_BLOCK
    block = jnp.arange(16, dtype=jnp.int32)
    place = block // 4 * 4 + jnp.where(block // 2 % 2 == z, 0, 2)
    here = place + jnp.where(block % 2 == core, 0, 1)
    there = place + jnp.where(block % 2 == core, 1, 0)
    scalars = jnp.stack([first, last - first + 1, clear, core])
    info = jnp.concatenate([scalars, here, there]).astype(jnp.int32)
    query_pos, query_start = query_pos[None, :], query_start[None, :]

    def copy(block, groups):
        return jnp.broadcast_to(block, (len(groups[0]), *block.shape))

    def exchange(copies, axis, groups):
        return lax.all_to_all(copies, axis, 0, 0, axis_index_groups=groups, tiled=True)

    def spread(block, axis, groups):
        return exchange(copy(block, groups), axis, groups)

    groups_x = [[x_ * 4 + zc for x_ in range(4)] for zc in range(4)]
    kept = jnp.where(core == 0, keys, values)
    got = dp_move(jnp.where(core == 0, values, keys), 0, 0, 1)
    chip = jnp.concatenate([kept, got], axis=0)
    chip_pair = jnp.concatenate([chip, dp_move(chip, 0, 1, 0)], axis=0)
    ring = spread(chip_pair, "dp", groups_x).reshape(-1, HEAD_WIDTH)

    depth = out_weight.shape[1]
    mine = lax.dynamic_slice_in_dim(grad_out, core * depth, depth, 1)
    other = lax.dynamic_slice_in_dim(grad_out, (1 - core) * depth, depth, 1)
    chip_grad = jnp.concatenate([mine, dp_move(other, 0, 0, 1)], axis=0)

    def around_x(block):
        return [dp_move(block, step, 0, 0) for step in (1, -1, 2)]

    own = [out_weight[:SPLIT], out_weight[SPLIT:]]
    plane1 = around_x(own[1])
    own0 = after(own[0], chip_pair)
    pair0 = dp_move(own0, 0, 1, 0)
    grad_pair = tensor_move(chip_grad, 1, 0)
    copies = copy(jnp.stack([own0, pair0]), groups_x)
    both_grads = jnp.stack([chip_grad, grad_pair])
    sent = jnp.stack([own[1], *plane1])
    ring, copies, both_grads, sent, info, query_pos, query_start = lax.optimization_barrier(
        (ring, copies, both_grads, sent, info, query_pos, query_start)
    )
    plane0 = exchange(copies, "dp", groups_x).reshape(8, SPLIT, depth)
    rest = dp_move(sent, 0, 1, 0)
    swapped = dp_move(ring, 0, 0, 1)
    all_grad = [both_grads] + [tensor_move(both_grads, 0, step) for step in (-1, -2, 1)]
    probs, outs = forward(info, query_pos, query_start, queries, ring, swapped)

    t = lax.axis_index("tensor")

    def slot(x_, z_):
        source = 2 * (x_ % 4) + z_
        return (source - t) % 4 * 2 + jnp.where(source // 4 == t // 4, 0, 1)

    near = [slot(x + i, z) for i in (0, -1, 1, 2)]
    slots = [
        jnp.stack([slot(i, z_) for i in range(4) for z_ in (z, 1 - z)]).astype(jnp.int32),
        jnp.stack(near + [slot(x + i, 1 - z) for i in (0, -1, 1, 2)]).astype(jnp.int32),
    ]
    slots[0] = after(slots[0], outs)
    stacks = [[plane0], [sent, rest]]
    terms = []
    for part in range(CHUNKS):
        mine, other = project(part, slots[part], all_grad, stacks[part])
        terms += [mine, dp_move(other, 0, 0, 1)]
    grad_queries, own_sums, other_sums = backward(info, terms, probs, outs, queries, ring, swapped)

    groups = [[2 * i + c for i in range(8)] for c in range(2)]
    chip_sums = (own_sums + dp_move(other_sums, 0, 0, 1).astype(F32)).astype(BF16)
    terms = lax.all_to_all(chip_sums, "dp", 0, 0, axis_index_groups=groups, tiled=True)
    done = jnp.sum(terms.astype(F32), axis=0).astype(BF16)
    return grad_queries, done[:, :HEAD_WIDTH], done[:, HEAD_WIDTH:]


def solution(mesh):
    return jax.shard_map(
        local,
        mesh=mesh,
        in_specs=(
            P("dp", "tensor"),
            P("dp", "tensor"),
            P("dp", "tensor"),
            P("dp", "tensor"),
            P("tensor", "dp"),
            P(),
        ),
        out_specs=(P("dp", "tensor"), P("dp", "tensor"), P("dp", "tensor")),
        check_vma=False,
    )
```

```python
import functools
import math

import jax
import jax.numpy as jnp
from jax import lax
from jax.experimental import pallas as pl
from jax.experimental.pallas import tpu as pltpu
from jax.sharding import PartitionSpec as P

HEAD_WIDTH = 128
KEY_BLOCK = 256
MOST = 2560
CHUNKS = 2
SPLIT = 4 * HEAD_WIDTH
PAIR = 2
MASKED = -1e30
SCALE = 1.0 / math.sqrt(HEAD_WIDTH)
LOG2E = 1.0 / math.log(2.0)
BF16 = jnp.bfloat16
F32 = jnp.float32
VMEM_LIMIT = 22 * 2**20

FIRST, COUNT, CLEAR, CORE, TABLE = 0, 1, 2, 3, 4


def dp_move(value, dx, dz, dc):
    pairs = []
    for x in range(4):
        for z in range(2):
            for c in range(2):
                target = ((x + dx) % 4) * 4 + ((z + dz) % 2) * 2 + (c + dc) % 2
                pairs.append((x * 4 + z * 2 + c, target))
    return lax.ppermute(value, "dp", pairs)


def tensor_move(value, dz, dy):
    pairs = []
    for z in range(2):
        for y in range(4):
            pairs.append((z * 4 + y, ((z + dz) % 2) * 4 + (y + dy) % 4))
    return lax.ppermute(value, "tensor", pairs)


def after(value, *others):
    return lax.optimization_barrier((value, *others))[0]


def in_hbm(value):
    return pltpu.with_memory_space_constraint(value, pltpu.HBM)


def dot(left, right):
    return lax.dot_general(left, right, (((1,), (0,)), ((), ())), preferred_element_type=F32)


def dot_t(left, right):
    return lax.dot_general(left, right, (((1,), (1,)), ((), ())), preferred_element_type=F32)


def block_rows(index):
    return pl.ds(pl.multiple_of(index * KEY_BLOCK, KEY_BLOCK), KEY_BLOCK)


def forward_kernel(
    info, pos_ref, start_ref, q_ref, here_ref, there_ref, probs_ref, out_ref, score, keys, vt
):
    first, count = info[FIRST], info[COUNT]
    rows = q_ref.shape[0]
    heads = q_ref.shape[1] // HEAD_WIDTH
    query_t = jnp.concatenate(
        [q_ref[:, h * HEAD_WIDTH : (h + 1) * HEAD_WIDTH].T for h in range(heads)], axis=1
    )
    wide = heads * rows

    def groups(values):
        return values.reshape(KEY_BLOCK // 8, 8, wide)

    @pl.when(pl.program_id(0) == 0)
    def _():
        def turn(index, _):
            here = here_ref[block_rows(info[TABLE + first + index]), :]
            there = there_ref[block_rows(info[TABLE + 16 + first + index]), :]
            keys[block_rows(index), :] = jnp.where(info[CORE] == 0, here, there)
            vt[:, block_rows(index)] = jnp.where(info[CORE] == 0, there, here).T
            return 0
        lax.fori_loop(0, count, turn, 0)

    def product(index):
        return dot(keys[block_rows(index), :], query_t)

    def masked_step(index, top):
        key_pos = (first + index) * KEY_BLOCK + lax.broadcasted_iota(jnp.int32, (KEY_BLOCK, rows), 0)
        live = (key_pos >= start_ref[...]) & (key_pos <= pos_ref[...])
        raw = product(index)
        raw = jnp.concatenate(
            [jnp.where(live, raw[:, h * rows : (h + 1) * rows], MASKED) for h in range(heads)], axis=1
        )
        score[block_rows(index), :] = raw
        return jnp.maximum(top, jnp.max(groups(raw), axis=0))

    def clear_step(index, top):
        raw = product(index)
        score[block_rows(index), :] = raw
        return jnp.maximum(top, jnp.max(groups(raw), axis=0))

    clear = jnp.minimum(info[CLEAR] - first, count - 1)
    top = jnp.full((8, wide), MASKED, F32)
    top = lax.fori_loop(0, clear, masked_step, top)
    top = lax.fori_loop(clear, count - 1, clear_step, top)
    top = masked_step(count - 1, top)
    top = jnp.max(top, axis=0, keepdims=True) * (SCALE * LOG2E)

    def mass_step(index, mass):
        weights = jnp.exp2(score[block_rows(index), :] * (SCALE * LOG2E) - top)
        score[block_rows(index), :] = weights
        return mass + jnp.sum(groups(weights), axis=0)

    mass = lax.fori_loop(0, count, mass_step, jnp.zeros((8, wide), F32))
    share = 1.0 / jnp.sum(mass, axis=0, keepdims=True)
    out_ref[...] = jnp.zeros_like(out_ref)

    def probs_step(index, _):
        probs = (score[block_rows(index), :] * share).astype(BF16)
        probs_ref[block_rows(index), :] = probs
        out_ref[...] += dot(vt[:, block_rows(index)], probs)
        return 0

    lax.fori_loop(0, count, probs_step, 0)


def most_blocks(rows):
    return (MOST + rows - 2) // KEY_BLOCK + 1


def forward(info, query_pos, query_start, queries, here, there):
    rows, width = queries.shape
    heads = width // HEAD_WIDTH
    live = most_blocks(rows) * KEY_BLOCK
    line = pl.BlockSpec((1, rows), lambda h, r: (0, 0))
    return pl.pallas_call(
        forward_kernel,
        grid_spec=pltpu.PrefetchScalarGridSpec(
            num_scalar_prefetch=1,
            grid=(heads // PAIR,),
            in_specs=[
                line,
                line,
                pl.BlockSpec((rows, PAIR * HEAD_WIDTH), lambda h, r: (0, h)),
            ]
            + [pl.BlockSpec(here.shape, lambda h, r: (0, 0), pipeline_mode=pl.Buffered(1))] * 2,
            out_specs=[
                pl.BlockSpec((live, PAIR * rows), lambda h, r: (0, h)),
                pl.BlockSpec((HEAD_WIDTH, PAIR * rows), lambda h, r: (0, h)),
            ],
            scratch_shapes=[
                pltpu.VMEM((live, PAIR * rows), F32),
                pltpu.VMEM((live, HEAD_WIDTH), BF16),
                pltpu.VMEM((HEAD_WIDTH, live), BF16),
            ],
        ),
        out_shape=[
            pltpu.HBM((live, heads * rows), BF16),
            pltpu.HBM((HEAD_WIDTH, heads * rows), F32),
        ],
        compiler_params=pltpu.CompilerParams(vmem_limit_bytes=VMEM_LIMIT),
        cost_estimate=pl.CostEstimate(flops=10**8, bytes_accessed=2**20, transcendentals=0),
        name="forward",
    )(info, query_pos, query_start, in_hbm(queries), here, there)


def backward_kernel(heads, info, *rest):
    terms, rest = rest[:4], rest[4:]
    probs_ref, out_ref, q_ref, here_ref, there_ref, gq_ref, own_ref, other_ref, *scratch = rest
    grad_t, stack, delta, total_q, dscores, other = scratch
    step = pl.program_id(0)
    count = info[COUNT]
    rows = q_ref.shape[0]

    @pl.when(step == 0)
    def _():
        own_ref[...] = jnp.zeros_like(own_ref)
        other[...] = jnp.zeros_like(other)
        total_q[...] = jnp.zeros_like(total_q)
        for h in range(heads):
            cols = slice(h * rows, (h + 1) * rows)
            wide = slice(h * HEAD_WIDTH, (h + 1) * HEAD_WIDTH)
            at = h * HEAD_WIDTH
            mine, got = terms[:2]
            if at >= mine.shape[1]:
                at -= mine.shape[1]
                mine, got = terms[2:]
            here = slice(at, at + HEAD_WIDTH)
            grad = (mine[:, here] + got[:, here]).astype(BF16)
            turned = grad.T
            grad_t[:, cols] = turned
            stack[cols, :HEAD_WIDTH] = q_ref[:, wide]
            stack[cols, HEAD_WIDTH:] = grad
            delta[:, cols] = jnp.sum(turned.astype(F32) * out_ref[:, cols], axis=0, keepdims=True)

    @pl.when(step < count)
    def _():
        block = info[FIRST] + step
        keys_t = jnp.where(info[CORE] == 0, here_ref[...], there_ref[...]).T
        values = jnp.where(info[CORE] == 0, there_ref[...], here_ref[...])
        for h in range(heads):
            cols = slice(h * rows, (h + 1) * rows)
            dprob = dot(values, grad_t[:, cols])
            dscores[:, cols] = (probs_ref[:, cols].astype(F32) * (dprob - delta[:, cols])).astype(BF16)
        total_q[...] += dot(keys_t, dscores[...])
        key_sum = dot(dscores[...], stack[:, :HEAD_WIDTH])
        value_sum = dot(probs_ref[...], stack[:, HEAD_WIDTH:])

        def add(ref):
            ref[block // 2, :, :HEAD_WIDTH] += key_sum * SCALE
            ref[block // 2, :, HEAD_WIDTH:] += value_sum

        pl.when(block % 2 == info[CORE])(lambda: add(own_ref))
        pl.when(block % 2 != info[CORE])(lambda: add(other))

    @pl.when(step == count - 1)
    def _():
        for h in range(heads):
            cols = slice(h * rows, (h + 1) * rows)
            wide = slice(h * HEAD_WIDTH, (h + 1) * HEAD_WIDTH)
            gq_ref[:, wide] = (total_q[:, cols].T * SCALE).astype(BF16)
        other_ref[...] = other[...].astype(BF16)


def backward(info, terms, probs, outs, queries, here, there):
    rows, width = queries.shape
    heads = width // HEAD_WIDTH
    sums = (8, KEY_BLOCK, 2 * HEAD_WIDTH)

    def near(i, r):
        return jnp.minimum(i, r[COUNT] - 1)

    def once(shape):
        return pl.BlockSpec(shape, lambda i, r: (0,) * len(shape), pipeline_mode=pl.Buffered(1))

    return pl.pallas_call(
        functools.partial(backward_kernel, heads),
        grid_spec=pltpu.PrefetchScalarGridSpec(
            num_scalar_prefetch=1,
            grid=(most_blocks(rows),),
            in_specs=[once(term.shape) for term in terms]
            + [
                pl.BlockSpec((KEY_BLOCK, heads * rows), lambda i, r: (near(i, r), 0)),
                once(outs.shape),
                once(queries.shape),
                pl.BlockSpec(
                    (KEY_BLOCK, HEAD_WIDTH), lambda i, r: (r[TABLE + r[FIRST] + near(i, r)], 0)
                ),
                pl.BlockSpec(
                    (KEY_BLOCK, HEAD_WIDTH), lambda i, r: (r[TABLE + 16 + r[FIRST] + near(i, r)], 0)
                ),
            ],
            out_specs=[once((rows, width)), once(sums), once(sums)],
            scratch_shapes=[
                pltpu.VMEM((HEAD_WIDTH, heads * rows), BF16),
                pltpu.VMEM((heads * rows, 2 * HEAD_WIDTH), BF16),
                pltpu.VMEM((1, heads * rows), F32),
                pltpu.VMEM((HEAD_WIDTH, heads * rows), F32),
                pltpu.VMEM((KEY_BLOCK, heads * rows), BF16),
                pltpu.VMEM(sums, F32),
            ],
        ),
        out_shape=[
            jax.ShapeDtypeStruct((rows, width), BF16),
            jax.ShapeDtypeStruct(sums, F32),
            jax.ShapeDtypeStruct(sums, BF16),
        ],
        compiler_params=pltpu.CompilerParams(vmem_limit_bytes=VMEM_LIMIT),
        cost_estimate=pl.CostEstimate(
            flops=8 * 10**9, bytes_accessed=10 * 2**20, transcendentals=0
        ),
        name="backward",
    )(info, *terms, in_hbm(probs), outs, in_hbm(queries), here, there)


def project_kernel(chips, slots, *rest):
    grads, (*stacks, own_ref, other_ref, grad) = rest[: chips // 2], rest[chips // 2 :]
    for i, ref in enumerate(grads):
        grad[2 * i : 2 * i + 2] = ref[...]
    half = own_ref.shape[0]
    k = 0
    for ref in stacks:
        blocks = [ref] if len(ref.shape) == 2 else [ref.at[j] for j in range(ref.shape[0])]
        for block in blocks:
            for out, row in ((own_ref, 0), (other_ref, half)):
                term = dot_t(grad[slots[k], row : row + half, :], block[...])
                if k == 0:
                    out[...] = term
                else:
                    out[...] += term
            k += 1


def project(part, slots, grads, stacks):
    chips = 2 * len(grads)
    _, tokens, depth = grads[0].shape
    features = stacks[0].shape[-2]
    half = jax.ShapeDtypeStruct((tokens // 2, features), F32)

    def once(shape):
        return pl.BlockSpec(shape, lambda i: (0,) * len(shape), pipeline_mode=pl.Buffered(1))

    return pl.pallas_call(
        functools.partial(project_kernel, chips),
        grid=(1,),
        in_specs=[pl.BlockSpec(memory_space=pltpu.SMEM)]
        + [once(ref.shape) for ref in (*grads, *stacks)],
        out_specs=[once(half.shape)] * 2,
        out_shape=[half, half],
        scratch_shapes=[pltpu.VMEM((chips, tokens, depth), BF16)],
        compiler_params=pltpu.CompilerParams(vmem_limit_bytes=VMEM_LIMIT),
        cost_estimate=pl.CostEstimate(
            flops=2 * tokens * features * depth * chips,
            bytes_accessed=10 * 2**20,
            transcendentals=0,
        ),
        name="project%d" % part,
    )(slots, *grads, *[in_hbm(stack) if len(stack.shape) == 3 else stack for stack in stacks])


def local(queries, keys, values, grad_out, out_weight, lengths):
    rows = queries.shape[0]
    rank = lax.axis_index("dp")
    core = rank % 2
    x, z = rank // 4, (rank // 2) % 2

    def copy(block, groups):
        return jnp.broadcast_to(block, (len(groups[0]), *block.shape))

    def exchange(copies, axis, groups):
        return lax.all_to_all(copies, axis, 0, 0, axis_index_groups=groups, tiled=True)

    groups_x = [[x_ * 4 + zc for x_ in range(4)] for zc in range(4)]
    kept = jnp.where(core == 0, keys, values)
    got = dp_move(jnp.where(core == 0, values, keys), 0, 0, 1)
    chip = jnp.concatenate([kept, got], axis=0)
    chip_pair = jnp.concatenate([chip, dp_move(chip, 0, 1, 0)], axis=0)

    depth = out_weight.shape[1]
    mine = lax.dynamic_slice_in_dim(grad_out, core * depth, depth, 1)
    other = lax.dynamic_slice_in_dim(grad_out, (1 - core) * depth, depth, 1)
    chip_grad = jnp.concatenate([mine, dp_move(other, 0, 0, 1)], axis=0)
    copies, chip_grad = lax.optimization_barrier((copy(chip_pair, groups_x), chip_grad))
    ring = exchange(copies, "dp", groups_x).reshape(-1, HEAD_WIDTH)
    lengths = after(lengths, copies)

    query_pos = rank * rows + jnp.arange(rows, dtype=jnp.int32)
    ends = jnp.cumsum(lengths)[:-1]
    query_start = jnp.max(
        jnp.where(ends[None, :] <= query_pos[:, None], ends[None, :], 0), axis=1
    )
    first = query_start[0] // KEY_BLOCK
    last = query_pos[-1] // KEY_BLOCK
    clear = (query_start[-1] + KEY_BLOCK - 1) // KEY_BLOCK
    block = jnp.arange(16, dtype=jnp.int32)
    place = block // 4 * 4 + jnp.where(block // 2 % 2 == z, 0, 2)
    here = place + jnp.where(block % 2 == core, 0, 1)
    there = place + jnp.where(block % 2 == core, 1, 0)
    scalars = jnp.stack([first, last - first + 1, clear, core])
    info = jnp.concatenate([scalars, here, there]).astype(jnp.int32)
    query_pos, query_start = query_pos[None, :], query_start[None, :]


    def around_x(block):
        return [dp_move(block, step, 0, 0) for step in (1, -1, 2)]

    own = [out_weight[:SPLIT], out_weight[SPLIT:]]
    plane1 = around_x(own[1])
    own0 = after(own[0], chip_pair)
    pair0 = dp_move(own0, 0, 1, 0)
    grad_pair = tensor_move(chip_grad, 1, 0)
    copies = copy(jnp.stack([own0, pair0]), groups_x)
    both_grads = jnp.stack([chip_grad, grad_pair])
    sent = jnp.stack([own[1], *plane1])
    ring, copies, both_grads, sent, info, query_pos, query_start = lax.optimization_barrier(
        (ring, copies, both_grads, sent, info, query_pos, query_start)
    )
    plane0 = exchange(copies, "dp", groups_x).reshape(8, SPLIT, depth)
    swapped = dp_move(ring, 0, 0, 1)
    swapped, held = lax.optimization_barrier((swapped, sent))
    rest = dp_move(held, 0, 1, 0)
    all_grad = [both_grads] + [tensor_move(both_grads, 0, step) for step in (-1, -2, 1)]
    probs, outs = forward(info, query_pos, query_start, queries, ring, swapped)

    t = lax.axis_index("tensor")

    def slot(x_, z_):
        source = 2 * (x_ % 4) + z_
        return (source - t) % 4 * 2 + jnp.where(source // 4 == t // 4, 0, 1)

    near = [slot(x + i, z) for i in (0, -1, 1, 2)]
    slots = [
        jnp.stack([slot(i, z_) for i in range(4) for z_ in (z, 1 - z)]).astype(jnp.int32),
        jnp.stack(near + [slot(x + i, 1 - z) for i in (0, -1, 1, 2)]).astype(jnp.int32),
    ]
    slots[0] = after(slots[0], outs)
    stacks = [[plane0], [sent, rest]]
    terms = []
    for part in range(CHUNKS):
        mine, other = project(part, slots[part], all_grad, stacks[part])
        terms += [mine, dp_move(other, 0, 0, 1)]
    grad_queries, own_sums, other_sums = backward(info, terms, probs, outs, queries, ring, swapped)

    groups = [[2 * i + c for i in range(8)] for c in range(2)]
    chip_sums = (own_sums + dp_move(other_sums, 0, 0, 1).astype(F32)).astype(BF16)
    terms = lax.all_to_all(chip_sums, "dp", 0, 0, axis_index_groups=groups, tiled=True)
    done = jnp.sum(terms.astype(F32), axis=0).astype(BF16)
    return grad_queries, done[:, :HEAD_WIDTH], done[:, HEAD_WIDTH:]


def solution(mesh):
    return jax.shard_map(
        local,
        mesh=mesh,
        in_specs=(
            P("dp", "tensor"),
            P("dp", "tensor"),
            P("dp", "tensor"),
            P("dp", "tensor"),
            P("tensor", "dp"),
            P(),
        ),
        out_specs=(P("dp", "tensor"), P("dp", "tensor"), P("dp", "tensor")),
        check_vma=False,
    )
```

```python
import functools
import math

import jax
import jax.numpy as jnp
from jax import lax
from jax.experimental import pallas as pl
from jax.experimental.pallas import tpu as pltpu
from jax.sharding import PartitionSpec as P

HEAD_WIDTH = 128
KEY_BLOCK = 256
MOST = 2560
SPLIT = 4 * HEAD_WIDTH
PAIR = 2
MASKED = -1e30
SCALE = 1.0 / math.sqrt(HEAD_WIDTH)
LOG2E = 1.0 / math.log(2.0)
BF16 = jnp.bfloat16
F32 = jnp.float32
VMEM_LIMIT = 22 * 2**20

FIRST, COUNT, CLEAR, CORE, TABLE = 0, 1, 2, 3, 4


def dp_move(value, dx, dz, dc):
    pairs = []
    for x in range(4):
        for z in range(2):
            for c in range(2):
                target = ((x + dx) % 4) * 4 + ((z + dz) % 2) * 2 + (c + dc) % 2
                pairs.append((x * 4 + z * 2 + c, target))
    return lax.ppermute(value, "dp", pairs)


def tensor_move(value, dz, dy):
    pairs = []
    for z in range(2):
        for y in range(4):
            pairs.append((z * 4 + y, ((z + dz) % 2) * 4 + (y + dy) % 4))
    return lax.ppermute(value, "tensor", pairs)


def after(value, *others):
    return lax.optimization_barrier((value, *others))[0]


def in_hbm(value):
    return pltpu.with_memory_space_constraint(value, pltpu.HBM)


def dot(left, right):
    return lax.dot_general(left, right, (((1,), (0,)), ((), ())), preferred_element_type=F32)


def dot_t(left, right):
    return lax.dot_general(left, right, (((1,), (1,)), ((), ())), preferred_element_type=F32)


def block_rows(index):
    return pl.ds(pl.multiple_of(index * KEY_BLOCK, KEY_BLOCK), KEY_BLOCK)


def forward_kernel(
    info, pos_ref, start_ref, q_ref, here_ref, there_ref, probs_ref, out_ref, score, keys, vt
):
    first, count = info[FIRST], info[COUNT]
    rows = q_ref.shape[0]
    heads = q_ref.shape[1] // HEAD_WIDTH
    query_t = jnp.concatenate(
        [q_ref[:, h * HEAD_WIDTH : (h + 1) * HEAD_WIDTH].T for h in range(heads)], axis=1
    )
    wide = heads * rows

    def groups(values):
        return values.reshape(KEY_BLOCK // 8, 8, wide)

    @pl.when(pl.program_id(0) == 0)
    def _():
        def turn(index, _):
            here = here_ref[block_rows(info[TABLE + first + index]), :]
            there = there_ref[block_rows(info[TABLE + 16 + first + index]), :]
            keys[block_rows(index), :] = jnp.where(info[CORE] == 0, here, there)
            vt[:, block_rows(index)] = jnp.where(info[CORE] == 0, there, here).T
            return 0
        lax.fori_loop(0, count, turn, 0)

    def product(index):
        return dot(keys[block_rows(index), :], query_t)

    def masked_step(index, top):
        key_pos = (first + index) * KEY_BLOCK + lax.broadcasted_iota(jnp.int32, (KEY_BLOCK, rows), 0)
        live = (key_pos >= start_ref[...]) & (key_pos <= pos_ref[...])
        raw = product(index)
        raw = jnp.concatenate(
            [jnp.where(live, raw[:, h * rows : (h + 1) * rows], MASKED) for h in range(heads)], axis=1
        )
        score[block_rows(index), :] = raw
        return jnp.maximum(top, jnp.max(groups(raw), axis=0))

    def clear_step(index, top):
        raw = product(index)
        score[block_rows(index), :] = raw
        return jnp.maximum(top, jnp.max(groups(raw), axis=0))

    clear = jnp.minimum(info[CLEAR] - first, count - 1)
    top = jnp.full((8, wide), MASKED, F32)
    top = lax.fori_loop(0, clear, masked_step, top)
    top = lax.fori_loop(clear, count - 1, clear_step, top)
    top = masked_step(count - 1, top)
    top = jnp.max(top, axis=0, keepdims=True) * (SCALE * LOG2E)

    def mass_step(index, mass):
        weights = jnp.exp2(score[block_rows(index), :] * (SCALE * LOG2E) - top)
        score[block_rows(index), :] = weights
        return mass + jnp.sum(groups(weights), axis=0)

    mass = lax.fori_loop(0, count, mass_step, jnp.zeros((8, wide), F32))
    share = 1.0 / jnp.sum(mass, axis=0, keepdims=True)
    out_ref[...] = jnp.zeros_like(out_ref)

    def probs_step(index, _):
        probs = (score[block_rows(index), :] * share).astype(BF16)
        probs_ref[block_rows(index), :] = probs
        out_ref[...] += dot(vt[:, block_rows(index)], probs)
        return 0

    lax.fori_loop(0, count, probs_step, 0)


def most_blocks(rows):
    return (MOST + rows - 2) // KEY_BLOCK + 1


def forward(info, query_pos, query_start, queries, here, there):
    rows, width = queries.shape
    heads = width // HEAD_WIDTH
    live = most_blocks(rows) * KEY_BLOCK
    line = pl.BlockSpec((1, rows), lambda h, r: (0, 0))
    return pl.pallas_call(
        forward_kernel,
        grid_spec=pltpu.PrefetchScalarGridSpec(
            num_scalar_prefetch=1,
            grid=(heads // PAIR,),
            in_specs=[
                line,
                line,
                pl.BlockSpec((rows, PAIR * HEAD_WIDTH), lambda h, r: (0, h)),
            ]
            + [pl.BlockSpec(here.shape, lambda h, r: (0, 0), pipeline_mode=pl.Buffered(1))] * 2,
            out_specs=[
                pl.BlockSpec((live, PAIR * rows), lambda h, r: (0, h)),
                pl.BlockSpec((HEAD_WIDTH, PAIR * rows), lambda h, r: (0, h)),
            ],
            scratch_shapes=[
                pltpu.VMEM((live, PAIR * rows), F32),
                pltpu.VMEM((live, HEAD_WIDTH), BF16),
                pltpu.VMEM((HEAD_WIDTH, live), BF16),
            ],
        ),
        out_shape=[
            pltpu.HBM((live, heads * rows), BF16),
            pltpu.HBM((HEAD_WIDTH, heads * rows), F32),
        ],
        compiler_params=pltpu.CompilerParams(vmem_limit_bytes=VMEM_LIMIT),
        cost_estimate=pl.CostEstimate(flops=10**8, bytes_accessed=2**20, transcendentals=0),
        name="forward",
    )(info, query_pos, query_start, in_hbm(queries), here, there)


def backward_kernel(heads, info, *rest):
    (mine, got), rest = rest[:2], rest[2:]
    probs_ref, out_ref, q_ref, here_ref, there_ref, gq_ref, own_ref, other_ref, *scratch = rest
    grad_t, stack, delta, total_q, dscores, other = scratch
    step = pl.program_id(0)
    count = info[COUNT]
    rows = q_ref.shape[0]

    @pl.when(step == 0)
    def _():
        own_ref[...] = jnp.zeros_like(own_ref)
        other[...] = jnp.zeros_like(other)
        total_q[...] = jnp.zeros_like(total_q)
        for h in range(heads):
            cols = slice(h * rows, (h + 1) * rows)
            wide = slice(h * HEAD_WIDTH, (h + 1) * HEAD_WIDTH)
            grad = (mine[:, wide] + got[:, wide].astype(F32)).astype(BF16)
            turned = grad.T
            grad_t[:, cols] = turned
            stack[cols, :HEAD_WIDTH] = q_ref[:, wide]
            stack[cols, HEAD_WIDTH:] = grad
            delta[:, cols] = jnp.sum(turned.astype(F32) * out_ref[:, cols], axis=0, keepdims=True)

    @pl.when(step < count)
    def _():
        block = info[FIRST] + step
        keys_t = jnp.where(info[CORE] == 0, here_ref[...], there_ref[...]).T
        values = jnp.where(info[CORE] == 0, there_ref[...], here_ref[...])
        for h in range(heads):
            cols = slice(h * rows, (h + 1) * rows)
            dprob = dot(values, grad_t[:, cols])
            dscores[:, cols] = (probs_ref[:, cols].astype(F32) * (dprob - delta[:, cols])).astype(BF16)
        total_q[...] += dot(keys_t, dscores[...])
        key_sum = dot(dscores[...], stack[:, :HEAD_WIDTH])
        value_sum = dot(probs_ref[...], stack[:, HEAD_WIDTH:])

        def add(ref):
            ref[block // 2, :, :HEAD_WIDTH] += key_sum * SCALE
            ref[block // 2, :, HEAD_WIDTH:] += value_sum

        pl.when(block % 2 == info[CORE])(lambda: add(own_ref))
        pl.when(block % 2 != info[CORE])(lambda: add(other))

    @pl.when(step == count - 1)
    def _():
        for h in range(heads):
            cols = slice(h * rows, (h + 1) * rows)
            wide = slice(h * HEAD_WIDTH, (h + 1) * HEAD_WIDTH)
            gq_ref[:, wide] = (total_q[:, cols].T * SCALE).astype(BF16)
        other_ref[...] = other[...].astype(BF16)


def backward(info, terms, probs, outs, queries, here, there):
    rows, width = queries.shape
    heads = width // HEAD_WIDTH
    sums = (8, KEY_BLOCK, 2 * HEAD_WIDTH)

    def near(i, r):
        return jnp.minimum(i, r[COUNT] - 1)

    def once(shape):
        return pl.BlockSpec(shape, lambda i, r: (0,) * len(shape), pipeline_mode=pl.Buffered(1))

    return pl.pallas_call(
        functools.partial(backward_kernel, heads),
        grid_spec=pltpu.PrefetchScalarGridSpec(
            num_scalar_prefetch=1,
            grid=(most_blocks(rows),),
            in_specs=[once(term.shape) for term in terms]
            + [
                pl.BlockSpec((KEY_BLOCK, heads * rows), lambda i, r: (near(i, r), 0)),
                once(outs.shape),
                once(queries.shape),
                pl.BlockSpec(
                    (KEY_BLOCK, HEAD_WIDTH), lambda i, r: (r[TABLE + r[FIRST] + near(i, r)], 0)
                ),
                pl.BlockSpec(
                    (KEY_BLOCK, HEAD_WIDTH), lambda i, r: (r[TABLE + 16 + r[FIRST] + near(i, r)], 0)
                ),
            ],
            out_specs=[once((rows, width)), once(sums), once(sums)],
            scratch_shapes=[
                pltpu.VMEM((HEAD_WIDTH, heads * rows), BF16),
                pltpu.VMEM((heads * rows, 2 * HEAD_WIDTH), BF16),
                pltpu.VMEM((1, heads * rows), F32),
                pltpu.VMEM((HEAD_WIDTH, heads * rows), F32),
                pltpu.VMEM((KEY_BLOCK, heads * rows), BF16),
                pltpu.VMEM(sums, F32),
            ],
        ),
        out_shape=[
            jax.ShapeDtypeStruct((rows, width), BF16),
            jax.ShapeDtypeStruct(sums, F32),
            jax.ShapeDtypeStruct(sums, BF16),
        ],
        compiler_params=pltpu.CompilerParams(vmem_limit_bytes=VMEM_LIMIT),
        cost_estimate=pl.CostEstimate(
            flops=8 * 10**9, bytes_accessed=10 * 2**20, transcendentals=0
        ),
        name="backward",
    )(info, *terms, in_hbm(probs), outs, in_hbm(queries), here, there)


def project_kernel(slots, *rest):
    *operands, own_ref, other_ref, grad, weight, total, sems = rest
    chips = grad.shape[0]
    grads, stacks = operands[: chips // 2], operands[chips // 2 :]
    sources = [ref.at[j] for ref in stacks for j in range(ref.shape[0])]
    copies = [
        pltpu.make_async_copy(source, weight.at[k], sems.at[k]) for k, source in enumerate(sources)
    ]
    for copy in copies:
        copy.start()
    for i, ref in enumerate(grads):
        grad[2 * i : 2 * i + 2] = ref[...]
    half = own_ref.shape[0]
    features = weight.shape[1]
    for k, copy in enumerate(copies):
        copy.wait()
        cols = slice(k // chips * features, (k // chips + 1) * features)
        for out, row in ((own_ref, 0), (total, half)):
            term = dot_t(grad[slots[k], row : row + half, :], weight[k])
            if k % chips == 0:
                out[:, cols] = term
            else:
                out[:, cols] += term
    other_ref[...] = total[...].astype(BF16)


def project(slots, grads, stacks):
    chips = 2 * len(grads)
    _, tokens, depth = grads[0].shape
    blocks = sum(stack.shape[0] for stack in stacks)
    features = stacks[0].shape[1]
    shape = (tokens // 2, blocks // chips * features)

    def once(shape):
        return pl.BlockSpec(shape, lambda i: (0,) * len(shape), pipeline_mode=pl.Buffered(1))

    return pl.pallas_call(
        project_kernel,
        grid=(1,),
        in_specs=[pl.BlockSpec(memory_space=pltpu.SMEM)]
        + [once(ref.shape) for ref in grads]
        + [pl.BlockSpec(memory_space=pl.ANY)] * len(stacks),
        out_specs=[once(shape)] * 2,
        out_shape=[jax.ShapeDtypeStruct(shape, F32), jax.ShapeDtypeStruct(shape, BF16)],
        scratch_shapes=[
            pltpu.VMEM((chips, tokens, depth), BF16),
            pltpu.VMEM((blocks, features, depth), BF16),
            pltpu.VMEM(shape, F32),
            pltpu.SemaphoreType.DMA((blocks,)),
        ],
        compiler_params=pltpu.CompilerParams(vmem_limit_bytes=VMEM_LIMIT),
        cost_estimate=pl.CostEstimate(
            flops=2 * tokens * features * depth * blocks,
            bytes_accessed=12 * 2**20,
            transcendentals=0,
        ),
        name="project",
    )(slots, *grads, *[in_hbm(stack) for stack in stacks])


def local(queries, keys, values, grad_out, out_weight, lengths):
    rows = queries.shape[0]
    rank = lax.axis_index("dp")
    core = rank % 2
    x, z = rank // 4, (rank // 2) % 2

    def copy(block, groups):
        return jnp.broadcast_to(block, (len(groups[0]), *block.shape))

    def exchange(copies, axis, groups):
        return lax.all_to_all(copies, axis, 0, 0, axis_index_groups=groups, tiled=True)

    groups_x = [[x_ * 4 + zc for x_ in range(4)] for zc in range(4)]
    kept = jnp.where(core == 0, keys, values)
    got = dp_move(jnp.where(core == 0, values, keys), 0, 0, 1)
    chip = jnp.concatenate([kept, got], axis=0)
    chip_pair = jnp.concatenate([chip, dp_move(chip, 0, 1, 0)], axis=0)

    depth = out_weight.shape[1]
    mine = lax.dynamic_slice_in_dim(grad_out, core * depth, depth, 1)
    other = lax.dynamic_slice_in_dim(grad_out, (1 - core) * depth, depth, 1)
    chip_grad = jnp.concatenate([mine, dp_move(other, 0, 0, 1)], axis=0)
    copies, chip_grad = lax.optimization_barrier((copy(chip_pair, groups_x), chip_grad))
    ring = exchange(copies, "dp", groups_x).reshape(-1, HEAD_WIDTH)
    lengths = after(lengths, copies)

    query_pos = rank * rows + jnp.arange(rows, dtype=jnp.int32)
    ends = jnp.cumsum(lengths)[:-1]
    query_start = jnp.max(
        jnp.where(ends[None, :] <= query_pos[:, None], ends[None, :], 0), axis=1
    )
    first = query_start[0] // KEY_BLOCK
    last = query_pos[-1] // KEY_BLOCK
    clear = (query_start[-1] + KEY_BLOCK - 1) // KEY_BLOCK
    block = jnp.arange(16, dtype=jnp.int32)
    place = block // 4 * 4 + jnp.where(block // 2 % 2 == z, 0, 2)
    here = place + jnp.where(block % 2 == core, 0, 1)
    there = place + jnp.where(block % 2 == core, 1, 0)
    scalars = jnp.stack([first, last - first + 1, clear, core])
    info = jnp.concatenate([scalars, here, there]).astype(jnp.int32)
    query_pos, query_start = query_pos[None, :], query_start[None, :]


    def around_x(block):
        return [dp_move(block, step, 0, 0) for step in (1, -1, 2)]

    own = [out_weight[:SPLIT], out_weight[SPLIT:]]
    plane1 = around_x(own[1])
    own0 = after(own[0], chip_pair)
    pair0 = dp_move(own0, 0, 1, 0)
    grad_pair = tensor_move(chip_grad, 1, 0)
    copies = copy(jnp.stack([own0, pair0]), groups_x)
    both_grads = jnp.stack([chip_grad, grad_pair])
    sent = jnp.stack([own[1], *plane1])
    ring, copies, both_grads, sent, info, query_pos, query_start = lax.optimization_barrier(
        (ring, copies, both_grads, sent, info, query_pos, query_start)
    )
    plane0 = exchange(copies, "dp", groups_x).reshape(8, SPLIT, depth)
    swapped = dp_move(ring, 0, 0, 1)
    swapped, held = lax.optimization_barrier((swapped, sent))
    rest = dp_move(held, 0, 1, 0)
    all_grad = [both_grads] + [tensor_move(both_grads, 0, step) for step in (-1, -2, 1)]
    probs, outs = forward(info, query_pos, query_start, queries, ring, swapped)

    t = lax.axis_index("tensor")

    def slot(x_, z_):
        source = 2 * (x_ % 4) + z_
        return (source - t) % 4 * 2 + jnp.where(source // 4 == t // 4, 0, 1)

    near = [slot(x + i, z) for i in (0, -1, 1, 2)]
    slots = [slot(i, z_) for i in range(4) for z_ in (z, 1 - z)]
    slots += near + [slot(x + i, 1 - z) for i in (0, -1, 1, 2)]
    slots = after(jnp.stack(slots).astype(jnp.int32), outs)
    mine, other = project(slots, all_grad, [plane0, sent, rest])
    terms = [mine, dp_move(other, 0, 0, 1)]
    grad_queries, own_sums, other_sums = backward(info, terms, probs, outs, queries, ring, swapped)

    groups = [[2 * i + c for i in range(8)] for c in range(2)]
    chip_sums = (own_sums + dp_move(other_sums, 0, 0, 1).astype(F32)).astype(BF16)
    terms = lax.all_to_all(chip_sums, "dp", 0, 0, axis_index_groups=groups, tiled=True)
    done = jnp.sum(terms.astype(F32), axis=0).astype(BF16)
    return grad_queries, done[:, :HEAD_WIDTH], done[:, HEAD_WIDTH:]


def solution(mesh):
    return jax.shard_map(
        local,
        mesh=mesh,
        in_specs=(
            P("dp", "tensor"),
            P("dp", "tensor"),
            P("dp", "tensor"),
            P("dp", "tensor"),
            P("tensor", "dp"),
            P(),
        ),
        out_specs=(P("dp", "tensor"), P("dp", "tensor"), P("dp", "tensor")),
        check_vma=False,
    )
```

```python
import functools
import math

import jax
import jax.numpy as jnp
from jax import lax
from jax.experimental import pallas as pl
from jax.experimental.pallas import tpu as pltpu
from jax.sharding import PartitionSpec as P

HEAD_WIDTH = 128
KEY_BLOCK = 256
MOST = 2560
SPLIT = 4 * HEAD_WIDTH
PAIR = 2
MASKED = -1e30
SCALE = 1.0 / math.sqrt(HEAD_WIDTH)
LOG2E = 1.0 / math.log(2.0)
BF16 = jnp.bfloat16
F32 = jnp.float32
VMEM_LIMIT = 22 * 2**20

FIRST, COUNT, CLEAR, CORE, TABLE = 0, 1, 2, 3, 4


def dp_move(value, dx, dz, dc):
    pairs = []
    for x in range(4):
        for z in range(2):
            for c in range(2):
                target = ((x + dx) % 4) * 4 + ((z + dz) % 2) * 2 + (c + dc) % 2
                pairs.append((x * 4 + z * 2 + c, target))
    return lax.ppermute(value, "dp", pairs)


def tensor_move(value, dz, dy):
    pairs = []
    for z in range(2):
        for y in range(4):
            pairs.append((z * 4 + y, ((z + dz) % 2) * 4 + (y + dy) % 4))
    return lax.ppermute(value, "tensor", pairs)


def after(value, *others):
    return lax.optimization_barrier((value, *others))[0]


def in_hbm(value):
    return pltpu.with_memory_space_constraint(value, pltpu.HBM)


def dot(left, right):
    return lax.dot_general(left, right, (((1,), (0,)), ((), ())), preferred_element_type=F32)


def dot_t(left, right):
    return lax.dot_general(left, right, (((1,), (1,)), ((), ())), preferred_element_type=F32)


def block_rows(index):
    return pl.ds(pl.multiple_of(index * KEY_BLOCK, KEY_BLOCK), KEY_BLOCK)


def forward_kernel(
    info, pos_ref, start_ref, q_ref, here_ref, there_ref, probs_ref, out_ref, score, keys, vt
):
    first, count = info[FIRST], info[COUNT]
    rows = q_ref.shape[0]
    heads = q_ref.shape[1] // HEAD_WIDTH
    query_t = jnp.concatenate(
        [q_ref[:, h * HEAD_WIDTH : (h + 1) * HEAD_WIDTH].T for h in range(heads)], axis=1
    )
    wide = heads * rows

    def groups(values):
        return values.reshape(KEY_BLOCK // 8, 8, wide)

    @pl.when(pl.program_id(0) == 0)
    def _():
        def turn(index, _):
            here = here_ref[block_rows(info[TABLE + first + index]), :]
            there = there_ref[block_rows(info[TABLE + 16 + first + index]), :]
            keys[block_rows(index), :] = jnp.where(info[CORE] == 0, here, there)
            vt[:, block_rows(index)] = jnp.where(info[CORE] == 0, there, here).T
            return 0
        lax.fori_loop(0, count, turn, 0)

    def product(index):
        return dot(keys[block_rows(index), :], query_t)

    def masked_step(index, top):
        key_pos = (first + index) * KEY_BLOCK + lax.broadcasted_iota(jnp.int32, (KEY_BLOCK, rows), 0)
        live = (key_pos >= start_ref[...]) & (key_pos <= pos_ref[...])
        raw = product(index)
        raw = jnp.concatenate(
            [jnp.where(live, raw[:, h * rows : (h + 1) * rows], MASKED) for h in range(heads)], axis=1
        )
        score[block_rows(index), :] = raw
        return jnp.maximum(top, jnp.max(groups(raw), axis=0))

    def clear_step(index, top):
        raw = product(index)
        score[block_rows(index), :] = raw
        return jnp.maximum(top, jnp.max(groups(raw), axis=0))

    clear = jnp.minimum(info[CLEAR] - first, count - 1)
    top = jnp.full((8, wide), MASKED, F32)
    top = lax.fori_loop(0, clear, masked_step, top)
    top = lax.fori_loop(clear, count - 1, clear_step, top)
    top = masked_step(count - 1, top)
    top = jnp.max(top, axis=0, keepdims=True) * (SCALE * LOG2E)

    def mass_step(index, mass):
        weights = jnp.exp2(score[block_rows(index), :] * (SCALE * LOG2E) - top)
        score[block_rows(index), :] = weights
        return mass + jnp.sum(groups(weights), axis=0)

    mass = lax.fori_loop(0, count, mass_step, jnp.zeros((8, wide), F32))
    share = 1.0 / jnp.sum(mass, axis=0, keepdims=True)
    out_ref[...] = jnp.zeros_like(out_ref)

    def probs_step(index, _):
        probs = (score[block_rows(index), :] * share).astype(BF16)
        probs_ref[block_rows(index), :] = probs
        out_ref[...] += dot(vt[:, block_rows(index)], probs)
        return 0

    lax.fori_loop(0, count, probs_step, 0)


def most_blocks(rows):
    return (MOST + rows - 2) // KEY_BLOCK + 1


def forward(info, query_pos, query_start, queries, here, there):
    rows, width = queries.shape
    heads = width // HEAD_WIDTH
    live = most_blocks(rows) * KEY_BLOCK
    line = pl.BlockSpec((1, rows), lambda h, r: (0, 0))
    return pl.pallas_call(
        forward_kernel,
        grid_spec=pltpu.PrefetchScalarGridSpec(
            num_scalar_prefetch=1,
            grid=(heads // PAIR,),
            in_specs=[
                line,
                line,
                pl.BlockSpec((rows, PAIR * HEAD_WIDTH), lambda h, r: (0, h)),
            ]
            + [pl.BlockSpec(here.shape, lambda h, r: (0, 0), pipeline_mode=pl.Buffered(1))] * 2,
            out_specs=[
                pl.BlockSpec((live, PAIR * rows), lambda h, r: (0, h)),
                pl.BlockSpec((HEAD_WIDTH, PAIR * rows), lambda h, r: (0, h)),
            ],
            scratch_shapes=[
                pltpu.VMEM((live, PAIR * rows), F32),
                pltpu.VMEM((live, HEAD_WIDTH), BF16),
                pltpu.VMEM((HEAD_WIDTH, live), BF16),
            ],
        ),
        out_shape=[
            pltpu.HBM((live, heads * rows), BF16),
            pltpu.HBM((HEAD_WIDTH, heads * rows), F32),
        ],
        compiler_params=pltpu.CompilerParams(vmem_limit_bytes=VMEM_LIMIT),
        cost_estimate=pl.CostEstimate(flops=10**8, bytes_accessed=2**20, transcendentals=0),
        name="forward",
    )(info, query_pos, query_start, in_hbm(queries), here, there)


def backward_kernel(heads, info, *rest):
    (mine, got), rest = rest[:2], rest[2:]
    probs_ref, out_ref, q_ref, here_ref, there_ref, gq_ref, own_ref, other_ref, *scratch = rest
    grad_t, stack, delta, total_q, dscores, other = scratch
    step = pl.program_id(0)
    count = info[COUNT]
    rows = q_ref.shape[0]

    @pl.when(step == 0)
    def _():
        own_ref[...] = jnp.zeros_like(own_ref)
        other[...] = jnp.zeros_like(other)
        total_q[...] = jnp.zeros_like(total_q)
        for h in range(heads):
            cols = slice(h * rows, (h + 1) * rows)
            wide = slice(h * HEAD_WIDTH, (h + 1) * HEAD_WIDTH)
            grad = (mine[:, wide] + got[:, wide].astype(F32)).astype(BF16)
            turned = grad.T
            grad_t[:, cols] = turned
            stack[cols, :HEAD_WIDTH] = q_ref[:, wide]
            stack[cols, HEAD_WIDTH:] = grad
            delta[:, cols] = jnp.sum(turned.astype(F32) * out_ref[:, cols], axis=0, keepdims=True)

    @pl.when(step < count)
    def _():
        block = info[FIRST] + step
        keys_t = jnp.where(info[CORE] == 0, here_ref[...], there_ref[...]).T
        values = jnp.where(info[CORE] == 0, there_ref[...], here_ref[...])
        for h in range(heads):
            cols = slice(h * rows, (h + 1) * rows)
            dprob = dot(values, grad_t[:, cols])
            dscores[:, cols] = (probs_ref[:, cols].astype(F32) * (dprob - delta[:, cols])).astype(BF16)
        total_q[...] += dot(keys_t, dscores[...])
        key_sum = dot(dscores[...], stack[:, :HEAD_WIDTH])
        value_sum = dot(probs_ref[...], stack[:, HEAD_WIDTH:])

        def add(ref):
            ref[block // 2, :, :HEAD_WIDTH] += key_sum * SCALE
            ref[block // 2, :, HEAD_WIDTH:] += value_sum

        pl.when(block % 2 == info[CORE])(lambda: add(own_ref))
        pl.when(block % 2 != info[CORE])(lambda: add(other))

    @pl.when(step == count - 1)
    def _():
        for h in range(heads):
            cols = slice(h * rows, (h + 1) * rows)
            wide = slice(h * HEAD_WIDTH, (h + 1) * HEAD_WIDTH)
            gq_ref[:, wide] = (total_q[:, cols].T * SCALE).astype(BF16)
        other_ref[...] = other[...].astype(BF16)


def backward(info, terms, probs, outs, queries, here, there):
    rows, width = queries.shape
    heads = width // HEAD_WIDTH
    sums = (8, KEY_BLOCK, 2 * HEAD_WIDTH)

    def near(i, r):
        return jnp.minimum(i, r[COUNT] - 1)

    def once(shape):
        return pl.BlockSpec(shape, lambda i, r: (0,) * len(shape), pipeline_mode=pl.Buffered(1))

    return pl.pallas_call(
        functools.partial(backward_kernel, heads),
        grid_spec=pltpu.PrefetchScalarGridSpec(
            num_scalar_prefetch=1,
            grid=(most_blocks(rows),),
            in_specs=[once(term.shape) for term in terms]
            + [
                pl.BlockSpec((KEY_BLOCK, heads * rows), lambda i, r: (near(i, r), 0)),
                once(outs.shape),
                once(queries.shape),
                pl.BlockSpec(
                    (KEY_BLOCK, HEAD_WIDTH), lambda i, r: (r[TABLE + r[FIRST] + near(i, r)], 0)
                ),
                pl.BlockSpec(
                    (KEY_BLOCK, HEAD_WIDTH), lambda i, r: (r[TABLE + 16 + r[FIRST] + near(i, r)], 0)
                ),
            ],
            out_specs=[once((rows, width)), once(sums), once(sums)],
            scratch_shapes=[
                pltpu.VMEM((HEAD_WIDTH, heads * rows), BF16),
                pltpu.VMEM((heads * rows, 2 * HEAD_WIDTH), BF16),
                pltpu.VMEM((1, heads * rows), F32),
                pltpu.VMEM((HEAD_WIDTH, heads * rows), F32),
                pltpu.VMEM((KEY_BLOCK, heads * rows), BF16),
                pltpu.VMEM(sums, F32),
            ],
        ),
        out_shape=[
            jax.ShapeDtypeStruct((rows, width), BF16),
            jax.ShapeDtypeStruct(sums, F32),
            jax.ShapeDtypeStruct(sums, BF16),
        ],
        compiler_params=pltpu.CompilerParams(vmem_limit_bytes=VMEM_LIMIT),
        cost_estimate=pl.CostEstimate(
            flops=8 * 10**9, bytes_accessed=10 * 2**20, transcendentals=0
        ),
        name="backward",
    )(info, *terms, in_hbm(probs), outs, in_hbm(queries), here, there)


def project_kernel(slots, *rest):
    *operands, own_ref, other_ref, grad, weight, sems = rest
    parts, features, width = weight.shape
    count = sems.shape[0]
    pairs = [ref for ref in operands if ref.shape[0] == 2]
    stacks = [ref for ref in operands if ref.shape[0] > 2]
    depth = pairs[0].shape[2]
    chips = width // depth
    sources = [ref.at[j] for ref in stacks for j in range(ref.shape[0])]
    copies = []
    for k in range(count):
        place = pl.ds(pl.multiple_of(slots[k] * depth, depth), depth)
        copies.append(
            pltpu.make_async_copy(sources[k], weight.at[k // chips, :, place], sems.at[k])
        )
    for copy in copies:
        copy.start()
    for i, ref in enumerate(pairs):
        for j in range(2):
            at = (2 * i + j) * depth
            grad[:, at : at + depth] = ref[j]
    half = own_ref.shape[0]
    for part in range(parts):
        for copy in copies[part * chips : (part + 1) * chips]:
            copy.wait()
        cols = slice(part * features, (part + 1) * features)
        own_ref[:, cols] = dot_t(grad[:half, :], weight[part])
        other_ref[:, cols] = dot_t(grad[half:, :], weight[part]).astype(BF16)


def project(slots, grads, stacks):
    chips = 2 * len(grads)
    _, tokens, depth = grads[0].shape
    blocks = sum(stack.shape[0] for stack in stacks)
    features = stacks[0].shape[1]
    shape = (tokens // 2, blocks // chips * features)

    def once(shape):
        return pl.BlockSpec(shape, lambda i: (0,) * len(shape), pipeline_mode=pl.Buffered(1))

    return pl.pallas_call(
        project_kernel,
        grid=(1,),
        in_specs=[pl.BlockSpec(memory_space=pltpu.SMEM)]
        + [once(ref.shape) for ref in grads]
        + [pl.BlockSpec(memory_space=pl.ANY)] * len(stacks),
        out_specs=[once(shape)] * 2,
        out_shape=[jax.ShapeDtypeStruct(shape, F32), jax.ShapeDtypeStruct(shape, BF16)],
        scratch_shapes=[
            pltpu.VMEM((tokens, chips * depth), BF16),
            pltpu.VMEM((blocks // chips, features, chips * depth), BF16),
            pltpu.SemaphoreType.DMA((blocks,)),
        ],
        compiler_params=pltpu.CompilerParams(vmem_limit_bytes=VMEM_LIMIT),
        cost_estimate=pl.CostEstimate(
            flops=2 * tokens * features * depth * blocks,
            bytes_accessed=12 * 2**20,
            transcendentals=0,
        ),
        name="project",
    )(slots, *grads, *[in_hbm(stack) for stack in stacks])


def local(queries, keys, values, grad_out, out_weight, lengths):
    rows = queries.shape[0]
    rank = lax.axis_index("dp")
    core = rank % 2
    x, z = rank // 4, (rank // 2) % 2

    def copy(block, groups):
        return jnp.broadcast_to(block, (len(groups[0]), *block.shape))

    def exchange(copies, axis, groups):
        return lax.all_to_all(copies, axis, 0, 0, axis_index_groups=groups, tiled=True)

    groups_x = [[x_ * 4 + zc for x_ in range(4)] for zc in range(4)]
    kept = jnp.where(core == 0, keys, values)
    got = dp_move(jnp.where(core == 0, values, keys), 0, 0, 1)
    chip = jnp.concatenate([kept, got], axis=0)
    chip_pair = jnp.concatenate([chip, dp_move(chip, 0, 1, 0)], axis=0)

    depth = out_weight.shape[1]
    mine = lax.dynamic_slice_in_dim(grad_out, core * depth, depth, 1)
    other = lax.dynamic_slice_in_dim(grad_out, (1 - core) * depth, depth, 1)
    chip_grad = jnp.concatenate([mine, dp_move(other, 0, 0, 1)], axis=0)
    copies, chip_grad = lax.optimization_barrier((copy(chip_pair, groups_x), chip_grad))
    ring = exchange(copies, "dp", groups_x).reshape(-1, HEAD_WIDTH)
    lengths = after(lengths, copies)

    query_pos = rank * rows + jnp.arange(rows, dtype=jnp.int32)
    ends = jnp.cumsum(lengths)[:-1]
    query_start = jnp.max(
        jnp.where(ends[None, :] <= query_pos[:, None], ends[None, :], 0), axis=1
    )
    first = query_start[0] // KEY_BLOCK
    last = query_pos[-1] // KEY_BLOCK
    clear = (query_start[-1] + KEY_BLOCK - 1) // KEY_BLOCK
    block = jnp.arange(16, dtype=jnp.int32)
    place = block // 4 * 4 + jnp.where(block // 2 % 2 == z, 0, 2)
    here = place + jnp.where(block % 2 == core, 0, 1)
    there = place + jnp.where(block % 2 == core, 1, 0)
    scalars = jnp.stack([first, last - first + 1, clear, core])
    info = jnp.concatenate([scalars, here, there]).astype(jnp.int32)
    query_pos, query_start = query_pos[None, :], query_start[None, :]


    def around_x(block):
        return [dp_move(block, step, 0, 0) for step in (1, -1, 2)]

    own = [out_weight[:SPLIT], out_weight[SPLIT:]]
    plane1 = around_x(own[1])
    own0 = after(own[0], chip_pair)
    pair0 = dp_move(own0, 0, 1, 0)
    grad_pair = tensor_move(chip_grad, 1, 0)
    copies = copy(jnp.stack([own0, pair0]), groups_x)
    both_grads = jnp.stack([chip_grad, grad_pair])
    sent = jnp.stack([own[1], *plane1])
    ring, copies, both_grads, sent, info, query_pos, query_start = lax.optimization_barrier(
        (ring, copies, both_grads, sent, info, query_pos, query_start)
    )
    plane0 = exchange(copies, "dp", groups_x).reshape(8, SPLIT, depth)
    swapped = dp_move(ring, 0, 0, 1)
    swapped, held = lax.optimization_barrier((swapped, sent))
    rest = dp_move(held, 0, 1, 0)
    all_grad = [both_grads] + [tensor_move(both_grads, 0, step) for step in (-1, -2, 1)]
    probs, outs = forward(info, query_pos, query_start, queries, ring, swapped)

    t = lax.axis_index("tensor")

    def slot(x_, z_):
        source = 2 * (x_ % 4) + z_
        return (source - t) % 4 * 2 + jnp.where(source // 4 == t // 4, 0, 1)

    near = [slot(x + i, z) for i in (0, -1, 1, 2)]
    slots = [slot(i, z_) for i in range(4) for z_ in (z, 1 - z)]
    slots += near + [slot(x + i, 1 - z) for i in (0, -1, 1, 2)]
    slots = after(jnp.stack(slots).astype(jnp.int32), outs)
    mine, other = project(slots, all_grad, [plane0, sent, rest])
    terms = [mine, dp_move(other, 0, 0, 1)]
    grad_queries, own_sums, other_sums = backward(info, terms, probs, outs, queries, ring, swapped)

    groups = [[2 * i + c for i in range(8)] for c in range(2)]
    chip_sums = (own_sums + dp_move(other_sums, 0, 0, 1).astype(F32)).astype(BF16)
    terms = lax.all_to_all(chip_sums, "dp", 0, 0, axis_index_groups=groups, tiled=True)
    done = jnp.sum(terms.astype(F32), axis=0).astype(BF16)
    return grad_queries, done[:, :HEAD_WIDTH], done[:, HEAD_WIDTH:]


def solution(mesh):
    return jax.shard_map(
        local,
        mesh=mesh,
        in_specs=(
            P("dp", "tensor"),
            P("dp", "tensor"),
            P("dp", "tensor"),
            P("dp", "tensor"),
            P("tensor", "dp"),
            P(),
        ),
        out_specs=(P("dp", "tensor"), P("dp", "tensor"), P("dp", "tensor")),
        check_vma=False,
    )
```

```python
import functools
import math

import jax
import jax.numpy as jnp
from jax import lax
from jax.experimental import pallas as pl
from jax.experimental.pallas import tpu as pltpu
from jax.sharding import PartitionSpec as P

HEAD_WIDTH = 128
KEY_BLOCK = 256
MOST = 2560
SPLIT = 4 * HEAD_WIDTH
PAIR = 2
MASKED = -1e30
SCALE = 1.0 / math.sqrt(HEAD_WIDTH)
LOG2E = 1.0 / math.log(2.0)
BF16 = jnp.bfloat16
F32 = jnp.float32
VMEM_LIMIT = 22 * 2**20

FIRST, COUNT, CLEAR, CORE, TABLE = 0, 1, 2, 3, 4


def dp_move(value, dx, dz, dc):
    pairs = []
    for x in range(4):
        for z in range(2):
            for c in range(2):
                target = ((x + dx) % 4) * 4 + ((z + dz) % 2) * 2 + (c + dc) % 2
                pairs.append((x * 4 + z * 2 + c, target))
    return lax.ppermute(value, "dp", pairs)


def tensor_move(value, dz, dy):
    pairs = []
    for z in range(2):
        for y in range(4):
            pairs.append((z * 4 + y, ((z + dz) % 2) * 4 + (y + dy) % 4))
    return lax.ppermute(value, "tensor", pairs)


def after(value, *others):
    return lax.optimization_barrier((value, *others))[0]


def in_hbm(value):
    return pltpu.with_memory_space_constraint(value, pltpu.HBM)


def dot(left, right):
    return lax.dot_general(left, right, (((1,), (0,)), ((), ())), preferred_element_type=F32)


def dot_t(left, right):
    return lax.dot_general(left, right, (((1,), (1,)), ((), ())), preferred_element_type=F32)


def block_rows(index):
    return pl.ds(pl.multiple_of(index * KEY_BLOCK, KEY_BLOCK), KEY_BLOCK)


def forward_kernel(
    info, pos_ref, start_ref, q_ref, here_ref, there_ref, probs_ref, out_ref, score, keys, vt
):
    first, count = info[FIRST], info[COUNT]
    rows = q_ref.shape[0]
    heads = q_ref.shape[1] // HEAD_WIDTH
    query_t = jnp.concatenate(
        [q_ref[:, h * HEAD_WIDTH : (h + 1) * HEAD_WIDTH].T for h in range(heads)], axis=1
    )
    wide = heads * rows

    def groups(values):
        return values.reshape(KEY_BLOCK // 8, 8, wide)

    @pl.when(pl.program_id(0) == 0)
    def _():
        def turn(index, _):
            here = here_ref[block_rows(info[TABLE + first + index]), :]
            there = there_ref[block_rows(info[TABLE + 16 + first + index]), :]
            keys[block_rows(index), :] = jnp.where(info[CORE] == 0, here, there)
            vt[:, block_rows(index)] = jnp.where(info[CORE] == 0, there, here).T
            return 0
        lax.fori_loop(0, count, turn, 0)

    def product(index):
        return dot(keys[block_rows(index), :], query_t)

    def masked_step(index, top):
        key_pos = (first + index) * KEY_BLOCK + lax.broadcasted_iota(jnp.int32, (KEY_BLOCK, rows), 0)
        live = (key_pos >= start_ref[...]) & (key_pos <= pos_ref[...])
        raw = product(index)
        raw = jnp.concatenate(
            [jnp.where(live, raw[:, h * rows : (h + 1) * rows], MASKED) for h in range(heads)], axis=1
        )
        score[block_rows(index), :] = raw
        return jnp.maximum(top, jnp.max(groups(raw), axis=0))

    def clear_step(index, top):
        raw = product(index)
        score[block_rows(index), :] = raw
        return jnp.maximum(top, jnp.max(groups(raw), axis=0))

    clear = jnp.minimum(info[CLEAR] - first, count - 1)
    top = jnp.full((8, wide), MASKED, F32)
    top = lax.fori_loop(0, clear, masked_step, top)
    top = lax.fori_loop(clear, count - 1, clear_step, top)
    top = masked_step(count - 1, top)
    top = jnp.max(top, axis=0, keepdims=True) * (SCALE * LOG2E)

    def mass_step(index, mass):
        weights = jnp.exp2(score[block_rows(index), :] * (SCALE * LOG2E) - top)
        score[block_rows(index), :] = weights
        return mass + jnp.sum(groups(weights), axis=0)

    mass = lax.fori_loop(0, count, mass_step, jnp.zeros((8, wide), F32))
    share = 1.0 / jnp.sum(mass, axis=0, keepdims=True)
    out_ref[...] = jnp.zeros_like(out_ref)

    def probs_step(index, _):
        probs = (score[block_rows(index), :] * share).astype(BF16)
        probs_ref[block_rows(index), :] = probs
        out_ref[...] += dot(vt[:, block_rows(index)], probs)
        return 0

    lax.fori_loop(0, count, probs_step, 0)


def most_blocks(rows):
    return (MOST + rows - 2) // KEY_BLOCK + 1


def forward(info, query_pos, query_start, queries, here, there):
    rows, width = queries.shape
    heads = width // HEAD_WIDTH
    live = most_blocks(rows) * KEY_BLOCK
    line = pl.BlockSpec((1, rows), lambda h, r: (0, 0))
    return pl.pallas_call(
        forward_kernel,
        grid_spec=pltpu.PrefetchScalarGridSpec(
            num_scalar_prefetch=1,
            grid=(heads // PAIR,),
            in_specs=[
                line,
                line,
                pl.BlockSpec((rows, PAIR * HEAD_WIDTH), lambda h, r: (0, h)),
            ]
            + [pl.BlockSpec(here.shape, lambda h, r: (0, 0), pipeline_mode=pl.Buffered(1))] * 2,
            out_specs=[
                pl.BlockSpec((live, PAIR * rows), lambda h, r: (0, h)),
                pl.BlockSpec((HEAD_WIDTH, PAIR * rows), lambda h, r: (0, h)),
            ],
            scratch_shapes=[
                pltpu.VMEM((live, PAIR * rows), F32),
                pltpu.VMEM((live, HEAD_WIDTH), BF16),
                pltpu.VMEM((HEAD_WIDTH, live), BF16),
            ],
        ),
        out_shape=[
            pltpu.HBM((live, heads * rows), BF16),
            pltpu.HBM((HEAD_WIDTH, heads * rows), F32),
        ],
        compiler_params=pltpu.CompilerParams(vmem_limit_bytes=VMEM_LIMIT),
        cost_estimate=pl.CostEstimate(flops=10**8, bytes_accessed=2**20, transcendentals=0),
        name="forward",
    )(info, query_pos, query_start, in_hbm(queries), here, there)


def backward_kernel(heads, info, *rest):
    (mine, got), rest = rest[:2], rest[2:]
    probs_ref, out_ref, q_ref, here_ref, there_ref, gq_ref, own_ref, other_ref, *scratch = rest
    grad_t, stack, delta, total_q, dscores, other = scratch
    step = pl.program_id(0)
    count = info[COUNT]
    rows = q_ref.shape[0]

    @pl.when(step == 0)
    def _():
        own_ref[...] = jnp.zeros_like(own_ref)
        other[...] = jnp.zeros_like(other)
        total_q[...] = jnp.zeros_like(total_q)
        for h in range(heads):
            cols = slice(h * rows, (h + 1) * rows)
            wide = slice(h * HEAD_WIDTH, (h + 1) * HEAD_WIDTH)
            grad = (mine[:, wide] + got[:, wide].astype(F32)).astype(BF16)
            turned = grad.T
            grad_t[:, cols] = turned
            stack[cols, :HEAD_WIDTH] = q_ref[:, wide]
            stack[cols, HEAD_WIDTH:] = grad
            delta[:, cols] = jnp.sum(turned.astype(F32) * out_ref[:, cols], axis=0, keepdims=True)

    @pl.when(step < count)
    def _():
        block = info[FIRST] + step
        keys_t = jnp.where(info[CORE] == 0, here_ref[...], there_ref[...]).T
        values = jnp.where(info[CORE] == 0, there_ref[...], here_ref[...])
        for h in range(heads):
            cols = slice(h * rows, (h + 1) * rows)
            dprob = dot(values, grad_t[:, cols])
            dscores[:, cols] = (probs_ref[:, cols].astype(F32) * (dprob - delta[:, cols])).astype(BF16)
        total_q[...] += dot(keys_t, dscores[...])
        key_sum = dot(dscores[...], stack[:, :HEAD_WIDTH])
        value_sum = dot(probs_ref[...], stack[:, HEAD_WIDTH:])

        def add(ref):
            ref[block // 2, :, :HEAD_WIDTH] += key_sum * SCALE
            ref[block // 2, :, HEAD_WIDTH:] += value_sum

        pl.when(block % 2 == info[CORE])(lambda: add(own_ref))
        pl.when(block % 2 != info[CORE])(lambda: add(other))

    @pl.when(step == count - 1)
    def _():
        for h in range(heads):
            cols = slice(h * rows, (h + 1) * rows)
            wide = slice(h * HEAD_WIDTH, (h + 1) * HEAD_WIDTH)
            gq_ref[:, wide] = (total_q[:, cols].T * SCALE).astype(BF16)
        other_ref[...] = other[...].astype(BF16)


def backward(info, terms, probs, outs, queries, here, there):
    rows, width = queries.shape
    heads = width // HEAD_WIDTH
    sums = (8, KEY_BLOCK, 2 * HEAD_WIDTH)

    def near(i, r):
        return jnp.minimum(i, r[COUNT] - 1)

    def once(shape):
        return pl.BlockSpec(shape, lambda i, r: (0,) * len(shape), pipeline_mode=pl.Buffered(1))

    return pl.pallas_call(
        functools.partial(backward_kernel, heads),
        grid_spec=pltpu.PrefetchScalarGridSpec(
            num_scalar_prefetch=1,
            grid=(most_blocks(rows),),
            in_specs=[once(term.shape) for term in terms]
            + [
                pl.BlockSpec((KEY_BLOCK, heads * rows), lambda i, r: (near(i, r), 0)),
                once(outs.shape),
                once(queries.shape),
                pl.BlockSpec(
                    (KEY_BLOCK, HEAD_WIDTH), lambda i, r: (r[TABLE + r[FIRST] + near(i, r)], 0)
                ),
                pl.BlockSpec(
                    (KEY_BLOCK, HEAD_WIDTH), lambda i, r: (r[TABLE + 16 + r[FIRST] + near(i, r)], 0)
                ),
            ],
            out_specs=[once((rows, width)), once(sums), once(sums)],
            scratch_shapes=[
                pltpu.VMEM((HEAD_WIDTH, heads * rows), BF16),
                pltpu.VMEM((heads * rows, 2 * HEAD_WIDTH), BF16),
                pltpu.VMEM((1, heads * rows), F32),
                pltpu.VMEM((HEAD_WIDTH, heads * rows), F32),
                pltpu.VMEM((KEY_BLOCK, heads * rows), BF16),
                pltpu.VMEM(sums, F32),
            ],
        ),
        out_shape=[
            jax.ShapeDtypeStruct((rows, width), BF16),
            jax.ShapeDtypeStruct(sums, F32),
            jax.ShapeDtypeStruct(sums, BF16),
        ],
        compiler_params=pltpu.CompilerParams(vmem_limit_bytes=VMEM_LIMIT),
        cost_estimate=pl.CostEstimate(
            flops=8 * 10**9, bytes_accessed=10 * 2**20, transcendentals=0
        ),
        name="backward",
    )(info, *terms, in_hbm(probs), outs, in_hbm(queries), here, there)


def project_kernel(slots, *rest):
    *operands, own_ref, other_ref, grad, weight, row_sems, sems = rest
    parts, features, width = weight.shape
    count = sems.shape[0]
    pairs = [ref for ref in operands if ref.shape[0] == 2]
    stacks = [ref for ref in operands if ref.shape[0] > 2]
    depth = pairs[0].shape[2]
    chips = width // depth
    sources = [ref.at[j] for ref in stacks for j in range(ref.shape[0])]
    rows = []
    for i in range(chips):
        place = pl.ds(i * depth, depth)
        rows.append(
            pltpu.make_async_copy(pairs[i // 2].at[i % 2], grad.at[:, place], row_sems.at[i])
        )
    copies = []
    for k in range(count):
        place = pl.ds(pl.multiple_of(slots[k] * depth, depth), depth)
        copies.append(
            pltpu.make_async_copy(sources[k], weight.at[k // chips, :, place], sems.at[k])
        )
    for copy in rows + copies:
        copy.start()
    for copy in rows:
        copy.wait()
    half = own_ref.shape[0]
    for part in range(parts):
        for copy in copies[part * chips : (part + 1) * chips]:
            copy.wait()
        cols = slice(part * features, (part + 1) * features)
        own_ref[:, cols] = dot_t(grad[:half, :], weight[part])
        other_ref[:, cols] = dot_t(grad[half:, :], weight[part]).astype(BF16)


def project(slots, grads, stacks):
    chips = 2 * len(grads)
    _, tokens, depth = grads[0].shape
    blocks = sum(stack.shape[0] for stack in stacks)
    features = stacks[0].shape[1]
    shape = (tokens // 2, blocks // chips * features)

    def once(shape):
        return pl.BlockSpec(shape, lambda i: (0,) * len(shape), pipeline_mode=pl.Buffered(1))

    return pl.pallas_call(
        project_kernel,
        grid=(1,),
        in_specs=[pl.BlockSpec(memory_space=pltpu.SMEM)]
        + [pl.BlockSpec(memory_space=pl.ANY)] * (len(grads) + len(stacks)),
        out_specs=[once(shape)] * 2,
        out_shape=[jax.ShapeDtypeStruct(shape, F32), jax.ShapeDtypeStruct(shape, BF16)],
        scratch_shapes=[
            pltpu.VMEM((tokens, chips * depth), BF16),
            pltpu.VMEM((blocks // chips, features, chips * depth), BF16),
            pltpu.SemaphoreType.DMA((chips,)),
            pltpu.SemaphoreType.DMA((blocks,)),
        ],
        compiler_params=pltpu.CompilerParams(vmem_limit_bytes=VMEM_LIMIT),
        cost_estimate=pl.CostEstimate(
            flops=2 * tokens * features * depth * blocks,
            bytes_accessed=12 * 2**20,
            transcendentals=0,
        ),
        name="project",
    )(slots, *[in_hbm(array) for array in (*grads, *stacks)])


def local(queries, keys, values, grad_out, out_weight, lengths):
    rows = queries.shape[0]
    rank = lax.axis_index("dp")
    core = rank % 2
    x, z = rank // 4, (rank // 2) % 2

    def copy(block, groups):
        return jnp.broadcast_to(block, (len(groups[0]), *block.shape))

    def exchange(copies, axis, groups):
        return lax.all_to_all(copies, axis, 0, 0, axis_index_groups=groups, tiled=True)

    groups_x = [[x_ * 4 + zc for x_ in range(4)] for zc in range(4)]
    kept = jnp.where(core == 0, keys, values)
    got = dp_move(jnp.where(core == 0, values, keys), 0, 0, 1)
    chip = jnp.concatenate([kept, got], axis=0)
    chip_pair = jnp.concatenate([chip, dp_move(chip, 0, 1, 0)], axis=0)

    depth = out_weight.shape[1]
    mine = lax.dynamic_slice_in_dim(grad_out, core * depth, depth, 1)
    other = lax.dynamic_slice_in_dim(grad_out, (1 - core) * depth, depth, 1)
    chip_grad = jnp.concatenate([mine, dp_move(other, 0, 0, 1)], axis=0)
    copies, chip_grad = lax.optimization_barrier((copy(chip_pair, groups_x), chip_grad))
    ring = exchange(copies, "dp", groups_x).reshape(-1, HEAD_WIDTH)
    lengths = after(lengths, copies)

    query_pos = rank * rows + jnp.arange(rows, dtype=jnp.int32)
    ends = jnp.cumsum(lengths)[:-1]
    query_start = jnp.max(
        jnp.where(ends[None, :] <= query_pos[:, None], ends[None, :], 0), axis=1
    )
    first = query_start[0] // KEY_BLOCK
    last = query_pos[-1] // KEY_BLOCK
    clear = (query_start[-1] + KEY_BLOCK - 1) // KEY_BLOCK
    block = jnp.arange(16, dtype=jnp.int32)
    place = block // 4 * 4 + jnp.where(block // 2 % 2 == z, 0, 2)
    here = place + jnp.where(block % 2 == core, 0, 1)
    there = place + jnp.where(block % 2 == core, 1, 0)
    scalars = jnp.stack([first, last - first + 1, clear, core])
    info = jnp.concatenate([scalars, here, there]).astype(jnp.int32)
    query_pos, query_start = query_pos[None, :], query_start[None, :]


    def around_x(block):
        return [dp_move(block, step, 0, 0) for step in (1, -1, 2)]

    own = [out_weight[:SPLIT], out_weight[SPLIT:]]
    plane1 = around_x(own[1])
    own0 = after(own[0], chip_pair)
    pair0 = dp_move(own0, 0, 1, 0)
    grad_pair = tensor_move(chip_grad, 1, 0)
    copies = copy(jnp.stack([own0, pair0]), groups_x)
    both_grads = jnp.stack([chip_grad, grad_pair])
    sent = jnp.stack([own[1], *plane1])
    ring, copies, both_grads, sent, info, query_pos, query_start = lax.optimization_barrier(
        (ring, copies, both_grads, sent, info, query_pos, query_start)
    )
    plane0 = exchange(copies, "dp", groups_x).reshape(8, SPLIT, depth)
    swapped = dp_move(ring, 0, 0, 1)
    swapped, held = lax.optimization_barrier((swapped, sent))
    rest = dp_move(held, 0, 1, 0)
    all_grad = [both_grads] + [tensor_move(both_grads, 0, step) for step in (-1, -2, 1)]
    probs, outs = forward(info, query_pos, query_start, queries, ring, swapped)

    t = lax.axis_index("tensor")

    def slot(x_, z_):
        source = 2 * (x_ % 4) + z_
        return (source - t) % 4 * 2 + jnp.where(source // 4 == t // 4, 0, 1)

    near = [slot(x + i, z) for i in (0, -1, 1, 2)]
    slots = [slot(i, z_) for i in range(4) for z_ in (z, 1 - z)]
    slots += near + [slot(x + i, 1 - z) for i in (0, -1, 1, 2)]
    slots = after(jnp.stack(slots).astype(jnp.int32), outs)
    mine, other = project(slots, all_grad, [plane0, sent, rest])
    terms = [mine, dp_move(other, 0, 0, 1)]
    grad_queries, own_sums, other_sums = backward(info, terms, probs, outs, queries, ring, swapped)

    groups = [[2 * i + c for i in range(8)] for c in range(2)]
    chip_sums = (own_sums + dp_move(other_sums, 0, 0, 1).astype(F32)).astype(BF16)
    terms = lax.all_to_all(chip_sums, "dp", 0, 0, axis_index_groups=groups, tiled=True)
    done = jnp.sum(terms.astype(F32), axis=0).astype(BF16)
    return grad_queries, done[:, :HEAD_WIDTH], done[:, HEAD_WIDTH:]


def solution(mesh):
    return jax.shard_map(
        local,
        mesh=mesh,
        in_specs=(
            P("dp", "tensor"),
            P("dp", "tensor"),
            P("dp", "tensor"),
            P("dp", "tensor"),
            P("tensor", "dp"),
            P(),
        ),
        out_specs=(P("dp", "tensor"), P("dp", "tensor"), P("dp", "tensor")),
        check_vma=False,
    )
```

```python
import functools
import math

import jax
import jax.numpy as jnp
from jax import lax
from jax.experimental import pallas as pl
from jax.experimental.pallas import tpu as pltpu
from jax.sharding import PartitionSpec as P

HEAD_WIDTH = 128
KEY_BLOCK = 256
MOST = 2560
SPLIT = 4 * HEAD_WIDTH
PAIR = 2
MASKED = -1e30
SCALE = 1.0 / math.sqrt(HEAD_WIDTH)
LOG2E = 1.0 / math.log(2.0)
BF16 = jnp.bfloat16
F32 = jnp.float32
VMEM_LIMIT = 22 * 2**20

FIRST, COUNT, CLEAR, CORE, TABLE = 0, 1, 2, 3, 4


def dp_move(value, dx, dz, dc):
    pairs = []
    for x in range(4):
        for z in range(2):
            for c in range(2):
                target = ((x + dx) % 4) * 4 + ((z + dz) % 2) * 2 + (c + dc) % 2
                pairs.append((x * 4 + z * 2 + c, target))
    return lax.ppermute(value, "dp", pairs)


def tensor_move(value, dz, dy):
    pairs = []
    for z in range(2):
        for y in range(4):
            pairs.append((z * 4 + y, ((z + dz) % 2) * 4 + (y + dy) % 4))
    return lax.ppermute(value, "tensor", pairs)


def after(value, *others):
    return lax.optimization_barrier((value, *others))[0]


def in_hbm(value):
    return pltpu.with_memory_space_constraint(value, pltpu.HBM)


def dot(left, right):
    return lax.dot_general(left, right, (((1,), (0,)), ((), ())), preferred_element_type=F32)


def dot_t(left, right):
    return lax.dot_general(left, right, (((1,), (1,)), ((), ())), preferred_element_type=F32)


def block_rows(index):
    return pl.ds(pl.multiple_of(index * KEY_BLOCK, KEY_BLOCK), KEY_BLOCK)


def forward_kernel(
    info, pos_ref, start_ref, q_ref, here_ref, there_ref, probs_ref, out_ref, score, keys, vt
):
    first, count = info[FIRST], info[COUNT]
    rows = q_ref.shape[0]
    heads = q_ref.shape[1] // HEAD_WIDTH
    query_t = jnp.concatenate(
        [q_ref[:, h * HEAD_WIDTH : (h + 1) * HEAD_WIDTH].T for h in range(heads)], axis=1
    )
    wide = heads * rows

    def groups(values):
        return values.reshape(KEY_BLOCK // 8, 8, wide)

    @pl.when(pl.program_id(0) == 0)
    def _():
        def turn(index, _):
            here = here_ref[block_rows(info[TABLE + first + index]), :]
            there = there_ref[block_rows(info[TABLE + 16 + first + index]), :]
            keys[block_rows(index), :] = jnp.where(info[CORE] == 0, here, there)
            vt[:, block_rows(index)] = jnp.where(info[CORE] == 0, there, here).T
            return 0
        lax.fori_loop(0, count, turn, 0)

    def product(index):
        return dot(keys[block_rows(index), :], query_t)

    def masked_step(index, top):
        key_pos = (first + index) * KEY_BLOCK + lax.broadcasted_iota(jnp.int32, (KEY_BLOCK, rows), 0)
        live = (key_pos >= start_ref[...]) & (key_pos <= pos_ref[...])
        raw = product(index)
        raw = jnp.concatenate(
            [jnp.where(live, raw[:, h * rows : (h + 1) * rows], MASKED) for h in range(heads)], axis=1
        )
        score[block_rows(index), :] = raw
        return jnp.maximum(top, jnp.max(groups(raw), axis=0))

    def clear_step(index, top):
        raw = product(index)
        score[block_rows(index), :] = raw
        return jnp.maximum(top, jnp.max(groups(raw), axis=0))

    clear = jnp.minimum(info[CLEAR] - first, count - 1)
    top = jnp.full((8, wide), MASKED, F32)
    top = lax.fori_loop(0, clear, masked_step, top)
    top = lax.fori_loop(clear, count - 1, clear_step, top)
    top = masked_step(count - 1, top)
    top = jnp.max(top, axis=0, keepdims=True) * (SCALE * LOG2E)

    def mass_step(index, mass):
        weights = jnp.exp2(score[block_rows(index), :] * (SCALE * LOG2E) - top)
        score[block_rows(index), :] = weights
        return mass + jnp.sum(groups(weights), axis=0)

    mass = lax.fori_loop(0, count, mass_step, jnp.zeros((8, wide), F32))
    share = 1.0 / jnp.sum(mass, axis=0, keepdims=True)
    out_ref[...] = jnp.zeros_like(out_ref)

    def probs_step(index, _):
        probs = (score[block_rows(index), :] * share).astype(BF16)
        probs_ref[block_rows(index), :] = probs
        out_ref[...] += dot(vt[:, block_rows(index)], probs)
        return 0

    lax.fori_loop(0, count, probs_step, 0)


def most_blocks(rows):
    return (MOST + rows - 2) // KEY_BLOCK + 1


def forward(info, query_pos, query_start, queries, here, there):
    rows, width = queries.shape
    heads = width // HEAD_WIDTH
    live = most_blocks(rows) * KEY_BLOCK
    line = pl.BlockSpec((1, rows), lambda h, r: (0, 0))
    return pl.pallas_call(
        forward_kernel,
        grid_spec=pltpu.PrefetchScalarGridSpec(
            num_scalar_prefetch=1,
            grid=(heads // PAIR,),
            in_specs=[
                line,
                line,
                pl.BlockSpec((rows, PAIR * HEAD_WIDTH), lambda h, r: (0, h)),
            ]
            + [pl.BlockSpec(here.shape, lambda h, r: (0, 0), pipeline_mode=pl.Buffered(1))] * 2,
            out_specs=[
                pl.BlockSpec((live, PAIR * rows), lambda h, r: (0, h)),
                pl.BlockSpec((HEAD_WIDTH, PAIR * rows), lambda h, r: (0, h)),
            ],
            scratch_shapes=[
                pltpu.VMEM((live, PAIR * rows), F32),
                pltpu.VMEM((live, HEAD_WIDTH), BF16),
                pltpu.VMEM((HEAD_WIDTH, live), BF16),
            ],
        ),
        out_shape=[
            pltpu.HBM((live, heads * rows), BF16),
            pltpu.HBM((HEAD_WIDTH, heads * rows), F32),
        ],
        compiler_params=pltpu.CompilerParams(vmem_limit_bytes=VMEM_LIMIT),
        cost_estimate=pl.CostEstimate(flops=10**8, bytes_accessed=2**20, transcendentals=0),
        name="forward",
    )(info, query_pos, query_start, in_hbm(queries), here, there)


def backward_kernel(heads, info, *rest):
    (mine, got), rest = rest[:2], rest[2:]
    probs_ref, out_ref, q_ref, here_ref, there_ref, gq_ref, own_ref, other_ref, *scratch = rest
    grad_t, stack, delta, total_q, dscores, other = scratch
    step = pl.program_id(0)
    count = info[COUNT]
    rows = q_ref.shape[0]

    @pl.when(step == 0)
    def _():
        own_ref[...] = jnp.zeros_like(own_ref)
        other[...] = jnp.zeros_like(other)
        total_q[...] = jnp.zeros_like(total_q)
        for h in range(heads):
            cols = slice(h * rows, (h + 1) * rows)
            wide = slice(h * HEAD_WIDTH, (h + 1) * HEAD_WIDTH)
            grad = (mine[:, wide] + got[:, wide].astype(F32)).astype(BF16)
            turned = grad.T
            grad_t[:, cols] = turned
            stack[cols, :HEAD_WIDTH] = q_ref[:, wide]
            stack[cols, HEAD_WIDTH:] = grad
            delta[:, cols] = jnp.sum(turned.astype(F32) * out_ref[:, cols], axis=0, keepdims=True)

    @pl.when(step < count)
    def _():
        block = info[FIRST] + step
        keys_t = jnp.where(info[CORE] == 0, here_ref[...], there_ref[...]).T
        values = jnp.where(info[CORE] == 0, there_ref[...], here_ref[...])
        for h in range(heads):
            cols = slice(h * rows, (h + 1) * rows)
            dprob = dot(values, grad_t[:, cols])
            dscores[:, cols] = (probs_ref[:, cols].astype(F32) * (dprob - delta[:, cols])).astype(BF16)
        total_q[...] += dot(keys_t, dscores[...])
        key_sum = dot(dscores[...], stack[:, :HEAD_WIDTH])
        value_sum = dot(probs_ref[...], stack[:, HEAD_WIDTH:])

        def add(ref):
            ref[block // 2, :, :HEAD_WIDTH] += key_sum * SCALE
            ref[block // 2, :, HEAD_WIDTH:] += value_sum

        pl.when(block % 2 == info[CORE])(lambda: add(own_ref))
        pl.when(block % 2 != info[CORE])(lambda: add(other))

    @pl.when(step == count - 1)
    def _():
        for h in range(heads):
            cols = slice(h * rows, (h + 1) * rows)
            wide = slice(h * HEAD_WIDTH, (h + 1) * HEAD_WIDTH)
            gq_ref[:, wide] = (total_q[:, cols].T * SCALE).astype(BF16)
        other_ref[...] = other[...].astype(BF16)


def backward(info, terms, probs, outs, queries, here, there):
    rows, width = queries.shape
    heads = width // HEAD_WIDTH
    sums = (8, KEY_BLOCK, 2 * HEAD_WIDTH)

    def near(i, r):
        return jnp.minimum(i, r[COUNT] - 1)

    def once(shape):
        return pl.BlockSpec(shape, lambda i, r: (0,) * len(shape), pipeline_mode=pl.Buffered(1))

    return pl.pallas_call(
        functools.partial(backward_kernel, heads),
        grid_spec=pltpu.PrefetchScalarGridSpec(
            num_scalar_prefetch=1,
            grid=(most_blocks(rows),),
            in_specs=[once(term.shape) for term in terms]
            + [
                pl.BlockSpec((KEY_BLOCK, heads * rows), lambda i, r: (near(i, r), 0)),
                once(outs.shape),
                once(queries.shape),
                pl.BlockSpec(
                    (KEY_BLOCK, HEAD_WIDTH), lambda i, r: (r[TABLE + r[FIRST] + near(i, r)], 0)
                ),
                pl.BlockSpec(
                    (KEY_BLOCK, HEAD_WIDTH), lambda i, r: (r[TABLE + 16 + r[FIRST] + near(i, r)], 0)
                ),
            ],
            out_specs=[once((rows, width)), once(sums), once(sums)],
            scratch_shapes=[
                pltpu.VMEM((HEAD_WIDTH, heads * rows), BF16),
                pltpu.VMEM((heads * rows, 2 * HEAD_WIDTH), BF16),
                pltpu.VMEM((1, heads * rows), F32),
                pltpu.VMEM((HEAD_WIDTH, heads * rows), F32),
                pltpu.VMEM((KEY_BLOCK, heads * rows), BF16),
                pltpu.VMEM(sums, F32),
            ],
        ),
        out_shape=[
            jax.ShapeDtypeStruct((rows, width), BF16),
            jax.ShapeDtypeStruct(sums, F32),
            jax.ShapeDtypeStruct(sums, BF16),
        ],
        compiler_params=pltpu.CompilerParams(vmem_limit_bytes=VMEM_LIMIT),
        cost_estimate=pl.CostEstimate(
            flops=8 * 10**9, bytes_accessed=10 * 2**20, transcendentals=0
        ),
        name="backward",
    )(info, *terms, in_hbm(probs), outs, in_hbm(queries), here, there)


def project_kernel(slots, *rest):
    *operands, own_ref, other_ref, grad, weight, sems = rest
    parts, features, width = weight.shape
    count = sems.shape[0]
    pairs = [ref for ref in operands if ref.shape[0] == 2]
    stacks = [ref for ref in operands if ref.shape[0] > 2]
    depth = pairs[0].shape[2]
    chips = width // depth
    sources = [ref.at[j] for ref in stacks for j in range(ref.shape[0])]
    copies = []
    for k in range(count):
        place = pl.ds(pl.multiple_of(slots[k] * depth, depth), depth)
        copies.append(
            pltpu.make_async_copy(sources[k], weight.at[k // chips, :, place], sems.at[k])
        )
    for copy in copies:
        copy.start()
    for i, ref in enumerate(pairs):
        for j in range(2):
            at = (2 * i + j) * depth
            grad[:, at : at + depth] = ref[j]
    half = own_ref.shape[0]
    for part in range(parts):
        for copy in copies[part * chips : (part + 1) * chips]:
            copy.wait()
        cols = slice(part * features, (part + 1) * features)
        own_ref[:, cols] = dot_t(grad[:half, :], weight[part])
        other_ref[:, cols] = dot_t(grad[half:, :], weight[part]).astype(BF16)


def project(slots, grads, stacks):
    chips = 2 * len(grads)
    _, tokens, depth = grads[0].shape
    blocks = sum(stack.shape[0] for stack in stacks)
    features = stacks[0].shape[1]
    shape = (tokens // 2, blocks // chips * features)

    def once(shape):
        return pl.BlockSpec(shape, lambda i: (0,) * len(shape), pipeline_mode=pl.Buffered(1))

    return pl.pallas_call(
        project_kernel,
        grid=(1,),
        in_specs=[pl.BlockSpec(memory_space=pltpu.SMEM)]
        + [once(ref.shape) for ref in grads]
        + [pl.BlockSpec(memory_space=pl.ANY)] * len(stacks),
        out_specs=[once(shape)] * 2,
        out_shape=[jax.ShapeDtypeStruct(shape, F32), jax.ShapeDtypeStruct(shape, BF16)],
        scratch_shapes=[
            pltpu.VMEM((tokens, chips * depth), BF16),
            pltpu.VMEM((blocks // chips, features, chips * depth), BF16),
            pltpu.SemaphoreType.DMA((blocks,)),
        ],
        compiler_params=pltpu.CompilerParams(vmem_limit_bytes=VMEM_LIMIT),
        cost_estimate=pl.CostEstimate(
            flops=2 * tokens * features * depth * blocks,
            bytes_accessed=12 * 2**20,
            transcendentals=0,
        ),
        name="project",
    )(slots, *grads, *[in_hbm(stack) for stack in stacks])


def local(queries, keys, values, grad_out, out_weight, lengths):
    rows = queries.shape[0]
    rank = lax.axis_index("dp")
    core = rank % 2
    x, z = rank // 4, (rank // 2) % 2

    def copy(block, groups):
        return jnp.broadcast_to(block, (len(groups[0]), *block.shape))

    def exchange(copies, axis, groups):
        return lax.all_to_all(copies, axis, 0, 0, axis_index_groups=groups, tiled=True)

    groups_x = [[x_ * 4 + zc for x_ in range(4)] for zc in range(4)]
    kept = jnp.where(core == 0, keys, values)
    got = dp_move(jnp.where(core == 0, values, keys), 0, 0, 1)
    chip = jnp.concatenate([kept, got], axis=0)
    chip_pair = jnp.concatenate([chip, dp_move(chip, 0, 1, 0)], axis=0)

    depth = out_weight.shape[1]
    mine = lax.dynamic_slice_in_dim(grad_out, core * depth, depth, 1)
    other = lax.dynamic_slice_in_dim(grad_out, (1 - core) * depth, depth, 1)
    chip_grad = jnp.concatenate([mine, dp_move(other, 0, 0, 1)], axis=0)
    copies, chip_grad = lax.optimization_barrier((copy(chip_pair, groups_x), chip_grad))
    ring = exchange(copies, "dp", groups_x).reshape(-1, HEAD_WIDTH)
    lengths = after(lengths, copies)

    query_pos = rank * rows + jnp.arange(rows, dtype=jnp.int32)
    ends = jnp.cumsum(lengths)[:-1]
    query_start = jnp.max(
        jnp.where(ends[None, :] <= query_pos[:, None], ends[None, :], 0), axis=1
    )
    first = query_start[0] // KEY_BLOCK
    last = query_pos[-1] // KEY_BLOCK
    clear = (query_start[-1] + KEY_BLOCK - 1) // KEY_BLOCK
    block = jnp.arange(16, dtype=jnp.int32)
    place = block // 4 * 4 + jnp.where(block // 2 % 2 == z, 0, 2)
    here = place + jnp.where(block % 2 == core, 0, 1)
    there = place + jnp.where(block % 2 == core, 1, 0)
    scalars = jnp.stack([first, last - first + 1, clear, core])
    info = jnp.concatenate([scalars, here, there]).astype(jnp.int32)
    query_pos, query_start = query_pos[None, :], query_start[None, :]


    def around_x(block):
        return [dp_move(block, step, 0, 0) for step in (1, -1, 2)]

    own = [out_weight[:SPLIT], out_weight[SPLIT:]]
    plane1 = around_x(own[1])
    own0 = after(own[0], chip_pair)
    pair0 = dp_move(own0, 0, 1, 0)
    grad_pair = tensor_move(chip_grad, 1, 0)
    copies = copy(jnp.stack([own0, pair0]), groups_x)
    both_grads = jnp.stack([chip_grad, grad_pair])
    sent = jnp.stack([own[1], *plane1])
    ring, copies, sent, info, query_pos, query_start = lax.optimization_barrier(
        (ring, copies, sent, info, query_pos, query_start)
    )
    plane0 = exchange(copies, "dp", groups_x).reshape(8, SPLIT, depth)
    swapped = dp_move(ring, 0, 0, 1)
    swapped, held = lax.optimization_barrier((swapped, sent))
    rest = dp_move(held, 0, 1, 0)
    both_grads, later = lax.optimization_barrier((both_grads, queries))
    all_grad = [both_grads] + [tensor_move(both_grads, 0, step) for step in (-1, -2, 1)]
    probs, outs = forward(info, query_pos, query_start, later, ring, swapped)

    t = lax.axis_index("tensor")

    def slot(x_, z_):
        source = 2 * (x_ % 4) + z_
        return (source - t) % 4 * 2 + jnp.where(source // 4 == t // 4, 0, 1)

    near = [slot(x + i, z) for i in (0, -1, 1, 2)]
    slots = [slot(i, z_) for i in range(4) for z_ in (z, 1 - z)]
    slots += near + [slot(x + i, 1 - z) for i in (0, -1, 1, 2)]
    slots = after(jnp.stack(slots).astype(jnp.int32), outs)
    mine, other = project(slots, all_grad, [plane0, sent, rest])
    terms = [mine, dp_move(other, 0, 0, 1)]
    grad_queries, own_sums, other_sums = backward(info, terms, probs, outs, queries, ring, swapped)

    groups = [[2 * i + c for i in range(8)] for c in range(2)]
    chip_sums = (own_sums + dp_move(other_sums, 0, 0, 1).astype(F32)).astype(BF16)
    terms = lax.all_to_all(chip_sums, "dp", 0, 0, axis_index_groups=groups, tiled=True)
    done = jnp.sum(terms.astype(F32), axis=0).astype(BF16)
    return grad_queries, done[:, :HEAD_WIDTH], done[:, HEAD_WIDTH:]


def solution(mesh):
    return jax.shard_map(
        local,
        mesh=mesh,
        in_specs=(
            P("dp", "tensor"),
            P("dp", "tensor"),
            P("dp", "tensor"),
            P("dp", "tensor"),
            P("tensor", "dp"),
            P(),
        ),
        out_specs=(P("dp", "tensor"), P("dp", "tensor"), P("dp", "tensor")),
        check_vma=False,
    )
```

```python
import functools
import math

import jax
import jax.numpy as jnp
from jax import lax
from jax.experimental import pallas as pl
from jax.experimental.pallas import tpu as pltpu
from jax.sharding import PartitionSpec as P

HEAD_WIDTH = 128
KEY_BLOCK = 256
MOST = 2560
SPLIT = 4 * HEAD_WIDTH
PAIR = 2
MASKED = -1e30
SCALE = 1.0 / math.sqrt(HEAD_WIDTH)
LOG2E = 1.0 / math.log(2.0)
BF16 = jnp.bfloat16
F32 = jnp.float32
VMEM_LIMIT = 22 * 2**20

FIRST, COUNT, CLEAR, CORE, TABLE = 0, 1, 2, 3, 4


def dp_move(value, dx, dz, dc):
    pairs = []
    for x in range(4):
        for z in range(2):
            for c in range(2):
                target = ((x + dx) % 4) * 4 + ((z + dz) % 2) * 2 + (c + dc) % 2
                pairs.append((x * 4 + z * 2 + c, target))
    return lax.ppermute(value, "dp", pairs)


def tensor_move(value, dz, dy):
    pairs = []
    for z in range(2):
        for y in range(4):
            pairs.append((z * 4 + y, ((z + dz) % 2) * 4 + (y + dy) % 4))
    return lax.ppermute(value, "tensor", pairs)


def after(value, *others):
    return lax.optimization_barrier((value, *others))[0]


def in_hbm(value):
    return pltpu.with_memory_space_constraint(value, pltpu.HBM)


def dot(left, right):
    return lax.dot_general(left, right, (((1,), (0,)), ((), ())), preferred_element_type=F32)


def dot_t(left, right):
    return lax.dot_general(left, right, (((1,), (1,)), ((), ())), preferred_element_type=F32)


def block_rows(index):
    return pl.ds(pl.multiple_of(index * KEY_BLOCK, KEY_BLOCK), KEY_BLOCK)


def forward_kernel(
    info, pos_ref, start_ref, q_ref, here_ref, there_ref, probs_ref, out_ref, score, keys, vt
):
    first, count = info[FIRST], info[COUNT]
    rows = q_ref.shape[0]
    heads = q_ref.shape[1] // HEAD_WIDTH
    query_t = jnp.concatenate(
        [q_ref[:, h * HEAD_WIDTH : (h + 1) * HEAD_WIDTH].T for h in range(heads)], axis=1
    )
    wide = heads * rows

    def groups(values):
        return values.reshape(KEY_BLOCK // 8, 8, wide)

    @pl.when(pl.program_id(0) == 0)
    def _():
        def turn(index, _):
            here = here_ref[block_rows(info[TABLE + first + index]), :]
            there = there_ref[block_rows(info[TABLE + 16 + first + index]), :]
            keys[block_rows(index), :] = jnp.where(info[CORE] == 0, here, there)
            vt[:, block_rows(index)] = jnp.where(info[CORE] == 0, there, here).T
            return 0
        lax.fori_loop(0, count, turn, 0)

    def product(index):
        return dot(keys[block_rows(index), :], query_t)

    def masked_step(index, top):
        key_pos = (first + index) * KEY_BLOCK + lax.broadcasted_iota(jnp.int32, (KEY_BLOCK, rows), 0)
        live = (key_pos >= start_ref[...]) & (key_pos <= pos_ref[...])
        raw = product(index)
        raw = jnp.concatenate(
            [jnp.where(live, raw[:, h * rows : (h + 1) * rows], MASKED) for h in range(heads)], axis=1
        )
        score[block_rows(index), :] = raw
        return jnp.maximum(top, jnp.max(groups(raw), axis=0))

    def clear_step(index, top):
        raw = product(index)
        score[block_rows(index), :] = raw
        return jnp.maximum(top, jnp.max(groups(raw), axis=0))

    clear = jnp.minimum(info[CLEAR] - first, count - 1)
    top = jnp.full((8, wide), MASKED, F32)
    top = lax.fori_loop(0, clear, masked_step, top)
    top = lax.fori_loop(clear, count - 1, clear_step, top)
    top = masked_step(count - 1, top)
    top = jnp.max(top, axis=0, keepdims=True) * (SCALE * LOG2E)

    def mass_step(index, mass):
        weights = jnp.exp2(score[block_rows(index), :] * (SCALE * LOG2E) - top)
        score[block_rows(index), :] = weights
        return mass + jnp.sum(groups(weights), axis=0)

    mass = lax.fori_loop(0, count, mass_step, jnp.zeros((8, wide), F32))
    share = 1.0 / jnp.sum(mass, axis=0, keepdims=True)
    out_ref[...] = jnp.zeros_like(out_ref)

    def probs_step(index, _):
        probs = (score[block_rows(index), :] * share).astype(BF16)
        probs_ref[block_rows(index), :] = probs
        out_ref[...] += dot(vt[:, block_rows(index)], probs)
        return 0

    lax.fori_loop(0, count, probs_step, 0)


def most_blocks(rows):
    return (MOST + rows - 2) // KEY_BLOCK + 1


def forward(info, query_pos, query_start, queries, here, there):
    rows, width = queries.shape
    heads = width // HEAD_WIDTH
    live = most_blocks(rows) * KEY_BLOCK
    line = pl.BlockSpec((1, rows), lambda h, r: (0, 0))
    return pl.pallas_call(
        forward_kernel,
        grid_spec=pltpu.PrefetchScalarGridSpec(
            num_scalar_prefetch=1,
            grid=(heads // PAIR,),
            in_specs=[
                line,
                line,
                pl.BlockSpec((rows, PAIR * HEAD_WIDTH), lambda h, r: (0, h)),
            ]
            + [pl.BlockSpec(here.shape, lambda h, r: (0, 0), pipeline_mode=pl.Buffered(1))] * 2,
            out_specs=[
                pl.BlockSpec((live, PAIR * rows), lambda h, r: (0, h)),
                pl.BlockSpec((HEAD_WIDTH, PAIR * rows), lambda h, r: (0, h)),
            ],
            scratch_shapes=[
                pltpu.VMEM((live, PAIR * rows), F32),
                pltpu.VMEM((live, HEAD_WIDTH), BF16),
                pltpu.VMEM((HEAD_WIDTH, live), BF16),
            ],
        ),
        out_shape=[
            pltpu.HBM((live, heads * rows), BF16),
            pltpu.HBM((HEAD_WIDTH, heads * rows), F32),
        ],
        compiler_params=pltpu.CompilerParams(vmem_limit_bytes=VMEM_LIMIT),
        cost_estimate=pl.CostEstimate(flops=10**8, bytes_accessed=2**20, transcendentals=0),
        name="forward",
    )(info, query_pos, query_start, in_hbm(queries), here, there)


def backward_kernel(heads, info, *rest):
    (mine, got), rest = rest[:2], rest[2:]
    probs_ref, out_ref, q_ref, here_ref, there_ref, gq_ref, own_ref, other_ref, *scratch = rest
    grad_t, stack, delta, total_q, dscores, other = scratch
    step = pl.program_id(0)
    count = info[COUNT]
    rows = q_ref.shape[0]

    @pl.when(step == 0)
    def _():
        own_ref[...] = jnp.zeros_like(own_ref)
        other[...] = jnp.zeros_like(other)
        total_q[...] = jnp.zeros_like(total_q)
        for h in range(heads):
            cols = slice(h * rows, (h + 1) * rows)
            wide = slice(h * HEAD_WIDTH, (h + 1) * HEAD_WIDTH)
            grad = (mine[:, wide] + got[:, wide].astype(F32)).astype(BF16)
            turned = grad.T
            grad_t[:, cols] = turned
            stack[cols, :HEAD_WIDTH] = q_ref[:, wide]
            stack[cols, HEAD_WIDTH:] = grad
            delta[:, cols] = jnp.sum(turned.astype(F32) * out_ref[:, cols], axis=0, keepdims=True)

    @pl.when(step < count)
    def _():
        block = info[FIRST] + step
        keys_t = jnp.where(info[CORE] == 0, here_ref[...], there_ref[...]).T
        values = jnp.where(info[CORE] == 0, there_ref[...], here_ref[...])
        for h in range(heads):
            cols = slice(h * rows, (h + 1) * rows)
            dprob = dot(values, grad_t[:, cols])
            dscores[:, cols] = (probs_ref[:, cols].astype(F32) * (dprob - delta[:, cols])).astype(BF16)
        total_q[...] += dot(keys_t, dscores[...])
        key_sum = dot(dscores[...], stack[:, :HEAD_WIDTH])
        value_sum = dot(probs_ref[...], stack[:, HEAD_WIDTH:])

        def add(ref):
            ref[block // 2, :, :HEAD_WIDTH] += key_sum * SCALE
            ref[block // 2, :, HEAD_WIDTH:] += value_sum

        pl.when(block % 2 == info[CORE])(lambda: add(own_ref))
        pl.when(block % 2 != info[CORE])(lambda: add(other))

    @pl.when(step == count - 1)
    def _():
        for h in range(heads):
            cols = slice(h * rows, (h + 1) * rows)
            wide = slice(h * HEAD_WIDTH, (h + 1) * HEAD_WIDTH)
            gq_ref[:, wide] = (total_q[:, cols].T * SCALE).astype(BF16)
        other_ref[...] = other[...].astype(BF16)


def backward(info, terms, probs, outs, queries, here, there):
    rows, width = queries.shape
    heads = width // HEAD_WIDTH
    sums = (8, KEY_BLOCK, 2 * HEAD_WIDTH)

    def near(i, r):
        return jnp.minimum(i, r[COUNT] - 1)

    def once(shape):
        return pl.BlockSpec(shape, lambda i, r: (0,) * len(shape), pipeline_mode=pl.Buffered(1))

    return pl.pallas_call(
        functools.partial(backward_kernel, heads),
        grid_spec=pltpu.PrefetchScalarGridSpec(
            num_scalar_prefetch=1,
            grid=(most_blocks(rows),),
            in_specs=[once(term.shape) for term in terms]
            + [
                pl.BlockSpec((KEY_BLOCK, heads * rows), lambda i, r: (near(i, r), 0)),
                once(outs.shape),
                once(queries.shape),
                pl.BlockSpec(
                    (KEY_BLOCK, HEAD_WIDTH), lambda i, r: (r[TABLE + r[FIRST] + near(i, r)], 0)
                ),
                pl.BlockSpec(
                    (KEY_BLOCK, HEAD_WIDTH), lambda i, r: (r[TABLE + 16 + r[FIRST] + near(i, r)], 0)
                ),
            ],
            out_specs=[once((rows, width)), once(sums), once(sums)],
            scratch_shapes=[
                pltpu.VMEM((HEAD_WIDTH, heads * rows), BF16),
                pltpu.VMEM((heads * rows, 2 * HEAD_WIDTH), BF16),
                pltpu.VMEM((1, heads * rows), F32),
                pltpu.VMEM((HEAD_WIDTH, heads * rows), F32),
                pltpu.VMEM((KEY_BLOCK, heads * rows), BF16),
                pltpu.VMEM(sums, F32),
            ],
        ),
        out_shape=[
            jax.ShapeDtypeStruct((rows, width), BF16),
            jax.ShapeDtypeStruct(sums, F32),
            jax.ShapeDtypeStruct(sums, BF16),
        ],
        compiler_params=pltpu.CompilerParams(vmem_limit_bytes=VMEM_LIMIT),
        cost_estimate=pl.CostEstimate(
            flops=8 * 10**9, bytes_accessed=10 * 2**20, transcendentals=0
        ),
        name="backward",
    )(info, *terms, in_hbm(probs), outs, in_hbm(queries), here, there)


def project_kernel(slots, *rest):
    *operands, own_ref, other_ref, grad, weight, sems = rest
    parts, features, width = weight.shape
    count = sems.shape[0]
    pairs = [ref for ref in operands if ref.shape[0] == 2]
    stacks = [ref for ref in operands if ref.shape[0] > 2]
    depth = pairs[0].shape[2]
    chips = width // depth
    sources = [ref.at[j] for ref in stacks for j in range(ref.shape[0])]
    copies = []
    for k in range(count):
        place = pl.ds(pl.multiple_of(slots[k] * depth, depth), depth)
        copies.append(
            pltpu.make_async_copy(sources[k], weight.at[k // chips, :, place], sems.at[k])
        )
    for copy in copies:
        copy.start()
    for i, ref in enumerate(pairs):
        for j in range(2):
            at = (2 * i + j) * depth
            grad[:, at : at + depth] = ref[j]
    half = own_ref.shape[0]
    for part in range(parts):
        for copy in copies[part * chips : (part + 1) * chips]:
            copy.wait()
        cols = slice(part * features, (part + 1) * features)
        own_ref[:, cols] = dot_t(grad[:half, :], weight[part])
        other_ref[:, cols] = dot_t(grad[half:, :], weight[part]).astype(BF16)


def project(slots, grads, stacks):
    chips = 2 * len(grads)
    _, tokens, depth = grads[0].shape
    blocks = sum(stack.shape[0] for stack in stacks)
    features = stacks[0].shape[1]
    shape = (tokens // 2, blocks // chips * features)

    def once(shape):
        return pl.BlockSpec(shape, lambda i: (0,) * len(shape), pipeline_mode=pl.Buffered(1))

    return pl.pallas_call(
        project_kernel,
        grid=(1,),
        in_specs=[pl.BlockSpec(memory_space=pltpu.SMEM)]
        + [once(ref.shape) for ref in grads]
        + [pl.BlockSpec(memory_space=pl.ANY)] * len(stacks),
        out_specs=[once(shape)] * 2,
        out_shape=[jax.ShapeDtypeStruct(shape, F32), jax.ShapeDtypeStruct(shape, BF16)],
        scratch_shapes=[
            pltpu.VMEM((tokens, chips * depth), BF16),
            pltpu.VMEM((blocks // chips, features, chips * depth), BF16),
            pltpu.SemaphoreType.DMA((blocks,)),
        ],
        compiler_params=pltpu.CompilerParams(vmem_limit_bytes=VMEM_LIMIT),
        cost_estimate=pl.CostEstimate(
            flops=2 * tokens * features * depth * blocks,
            bytes_accessed=12 * 2**20,
            transcendentals=0,
        ),
        name="project",
    )(slots, *grads, *[in_hbm(stack) for stack in stacks])


def local(queries, keys, values, grad_out, out_weight, lengths):
    rows = queries.shape[0]
    rank = lax.axis_index("dp")
    core = rank % 2
    x, z = rank // 4, (rank // 2) % 2

    def copy(block, groups):
        return jnp.broadcast_to(block, (len(groups[0]), *block.shape))

    def exchange(copies, axis, groups):
        return lax.all_to_all(copies, axis, 0, 0, axis_index_groups=groups, tiled=True)

    groups_x = [[x_ * 4 + zc for x_ in range(4)] for zc in range(4)]
    kept = jnp.where(core == 0, keys, values)
    got = dp_move(jnp.where(core == 0, values, keys), 0, 0, 1)
    chip = jnp.concatenate([kept, got], axis=0)
    chip_pair = jnp.concatenate([chip, dp_move(chip, 0, 1, 0)], axis=0)

    depth = out_weight.shape[1]
    mine = lax.dynamic_slice_in_dim(grad_out, core * depth, depth, 1)
    other = lax.dynamic_slice_in_dim(grad_out, (1 - core) * depth, depth, 1)
    chip_grad = jnp.concatenate([mine, dp_move(other, 0, 0, 1)], axis=0)
    copies, chip_grad = lax.optimization_barrier((copy(chip_pair, groups_x), chip_grad))
    ring = exchange(copies, "dp", groups_x).reshape(-1, HEAD_WIDTH)
    lengths = after(lengths, copies)

    query_pos = rank * rows + jnp.arange(rows, dtype=jnp.int32)
    ends = jnp.cumsum(lengths)[:-1]
    query_start = jnp.max(
        jnp.where(ends[None, :] <= query_pos[:, None], ends[None, :], 0), axis=1
    )
    first = query_start[0] // KEY_BLOCK
    last = query_pos[-1] // KEY_BLOCK
    clear = (query_start[-1] + KEY_BLOCK - 1) // KEY_BLOCK
    block = jnp.arange(16, dtype=jnp.int32)
    place = block // 4 * 4 + jnp.where(block // 2 % 2 == z, 0, 2)
    here = place + jnp.where(block % 2 == core, 0, 1)
    there = place + jnp.where(block % 2 == core, 1, 0)
    scalars = jnp.stack([first, last - first + 1, clear, core])
    info = jnp.concatenate([scalars, here, there]).astype(jnp.int32)
    query_pos, query_start = query_pos[None, :], query_start[None, :]


    def around_x(block):
        return [dp_move(block, step, 0, 0) for step in (1, -1, 2)]

    own = [out_weight[:SPLIT], out_weight[SPLIT:]]
    plane1 = around_x(own[1])
    own0 = own[0]
    pair0 = dp_move(own0, 0, 1, 0)
    grad_pair = tensor_move(chip_grad, 1, 0)
    copies = copy(jnp.stack([own0, pair0]), groups_x)
    both_grads = jnp.stack([chip_grad, grad_pair])
    sent = jnp.stack([own[1], *plane1])
    ring, copies, both_grads, sent, info, query_pos, query_start = lax.optimization_barrier(
        (ring, copies, both_grads, sent, info, query_pos, query_start)
    )
    plane0 = exchange(copies, "dp", groups_x).reshape(8, SPLIT, depth)
    swapped = dp_move(ring, 0, 0, 1)
    swapped, held = lax.optimization_barrier((swapped, sent))
    rest = dp_move(held, 0, 1, 0)
    all_grad = [both_grads] + [tensor_move(both_grads, 0, step) for step in (-1, -2, 1)]
    probs, outs = forward(info, query_pos, query_start, queries, ring, swapped)

    t = lax.axis_index("tensor")

    def slot(x_, z_):
        source = 2 * (x_ % 4) + z_
        return (source - t) % 4 * 2 + jnp.where(source // 4 == t // 4, 0, 1)

    near = [slot(x + i, z) for i in (0, -1, 1, 2)]
    slots = [slot(i, z_) for i in range(4) for z_ in (z, 1 - z)]
    slots += near + [slot(x + i, 1 - z) for i in (0, -1, 1, 2)]
    slots = after(jnp.stack(slots).astype(jnp.int32), outs)
    mine, other = project(slots, all_grad, [plane0, sent, rest])
    terms = [mine, dp_move(other, 0, 0, 1)]
    grad_queries, own_sums, other_sums = backward(info, terms, probs, outs, queries, ring, swapped)

    groups = [[2 * i + c for i in range(8)] for c in range(2)]
    chip_sums = (own_sums + dp_move(other_sums, 0, 0, 1).astype(F32)).astype(BF16)
    terms = lax.all_to_all(chip_sums, "dp", 0, 0, axis_index_groups=groups, tiled=True)
    done = jnp.sum(terms.astype(F32), axis=0).astype(BF16)
    return grad_queries, done[:, :HEAD_WIDTH], done[:, HEAD_WIDTH:]


def solution(mesh):
    return jax.shard_map(
        local,
        mesh=mesh,
        in_specs=(
            P("dp", "tensor"),
            P("dp", "tensor"),
            P("dp", "tensor"),
            P("dp", "tensor"),
            P("tensor", "dp"),
            P(),
        ),
        out_specs=(P("dp", "tensor"), P("dp", "tensor"), P("dp", "tensor")),
        check_vma=False,
    )
```
